32 devices in a mesh: parts: 2 (over y), patch: 4 (over z), sub: 4 (over x, core).
Axes of the slice: x: 2, y: 2, z: 4, core: 2. Of those that a mesh axis runs over, the one named last changes fastest.
Arguments:
- node_latents: bfloat16 [4096, 512], P(('parts', 'patch', 'sub')), parts along dimension 0, may hold values from -6 to 6
- edge_latents: bfloat16 [16384, 512], P(('parts', 'patch', 'sub')), parts along dimension 0, may hold values from -6 to 6
- coarse_edges: bfloat16 [2048, 512], P(('parts', 'patch', 'sub')), parts along dimension 0, may hold values from -6 to 6
- w_edge_in: bfloat16 [1536, 512], replicated, may hold values from -0.15625 to 0.15625
- w_edge_out: bfloat16 [512, 512], replicated, may hold values from -0.25 to 0.25
- w_node_in: bfloat16 [1024, 512], replicated, may hold values from -0.1875 to 0.1875
- w_node_out: bfloat16 [512, 512], replicated, may hold values from -0.25 to 0.25
- fine_senders: int32 [16384], P(('parts', 'patch', 'sub')), parts along dimension 0, may hold values from 0 to 159
- fine_receivers: int32 [16384], P(('parts', 'patch', 'sub')), parts along dimension 0, may hold values from -1 to 127, as said below
- halo_lists: int32 [32, 2, 16], P(('parts', 'patch', 'sub')), parts along dimension 0, may hold values from 0 to 127, as said below
- coarse_senders: int32 [2048], P(('parts', 'patch', 'sub')), parts along dimension 0, may hold values from 0 to 63
- coarse_receivers: int32 [2048], P(('parts', 'patch', 'sub')), parts along dimension 0, may hold values from 0 to 63
Outputs:
- new_nodes: bfloat16 [4096, 512], P(('parts', 'patch', 'sub')), parts along dimension 0
- new_edges: bfloat16 [16384, 512], P(('parts', 'patch', 'sub')), parts along dimension 0
- new_coarse: bfloat16 [2048, 512], P(('parts', 'patch', 'sub')), parts along dimension 0
The draws below stay inside these ranges and needn't reach their ends.
There are 2 independent parts, one for each index of `parts`. The reference program is written for one: setup_inputs(seed, part) draws one part's arguments, and reference() takes and returns one part's arrays. A program takes and returns all parts, laid end to end along the dimension named above; an argument that names none is the same for every part. Nothing has to cross between parts.
Inputs may be any that keep to these rules, and one draw needn't show every extreme that they name: `fine_receivers`: in each device's block of 512 slots the used slots come first and name a local row; the rest hold -1. At least half of a device's slots are used, and some device uses all of them. `halo_lists`: each of a device's two lists holds 16 distinct local rows.
All inputs are finite; a program needn't handle non-finite values.
Results may differ from the reference program's by a relative error of at most 0.0053.
Values may be sent and summed in bfloat16 or wider, within the bound.
No kernel may reach another device: no remote copies, remote signals or barrier semaphores. Data moves between devices by JAX's collectives and lax.ppermute only.
A program may use at most 64 MiB of HBM per device.

```python
import jax
import jax.numpy as jnp
from jax import lax

D = 512
NODE_DEV = 128
HALO = 16
CO_DEV = 4
GROUP = 16
EDGE_DEV = 512
CEDGE_DEV = 64
NODES = 2048
EDGES = 8192
CEDGES = 1024
N_PATCH = 4
N_SUB = 4


def draw_fine_receivers(key, part):
    key_counts = jax.random.fold_in(key, 11)
    key_full = jax.random.fold_in(key, 12)
    key_rows = jax.random.fold_in(key, 13)
    counts = jax.random.randint(key_counts, (GROUP,), EDGE_DEV // 2, EDGE_DEV + 1)
    full = jax.random.randint(key_full, (), 0, GROUP)
    counts = jnp.where(jnp.arange(GROUP) == full, EDGE_DEV, counts)
    rows = jax.random.randint(key_rows, (GROUP, EDGE_DEV), 0, NODE_DEV)
    slots = jnp.arange(EDGE_DEV)[None, :]
    return jnp.where(slots < counts[:, None], rows, -1).reshape(GROUP * EDGE_DEV).astype(jnp.int32)


def draw_halo_lists(key, part):
    keys = jax.random.split(jax.random.fold_in(key, 21), GROUP * 2)
    chosen = jax.vmap(lambda single: jax.random.permutation(single, NODE_DEV)[:HALO])(keys)
    return chosen.reshape(GROUP, 2, HALO).astype(jnp.int32)


def whole_part_ids(key):
    return jax.random.randint(key, (GROUP * CEDGE_DEV,), 0, GROUP * CO_DEV).astype(jnp.int32)


def draw_coarse_senders(key, part):
    return whole_part_ids(jax.random.fold_in(key, 31))


def draw_coarse_receivers(key, part):
    return whole_part_ids(jax.random.fold_in(key, 32))


def plant(result, stream_key, least, high):
    index_at = [jax.random.randint(jax.random.fold_in(stream_key, axis), (), 0, length) for axis, length in enumerate(result.shape)]
    longest = result.shape.index(max(result.shape))
    neighbour = index_at[:longest] + [(index_at[longest] + 1) % result.shape[longest]] + index_at[longest + 1:]
    return result.at[tuple(index_at)].set(least).at[tuple(neighbour)].set(high)


def steps_of(own_key, dims, cuts, least, high):
    def one(position, shards_of):
        steps = jax.random.uniform(jax.random.fold_in(jax.random.fold_in(own_key, 6), position), (shards_of,), jnp.float32, least / len(cuts), high / len(cuts))
        return jnp.repeat(jnp.exp(steps), dims[position] // shards_of).reshape((-1,) + (1,) * (len(dims) - position - 1))

    factor_of = one(*cuts[0])
    for cut in cuts[1:]:
        factor_of = factor_of * one(*cut)
    return factor_of


def gaussian(stream_key, dims, spread, most, pieces=(), kind=jnp.bfloat16):
    array = spread * jax.random.normal(stream_key, dims, jnp.float32)
    if pieces:
        array = array * steps_of(stream_key, dims, pieces, -0.22, 0.18)
    return jnp.clip(array, -most, most).astype(kind)


def setup_inputs(seed: int = 0, part: int = 0) -> dict:
    key_list = jax.random.split(jax.random.key(seed), 13)
    part_splits = jax.random.split(jax.random.fold_in(key_list[12], part), 13)
    node_latents = gaussian(part_splits[0], (NODES, D), 1.0, 6.0, ((0, 16),))
    edge_latents = gaussian(part_splits[1], (EDGES, D), 1.0, 6.0, ((0, 16),))
    coarse_edges = gaussian(part_splits[2], (CEDGES, D), 1.0, 6.0, ((0, 16),))
    w_edge_in = gaussian(key_list[3], (3 * D, D), (3 * D) ** -0.5, 0.15625)
    w_edge_out = gaussian(key_list[4], (D, D), D ** -0.5, 0.25)
    w_node_in = gaussian(key_list[5], (2 * D, D), (2 * D) ** -0.5, 0.1875)
    w_node_out = gaussian(key_list[6], (D, D), D ** -0.5, 0.25)
    fine_senders = plant(jax.random.randint(part_splits[7], (EDGES,), 0, NODE_DEV + 2 * HALO), jax.random.fold_in(part_splits[7], 1), 0, (NODE_DEV + 2 * HALO) - 1).astype(jnp.int32)
    fine_receivers = draw_fine_receivers(jax.random.fold_in(jax.random.fold_in(key_list[12], part), 71), part)
    halo_lists = draw_halo_lists(jax.random.fold_in(jax.random.fold_in(key_list[12], part), 71), part)
    coarse_senders = draw_coarse_senders(jax.random.fold_in(jax.random.fold_in(key_list[12], part), 71), part)
    coarse_receivers = draw_coarse_receivers(jax.random.fold_in(jax.random.fold_in(key_list[12], part), 71), part)
    return dict(node_latents=node_latents, edge_latents=edge_latents, coarse_edges=coarse_edges, w_edge_in=w_edge_in, w_edge_out=w_edge_out, w_node_in=w_node_in, w_node_out=w_node_out, fine_senders=fine_senders, fine_receivers=fine_receivers, halo_lists=halo_lists, coarse_senders=coarse_senders, coarse_receivers=coarse_receivers)


def norm_rows(values):
    mean = lax.optimization_barrier(jnp.mean(values, axis=-1, keepdims=True))
    centred = values - mean
    return centred * lax.rsqrt(lax.optimization_barrier(jnp.mean(centred * centred, axis=-1, keepdims=True)) + 1e-05)

def edge_delta(inputs, w_edge_in, w_edge_out):
    pre = jnp.dot(inputs, w_edge_in, preferred_element_type=jnp.float32)
    hidden = jax.nn.silu(pre).astype(jnp.bfloat16)
    return norm_rows(jnp.dot(hidden, w_edge_out, preferred_element_type=jnp.float32))

def reference(node_latents, edge_latents, coarse_edges, w_edge_in, w_edge_out, w_node_in, w_node_out, fine_senders, fine_receivers, halo_lists, coarse_senders, coarse_receivers):
    group = N_PATCH * N_SUB
    nodes = node_latents.reshape(group, NODE_DEV, D)
    sent_next = jax.vmap(lambda block, lists: block[lists[0]])(nodes, halo_lists)
    sent_prev = jax.vmap(lambda block, lists: block[lists[1]])(nodes, halo_lists)
    extended = jnp.concatenate([jnp.roll(sent_next, 1, axis=0), nodes, jnp.roll(sent_prev, -1, axis=0)], axis=1)
    coarse_latents = nodes[:, :CO_DEV].reshape(group * CO_DEV, D)

    def per_device(items):
        ext, own, edges, cedges, senders, receivers, csend, crecv = items
        fine_in = jnp.concatenate([edges, ext[senders], own[jnp.maximum(receivers, 0)]], axis=1)
        coarse_in = jnp.concatenate([cedges, coarse_latents[csend], coarse_latents[crecv]], axis=1)
        delta = edge_delta(jnp.concatenate([fine_in, coarse_in], axis=0), w_edge_in, w_edge_out)
        valid = (receivers >= 0)[:, None]
        fine_new = (edges.astype(jnp.float32) + jnp.where(valid, delta[:EDGE_DEV], 0.0)).astype(jnp.bfloat16)
        coarse_new = (cedges.astype(jnp.float32) + delta[EDGE_DEV:]).astype(jnp.bfloat16)
        onehot = (jnp.arange(NODE_DEV, dtype=jnp.int32)[:, None] == receivers[None, :]).astype(jnp.bfloat16)
        fine_agg = jnp.dot(onehot, fine_new, preferred_element_type=jnp.float32)
        return (fine_new, coarse_new, fine_agg)
    fine_new, coarse_new, fine_agg = lax.map(per_device, (extended, nodes, edge_latents.reshape(group, EDGE_DEV, D), coarse_edges.reshape(group, CEDGE_DEV, D), fine_senders.reshape(group, EDGE_DEV), fine_receivers.reshape(group, EDGE_DEV), coarse_senders.reshape(group, CEDGE_DEV), coarse_receivers.reshape(group, CEDGE_DEV)))
    coarse_flat = coarse_new.reshape(group * CEDGE_DEV, D)
    coarse_agg = jax.ops.segment_sum(coarse_flat.astype(jnp.float32), coarse_receivers, group * CO_DEV)
    aggregate = fine_agg.at[:, :CO_DEV].add(coarse_agg.reshape(group, CO_DEV, D))
    aggregate = aggregate.reshape(group * NODE_DEV, D).astype(jnp.bfloat16)
    pre = jnp.dot(jnp.concatenate([node_latents, aggregate], axis=1), w_node_in, preferred_element_type=jnp.float32)
    hidden = jax.nn.silu(pre).astype(jnp.bfloat16)
    delta = norm_rows(jnp.dot(hidden, w_node_out, preferred_element_type=jnp.float32))
    new_nodes = (node_latents.astype(jnp.float32) + delta).astype(jnp.bfloat16)
    return (new_nodes, fine_new.reshape(group * EDGE_DEV, D), coarse_flat)
```

```python
import jax
import jax.numpy as jnp
from jax import lax
from jax.experimental import pallas as pl
from jax.experimental.pallas import tpu as pltpu
from jax.sharding import PartitionSpec as P

CO_DEV = 4
GROUP_AXES = ("patch", "sub")
TOP = 16
MIB = 1 << 20


def from_behind(value, axis, by):
    devices = lax.axis_size(axis)
    return lax.ppermute(value, axis, [(i, (i + by) % devices) for i in range(devices)])


def dot(a, b):
    return jnp.dot(a, b, preferred_element_type=jnp.float32)


def dot_t(a, b):
    return lax.dot_general(a, b, (((0,), (0,)), ((), ())), preferred_element_type=jnp.float32)


def onehot_t(rows, ids):
    at = lax.broadcasted_iota(jnp.int32, (rows, ids.shape[1]), 0)
    return jnp.where(at == ids, 1.0, 0.0).astype(jnp.bfloat16)


def silu(v):
    return v / (1.0 + jnp.exp(-v))


def norm_parts(values):
    mean = jnp.mean(values, axis=-1, keepdims=True)
    centred = values - mean
    return centred, lax.rsqrt(jnp.mean(centred * centred, axis=-1, keepdims=True) + 1e-05)


def whole(shape):
    return pl.BlockSpec(shape, lambda: (0,) * len(shape))


def select_kernel(nodes_ref, lists_ref, next_ref, prev_ref, heads_ref):
    nodes = nodes_ref[...]
    count = nodes.shape[0]
    lists = lists_ref[0]
    next_ref[...] = dot_t(onehot_t(count, lists[0:1, :]), nodes).astype(jnp.bfloat16)
    prev_ref[...] = dot_t(onehot_t(count, lists[1:2, :]), nodes).astype(jnp.bfloat16)
    copies = heads_ref.shape[0]
    pick = lax.broadcasted_iota(jnp.int32, (copies, count), 0) % CO_DEV
    pick = jnp.where(pick == lax.broadcasted_iota(jnp.int32, (copies, count), 1), 1.0, 0.0)
    heads_ref[...] = dot(pick.astype(jnp.bfloat16), nodes).astype(jnp.bfloat16)


def coarse_kernel(lat_ref, edges_ref, send_ref, recv_ref, w_in_ref, w_out_ref, new_ref, sums_ref):
    lat = lat_ref[...]
    width = lat.shape[1]
    edges = edges_ref[...]
    count = lat.shape[0]
    picks = onehot_t(count, recv_ref[...])
    senders = dot_t(onehot_t(count, send_ref[...]), lat).astype(jnp.bfloat16)
    receivers = dot_t(picks, lat).astype(jnp.bfloat16)
    pre = (
        dot(edges, w_in_ref[0:width, :])
        + dot(senders, w_in_ref[width : 2 * width, :])
        + dot(receivers, w_in_ref[2 * width :, :])
    )
    hidden = silu(pre).astype(jnp.bfloat16)
    centred, scale = norm_parts(dot(hidden, w_out_ref[...]))
    new = (edges.astype(jnp.float32) + centred * scale).astype(jnp.bfloat16)
    new_ref[...] = new
    sums_ref[...] = dot(picks, new).astype(jnp.bfloat16)


def fine_kernel(
    prev_ref, nodes_ref, next_ref, edges_ref, send_ref, recv_ref, w_in_ref, w_out_ref, wn_in_ref, wn_out_ref,
    new_ref, agg_ref, pre_ref, nodes_out_ref,
):
    nodes = nodes_ref[...]
    width = nodes.shape[1]
    count = nodes.shape[0]
    extended = jnp.concatenate([prev_ref[...], nodes, next_ref[...]], axis=0)
    ones = jnp.ones((count, 128), jnp.bfloat16)
    agg = jnp.zeros((count, width), jnp.float32)
    step = 128
    for at in range(0, edges_ref.shape[0], step):
        part = pl.ds(at, step)
        edges = edges_ref[part, :]
        picks = onehot_t(count, recv_ref[:, part])
        senders = dot_t(onehot_t(extended.shape[0], send_ref[:, part]), extended).astype(jnp.bfloat16)
        receivers = dot_t(picks, nodes).astype(jnp.bfloat16)
        valid = dot_t(picks, ones)[:, 0:1]
        pre = (
            dot(edges, w_in_ref[0:width, :])
            + dot(senders, w_in_ref[width : 2 * width, :])
            + dot(receivers, w_in_ref[2 * width :, :])
        )
        hidden = silu(pre).astype(jnp.bfloat16)
        centred, scale = norm_parts(dot(hidden, w_out_ref[...]))
        new = (edges.astype(jnp.float32) + centred * (scale * valid)).astype(jnp.bfloat16)
        new_ref[part, :] = new
        agg = agg + dot(picks, new)
    pre = dot(nodes, wn_in_ref[0:width, :])
    agg_ref[...] = agg[0:TOP, :]
    pre_ref[...] = pre[0:TOP, :]
    pre = pre + dot(agg.astype(jnp.bfloat16), wn_in_ref[width:, :])
    hidden = silu(pre).astype(jnp.bfloat16)
    centred, scale = norm_parts(dot(hidden, wn_out_ref[...]))
    nodes_out_ref[...] = (nodes.astype(jnp.float32) + centred * scale).astype(jnp.bfloat16)


def top_kernel(sums_ref, agg_ref, pre_ref, nodes_ref, wn_in_ref, wn_out_ref, rest_ref, out_ref):
    del rest_ref
    terms = sums_ref.shape[0]
    at = lax.broadcasted_iota(jnp.int32, (TOP, terms), 1) % CO_DEV
    pick = jnp.where(at == lax.broadcasted_iota(jnp.int32, (TOP, terms), 0), 1.0, 0.0).astype(jnp.bfloat16)
    agg = (agg_ref[...] + dot(pick, sums_ref[...])).astype(jnp.bfloat16)
    pre = pre_ref[...] + dot(agg, wn_in_ref[...])
    hidden = silu(pre).astype(jnp.bfloat16)
    centred, scale = norm_parts(dot(hidden, wn_out_ref[...]))
    out_ref[...] = (nodes_ref[...].astype(jnp.float32) + centred * scale).astype(jnp.bfloat16)


def body(
    node_latents,
    edge_latents,
    coarse_edges,
    w_edge_in,
    w_edge_out,
    w_node_in,
    w_node_out,
    fine_senders,
    fine_receivers,
    halo_lists,
    coarse_senders,
    coarse_receivers,
):
    bf16, f32 = jnp.bfloat16, jnp.float32
    count, width = node_latents.shape
    halo = halo_lists.shape[2]
    group = lax.axis_size(GROUP_AXES)
    shape = jax.ShapeDtypeStruct
    params = pltpu.CompilerParams(vmem_limit_bytes=24 * MIB)

    to_next, to_prev, heads = pl.pallas_call(
        select_kernel,
        out_shape=(
            shape((halo, width), bf16),
            shape((halo, width), bf16),
            shape((group * CO_DEV, width), bf16),
        ),
        compiler_params=params,
        name="select",
    )(node_latents, halo_lists)
    coarse_latents = lax.all_to_all(heads, GROUP_AXES, 0, 0, tiled=True)
    from_prev = from_behind(to_next, GROUP_AXES, 1)
    from_next = from_behind(to_prev, GROUP_AXES, -1)

    new_coarse, sums = pl.pallas_call(
        coarse_kernel,
        out_shape=(shape(coarse_edges.shape, bf16), shape((group * CO_DEV, width), bf16)),
        compiler_params=params,
        name="coarse",
    )(coarse_latents, coarse_edges, coarse_senders[None, :], coarse_receivers[None, :], w_edge_in, w_edge_out)
    sums = lax.all_to_all(sums, GROUP_AXES, 0, 0, tiled=True)

    new_edges, agg, pre, rest = pl.pallas_call(
        fine_kernel,
        out_shape=(
            shape(edge_latents.shape, bf16),
            shape((TOP, width), f32),
            shape((TOP, width), f32),
            shape((count, width), bf16),
        ),
        cost_estimate=pl.CostEstimate(flops=2 * 512 * 3000 * 512, bytes_accessed=6 * MIB, transcendentals=0),
        compiler_params=params,
        name="fine",
    )(
        from_prev, node_latents, from_next, edge_latents, fine_senders[None, :], fine_receivers[None, :],
        w_edge_in, w_edge_out, w_node_in, w_node_out,
    )

    new_nodes = pl.pallas_call(
        top_kernel,
        grid=(1,),
        out_shape=shape((count, width), bf16),
        in_specs=[
            pl.BlockSpec(sums.shape, lambda i: (0, 0)),
            pl.BlockSpec((TOP, width), lambda i: (0, 0)),
            pl.BlockSpec((TOP, width), lambda i: (0, 0)),
            pl.BlockSpec((TOP, width), lambda i: (0, 0)),
            pl.BlockSpec((width, width), lambda i: (1, 0)),
            pl.BlockSpec((width, width), lambda i: (0, 0)),
            pl.BlockSpec(memory_space=pl.ANY),
        ],
        out_specs=pl.BlockSpec((TOP, width), lambda i: (0, 0)),
        input_output_aliases={6: 0},
        compiler_params=params,
        name="top",
    )(sums, agg, pre, node_latents, w_node_in, w_node_out, rest)
    return (new_nodes, new_edges, new_coarse)


def solution(mesh):
    rows = P(("parts", "patch", "sub"), None)
    ids = P(("parts", "patch", "sub"))
    in_specs = (
        rows, rows, rows, P(), P(), P(), P(), ids, ids, P(("parts", "patch", "sub"), None, None), ids, ids,
    )
    return jax.shard_map(body, mesh=mesh, in_specs=in_specs, out_specs=(rows, rows, rows), check_vma=False)
```

```python
import jax
import jax.numpy as jnp
from jax import lax
from jax.experimental import pallas as pl
from jax.experimental.pallas import tpu as pltpu
from jax.sharding import PartitionSpec as P

CO_DEV = 4
GROUP_AXES = ("patch", "sub")
TOP = 16
MIB = 1 << 20
ANY = pl.BlockSpec(memory_space=pl.ANY)
VMEM = pl.BlockSpec(memory_space=pltpu.VMEM)


def from_behind(value, axis, by):
    devices = lax.axis_size(axis)
    return lax.ppermute(value, axis, [(i, (i + by) % devices) for i in range(devices)])


def dot(a, b):
    return jnp.dot(a, b, preferred_element_type=jnp.float32)


def dot_t(a, b):
    return lax.dot_general(a, b, (((0,), (0,)), ((), ())), preferred_element_type=jnp.float32)


def onehot_t(rows, ids):
    at = lax.broadcasted_iota(jnp.int32, (rows, ids.shape[1]), 0)
    return jnp.where(at == ids, 1.0, 0.0).astype(jnp.bfloat16)


def silu(v):
    half = 0.5 * v
    return half + half * jnp.tanh(half)


def norm_parts(values):
    mean = jnp.mean(values, axis=-1, keepdims=True)
    centred = values - mean
    return centred, lax.rsqrt(jnp.mean(centred * centred, axis=-1, keepdims=True) + 1e-05)


def select_kernel(nodes_hbm, lists_hbm, nodes_ref, next_ref, prev_ref, heads_ref, lists_ref, sems):
    copies = [
        pltpu.make_async_copy(nodes_hbm, nodes_ref, sems.at[0]),
        pltpu.make_async_copy(lists_hbm, lists_ref, sems.at[1]),
    ]
    for copy in copies:
        copy.start()
    for copy in copies:
        copy.wait()
    nodes = nodes_ref[...]
    count = nodes.shape[0]
    lists = lists_ref[0]
    next_ref[...] = dot_t(onehot_t(count, lists[0:1, :]), nodes).astype(jnp.bfloat16)
    prev_ref[...] = dot_t(onehot_t(count, lists[1:2, :]), nodes).astype(jnp.bfloat16)
    for at in range(heads_ref.shape[0]):
        heads_ref[at] = nodes[0:CO_DEV, :]


def early_kernel(*refs):
    moved = 10
    hbm, rest = refs[:moved], refs[moved:]
    nodes_ref, vmem, rest = rest[0], rest[1 : moved + 1], rest[moved + 1 :]
    fine_ref, coarse_ref, node_ref, sems = rest
    copies = [pltpu.make_async_copy(a, b, sems.at[i]) for i, (a, b) in enumerate(zip(hbm, vmem))]
    for copy in copies:
        copy.start()
    w_in, edges_ref, cedges_ref, recv_ref, wn_in = vmem[:5]
    width = nodes_ref.shape[1]
    nodes = nodes_ref[...]
    count = nodes.shape[0]
    for i in (2, 0):
        copies[i].wait()
    coarse_ref[...] = dot(cedges_ref[...], w_in[0:width, :])
    for i in (3, 1):
        copies[i].wait()
    step = 128
    for at in range(0, edges_ref.shape[0], step):
        part = pl.ds(at, step)
        receivers = dot_t(onehot_t(count, recv_ref[:, part]), nodes).astype(jnp.bfloat16)
        fine_ref[part, :] = dot(edges_ref[part, :], w_in[0:width, :]) + dot(receivers, w_in[2 * width :, :])
    copies[4].wait()
    node_ref[...] = dot(nodes, wn_in[0:width, :])
    for copy in copies[5:]:
        copy.wait()


def coarse_kernel(lat_ref, edges_ref, part_ref, send_ref, recv_ref, w_in_ref, w_out_ref, new_ref, sums_ref):
    lat = lat_ref[...]
    count, width = lat.shape
    picks = onehot_t(count, recv_ref[...])
    senders = dot_t(onehot_t(count, send_ref[...]), lat).astype(jnp.bfloat16)
    receivers = dot_t(picks, lat).astype(jnp.bfloat16)
    pre = (
        part_ref[...]
        + dot(senders, w_in_ref[width : 2 * width, :])
        + dot(receivers, w_in_ref[2 * width :, :])
    )
    hidden = silu(pre).astype(jnp.bfloat16)
    centred, scale = norm_parts(dot(hidden, w_out_ref[...]))
    new = (edges_ref[...].astype(jnp.float32) + centred * scale).astype(jnp.bfloat16)
    new_ref[...] = new
    sums = dot(picks, new).astype(jnp.bfloat16)
    for at in range(sums_ref.shape[0]):
        sums_ref[at] = sums[at * CO_DEV : (at + 1) * CO_DEV, :]


def fine_kernel(
    prev_ref, nodes_ref, next_ref, edges_ref, part_ref, npart_ref, send_ref, recv_ref, w_in_ref, w_out_ref, wn_in_ref,
    wn_out_ref, new_ref, agg_ref, nodes_out_ref,
):
    nodes = nodes_ref[...]
    count, width = nodes.shape
    extended = jnp.concatenate([prev_ref[...], nodes, next_ref[...]], axis=0)
    ones = jnp.ones((count, 128), jnp.bfloat16)
    agg = jnp.zeros((count, width), jnp.float32)
    step = 128
    for at in range(0, edges_ref.shape[0], step):
        part = pl.ds(at, step)
        picks = onehot_t(count, recv_ref[:, part])
        senders = dot_t(onehot_t(extended.shape[0], send_ref[:, part]), extended).astype(jnp.bfloat16)
        valid = dot_t(picks, ones)[:, 0:1]
        hidden = silu(part_ref[part, :] + dot(senders, w_in_ref[width : 2 * width, :])).astype(jnp.bfloat16)
        centred, scale = norm_parts(dot(hidden, w_out_ref[...]))
        new = (edges_ref[part, :].astype(jnp.float32) + centred * (scale * valid)).astype(jnp.bfloat16)
        new_ref[part, :] = new
        agg = agg + dot(picks, new)
    agg_ref[...] = agg[0:TOP, :]
    pre = npart_ref[...] + dot(agg.astype(jnp.bfloat16), wn_in_ref[width:, :])
    hidden = silu(pre).astype(jnp.bfloat16)
    centred, scale = norm_parts(dot(hidden, wn_out_ref[...]))
    nodes_out_ref[...] = (nodes.astype(jnp.float32) + centred * scale).astype(jnp.bfloat16)


def top_kernel(sums_ref, agg_ref, npart_ref, nodes_ref, wn_in_ref, wn_out_ref, rest_ref, out_ref):
    del rest_ref
    terms = sums_ref.shape[0]
    width = agg_ref.shape[1]
    at = lax.broadcasted_iota(jnp.int32, (TOP, terms), 1) % CO_DEV
    pick = jnp.where(at == lax.broadcasted_iota(jnp.int32, (TOP, terms), 0), 1.0, 0.0).astype(jnp.bfloat16)
    agg = (agg_ref[...] + dot(pick, sums_ref[...])).astype(jnp.bfloat16)
    pre = npart_ref[0:TOP, :] + dot(agg, wn_in_ref[width:, :])
    hidden = silu(pre).astype(jnp.bfloat16)
    centred, scale = norm_parts(dot(hidden, wn_out_ref[...]))
    out_ref[...] = (nodes_ref[0:TOP, :].astype(jnp.float32) + centred * scale).astype(jnp.bfloat16)


def in_hbm(*arrays):
    return [pltpu.with_memory_space_constraint(a, pltpu.HBM) for a in arrays]


def cost(flops, moved=0):
    return pl.CostEstimate(flops=flops, bytes_accessed=moved, transcendentals=0)


def body(
    node_latents,
    edge_latents,
    coarse_edges,
    w_edge_in,
    w_edge_out,
    w_node_in,
    w_node_out,
    fine_senders,
    fine_receivers,
    halo_lists,
    coarse_senders,
    coarse_receivers,
):
    bf16, f32 = jnp.bfloat16, jnp.float32
    count, width = node_latents.shape
    edge_count = edge_latents.shape[0]
    halo = halo_lists.shape[2]
    group = lax.axis_size(GROUP_AXES)
    shape = jax.ShapeDtypeStruct
    like = lambda a: shape(a.shape, a.dtype)
    params = pltpu.CompilerParams(vmem_limit_bytes=16 * MIB)

    nodes, to_next, to_prev, heads = pl.pallas_call(
        select_kernel,
        out_shape=(
            like(node_latents),
            shape((halo, width), bf16),
            shape((halo, width), bf16),
            shape((group, CO_DEV, width), bf16),
        ),
        in_specs=[ANY, ANY],
        out_specs=[VMEM] * 4,
        scratch_shapes=[pltpu.VMEM(halo_lists.shape, jnp.int32), pltpu.SemaphoreType.DMA((2,))],
        compiler_params=params,
        name="select",
    )(*in_hbm(node_latents, halo_lists))
    coarse_latents = lax.all_to_all(heads, GROUP_AXES, 0, 0).reshape(group * CO_DEV, width)
    from_prev = from_behind(to_next, GROUP_AXES, 1)
    from_next = from_behind(to_prev, GROUP_AXES, -1)

    moved = (
        w_edge_in, edge_latents, coarse_edges, fine_receivers[None, :], w_node_in,
        w_edge_out, w_node_out, fine_senders[None, :], coarse_senders[None, :], coarse_receivers[None, :],
    )
    early = pl.pallas_call(
        early_kernel,
        out_shape=tuple(like(a) for a in moved)
        + (shape((edge_count, width), f32), shape(coarse_edges.shape, f32), shape((count, width), f32)),
        in_specs=[ANY] * len(moved) + [VMEM],
        out_specs=[VMEM] * (len(moved) + 3),
        scratch_shapes=[pltpu.SemaphoreType.DMA((len(moved),))],
        compiler_params=params,
        cost_estimate=cost(2 * edge_count * width * 3 * width, 5 * MIB),
        name="early",
    )(*in_hbm(*moved), nodes)
    w_in, edges, cedges, recv, wn_in, w_out, wn_out, send, csend, crecv, fine_part, coarse_part, node_part = early

    new_coarse, sums = pl.pallas_call(
        coarse_kernel,
        out_shape=(like(coarse_edges), shape((group, CO_DEV, width), bf16)),
        compiler_params=params,
        name="coarse",
    )(coarse_latents, cedges, coarse_part, csend, crecv, w_in, w_out)
    sums = lax.all_to_all(sums, GROUP_AXES, 0, 0).reshape(group * CO_DEV, width)

    new_edges, agg, rest = pl.pallas_call(
        fine_kernel,
        out_shape=(like(edge_latents), shape((TOP, width), f32), like(node_latents)),
        cost_estimate=cost(2 * edge_count * width * 3 * width, 4 * MIB),
        compiler_params=params,
        name="fine",
    )(from_prev, nodes, from_next, edges, fine_part, node_part, send, recv, w_in, w_out, wn_in, wn_out)

    new_nodes = pl.pallas_call(
        top_kernel,
        grid=(1,),
        out_shape=like(node_latents),
        in_specs=[VMEM] * 6 + [ANY],
        out_specs=pl.BlockSpec((TOP, width), lambda i: (0, 0)),
        input_output_aliases={6: 0},
        compiler_params=params,
        name="top",
    )(sums, agg, node_part, nodes, wn_in, wn_out, rest)
    return (new_nodes, new_edges, new_coarse)


def solution(mesh):
    rows = P(("parts", "patch", "sub"), None)
    ids = P(("parts", "patch", "sub"))
    in_specs = (
        rows, rows, rows, P(), P(), P(), P(), ids, ids, P(("parts", "patch", "sub"), None, None), ids, ids,
    )
    return jax.shard_map(body, mesh=mesh, in_specs=in_specs, out_specs=(rows, rows, rows), check_vma=False)
```

```python
import functools

import jax
import jax.numpy as jnp
from jax import lax
from jax.experimental import pallas as pl
from jax.experimental.pallas import tpu as pltpu
from jax.sharding import PartitionSpec as P

CO_DEV = 4
GROUP_AXES = ("patch", "sub")
TOP = 16
STEP = 128
MIB = 1 << 20
ANY = pl.BlockSpec(memory_space=pl.ANY)
VMEM = pl.BlockSpec(memory_space=pltpu.VMEM)
BF16, F32 = jnp.bfloat16, jnp.float32


def shift(value, by):
    devices = lax.axis_size(GROUP_AXES)
    return lax.ppermute(value, GROUP_AXES, [(i, (i + by) % devices) for i in range(devices)])


def swap(value, mask):
    devices = lax.axis_size(GROUP_AXES)
    return lax.ppermute(value, GROUP_AXES, [(i, i ^ mask) for i in range(devices)])


def dot(a, b):
    return jnp.dot(a, b, preferred_element_type=F32)


def dot_t(a, b):
    return lax.dot_general(a, b, (((0,), (0,)), ((), ())), preferred_element_type=F32)


def onehot_t(rows, ids):
    at = lax.broadcasted_iota(jnp.int32, (rows, ids.shape[1]), 0)
    return jnp.where(at == ids, 1.0, 0.0).astype(BF16)


def silu(v):
    half = 0.5 * v
    return half + half * jnp.tanh(half)


def norm_parts(values):
    mean = jnp.mean(values, axis=-1, keepdims=True)
    centred = values - mean
    return centred, lax.rsqrt(jnp.mean(centred * centred, axis=-1, keepdims=True) + 1e-05)


def head_kernel(nodes_hbm, head_ref, rows_ref, sem):
    copy = pltpu.make_async_copy(nodes_hbm.at[pl.ds(0, TOP)], rows_ref, sem)
    copy.start()
    copy.wait()
    head_ref[...] = rows_ref[0:CO_DEV, :]


def load_kernel(masks, moved, *refs):
    hbm, rest = refs[:moved], refs[moved + 1 :]
    vmem, (next_ref, prev_ref, gather_ref, picks_ref, sems) = rest[:moved], rest[moved:]
    copies = [pltpu.make_async_copy(a, b, sems.at[i]) for i, (a, b) in enumerate(zip(hbm, vmem))]
    for copy in copies:
        copy.start()
    nodes_ref, lists_ref, csend_ref, crecv_ref = vmem[:4]
    for copy in copies[:2]:
        copy.wait()
    nodes = nodes_ref[...]
    count = nodes.shape[0]
    lists = lists_ref[0]
    next_ref[...] = dot_t(onehot_t(count, lists[0:1, :]), nodes).astype(BF16)
    prev_ref[...] = dot_t(onehot_t(count, lists[1:2, :]), nodes).astype(BF16)
    for copy in copies[2:4]:
        copy.wait()
    rows, ids = picks_ref.shape
    at = lax.broadcasted_iota(jnp.int32, (rows, ids), 0)
    block = at // CO_DEV
    owner = jnp.full((rows, ids), lax.axis_index(GROUP_AXES), jnp.int32)
    for bit, mask in enumerate(masks):
        owner = owner ^ (((block >> bit) & 1) * mask)
    node = owner * CO_DEV + at % CO_DEV
    send = jnp.where(node == csend_ref[...], 1.0, 0.0).astype(BF16)
    recv = jnp.where(node == crecv_ref[...], 1.0, 0.0).astype(BF16)
    picks_ref[...] = recv
    across = lax.broadcasted_iota(jnp.int32, (rows, rows), 0) == lax.broadcasted_iota(jnp.int32, (rows, rows), 1)
    eye = jnp.where(across, 1.0, 0.0).astype(BF16)
    gather_ref[0:ids, :] = dot_t(send, eye).astype(BF16)
    gather_ref[ids:, :] = dot_t(recv, eye).astype(BF16)
    for copy in copies[4:]:
        copy.wait()


def join_kernel(*refs):
    a, b, out = refs[0], refs[1], refs[-1]
    out[...] = jnp.concatenate([a[...].astype(F32), b[...].astype(F32)], axis=0).astype(BF16)


def add_kernel(*refs):
    kept, got, keep_ref, send_ref = refs[0], refs[1], refs[-2], refs[-1]
    value = kept[...] + got[...].astype(F32)
    half = value.shape[0] // 2
    keep_ref[...] = value[0:half]
    send_ref[...] = value[half:].astype(BF16)


def part_kernel(nodes_ref, edges_ref, cedges_ref, recv_ref, w_in_ref, wn_in_ref, after, fine_ref, coarse_ref, node_ref):
    nodes = nodes_ref[...]
    count, width = nodes.shape
    coarse_ref[...] = dot(cedges_ref[...], w_in_ref[0:width, :])
    for at in range(0, edges_ref.shape[0], STEP):
        rows = pl.ds(at, STEP)
        receivers = dot_t(onehot_t(count, recv_ref[:, rows]), nodes).astype(BF16)
        fine_ref[rows, :] = dot(edges_ref[rows, :], w_in_ref[0:width, :]) + dot(receivers, w_in_ref[2 * width :, :])
    node_ref[...] = dot(nodes, wn_in_ref[0:width, :])


def coarse_kernel(low_ref, high_ref, edges_ref, part_ref, gather_ref, picks_ref, w_in_ref, w_out_ref, new_ref, keep_ref, send_ref):
    count, width = edges_ref.shape
    lat = jnp.concatenate([low_ref[...], high_ref[...]], axis=0)
    ends = dot(gather_ref[...], lat).astype(BF16)
    pre = (
        part_ref[...]
        + dot(ends[0:count], w_in_ref[width : 2 * width, :])
        + dot(ends[count:], w_in_ref[2 * width :, :])
    )
    hidden = silu(pre).astype(BF16)
    centred, scale = norm_parts(dot(hidden, w_out_ref[...]))
    new = (edges_ref[...].astype(F32) + centred * scale).astype(BF16)
    new_ref[...] = new
    sums = dot(picks_ref[...], new)
    half = keep_ref.shape[0]
    keep_ref[...] = sums[0:half]
    send_ref[...] = sums[half:].astype(BF16)


def fine_rows(at, prev_ref, nodes_ref, next_ref, edges_ref, part_ref, send_ref, recv_ref, w_in_ref, w_out_ref, new_ref):
    nodes = nodes_ref[...]
    count, width = nodes.shape
    extended = jnp.concatenate([prev_ref[...], nodes, next_ref[...]], axis=0)
    ones = jnp.ones((count, 128), BF16)
    total = jnp.zeros((count, width), F32)
    for to in range(0, new_ref.shape[0], STEP):
        rows = pl.ds(at + to, STEP)
        picks = onehot_t(count, recv_ref[:, rows])
        senders = dot_t(onehot_t(extended.shape[0], send_ref[:, rows]), extended).astype(BF16)
        valid = dot_t(picks, ones)[:, 0:1]
        hidden = silu(part_ref[rows, :] + dot(senders, w_in_ref[width : 2 * width, :])).astype(BF16)
        centred, scale = norm_parts(dot(hidden, w_out_ref[...]))
        new = (edges_ref[rows, :].astype(F32) + centred * (scale * valid)).astype(BF16)
        new_ref[pl.ds(to, STEP), :] = new
        total = total + dot(picks, new)
    return total


def first_kernel(*refs):
    ins, (after, new_ref, agg_ref) = refs[:9], refs[9:]
    agg_ref[...] = fine_rows(0, *ins, new_ref)


def second_kernel(*refs):
    ins, (first_ref, sum_ref, after, out_hbm, new_ref, agg_ref, sem) = refs[:9], refs[9:]
    half = first_ref.shape[0]
    copy = pltpu.make_async_copy(first_ref, out_hbm.at[pl.ds(0, half)], sem)
    copy.start()
    agg_ref[...] = sum_ref[...] + fine_rows(half, *ins, new_ref)
    copy.wait()


def node_kernel(new_ref, agg_ref, part_ref, nodes_ref, wn_in_ref, wn_out_ref, edges_hbm, after, out_hbm, out_ref, sem):
    half = new_ref.shape[0]
    copy = pltpu.make_async_copy(new_ref, out_hbm.at[pl.ds(half, half)], sem)
    copy.start()
    width = nodes_ref.shape[1]
    pre = part_ref[...] + dot(agg_ref[...].astype(BF16), wn_in_ref[width:, :])
    hidden = silu(pre).astype(BF16)
    centred, scale = norm_parts(dot(hidden, wn_out_ref[...]))
    out_ref[...] = (nodes_ref[...].astype(F32) + centred * scale).astype(BF16)
    copy.wait()


def top_kernel(kept_ref, got_ref, agg_ref, part_ref, nodes_ref, wn_in_ref, wn_out_ref, rest_ref, out_ref):
    width = agg_ref.shape[1]
    sums = kept_ref[...] + got_ref[...].astype(F32)
    sums = jnp.concatenate([sums, jnp.zeros((TOP - CO_DEV, width), F32)], axis=0)
    agg = (agg_ref[0:TOP, :] + sums).astype(BF16)
    pre = part_ref[0:TOP, :] + dot(agg, wn_in_ref[width:, :])
    hidden = silu(pre).astype(BF16)
    centred, scale = norm_parts(dot(hidden, wn_out_ref[...]))
    out_ref[...] = (nodes_ref[0:TOP, :].astype(F32) + centred * scale).astype(BF16)


def in_hbm(*arrays):
    return [pltpu.with_memory_space_constraint(a, pltpu.HBM) for a in arrays]


def cost(flops, moved=0):
    return pl.CostEstimate(flops=flops, bytes_accessed=moved, transcendentals=0)


def call(kernel, name, outs, ins, out_specs=None, scratch=(), hbm=(), flops=0, **more):
    return pl.pallas_call(
        kernel,
        out_shape=outs,
        in_specs=[ANY if i in hbm else VMEM for i in range(len(ins))],
        out_specs=[VMEM] * len(outs) if out_specs is None else out_specs,
        scratch_shapes=scratch,
        compiler_params=pltpu.CompilerParams(vmem_limit_bytes=16 * MIB),
        cost_estimate=cost(flops),
        name=name,
        **more,
    )(*ins)


def body(
    node_latents,
    edge_latents,
    coarse_edges,
    w_edge_in,
    w_edge_out,
    w_node_in,
    w_node_out,
    fine_senders,
    fine_receivers,
    halo_lists,
    coarse_senders,
    coarse_receivers,
):
    count, width = node_latents.shape
    edge_count = edge_latents.shape[0]
    half = edge_count // 2
    cedge_count = coarse_edges.shape[0]
    halo = halo_lists.shape[2]
    group = lax.axis_size(GROUP_AXES)
    assert group & (group - 1) == 0
    masks = [1 << bit for bit in reversed(range(group.bit_length() - 1))]
    coarse_count = group * CO_DEV
    shape = jax.ShapeDtypeStruct
    like = lambda a: shape(a.shape, a.dtype)
    square = 2 * width * width
    dma = pltpu.SemaphoreType.DMA

    (head,) = call(
        head_kernel, "head", (shape((CO_DEV, width), BF16),), in_hbm(node_latents), hbm=(0,),
        scratch=[pltpu.VMEM((TOP, width), BF16), dma(())],
    )
    moved = (
        node_latents, halo_lists, coarse_senders[None, :], coarse_receivers[None, :], w_edge_in, coarse_edges,
        edge_latents, fine_receivers[None, :], w_node_in, w_edge_out, w_node_out, fine_senders[None, :],
    )
    loaded = call(
        functools.partial(load_kernel, masks, len(moved)),
        "load",
        tuple(like(a) for a in moved)
        + (
            shape((halo, width), BF16),
            shape((halo, width), BF16),
            shape((2 * cedge_count, coarse_count), BF16),
            shape((coarse_count, cedge_count), BF16),
        ),
        in_hbm(*moved) + [head],
        hbm=range(len(moved) + 1),
        scratch=[dma((len(moved),))],
        flops=edge_count * square,
    )
    nodes, _, _, _, w_in, cedges, edges, recv, wn_in, w_out, wn_out, send, to_next, to_prev, gather, picks = loaded

    lat, got = head, swap(head, masks[0])
    from_prev, from_next = shift(to_next, 1), shift(to_prev, -1)
    fine = None
    for place, mask in enumerate(masks[1:]):
        after = []
        if place == 1:
            after = [fine_part]
        if place == 2:
            after = [first]
        (lat,) = call(
            join_kernel, "join", (shape((2 * lat.shape[0], width), BF16),), [lat, got] + after,
            hbm=range(2, 2 + len(after)),
        )
        got = swap(lat, mask)
        if place == 0:
            fine_part, coarse_part, node_part = call(
                part_kernel, "part",
                (shape((edge_count, width), F32), shape((cedge_count, width), F32), shape((count, width), F32)),
                [nodes, edges, cedges, recv, w_in, wn_in, lat], hbm=(6,), flops=2 * edge_count * square,
            )
            fine = [from_prev, nodes, from_next, edges, fine_part, send, recv, w_in, w_out]
        if place == 1:
            first, agg = call(
                first_kernel, "first", (shape((half, width), BF16), shape((count, width), F32)),
                fine + [lat], hbm=(9,), flops=2 * half * square,
            )

    keep_rows = coarse_count // 2
    new_coarse, keep, out = call(
        coarse_kernel, "coarse",
        (like(coarse_edges), shape((keep_rows, width), F32), shape((keep_rows, width), BF16)),
        [lat, got, cedges, coarse_part, gather, picks, w_in, w_out], flops=3 * cedge_count * square,
    )

    got = swap(out, masks[-1])
    new_edges = rest = None
    for place, mask in enumerate(reversed(masks[:-1])):
        after = []
        if place == 1:
            after = [second]
        if place == 2:
            after = [agg]
        keep_rows //= 2
        keep, out = call(
            add_kernel, "add", (shape((keep_rows, width), F32), shape((keep_rows, width), BF16)),
            [keep, got] + after, hbm=range(2, 2 + len(after)),
        )
        got = swap(out, mask)
        if place == 0:
            new_edges, second, agg = call(
                second_kernel, "second", (like(edge_latents), shape((half, width), BF16), shape((count, width), F32)),
                fine + [first, agg, out], hbm=(11,), out_specs=[ANY, VMEM, VMEM], scratch=[dma(())],
                flops=2 * half * square,
            )
        if place == 1:
            new_edges, rest = call(
                node_kernel, "nodes", (like(edge_latents), like(node_latents)),
                [second, agg, node_part, nodes, wn_in, wn_out, new_edges, out], hbm=(6, 7), out_specs=[ANY, VMEM],
                scratch=[dma(())], flops=2 * count * square, input_output_aliases={6: 0},
            )

    new_nodes = pl.pallas_call(
        top_kernel,
        grid=(1,),
        out_shape=like(node_latents),
        in_specs=[VMEM] * 7 + [ANY],
        out_specs=pl.BlockSpec((TOP, width), lambda i: (0, 0)),
        input_output_aliases={7: 0},
        compiler_params=pltpu.CompilerParams(vmem_limit_bytes=16 * MIB),
        name="top",
    )(keep, got, agg, node_part, nodes, wn_in, wn_out, rest)
    return (new_nodes, new_edges, new_coarse)


def solution(mesh):
    rows = P(("parts", "patch", "sub"), None)
    ids = P(("parts", "patch", "sub"))
    in_specs = (
        rows, rows, rows, P(), P(), P(), P(), ids, ids, P(("parts", "patch", "sub"), None, None), ids, ids,
    )
    return jax.shard_map(body, mesh=mesh, in_specs=in_specs, out_specs=(rows, rows, rows), check_vma=False)
```

```python
import jax
import jax.numpy as jnp
from jax import lax
from jax.experimental import pallas as pl
from jax.experimental.pallas import tpu as pltpu
from jax.sharding import PartitionSpec as P

CO_DEV = 4
GROUP_AXES = ("patch", "sub")
TOP = 16
STEP = 128
MIB = 1 << 20
ANY = pl.BlockSpec(memory_space=pl.ANY)
VMEM = pl.BlockSpec(memory_space=pltpu.VMEM)
BF16, F32 = jnp.bfloat16, jnp.float32


def shift(value, by):
    devices = lax.axis_size(GROUP_AXES)
    return lax.ppermute(value, GROUP_AXES, [(i, (i + by) % devices) for i in range(devices)])


def dot(a, b):
    return jnp.dot(a, b, preferred_element_type=F32)


def dot_t(a, b):
    return lax.dot_general(a, b, (((0,), (0,)), ((), ())), preferred_element_type=F32)


def onehot_t(rows, ids):
    at = lax.broadcasted_iota(jnp.int32, (rows, ids.shape[1]), 0)
    return jnp.where(at == ids, 1.0, 0.0).astype(BF16)


def silu(v):
    half = 0.5 * v
    return half + half * jnp.tanh(half)


def norm_parts(values):
    mean = jnp.mean(values, axis=-1, keepdims=True)
    centred = values - mean
    return centred, lax.rsqrt(jnp.mean(centred * centred, axis=-1, keepdims=True) + 1e-05)


def head_kernel(nodes_hbm, heads_ref, rows_ref, sem):
    copy = pltpu.make_async_copy(nodes_hbm.at[pl.ds(0, TOP)], rows_ref, sem)
    copy.start()
    copy.wait()
    head = rows_ref[0:CO_DEV, :]
    for at in range(heads_ref.shape[0]):
        heads_ref[at] = head


def start_copies(sources, targets, sems):
    copies = [pltpu.make_async_copy(a, b, sems.at[i]) for i, (a, b) in enumerate(zip(sources, targets))]
    for copy in copies:
        copy.start()
    return copies


def load_kernel(
    nodes_hbm, lists_hbm, cedges_hbm, w_in_hbm, csend_hbm, crecv_hbm, w_out_hbm, after,
    nodes_ref, cedges_ref, w_ends_ref, w_out_ref, next_ref, prev_ref, gather_ref, picks_ref, part_ref,
    lists_ref, w_self_ref, csend_ref, crecv_ref, sems,
):
    width = nodes_ref.shape[1]
    copies = start_copies(
        [
            nodes_hbm, lists_hbm, cedges_hbm, w_in_hbm.at[pl.ds(0, width)], csend_hbm, crecv_hbm,
            w_in_hbm.at[pl.ds(width, 2 * width)], w_out_hbm,
        ],
        [nodes_ref, lists_ref, cedges_ref, w_self_ref, csend_ref, crecv_ref, w_ends_ref, w_out_ref],
        sems,
    )
    for copy in copies[:2]:
        copy.wait()
    nodes = nodes_ref[...]
    count = nodes.shape[0]
    lists = lists_ref[0]
    next_ref[...] = dot_t(onehot_t(count, lists[0:1, :]), nodes).astype(BF16)
    prev_ref[...] = dot_t(onehot_t(count, lists[1:2, :]), nodes).astype(BF16)
    for copy in copies[2:6]:
        copy.wait()
    part_ref[...] = dot(cedges_ref[...], w_self_ref[...])
    rows, ids = picks_ref.shape
    send, recv = onehot_t(rows, csend_ref[...]), onehot_t(rows, crecv_ref[...])
    picks_ref[...] = recv
    across = lax.broadcasted_iota(jnp.int32, (rows, rows), 0) == lax.broadcasted_iota(jnp.int32, (rows, rows), 1)
    eye = jnp.where(across, 1.0, 0.0).astype(BF16)
    gather_ref[0:ids, :] = dot_t(send, eye).astype(BF16)
    gather_ref[ids:, :] = dot_t(recv, eye).astype(BF16)
    for copy in copies[6:]:
        copy.wait()


def coarse_kernel(lat_ref, edges_ref, part_ref, gather_ref, picks_ref, w_ends_ref, w_out_ref, new_ref, sums_ref):
    count, width = edges_ref.shape
    blocks = lat_ref.shape[0]
    lat = jnp.concatenate([lat_ref[at].astype(F32) for at in range(blocks)], axis=0).astype(BF16)
    ends = dot(gather_ref[...], lat).astype(BF16)
    pre = part_ref[...] + dot(ends[0:count], w_ends_ref[0:width, :]) + dot(ends[count:], w_ends_ref[width:, :])
    hidden = silu(pre).astype(BF16)
    centred, scale = norm_parts(dot(hidden, w_out_ref[...]))
    new = (edges_ref[...].astype(F32) + centred * scale).astype(BF16)
    new_ref[...] = new
    sums = dot(picks_ref[...], new).astype(BF16)
    for at in range(blocks):
        sums_ref[at] = sums[at * CO_DEV : (at + 1) * CO_DEV, :]


def fine_kernel(
    prev_ref, nodes_ref, next_ref, w_ends_ref, w_out_ref,
    edges_hbm, w_in_hbm, send_hbm, recv_hbm, wn_in_hbm, wn_out_hbm, after,
    new_hbm, out_ref, agg_ref, npart_ref, wn_agg_ref, wn_out_ref,
    edges_ref, w_self_ref, send_ref, recv_ref, wn_self_ref, new_ref, sems, out_sems,
):
    nodes = nodes_ref[...]
    count, width = nodes.shape
    copies = start_copies(
        [
            send_hbm, recv_hbm, edges_hbm, w_in_hbm.at[pl.ds(0, width)],
            wn_in_hbm.at[pl.ds(0, width)], wn_in_hbm.at[pl.ds(width, width)], wn_out_hbm,
        ],
        [send_ref, recv_ref, edges_ref, w_self_ref, wn_self_ref, wn_agg_ref, wn_out_ref],
        sems,
    )
    extended = jnp.concatenate([prev_ref[...], nodes, next_ref[...]], axis=0)
    ones = jnp.ones((count, 128), BF16)
    total = jnp.zeros((count, width), F32)
    for copy in copies[:4]:
        copy.wait()
    outs = []
    for at in range(0, edges_ref.shape[0], STEP):
        rows = pl.ds(at, STEP)
        picks = onehot_t(count, recv_ref[:, rows])
        senders = dot_t(onehot_t(extended.shape[0], send_ref[:, rows]), extended).astype(BF16)
        receivers = dot_t(picks, nodes).astype(BF16)
        valid = dot_t(picks, ones)[:, 0:1]
        edges = edges_ref[rows, :]
        pre = dot(edges, w_self_ref[...]) + dot(senders, w_ends_ref[0:width, :]) + dot(receivers, w_ends_ref[width:, :])
        hidden = silu(pre).astype(BF16)
        centred, scale = norm_parts(dot(hidden, w_out_ref[...]))
        new = (edges.astype(F32) + centred * (scale * valid)).astype(BF16)
        new_ref[rows, :] = new
        copy = pltpu.make_async_copy(new_ref.at[rows], new_hbm.at[rows], out_sems.at[at // STEP])
        copy.start()
        outs.append(copy)
        total = total + dot(picks, new)
    agg_ref[...] = total[0:TOP]
    for copy in copies[4:]:
        copy.wait()
    pre = dot(nodes, wn_self_ref[...])
    npart_ref[...] = pre[0:TOP]
    pre = pre + dot(total.astype(BF16), wn_agg_ref[...])
    hidden = silu(pre).astype(BF16)
    centred, scale = norm_parts(dot(hidden, wn_out_ref[...]))
    out_ref[...] = (nodes.astype(F32) + centred * scale).astype(BF16)
    for copy in outs:
        copy.wait()


def top_kernel(got_ref, agg_ref, part_ref, nodes_ref, wn_agg_ref, wn_out_ref, rest_ref, out_ref):
    width = agg_ref.shape[1]
    sums = got_ref[0].astype(F32)
    for at in range(1, got_ref.shape[0]):
        sums = sums + got_ref[at].astype(F32)
    sums = jnp.concatenate([sums, jnp.zeros((TOP - CO_DEV, width), F32)], axis=0)
    agg = (agg_ref[...] + sums).astype(BF16)
    hidden = silu(part_ref[...] + dot(agg, wn_agg_ref[...])).astype(BF16)
    centred, scale = norm_parts(dot(hidden, wn_out_ref[...]))
    out_ref[...] = (nodes_ref[0:TOP, :].astype(F32) + centred * scale).astype(BF16)


def in_hbm(*arrays):
    return [pltpu.with_memory_space_constraint(a, pltpu.HBM) for a in arrays]


def cost(flops, moved=0):
    return pl.CostEstimate(flops=flops, bytes_accessed=moved, transcendentals=0)


def call(kernel, name, outs, ins, out_specs=None, scratch=(), hbm=(), flops=0, **more):
    return pl.pallas_call(
        kernel,
        out_shape=outs,
        in_specs=[ANY if i in hbm else VMEM for i in range(len(ins))],
        out_specs=[VMEM] * len(outs) if out_specs is None else out_specs,
        scratch_shapes=scratch,
        compiler_params=pltpu.CompilerParams(vmem_limit_bytes=16 * MIB),
        cost_estimate=cost(flops),
        name=name,
        **more,
    )(*ins)


def body(
    node_latents,
    edge_latents,
    coarse_edges,
    w_edge_in,
    w_edge_out,
    w_node_in,
    w_node_out,
    fine_senders,
    fine_receivers,
    halo_lists,
    coarse_senders,
    coarse_receivers,
):
    count, width = node_latents.shape
    edge_count = edge_latents.shape[0]
    cedge_count = coarse_edges.shape[0]
    halo = halo_lists.shape[2]
    group = lax.axis_size(GROUP_AXES)
    coarse_count = group * CO_DEV
    shape = jax.ShapeDtypeStruct
    like = lambda a: shape(a.shape, a.dtype)
    vmem = pltpu.VMEM
    dma = pltpu.SemaphoreType.DMA
    square = 2 * width * width
    blocks = shape((group, CO_DEV, width), BF16)
    ids = lambda a: a[None, :]

    (heads,) = call(
        head_kernel, "head", (blocks,), in_hbm(node_latents), hbm=(0,), scratch=[vmem((TOP, width), BF16), dma(())],
    )
    lat = lax.all_to_all(heads, GROUP_AXES, 0, 0)
    nodes, cedges, w_ends, w_out, to_next, to_prev, gather, picks, coarse_part = call(
        load_kernel,
        "load",
        (
            like(node_latents),
            like(coarse_edges),
            shape((2 * width, width), BF16),
            like(w_edge_out),
            shape((halo, width), BF16),
            shape((halo, width), BF16),
            shape((2 * cedge_count, coarse_count), BF16),
            shape((coarse_count, cedge_count), BF16),
            shape((cedge_count, width), F32),
        ),
        in_hbm(node_latents, halo_lists, coarse_edges, w_edge_in, ids(coarse_senders), ids(coarse_receivers), w_edge_out)
        + [heads],
        hbm=range(8),
        scratch=[
            vmem(halo_lists.shape, jnp.int32), vmem((width, width), BF16),
            vmem((1, cedge_count), jnp.int32), vmem((1, cedge_count), jnp.int32), dma((8,)),
        ],
        flops=edge_count * square,
    )
    from_prev, from_next = shift(to_next, 1), shift(to_prev, -1)
    new_coarse, sums = call(
        coarse_kernel, "coarse", (like(coarse_edges), blocks),
        [lat, cedges, coarse_part, gather, picks, w_ends, w_out], flops=3 * cedge_count * square,
    )
    got = lax.all_to_all(sums, GROUP_AXES, 0, 0)
    new_edges, rest, agg, node_part, wn_agg, wn_out = call(
        fine_kernel,
        "fine",
        (
            like(edge_latents),
            like(node_latents),
            shape((TOP, width), F32),
            shape((TOP, width), F32),
            shape((width, width), BF16),
            like(w_node_out),
        ),
        [from_prev, nodes, from_next, w_ends, w_out]
        + in_hbm(edge_latents, w_edge_in, ids(fine_senders), ids(fine_receivers), w_node_in, w_node_out)
        + [sums],
        hbm=range(5, 12),
        out_specs=[ANY] + [VMEM] * 5,
        scratch=[
            vmem(edge_latents.shape, BF16), vmem((width, width), BF16), vmem((1, edge_count), jnp.int32),
            vmem((1, edge_count), jnp.int32), vmem((width, width), BF16), vmem(edge_latents.shape, BF16), dma((7,)),
            dma((edge_count // STEP,)),
        ],
        flops=4 * edge_count * square,
    )
    new_nodes = pl.pallas_call(
        top_kernel,
        grid=(1,),
        out_shape=like(node_latents),
        in_specs=[VMEM] * 6 + [ANY],
        out_specs=pl.BlockSpec((TOP, width), lambda i: (0, 0)),
        input_output_aliases={6: 0},
        compiler_params=pltpu.CompilerParams(vmem_limit_bytes=16 * MIB),
        name="top",
    )(got, agg, node_part, nodes, wn_agg, wn_out, rest)
    return (new_nodes, new_edges, new_coarse)


def solution(mesh):
    rows = P(("parts", "patch", "sub"), None)
    ids = P(("parts", "patch", "sub"))
    in_specs = (
        rows, rows, rows, P(), P(), P(), P(), ids, ids, P(("parts", "patch", "sub"), None, None), ids, ids,
    )
    return jax.shard_map(body, mesh=mesh, in_specs=in_specs, out_specs=(rows, rows, rows), check_vma=False)
```

```python
import jax
import jax.numpy as jnp
from jax import lax
from jax.experimental import pallas as pl
from jax.experimental.pallas import tpu as pltpu
from jax.sharding import PartitionSpec as P

CO_DEV = 4
GROUP_AXES = ("patch", "sub")
TOP = 16
STEP = 128
MIB = 1 << 20
ANY = pl.BlockSpec(memory_space=pl.ANY)
VMEM = pl.BlockSpec(memory_space=pltpu.VMEM)
BF16, F32 = jnp.bfloat16, jnp.float32


def shift(value, by):
    devices = lax.axis_size(GROUP_AXES)
    return lax.ppermute(value, GROUP_AXES, [(i, (i + by) % devices) for i in range(devices)])


def dot(a, b):
    return jnp.dot(a, b, preferred_element_type=F32)


def dot_t(a, b):
    return lax.dot_general(a, b, (((0,), (0,)), ((), ())), preferred_element_type=F32)


def onehot_t(rows, ids):
    at = lax.broadcasted_iota(jnp.int32, (rows, ids.shape[1]), 0)
    return jnp.where(at == ids, 1.0, 0.0).astype(BF16)


def silu(v):
    half = 0.5 * v
    return half + half * jnp.tanh(half)


def norm_parts(values):
    mean = jnp.mean(values, axis=-1, keepdims=True)
    centred = values - mean
    return centred, lax.rsqrt(jnp.mean(centred * centred, axis=-1, keepdims=True) + 1e-05)


def head_kernel(nodes_hbm, heads_ref, rows_ref, sem):
    copy = pltpu.make_async_copy(nodes_hbm.at[pl.ds(0, TOP)], rows_ref, sem)
    copy.start()
    copy.wait()
    head = rows_ref[0:CO_DEV, :]
    for at in range(heads_ref.shape[0]):
        heads_ref[at] = head


def pass_kernel(sums_ref, prev_ref, next_ref, out_ref):
    pass


def start_copies(sources, targets, sems):
    copies = [pltpu.make_async_copy(a, b, sems.at[i]) for i, (a, b) in enumerate(zip(sources, targets))]
    for copy in copies:
        copy.start()
    return copies


def load_kernel(
    nodes_hbm, lists_hbm, cedges_hbm, w_in_hbm, csend_hbm, crecv_hbm, w_out_hbm, after,
    nodes_ref, cedges_ref, w_ends_ref, w_out_ref, next_ref, prev_ref, gather_ref, picks_ref, part_ref,
    lists_ref, w_self_ref, csend_ref, crecv_ref, sems,
):
    width = nodes_ref.shape[1]
    copies = start_copies(
        [
            nodes_hbm, lists_hbm, cedges_hbm, w_in_hbm.at[pl.ds(0, width)], csend_hbm, crecv_hbm,
            w_in_hbm.at[pl.ds(width, 2 * width)], w_out_hbm,
        ],
        [nodes_ref, lists_ref, cedges_ref, w_self_ref, csend_ref, crecv_ref, w_ends_ref, w_out_ref],
        sems,
    )
    for copy in copies[:2]:
        copy.wait()
    nodes = nodes_ref[...]
    count = nodes.shape[0]
    lists = lists_ref[0]
    next_ref[...] = dot_t(onehot_t(count, lists[0:1, :]), nodes).astype(BF16)
    prev_ref[...] = dot_t(onehot_t(count, lists[1:2, :]), nodes).astype(BF16)
    for copy in copies[2:6]:
        copy.wait()
    part_ref[...] = dot(cedges_ref[...], w_self_ref[...])
    rows, ids = picks_ref.shape
    send, recv = onehot_t(rows, csend_ref[...]), onehot_t(rows, crecv_ref[...])
    picks_ref[...] = recv
    across = lax.broadcasted_iota(jnp.int32, (rows, rows), 0) == lax.broadcasted_iota(jnp.int32, (rows, rows), 1)
    eye = jnp.where(across, 1.0, 0.0).astype(BF16)
    gather_ref[0:ids, :] = dot_t(send, eye).astype(BF16)
    gather_ref[ids:, :] = dot_t(recv, eye).astype(BF16)
    for copy in copies[6:]:
        copy.wait()


def coarse_kernel(lat_ref, edges_ref, part_ref, gather_ref, picks_ref, w_ends_ref, w_out_ref, new_ref, sums_ref):
    count, width = edges_ref.shape
    blocks = lat_ref.shape[0]
    lat = jnp.concatenate([lat_ref[at].astype(F32) for at in range(blocks)], axis=0).astype(BF16)
    ends = dot(gather_ref[...], lat).astype(BF16)
    pre = part_ref[...] + dot(ends[0:count], w_ends_ref[0:width, :]) + dot(ends[count:], w_ends_ref[width:, :])
    hidden = silu(pre).astype(BF16)
    centred, scale = norm_parts(dot(hidden, w_out_ref[...]))
    new = (edges_ref[...].astype(F32) + centred * scale).astype(BF16)
    new_ref[...] = new
    sums = dot(picks_ref[...], new).astype(BF16)
    for at in range(blocks):
        sums_ref[at] = sums[at * CO_DEV : (at + 1) * CO_DEV, :]


def fine_kernel(
    prev_ref, nodes_ref, next_ref, w_ends_ref, w_out_ref,
    edges_hbm, w_in_hbm, send_hbm, recv_hbm, wn_in_hbm, wn_out_hbm, after,
    new_hbm, out_ref, agg_ref, npart_ref, wn_agg_ref, wn_out_ref,
    edges_ref, w_self_ref, send_ref, recv_ref, wn_self_ref, new_ref, sems, out_sems,
):
    nodes = nodes_ref[...]
    count, width = nodes.shape
    copies = start_copies(
        [
            send_hbm, recv_hbm, edges_hbm, w_in_hbm.at[pl.ds(0, width)],
            wn_in_hbm.at[pl.ds(0, width)], wn_in_hbm.at[pl.ds(width, width)], wn_out_hbm,
        ],
        [send_ref, recv_ref, edges_ref, w_self_ref, wn_self_ref, wn_agg_ref, wn_out_ref],
        sems,
    )
    extended = jnp.concatenate([prev_ref[...], nodes, next_ref[...]], axis=0)
    ones = jnp.ones((count, 128), BF16)
    total = jnp.zeros((count, width), F32)
    for copy in copies[:4]:
        copy.wait()
    outs = []
    for at in range(0, edges_ref.shape[0], STEP):
        rows = pl.ds(at, STEP)
        picks = onehot_t(count, recv_ref[:, rows])
        senders = dot_t(onehot_t(extended.shape[0], send_ref[:, rows]), extended).astype(BF16)
        receivers = dot_t(picks, nodes).astype(BF16)
        valid = dot_t(picks, ones)[:, 0:1]
        edges = edges_ref[rows, :]
        pre = dot(edges, w_self_ref[...]) + dot(senders, w_ends_ref[0:width, :]) + dot(receivers, w_ends_ref[width:, :])
        hidden = silu(pre).astype(BF16)
        centred, scale = norm_parts(dot(hidden, w_out_ref[...]))
        new = (edges.astype(F32) + centred * (scale * valid)).astype(BF16)
        new_ref[rows, :] = new
        copy = pltpu.make_async_copy(new_ref.at[rows], new_hbm.at[rows], out_sems.at[at // STEP])
        copy.start()
        outs.append(copy)
        total = total + dot(picks, new)
    agg_ref[...] = total[0:TOP]
    for copy in copies[4:]:
        copy.wait()
    pre = dot(nodes, wn_self_ref[...])
    npart_ref[...] = pre[0:TOP]
    pre = pre + dot(total.astype(BF16), wn_agg_ref[...])
    hidden = silu(pre).astype(BF16)
    centred, scale = norm_parts(dot(hidden, wn_out_ref[...]))
    out_ref[...] = (nodes.astype(F32) + centred * scale).astype(BF16)
    for copy in outs:
        copy.wait()


def top_kernel(got_ref, agg_ref, part_ref, nodes_ref, wn_agg_ref, wn_out_ref, rest_ref, out_ref):
    width = agg_ref.shape[1]
    sums = got_ref[0].astype(F32)
    for at in range(1, got_ref.shape[0]):
        sums = sums + got_ref[at].astype(F32)
    sums = jnp.concatenate([sums, jnp.zeros((TOP - CO_DEV, width), F32)], axis=0)
    agg = (agg_ref[...] + sums).astype(BF16)
    hidden = silu(part_ref[...] + dot(agg, wn_agg_ref[...])).astype(BF16)
    centred, scale = norm_parts(dot(hidden, wn_out_ref[...]))
    out_ref[...] = (nodes_ref[0:TOP, :].astype(F32) + centred * scale).astype(BF16)


def in_hbm(*arrays):
    return [pltpu.with_memory_space_constraint(a, pltpu.HBM) for a in arrays]


def cost(flops, moved=0):
    return pl.CostEstimate(flops=flops, bytes_accessed=moved, transcendentals=0)


def call(kernel, name, outs, ins, out_specs=None, scratch=(), hbm=(), flops=0, **more):
    return pl.pallas_call(
        kernel,
        out_shape=outs,
        in_specs=[ANY if i in hbm else VMEM for i in range(len(ins))],
        out_specs=[VMEM] * len(outs) if out_specs is None else out_specs,
        scratch_shapes=scratch,
        compiler_params=pltpu.CompilerParams(vmem_limit_bytes=16 * MIB),
        cost_estimate=cost(flops),
        name=name,
        **more,
    )(*ins)


def body(
    node_latents,
    edge_latents,
    coarse_edges,
    w_edge_in,
    w_edge_out,
    w_node_in,
    w_node_out,
    fine_senders,
    fine_receivers,
    halo_lists,
    coarse_senders,
    coarse_receivers,
):
    count, width = node_latents.shape
    edge_count = edge_latents.shape[0]
    cedge_count = coarse_edges.shape[0]
    halo = halo_lists.shape[2]
    group = lax.axis_size(GROUP_AXES)
    coarse_count = group * CO_DEV
    shape = jax.ShapeDtypeStruct
    like = lambda a: shape(a.shape, a.dtype)
    vmem = pltpu.VMEM
    dma = pltpu.SemaphoreType.DMA
    square = 2 * width * width
    blocks = shape((group, CO_DEV, width), BF16)
    ids = lambda a: a[None, :]

    (heads,) = call(
        head_kernel, "head", (blocks,), in_hbm(node_latents), hbm=(0,), scratch=[vmem((TOP, width), BF16), dma(())],
    )
    lat = lax.all_to_all(heads, GROUP_AXES, 0, 0)
    nodes, cedges, w_ends, w_out, to_next, to_prev, gather, picks, coarse_part = call(
        load_kernel,
        "load",
        (
            like(node_latents),
            like(coarse_edges),
            shape((2 * width, width), BF16),
            like(w_edge_out),
            shape((halo, width), BF16),
            shape((halo, width), BF16),
            shape((2 * cedge_count, coarse_count), BF16),
            shape((coarse_count, cedge_count), BF16),
            shape((cedge_count, width), F32),
        ),
        in_hbm(node_latents, halo_lists, coarse_edges, w_edge_in, ids(coarse_senders), ids(coarse_receivers), w_edge_out)
        + [heads],
        hbm=range(8),
        scratch=[
            vmem(halo_lists.shape, jnp.int32), vmem((width, width), BF16),
            vmem((1, cedge_count), jnp.int32), vmem((1, cedge_count), jnp.int32), dma((8,)),
        ],
        flops=edge_count * square,
    )
    from_prev, from_next = shift(to_next, 1), shift(to_prev, -1)
    new_coarse, sums = call(
        coarse_kernel, "coarse", (like(coarse_edges), blocks),
        [lat, cedges, coarse_part, gather, picks, w_ends, w_out], flops=3 * cedge_count * square,
    )
    (sums,) = call(
        pass_kernel, "pass", (blocks,), [sums, from_prev, from_next], hbm=range(3), out_specs=[ANY],
        input_output_aliases={0: 0},
    )
    got = lax.all_to_all(sums, GROUP_AXES, 0, 0)
    new_edges, rest, agg, node_part, wn_agg, wn_out = call(
        fine_kernel,
        "fine",
        (
            like(edge_latents),
            like(node_latents),
            shape((TOP, width), F32),
            shape((TOP, width), F32),
            shape((width, width), BF16),
            like(w_node_out),
        ),
        [from_prev, nodes, from_next, w_ends, w_out]
        + in_hbm(edge_latents, w_edge_in, ids(fine_senders), ids(fine_receivers), w_node_in, w_node_out)
        + [sums],
        hbm=range(5, 12),
        out_specs=[ANY] + [VMEM] * 5,
        scratch=[
            vmem(edge_latents.shape, BF16), vmem((width, width), BF16), vmem((1, edge_count), jnp.int32),
            vmem((1, edge_count), jnp.int32), vmem((width, width), BF16), vmem(edge_latents.shape, BF16), dma((7,)),
            dma((edge_count // STEP,)),
        ],
        flops=4 * edge_count * square,
    )
    new_nodes = pl.pallas_call(
        top_kernel,
        grid=(1,),
        out_shape=like(node_latents),
        in_specs=[VMEM] * 6 + [ANY],
        out_specs=pl.BlockSpec((TOP, width), lambda i: (0, 0)),
        input_output_aliases={6: 0},
        compiler_params=pltpu.CompilerParams(vmem_limit_bytes=16 * MIB),
        name="top",
    )(got, agg, node_part, nodes, wn_agg, wn_out, rest)
    return (new_nodes, new_edges, new_coarse)


def solution(mesh):
    rows = P(("parts", "patch", "sub"), None)
    ids = P(("parts", "patch", "sub"))
    in_specs = (
        rows, rows, rows, P(), P(), P(), P(), ids, ids, P(("parts", "patch", "sub"), None, None), ids, ids,
    )
    return jax.shard_map(body, mesh=mesh, in_specs=in_specs, out_specs=(rows, rows, rows), check_vma=False)
```

```python
import jax
import jax.numpy as jnp
from jax import lax
from jax.experimental import pallas as pl
from jax.experimental.pallas import tpu as pltpu
from jax.sharding import PartitionSpec as P

CO_DEV = 4
GROUP_AXES = ("patch", "sub")
TOP = 16
STEP = 128
MIB = 1 << 20
ANY = pl.BlockSpec(memory_space=pl.ANY)
VMEM = pl.BlockSpec(memory_space=pltpu.VMEM)
BF16, F32 = jnp.bfloat16, jnp.float32


def shift(value, by):
    devices = lax.axis_size(GROUP_AXES)
    return lax.ppermute(value, GROUP_AXES, [(i, (i + by) % devices) for i in range(devices)])


def dot(a, b):
    return jnp.dot(a, b, preferred_element_type=F32)


def dot_t(a, b):
    return lax.dot_general(a, b, (((0,), (0,)), ((), ())), preferred_element_type=F32)


def onehot_t(rows, ids):
    at = lax.broadcasted_iota(jnp.int32, (rows, ids.shape[1]), 0)
    return jnp.where(at == ids, 1.0, 0.0).astype(BF16)


def silu(v):
    half = 0.5 * v
    return half + half * jnp.tanh(half)


def norm_parts(values):
    mean = jnp.mean(values, axis=-1, keepdims=True)
    centred = values - mean
    return centred, lax.rsqrt(jnp.mean(centred * centred, axis=-1, keepdims=True) + 1e-05)


def head_kernel(nodes_hbm, heads_ref, rows_ref, sem):
    copy = pltpu.make_async_copy(nodes_hbm.at[pl.ds(0, TOP)], rows_ref, sem)
    copy.start()
    copy.wait()
    head = rows_ref[0:CO_DEV, :]
    for at in range(heads_ref.shape[0]):
        heads_ref[at] = head


def start_copies(sources, targets, sems):
    copies = [pltpu.make_async_copy(a, b, sems.at[i]) for i, (a, b) in enumerate(zip(sources, targets))]
    for copy in copies:
        copy.start()
    return copies


def load_kernel(
    nodes_hbm, lists_hbm, cedges_hbm, w_in_hbm, csend_hbm, crecv_hbm, w_out_hbm, after,
    nodes_ref, cedges_ref, w_ends_ref, w_out_ref, next_ref, prev_ref, gather_ref, picks_ref, part_ref,
    lists_ref, w_self_ref, csend_ref, crecv_ref, sems,
):
    width = nodes_ref.shape[1]
    copies = start_copies(
        [
            nodes_hbm, lists_hbm, cedges_hbm, w_in_hbm.at[pl.ds(0, width)], csend_hbm, crecv_hbm,
            w_in_hbm.at[pl.ds(width, 2 * width)], w_out_hbm,
        ],
        [nodes_ref, lists_ref, cedges_ref, w_self_ref, csend_ref, crecv_ref, w_ends_ref, w_out_ref],
        sems,
    )
    for copy in copies[:2]:
        copy.wait()
    nodes = nodes_ref[...]
    count = nodes.shape[0]
    lists = lists_ref[0]
    next_ref[...] = dot_t(onehot_t(count, lists[0:1, :]), nodes).astype(BF16)
    prev_ref[...] = dot_t(onehot_t(count, lists[1:2, :]), nodes).astype(BF16)
    for copy in copies[2:6]:
        copy.wait()
    part_ref[...] = dot(cedges_ref[...], w_self_ref[...])
    rows, ids = picks_ref.shape
    send, recv = onehot_t(rows, csend_ref[...]), onehot_t(rows, crecv_ref[...])
    picks_ref[...] = recv
    across = lax.broadcasted_iota(jnp.int32, (rows, rows), 0) == lax.broadcasted_iota(jnp.int32, (rows, rows), 1)
    eye = jnp.where(across, 1.0, 0.0).astype(BF16)
    gather_ref[0:ids, :] = dot_t(send, eye).astype(BF16)
    gather_ref[ids:, :] = dot_t(recv, eye).astype(BF16)
    for copy in copies[6:]:
        copy.wait()


def coarse_kernel(lat_ref, edges_ref, part_ref, gather_ref, picks_ref, w_ends_ref, w_out_ref, new_ref, sums_ref):
    count, width = edges_ref.shape
    blocks = lat_ref.shape[0]
    lat = jnp.concatenate([lat_ref[at].astype(F32) for at in range(blocks)], axis=0).astype(BF16)
    ends = dot(gather_ref[...], lat).astype(BF16)
    pre = part_ref[...] + dot(ends[0:count], w_ends_ref[0:width, :]) + dot(ends[count:], w_ends_ref[width:, :])
    hidden = silu(pre).astype(BF16)
    centred, scale = norm_parts(dot(hidden, w_out_ref[...]))
    new = (edges_ref[...].astype(F32) + centred * scale).astype(BF16)
    new_ref[...] = new
    sums = dot(picks_ref[...], new).astype(BF16)
    for at in range(blocks):
        sums_ref[at] = sums[at * CO_DEV : (at + 1) * CO_DEV, :]


def fine_kernel(
    prev_ref, nodes_ref, next_ref, w_ends_ref, w_out_ref,
    edges_hbm, w_in_hbm, send_hbm, recv_hbm, wn_in_hbm, wn_out_hbm, after,
    new_hbm, out_ref, agg_ref, npart_ref, wn_agg_ref, wn_out_ref,
    edges_ref, w_self_ref, send_ref, recv_ref, wn_self_ref, new_ref, sems, out_sems,
):
    nodes = nodes_ref[...]
    count, width = nodes.shape
    copies = start_copies(
        [
            send_hbm, recv_hbm, edges_hbm, w_in_hbm.at[pl.ds(0, width)],
            wn_in_hbm.at[pl.ds(0, width)], wn_in_hbm.at[pl.ds(width, width)], wn_out_hbm,
        ],
        [send_ref, recv_ref, edges_ref, w_self_ref, wn_self_ref, wn_agg_ref, wn_out_ref],
        sems,
    )
    extended = jnp.concatenate([prev_ref[...], nodes, next_ref[...]], axis=0)
    ones = jnp.ones((count, 128), BF16)
    total = jnp.zeros((count, width), F32)
    for copy in copies[:4]:
        copy.wait()
    outs = []
    for at in range(0, edges_ref.shape[0], STEP):
        rows = pl.ds(at, STEP)
        picks = onehot_t(count, recv_ref[:, rows])
        senders = dot_t(onehot_t(extended.shape[0], send_ref[:, rows]), extended).astype(BF16)
        receivers = dot_t(picks, nodes).astype(BF16)
        valid = dot_t(picks, ones)[:, 0:1]
        edges = edges_ref[rows, :]
        pre = dot(edges, w_self_ref[...]) + dot(senders, w_ends_ref[0:width, :]) + dot(receivers, w_ends_ref[width:, :])
        hidden = silu(pre).astype(BF16)
        centred, scale = norm_parts(dot(hidden, w_out_ref[...]))
        new = (edges.astype(F32) + centred * (scale * valid)).astype(BF16)
        new_ref[rows, :] = new
        copy = pltpu.make_async_copy(new_ref.at[rows], new_hbm.at[rows], out_sems.at[at // STEP])
        copy.start()
        outs.append(copy)
        total = total + dot(picks, new)
    agg_ref[...] = total[0:TOP]
    for copy in copies[4:]:
        copy.wait()
    pre = dot(nodes, wn_self_ref[...])
    npart_ref[...] = pre[0:TOP]
    pre = pre + dot(total.astype(BF16), wn_agg_ref[...])
    hidden = silu(pre).astype(BF16)
    centred, scale = norm_parts(dot(hidden, wn_out_ref[...]))
    out_ref[...] = (nodes.astype(F32) + centred * scale).astype(BF16)
    for copy in outs:
        copy.wait()


def top_kernel(got_ref, agg_ref, part_ref, nodes_ref, wn_agg_ref, wn_out_ref, rest_ref, out_ref):
    width = agg_ref.shape[1]
    sums = got_ref[0].astype(F32)
    for at in range(1, got_ref.shape[0]):
        sums = sums + got_ref[at].astype(F32)
    sums = jnp.concatenate([sums, jnp.zeros((TOP - CO_DEV, width), F32)], axis=0)
    agg = (agg_ref[...] + sums).astype(BF16)
    hidden = silu(part_ref[...] + dot(agg, wn_agg_ref[...])).astype(BF16)
    centred, scale = norm_parts(dot(hidden, wn_out_ref[...]))
    out_ref[...] = (nodes_ref[0:TOP, :].astype(F32) + centred * scale).astype(BF16)


def in_hbm(*arrays):
    return [pltpu.with_memory_space_constraint(a, pltpu.HBM) for a in arrays]


def cost(flops, moved=0):
    return pl.CostEstimate(flops=flops, bytes_accessed=moved, transcendentals=0)


def call(kernel, name, outs, ins, out_specs=None, scratch=(), hbm=(), flops=0, **more):
    return pl.pallas_call(
        kernel,
        out_shape=outs,
        in_specs=[ANY if i in hbm else VMEM for i in range(len(ins))],
        out_specs=[VMEM] * len(outs) if out_specs is None else out_specs,
        scratch_shapes=scratch,
        compiler_params=pltpu.CompilerParams(vmem_limit_bytes=16 * MIB),
        cost_estimate=cost(flops),
        name=name,
        **more,
    )(*ins)


def body(
    node_latents,
    edge_latents,
    coarse_edges,
    w_edge_in,
    w_edge_out,
    w_node_in,
    w_node_out,
    fine_senders,
    fine_receivers,
    halo_lists,
    coarse_senders,
    coarse_receivers,
):
    count, width = node_latents.shape
    edge_count = edge_latents.shape[0]
    cedge_count = coarse_edges.shape[0]
    halo = halo_lists.shape[2]
    group = lax.axis_size(GROUP_AXES)
    coarse_count = group * CO_DEV
    shape = jax.ShapeDtypeStruct
    like = lambda a: shape(a.shape, a.dtype)
    vmem = pltpu.VMEM
    dma = pltpu.SemaphoreType.DMA
    square = 2 * width * width
    blocks = shape((group, CO_DEV, width), BF16)
    ids = lambda a: a[None, :]

    (heads,) = call(
        head_kernel, "head", (blocks,), in_hbm(node_latents), hbm=(0,), scratch=[vmem((TOP, width), BF16), dma(())],
    )
    lat = lax.all_to_all(heads, GROUP_AXES, 0, 0)
    nodes, cedges, w_ends, w_out, to_next, to_prev, gather, picks, coarse_part = call(
        load_kernel,
        "load",
        (
            like(node_latents),
            like(coarse_edges),
            shape((2 * width, width), BF16),
            like(w_edge_out),
            shape((halo, width), BF16),
            shape((halo, width), BF16),
            shape((2 * cedge_count, coarse_count), BF16),
            shape((coarse_count, cedge_count), BF16),
            shape((cedge_count, width), F32),
        ),
        in_hbm(node_latents, halo_lists, coarse_edges, w_edge_in, ids(coarse_senders), ids(coarse_receivers), w_edge_out)
        + [heads],
        hbm=range(8),
        scratch=[
            vmem(halo_lists.shape, jnp.int32), vmem((width, width), BF16),
            vmem((1, cedge_count), jnp.int32), vmem((1, cedge_count), jnp.int32), dma((8,)),
        ],
        flops=edge_count * square,
    )
    from_prev, from_next = shift(to_next, 1), shift(to_prev, -1)
    new_coarse, sums = call(
        coarse_kernel, "coarse", (like(coarse_edges), blocks),
        [lat, cedges, coarse_part, gather, picks, w_ends, w_out], flops=0,
    )
    got = lax.all_to_all(sums, GROUP_AXES, 0, 0)
    new_edges, rest, agg, node_part, wn_agg, wn_out = call(
        fine_kernel,
        "fine",
        (
            like(edge_latents),
            like(node_latents),
            shape((TOP, width), F32),
            shape((TOP, width), F32),
            shape((width, width), BF16),
            like(w_node_out),
        ),
        [from_prev, nodes, from_next, w_ends, w_out]
        + in_hbm(edge_latents, w_edge_in, ids(fine_senders), ids(fine_receivers), w_node_in, w_node_out)
        + [sums],
        hbm=range(5, 12),
        out_specs=[ANY] + [VMEM] * 5,
        scratch=[
            vmem(edge_latents.shape, BF16), vmem((width, width), BF16), vmem((1, edge_count), jnp.int32),
            vmem((1, edge_count), jnp.int32), vmem((width, width), BF16), vmem(edge_latents.shape, BF16), dma((7,)),
            dma((edge_count // STEP,)),
        ],
        flops=64 * edge_count * square,
    )
    new_nodes = pl.pallas_call(
        top_kernel,
        grid=(1,),
        out_shape=like(node_latents),
        in_specs=[VMEM] * 6 + [ANY],
        out_specs=pl.BlockSpec((TOP, width), lambda i: (0, 0)),
        input_output_aliases={6: 0},
        compiler_params=pltpu.CompilerParams(vmem_limit_bytes=16 * MIB),
        name="top",
    )(got, agg, node_part, nodes, wn_agg, wn_out, rest)
    return (new_nodes, new_edges, new_coarse)


def solution(mesh):
    rows = P(("parts", "patch", "sub"), None)
    ids = P(("parts", "patch", "sub"))
    in_specs = (
        rows, rows, rows, P(), P(), P(), P(), ids, ids, P(("parts", "patch", "sub"), None, None), ids, ids,
    )
    return jax.shard_map(body, mesh=mesh, in_specs=in_specs, out_specs=(rows, rows, rows), check_vma=False)
```

```python
import jax
import jax.numpy as jnp
from jax import lax
from jax.experimental import pallas as pl
from jax.experimental.pallas import tpu as pltpu
from jax.sharding import PartitionSpec as P

CO_DEV = 4
GROUP_AXES = ("patch", "sub")
TOP = 16
STEP = 128
MIB = 1 << 20
ANY = pl.BlockSpec(memory_space=pl.ANY)
VMEM = pl.BlockSpec(memory_space=pltpu.VMEM)
BF16, F32 = jnp.bfloat16, jnp.float32


def shift(value, by):
    devices = lax.axis_size(GROUP_AXES)
    return lax.ppermute(value, GROUP_AXES, [(i, (i + by) % devices) for i in range(devices)])


def dot(a, b):
    return jnp.dot(a, b, preferred_element_type=F32)


def dot_t(a, b):
    return lax.dot_general(a, b, (((0,), (0,)), ((), ())), preferred_element_type=F32)


def onehot_t(rows, ids):
    at = lax.broadcasted_iota(jnp.int32, (rows, ids.shape[1]), 0)
    return jnp.where(at == ids, 1.0, 0.0).astype(BF16)


def silu(v):
    half = 0.5 * v
    return half + half * jnp.tanh(half)


def norm_parts(values):
    mean = jnp.mean(values, axis=-1, keepdims=True)
    centred = values - mean
    return centred, lax.rsqrt(jnp.mean(centred * centred, axis=-1, keepdims=True) + 1e-05)


def head_kernel(nodes_hbm, heads_hbm, sems):
    copies = [
        pltpu.make_async_copy(nodes_hbm.at[pl.ds(0, CO_DEV)], heads_hbm.at[at], sems.at[at])
        for at in range(heads_hbm.shape[0])
    ]
    for copy in copies:
        copy.start()
    for copy in copies:
        copy.wait()


def start_copies(sources, targets, sems):
    copies = [pltpu.make_async_copy(a, b, sems.at[i]) for i, (a, b) in enumerate(zip(sources, targets))]
    for copy in copies:
        copy.start()
    return copies


def load_kernel(
    nodes_hbm, lists_hbm, cedges_hbm, w_in_hbm, csend_hbm, crecv_hbm, w_out_hbm, after,
    nodes_ref, cedges_ref, w_ends_ref, w_out_ref, next_ref, prev_ref, gather_ref, picks_ref, part_ref,
    lists_ref, w_self_ref, csend_ref, crecv_ref, sems,
):
    width = nodes_ref.shape[1]
    copies = start_copies(
        [
            nodes_hbm, lists_hbm, cedges_hbm, w_in_hbm.at[pl.ds(0, width)], csend_hbm, crecv_hbm,
            w_in_hbm.at[pl.ds(width, 2 * width)], w_out_hbm,
        ],
        [nodes_ref, lists_ref, cedges_ref, w_self_ref, csend_ref, crecv_ref, w_ends_ref, w_out_ref],
        sems,
    )
    for copy in copies[:2]:
        copy.wait()
    nodes = nodes_ref[...]
    count = nodes.shape[0]
    lists = lists_ref[0]
    next_ref[...] = dot_t(onehot_t(count, lists[0:1, :]), nodes).astype(BF16)
    prev_ref[...] = dot_t(onehot_t(count, lists[1:2, :]), nodes).astype(BF16)
    for copy in copies[2:6]:
        copy.wait()
    part_ref[...] = dot(cedges_ref[...], w_self_ref[...])
    rows, ids = picks_ref.shape
    send, recv = onehot_t(rows, csend_ref[...]), onehot_t(rows, crecv_ref[...])
    picks_ref[...] = recv
    across = lax.broadcasted_iota(jnp.int32, (rows, rows), 0) == lax.broadcasted_iota(jnp.int32, (rows, rows), 1)
    eye = jnp.where(across, 1.0, 0.0).astype(BF16)
    gather_ref[0:ids, :] = dot_t(send, eye).astype(BF16)
    gather_ref[ids:, :] = dot_t(recv, eye).astype(BF16)
    for copy in copies[6:]:
        copy.wait()


def coarse_kernel(lat_ref, edges_ref, part_ref, gather_ref, picks_ref, w_ends_ref, w_out_ref, new_ref, sums_ref):
    count, width = edges_ref.shape
    blocks = lat_ref.shape[0]
    lat = jnp.concatenate([lat_ref[at].astype(F32) for at in range(blocks)], axis=0).astype(BF16)
    ends = dot(gather_ref[...], lat).astype(BF16)
    pre = part_ref[...] + dot(ends[0:count], w_ends_ref[0:width, :]) + dot(ends[count:], w_ends_ref[width:, :])
    hidden = silu(pre).astype(BF16)
    centred, scale = norm_parts(dot(hidden, w_out_ref[...]))
    new = (edges_ref[...].astype(F32) + centred * scale).astype(BF16)
    new_ref[...] = new
    sums = dot(picks_ref[...], new).astype(BF16)
    for at in range(blocks):
        sums_ref[at] = sums[at * CO_DEV : (at + 1) * CO_DEV, :]


def fine_kernel(
    prev_ref, nodes_ref, next_ref, w_ends_ref, w_out_ref,
    edges_hbm, w_in_hbm, send_hbm, recv_hbm, wn_in_hbm, wn_out_hbm, after,
    new_hbm, out_ref, agg_ref, npart_ref, wn_agg_ref, wn_out_ref,
    edges_ref, w_self_ref, send_ref, recv_ref, wn_self_ref, new_ref, sems, out_sems,
):
    nodes = nodes_ref[...]
    count, width = nodes.shape
    copies = start_copies(
        [
            send_hbm, recv_hbm, edges_hbm, w_in_hbm.at[pl.ds(0, width)],
            wn_in_hbm.at[pl.ds(0, width)], wn_in_hbm.at[pl.ds(width, width)], wn_out_hbm,
        ],
        [send_ref, recv_ref, edges_ref, w_self_ref, wn_self_ref, wn_agg_ref, wn_out_ref],
        sems,
    )
    extended = jnp.concatenate([prev_ref[...], nodes, next_ref[...]], axis=0)
    ones = jnp.ones((count, 128), BF16)
    total = jnp.zeros((count, width), F32)
    for copy in copies[:4]:
        copy.wait()
    outs = []
    for at in range(0, edges_ref.shape[0], STEP):
        rows = pl.ds(at, STEP)
        picks = onehot_t(count, recv_ref[:, rows])
        senders = dot_t(onehot_t(extended.shape[0], send_ref[:, rows]), extended).astype(BF16)
        receivers = dot_t(picks, nodes).astype(BF16)
        valid = dot_t(picks, ones)[:, 0:1]
        edges = edges_ref[rows, :]
        pre = dot(edges, w_self_ref[...]) + dot(senders, w_ends_ref[0:width, :]) + dot(receivers, w_ends_ref[width:, :])
        hidden = silu(pre).astype(BF16)
        centred, scale = norm_parts(dot(hidden, w_out_ref[...]))
        new = (edges.astype(F32) + centred * (scale * valid)).astype(BF16)
        new_ref[rows, :] = new
        copy = pltpu.make_async_copy(new_ref.at[rows], new_hbm.at[rows], out_sems.at[at // STEP])
        copy.start()
        outs.append(copy)
        total = total + dot(picks, new)
    agg_ref[...] = total[0:TOP]
    for copy in copies[4:]:
        copy.wait()
    pre = dot(nodes, wn_self_ref[...])
    npart_ref[...] = pre[0:TOP]
    pre = pre + dot(total.astype(BF16), wn_agg_ref[...])
    hidden = silu(pre).astype(BF16)
    centred, scale = norm_parts(dot(hidden, wn_out_ref[...]))
    out_ref[...] = (nodes.astype(F32) + centred * scale).astype(BF16)
    for copy in outs:
        copy.wait()


def top_kernel(got_ref, agg_ref, part_ref, nodes_ref, wn_agg_ref, wn_out_ref, rest_ref, out_ref):
    width = agg_ref.shape[1]
    sums = got_ref[0].astype(F32)
    for at in range(1, got_ref.shape[0]):
        sums = sums + got_ref[at].astype(F32)
    sums = jnp.concatenate([sums, jnp.zeros((TOP - CO_DEV, width), F32)], axis=0)
    agg = (agg_ref[...] + sums).astype(BF16)
    hidden = silu(part_ref[...] + dot(agg, wn_agg_ref[...])).astype(BF16)
    centred, scale = norm_parts(dot(hidden, wn_out_ref[...]))
    out_ref[...] = (nodes_ref[0:TOP, :].astype(F32) + centred * scale).astype(BF16)


def in_hbm(*arrays):
    return [pltpu.with_memory_space_constraint(a, pltpu.HBM) for a in arrays]


def cost(flops, moved=0):
    return pl.CostEstimate(flops=flops, bytes_accessed=moved, transcendentals=0)


def call(kernel, name, outs, ins, out_specs=None, scratch=(), hbm=(), flops=0, **more):
    return pl.pallas_call(
        kernel,
        out_shape=outs,
        in_specs=[ANY if i in hbm else VMEM for i in range(len(ins))],
        out_specs=[VMEM] * len(outs) if out_specs is None else out_specs,
        scratch_shapes=scratch,
        compiler_params=pltpu.CompilerParams(vmem_limit_bytes=16 * MIB),
        cost_estimate=cost(flops),
        name=name,
        **more,
    )(*ins)


def body(
    node_latents,
    edge_latents,
    coarse_edges,
    w_edge_in,
    w_edge_out,
    w_node_in,
    w_node_out,
    fine_senders,
    fine_receivers,
    halo_lists,
    coarse_senders,
    coarse_receivers,
):
    count, width = node_latents.shape
    edge_count = edge_latents.shape[0]
    cedge_count = coarse_edges.shape[0]
    halo = halo_lists.shape[2]
    group = lax.axis_size(GROUP_AXES)
    coarse_count = group * CO_DEV
    shape = jax.ShapeDtypeStruct
    like = lambda a: shape(a.shape, a.dtype)
    vmem = pltpu.VMEM
    dma = pltpu.SemaphoreType.DMA
    square = 2 * width * width
    blocks = shape((group, CO_DEV, width), BF16)
    ids = lambda a: a[None, :]

    (heads,) = call(
        head_kernel, "head", (blocks,), in_hbm(node_latents), hbm=(0,), out_specs=[ANY], scratch=[dma((group,))],
    )
    lat = lax.all_to_all(heads, GROUP_AXES, 0, 0)
    nodes, cedges, w_ends, w_out, to_next, to_prev, gather, picks, coarse_part = call(
        load_kernel,
        "load",
        (
            like(node_latents),
            like(coarse_edges),
            shape((2 * width, width), BF16),
            like(w_edge_out),
            shape((halo, width), BF16),
            shape((halo, width), BF16),
            shape((2 * cedge_count, coarse_count), BF16),
            shape((coarse_count, cedge_count), BF16),
            shape((cedge_count, width), F32),
        ),
        in_hbm(node_latents, halo_lists, coarse_edges, w_edge_in, ids(coarse_senders), ids(coarse_receivers), w_edge_out)
        + [heads],
        hbm=range(8),
        scratch=[
            vmem(halo_lists.shape, jnp.int32), vmem((width, width), BF16),
            vmem((1, cedge_count), jnp.int32), vmem((1, cedge_count), jnp.int32), dma((8,)),
        ],
        flops=edge_count * square,
    )
    from_prev, from_next = shift(to_next, 1), shift(to_prev, -1)
    new_coarse, sums = call(
        coarse_kernel, "coarse", (like(coarse_edges), blocks),
        [lat, cedges, coarse_part, gather, picks, w_ends, w_out], flops=0,
    )
    got = lax.all_to_all(sums, GROUP_AXES, 0, 0)
    new_edges, rest, agg, node_part, wn_agg, wn_out = call(
        fine_kernel,
        "fine",
        (
            like(edge_latents),
            like(node_latents),
            shape((TOP, width), F32),
            shape((TOP, width), F32),
            shape((width, width), BF16),
            like(w_node_out),
        ),
        [from_prev, nodes, from_next, w_ends, w_out]
        + in_hbm(edge_latents, w_edge_in, ids(fine_senders), ids(fine_receivers), w_node_in, w_node_out)
        + [sums],
        hbm=range(5, 12),
        out_specs=[ANY] + [VMEM] * 5,
        scratch=[
            vmem(edge_latents.shape, BF16), vmem((width, width), BF16), vmem((1, edge_count), jnp.int32),
            vmem((1, edge_count), jnp.int32), vmem((width, width), BF16), vmem(edge_latents.shape, BF16), dma((7,)),
            dma((edge_count // STEP,)),
        ],
        flops=64 * edge_count * square,
    )
    new_nodes = pl.pallas_call(
        top_kernel,
        grid=(1,),
        out_shape=like(node_latents),
        in_specs=[VMEM] * 6 + [ANY],
        out_specs=pl.BlockSpec((TOP, width), lambda i: (0, 0)),
        input_output_aliases={6: 0},
        compiler_params=pltpu.CompilerParams(vmem_limit_bytes=16 * MIB),
        name="top",
    )(got, agg, node_part, nodes, wn_agg, wn_out, rest)
    return (new_nodes, new_edges, new_coarse)


def solution(mesh):
    rows = P(("parts", "patch", "sub"), None)
    ids = P(("parts", "patch", "sub"))
    in_specs = (
        rows, rows, rows, P(), P(), P(), P(), ids, ids, P(("parts", "patch", "sub"), None, None), ids, ids,
    )
    return jax.shard_map(body, mesh=mesh, in_specs=in_specs, out_specs=(rows, rows, rows), check_vma=False)
```

```python
import functools

import jax
import jax.numpy as jnp
from jax import lax
from jax.experimental import pallas as pl
from jax.experimental.pallas import tpu as pltpu
from jax.sharding import PartitionSpec as P

CO_DEV = 4
GROUP_AXES = ("patch", "sub")
TOP = 16
STEP = 128
MIB = 1 << 20
ANY = pl.BlockSpec(memory_space=pl.ANY)
VMEM = pl.BlockSpec(memory_space=pltpu.VMEM)
BF16, F32 = jnp.bfloat16, jnp.float32


def swap(value, mask, axis):
    return lax.ppermute(value, axis, [(i, i ^ mask) for i in range(lax.axis_size(axis))])


def pair(value, first):
    devices = lax.axis_size(GROUP_AXES)
    pairs = [(i, (i + 1) % devices) for i in range(first, devices, 2)]
    return lax.ppermute(value, GROUP_AXES, pairs + [(b, a) for a, b in pairs])


def dot(a, b):
    return jnp.dot(a, b, preferred_element_type=F32)


def dot_t(a, b):
    return lax.dot_general(a, b, (((0,), (0,)), ((), ())), preferred_element_type=F32)


def onehot_t(rows, ids):
    at = lax.broadcasted_iota(jnp.int32, (rows, ids.shape[1]), 0)
    return jnp.where(at == ids, 1.0, 0.0).astype(BF16)


def silu(v):
    half = 0.5 * v
    return half + half * jnp.tanh(half)


def norm_parts(values):
    mean = jnp.mean(values, axis=-1, keepdims=True)
    centred = values - mean
    return centred, lax.rsqrt(jnp.mean(centred * centred, axis=-1, keepdims=True) + 1e-05)


def head_kernel(nodes_hbm, head_ref, rows_ref, sem):
    copy = pltpu.make_async_copy(nodes_hbm.at[pl.ds(0, TOP)], rows_ref, sem)
    copy.start()
    copy.wait()
    head_ref[...] = rows_ref[0:CO_DEV, :]


def join_rows(refs):
    return jnp.concatenate([ref[...].astype(F32) for ref in refs[:1] + refs[:0:-1]], axis=0).astype(BF16)


def join_kernel(*refs):
    refs, (after, out_ref) = refs[:-2], refs[-2:]
    out_ref[...] = join_rows(refs)


def pass_kernel(even_ref, odd_ref, after, even_out, odd_out):
    pass


def start_copies(sources, targets, sems):
    copies = [pltpu.make_async_copy(a, b, sems.at[i]) for i, (a, b) in enumerate(zip(sources, targets))]
    for copy in copies:
        copy.start()
    return copies


def load_kernel(
    nodes_hbm, lists_hbm, cedges_hbm, w_in_hbm, csend_hbm, crecv_hbm, w_out_hbm, after,
    nodes_ref, cedges_ref, w_ends_ref, w_out_ref, even_ref, odd_ref, gather_ref, picks_ref, part_ref,
    lists_ref, w_self_ref, csend_ref, crecv_ref, sems,
):
    width = nodes_ref.shape[1]
    copies = start_copies(
        [
            nodes_hbm, lists_hbm, cedges_hbm, w_in_hbm.at[pl.ds(0, width)], csend_hbm, crecv_hbm,
            w_in_hbm.at[pl.ds(width, 2 * width)], w_out_hbm,
        ],
        [nodes_ref, lists_ref, cedges_ref, w_self_ref, csend_ref, crecv_ref, w_ends_ref, w_out_ref],
        sems,
    )
    for copy in copies[:2]:
        copy.wait()
    nodes = nodes_ref[...]
    count = nodes.shape[0]
    lists = lists_ref[0]
    me = lax.axis_index(GROUP_AXES)
    odd = me % 2
    first = lists[0:1, :] * (1 - odd) + lists[1:2, :] * odd
    second = lists[1:2, :] * (1 - odd) + lists[0:1, :] * odd
    even_ref[...] = dot_t(onehot_t(count, first), nodes).astype(BF16)
    odd_ref[...] = dot_t(onehot_t(count, second), nodes).astype(BF16)
    for copy in copies[2:6]:
        copy.wait()
    part_ref[...] = dot(cedges_ref[...], w_self_ref[...])
    rows, ids = picks_ref.shape
    send = onehot_t(rows, csend_ref[...] ^ (me * CO_DEV))
    recv = onehot_t(rows, crecv_ref[...] ^ (me * CO_DEV))
    picks_ref[...] = onehot_t(rows, crecv_ref[...])
    across = lax.broadcasted_iota(jnp.int32, (rows, rows), 0) == lax.broadcasted_iota(jnp.int32, (rows, rows), 1)
    eye = jnp.where(across, 1.0, 0.0).astype(BF16)
    gather_ref[0:ids, :] = dot_t(send, eye).astype(BF16)
    gather_ref[ids:, :] = dot_t(recv, eye).astype(BF16)
    for copy in copies[6:]:
        copy.wait()


def coarse_kernel(parts, *refs):
    lats, refs = refs[:parts], refs[parts:]
    edges_ref, part_ref, gather_ref, picks_ref, w_ends_ref, w_out_ref, new_ref, sums_ref = refs
    count, width = edges_ref.shape
    lat = join_rows(lats)
    ends = dot(gather_ref[...], lat).astype(BF16)
    pre = part_ref[...] + dot(ends[0:count], w_ends_ref[0:width, :]) + dot(ends[count:], w_ends_ref[width:, :])
    hidden = silu(pre).astype(BF16)
    centred, scale = norm_parts(dot(hidden, w_out_ref[...]))
    new = (edges_ref[...].astype(F32) + centred * scale).astype(BF16)
    new_ref[...] = new
    sums = dot(picks_ref[...], new).astype(BF16)
    for at in range(sums_ref.shape[0]):
        sums_ref[at] = sums[at * CO_DEV : (at + 1) * CO_DEV, :]


def fine_kernel(
    even_ref, nodes_ref, odd_ref, w_ends_ref, w_out_ref,
    edges_hbm, w_in_hbm, send_hbm, recv_hbm, wn_in_hbm, wn_out_hbm, after,
    new_hbm, out_ref, agg_ref, npart_ref, wn_agg_ref, wn_out_ref,
    edges_ref, w_self_ref, send_ref, recv_ref, wn_self_ref, new_ref, sems, out_sems,
):
    nodes = nodes_ref[...]
    count, width = nodes.shape
    copies = start_copies(
        [
            send_hbm, recv_hbm, edges_hbm, w_in_hbm.at[pl.ds(0, width)],
            wn_in_hbm.at[pl.ds(0, width)], wn_in_hbm.at[pl.ds(width, width)], wn_out_hbm,
        ],
        [send_ref, recv_ref, edges_ref, w_self_ref, wn_self_ref, wn_agg_ref, wn_out_ref],
        sems,
    )
    odd = (lax.axis_index(GROUP_AXES) % 2).astype(F32)
    met, other = even_ref[...].astype(F32), odd_ref[...].astype(F32)
    prev = (met * odd + other * (1.0 - odd)).astype(BF16)
    following = (other * odd + met * (1.0 - odd)).astype(BF16)
    extended = jnp.concatenate([prev, nodes, following], axis=0)
    ones = jnp.ones((count, 128), BF16)
    total = jnp.zeros((count, width), F32)
    for copy in copies[:4]:
        copy.wait()
    outs = []
    for at in range(0, edges_ref.shape[0], STEP):
        rows = pl.ds(at, STEP)
        picks = onehot_t(count, recv_ref[:, rows])
        senders = dot_t(onehot_t(extended.shape[0], send_ref[:, rows]), extended).astype(BF16)
        receivers = dot_t(picks, nodes).astype(BF16)
        valid = dot_t(picks, ones)[:, 0:1]
        edges = edges_ref[rows, :]
        pre = dot(edges, w_self_ref[...]) + dot(senders, w_ends_ref[0:width, :]) + dot(receivers, w_ends_ref[width:, :])
        hidden = silu(pre).astype(BF16)
        centred, scale = norm_parts(dot(hidden, w_out_ref[...]))
        new = (edges.astype(F32) + centred * (scale * valid)).astype(BF16)
        new_ref[rows, :] = new
        copy = pltpu.make_async_copy(new_ref.at[rows], new_hbm.at[rows], out_sems.at[at // STEP])
        copy.start()
        outs.append(copy)
        total = total + dot(picks, new)
    agg_ref[...] = total[0:TOP]
    for copy in copies[4:]:
        copy.wait()
    pre = dot(nodes, wn_self_ref[...])
    npart_ref[...] = pre[0:TOP]
    pre = pre + dot(total.astype(BF16), wn_agg_ref[...])
    hidden = silu(pre).astype(BF16)
    centred, scale = norm_parts(dot(hidden, wn_out_ref[...]))
    out_ref[...] = (nodes.astype(F32) + centred * scale).astype(BF16)
    for copy in outs:
        copy.wait()


def top_kernel(got_ref, agg_ref, part_ref, nodes_ref, wn_agg_ref, wn_out_ref, rest_ref, out_ref):
    width = agg_ref.shape[1]
    sums = got_ref[0].astype(F32)
    for at in range(1, got_ref.shape[0]):
        sums = sums + got_ref[at].astype(F32)
    sums = jnp.concatenate([sums, jnp.zeros((TOP - CO_DEV, width), F32)], axis=0)
    agg = (agg_ref[...] + sums).astype(BF16)
    hidden = silu(part_ref[...] + dot(agg, wn_agg_ref[...])).astype(BF16)
    centred, scale = norm_parts(dot(hidden, wn_out_ref[...]))
    out_ref[...] = (nodes_ref[0:TOP, :].astype(F32) + centred * scale).astype(BF16)


def in_hbm(*arrays):
    return [pltpu.with_memory_space_constraint(a, pltpu.HBM) for a in arrays]


def cost(flops, moved=0):
    return pl.CostEstimate(flops=flops, bytes_accessed=moved, transcendentals=0)


def call(kernel, name, outs, ins, out_specs=None, scratch=(), hbm=(), flops=0, **more):
    return pl.pallas_call(
        kernel,
        out_shape=outs,
        in_specs=[ANY if i in hbm else VMEM for i in range(len(ins))],
        out_specs=[VMEM] * len(outs) if out_specs is None else out_specs,
        scratch_shapes=scratch,
        compiler_params=pltpu.CompilerParams(vmem_limit_bytes=16 * MIB),
        cost_estimate=cost(flops),
        name=name,
        **more,
    )(*ins)


def body(
    node_latents,
    edge_latents,
    coarse_edges,
    w_edge_in,
    w_edge_out,
    w_node_in,
    w_node_out,
    fine_senders,
    fine_receivers,
    halo_lists,
    coarse_senders,
    coarse_receivers,
):
    count, width = node_latents.shape
    edge_count = edge_latents.shape[0]
    cedge_count = coarse_edges.shape[0]
    halo = halo_lists.shape[2]
    group = lax.axis_size(GROUP_AXES)
    coarse_count = group * CO_DEV
    shape = jax.ShapeDtypeStruct
    like = lambda a: shape(a.shape, a.dtype)
    vmem = pltpu.VMEM
    dma = pltpu.SemaphoreType.DMA
    square = 2 * width * width
    blocks = shape((group, CO_DEV, width), BF16)
    ids = lambda a: a[None, :]

    (head,) = call(
        head_kernel, "head", (shape((CO_DEV, width), BF16),), in_hbm(node_latents), hbm=(0,),
        scratch=[vmem((TOP, width), BF16), dma(())],
    )
    sub, patch = lax.axis_size("sub"), lax.axis_size("patch")
    assert sub & (sub - 1) == 0 and patch & (patch - 1) == 0
    near = [swap(head, mask, "sub") for mask in reversed(range(1, sub))]
    nodes, cedges, w_ends, w_out, to_even, to_odd, gather, picks, coarse_part = call(
        load_kernel,
        "load",
        (
            like(node_latents),
            like(coarse_edges),
            shape((2 * width, width), BF16),
            like(w_edge_out),
            shape((halo, width), BF16),
            shape((halo, width), BF16),
            shape((2 * cedge_count, coarse_count), BF16),
            shape((coarse_count, cedge_count), BF16),
            shape((cedge_count, width), F32),
        ),
        in_hbm(node_latents, halo_lists, coarse_edges, w_edge_in, ids(coarse_senders), ids(coarse_receivers), w_edge_out)
        + [head],
        hbm=range(8),
        scratch=[
            vmem(halo_lists.shape, jnp.int32), vmem((width, width), BF16),
            vmem((1, cedge_count), jnp.int32), vmem((1, cedge_count), jnp.int32), dma((8,)),
        ],
        flops=edge_count * square,
    )
    (lat,) = call(
        join_kernel, "join", (shape((sub * CO_DEV, width), BF16),), [head] + near + [nodes], hbm=(sub,),
    )
    far = [swap(lat, mask, "patch") for mask in reversed(range(1, patch))]
    to_even, to_odd = call(
        pass_kernel, "pass", (like(to_even), like(to_odd)), [to_even, to_odd, lat], hbm=range(3), out_specs=[ANY, ANY],
        input_output_aliases={0: 0, 1: 1},
    )
    from_even, from_odd = pair(to_even, 0), pair(to_odd, 1)
    new_coarse, sums = call(
        functools.partial(coarse_kernel, patch), "coarse", (like(coarse_edges), blocks),
        [lat] + far + [cedges, coarse_part, gather, picks, w_ends, w_out], flops=0,
    )
    got = lax.all_to_all(sums, GROUP_AXES, 0, 0)
    new_edges, rest, agg, node_part, wn_agg, wn_out = call(
        fine_kernel,
        "fine",
        (
            like(edge_latents),
            like(node_latents),
            shape((TOP, width), F32),
            shape((TOP, width), F32),
            shape((width, width), BF16),
            like(w_node_out),
        ),
        [from_even, nodes, from_odd, w_ends, w_out]
        + in_hbm(edge_latents, w_edge_in, ids(fine_senders), ids(fine_receivers), w_node_in, w_node_out)
        + [sums],
        hbm=range(5, 12),
        out_specs=[ANY] + [VMEM] * 5,
        scratch=[
            vmem(edge_latents.shape, BF16), vmem((width, width), BF16), vmem((1, edge_count), jnp.int32),
            vmem((1, edge_count), jnp.int32), vmem((width, width), BF16), vmem(edge_latents.shape, BF16), dma((7,)),
            dma((edge_count // STEP,)),
        ],
        flops=64 * edge_count * square,
    )
    new_nodes = pl.pallas_call(
        top_kernel,
        grid=(1,),
        out_shape=like(node_latents),
        in_specs=[VMEM] * 6 + [ANY],
        out_specs=pl.BlockSpec((TOP, width), lambda i: (0, 0)),
        input_output_aliases={6: 0},
        compiler_params=pltpu.CompilerParams(vmem_limit_bytes=16 * MIB),
        name="top",
    )(got, agg, node_part, nodes, wn_agg, wn_out, rest)
    return (new_nodes, new_edges, new_coarse)


def solution(mesh):
    rows = P(("parts", "patch", "sub"), None)
    ids = P(("parts", "patch", "sub"))
    in_specs = (
        rows, rows, rows, P(), P(), P(), P(), ids, ids, P(("parts", "patch", "sub"), None, None), ids, ids,
    )
    return jax.shard_map(body, mesh=mesh, in_specs=in_specs, out_specs=(rows, rows, rows), check_vma=False)
```

```python
import functools

import jax
import jax.numpy as jnp
from jax import lax
from jax.experimental import pallas as pl
from jax.experimental.pallas import tpu as pltpu
from jax.sharding import PartitionSpec as P

CO_DEV = 4
GROUP_AXES = ("patch", "sub")
TOP = 16
STEP = 128
MIB = 1 << 20
ANY = pl.BlockSpec(memory_space=pl.ANY)
VMEM = pl.BlockSpec(memory_space=pltpu.VMEM)
BF16, F32 = jnp.bfloat16, jnp.float32


def swap(value, mask, axis):
    return lax.ppermute(value, axis, [(i, i ^ mask) for i in range(lax.axis_size(axis))])


def ring_place(index, devices):
    half = devices // 2
    return 2 * (index % half) + index // half


def ring_device(place, devices):
    return (place % 2) * (devices // 2) + place // 2


def turn(value, by):
    devices = lax.axis_size("patch")
    ring = [ring_device(place, devices) for place in range(devices)]
    return lax.ppermute(value, "patch", [(ring[i], ring[(i + by) % devices]) for i in range(devices)])


def pair(value, first):
    devices = lax.axis_size(GROUP_AXES)
    pairs = [(i, (i + 1) % devices) for i in range(first, devices, 2)]
    return lax.ppermute(value, GROUP_AXES, pairs + [(b, a) for a, b in pairs])


def dot(a, b):
    return jnp.dot(a, b, preferred_element_type=F32)


def dot_t(a, b):
    return lax.dot_general(a, b, (((0,), (0,)), ((), ())), preferred_element_type=F32)


def onehot_t(rows, ids):
    at = lax.broadcasted_iota(jnp.int32, (rows, ids.shape[1]), 0)
    return jnp.where(at == ids, 1.0, 0.0).astype(BF16)


def silu(v):
    half = 0.5 * v
    return half + half * jnp.tanh(half)


def norm_parts(values):
    mean = jnp.mean(values, axis=-1, keepdims=True)
    centred = values - mean
    return centred, lax.rsqrt(jnp.mean(centred * centred, axis=-1, keepdims=True) + 1e-05)


def head_kernel(nodes_hbm, head_ref, rows_ref, sem):
    copy = pltpu.make_async_copy(nodes_hbm.at[pl.ds(0, TOP)], rows_ref, sem)
    copy.start()
    copy.wait()
    head_ref[...] = rows_ref[0:CO_DEV, :]


def join_rows(refs, order):
    refs = [refs[0]] + [ref for _, ref in sorted(zip(order, refs[1:]), key=lambda item: item[0])]
    return jnp.concatenate([ref[...].astype(F32) for ref in refs], axis=0).astype(BF16)


def join_kernel(masks, *refs):
    refs, (after, out_ref) = refs[:-2], refs[-2:]
    out_ref[...] = join_rows(refs, masks)


def pass_kernel(even_ref, odd_ref, after, even_out, odd_out):
    pass


def start_copies(sources, targets, sems):
    copies = [pltpu.make_async_copy(a, b, sems.at[i]) for i, (a, b) in enumerate(zip(sources, targets))]
    for copy in copies:
        copy.start()
    return copies


def load_kernel(
    nodes_hbm, lists_hbm, cedges_hbm, w_in_hbm, csend_hbm, crecv_hbm, w_out_hbm, after,
    nodes_ref, cedges_ref, w_ends_ref, w_out_ref, even_ref, odd_ref, gather_ref, picks_ref, part_ref,
    lists_ref, w_self_ref, csend_ref, crecv_ref, sems,
):
    width = nodes_ref.shape[1]
    copies = start_copies(
        [
            nodes_hbm, lists_hbm, cedges_hbm, w_in_hbm.at[pl.ds(0, width)], csend_hbm, crecv_hbm,
            w_in_hbm.at[pl.ds(width, 2 * width)], w_out_hbm,
        ],
        [nodes_ref, lists_ref, cedges_ref, w_self_ref, csend_ref, crecv_ref, w_ends_ref, w_out_ref],
        sems,
    )
    for copy in copies[:2]:
        copy.wait()
    nodes = nodes_ref[...]
    count = nodes.shape[0]
    lists = lists_ref[0]
    me = lax.axis_index(GROUP_AXES)
    odd = me % 2
    first = lists[0:1, :] * (1 - odd) + lists[1:2, :] * odd
    second = lists[1:2, :] * (1 - odd) + lists[0:1, :] * odd
    even_ref[...] = dot_t(onehot_t(count, first), nodes).astype(BF16)
    odd_ref[...] = dot_t(onehot_t(count, second), nodes).astype(BF16)
    for copy in copies[2:6]:
        copy.wait()
    part_ref[...] = dot(cedges_ref[...], w_self_ref[...])
    rows, ids = picks_ref.shape
    sub, patch = lax.axis_size("sub"), lax.axis_size("patch")
    at = lax.broadcasted_iota(jnp.int32, (rows, ids), 0)
    block = at // CO_DEV
    place = ring_place(lax.axis_index("patch"), patch) + patch - block // sub
    device = ring_device(place % patch, patch) * sub + (lax.axis_index("sub") ^ (block % sub))
    node = device * CO_DEV + at % CO_DEV
    send = jnp.where(node == csend_ref[...], 1.0, 0.0).astype(BF16)
    recv = jnp.where(node == crecv_ref[...], 1.0, 0.0).astype(BF16)
    picks_ref[...] = onehot_t(rows, crecv_ref[...])
    across = lax.broadcasted_iota(jnp.int32, (rows, rows), 0) == lax.broadcasted_iota(jnp.int32, (rows, rows), 1)
    eye = jnp.where(across, 1.0, 0.0).astype(BF16)
    gather_ref[0:ids, :] = dot_t(send, eye).astype(BF16)
    gather_ref[ids:, :] = dot_t(recv, eye).astype(BF16)
    for copy in copies[6:]:
        copy.wait()


def coarse_kernel(turns, *refs):
    parts = len(turns) + 1
    lats, refs = refs[:parts], refs[parts:]
    edges_ref, part_ref, gather_ref, picks_ref, w_ends_ref, w_out_ref, new_ref, sums_ref = refs
    count, width = edges_ref.shape
    lat = join_rows(lats, turns)
    ends = dot(gather_ref[...], lat).astype(BF16)
    pre = part_ref[...] + dot(ends[0:count], w_ends_ref[0:width, :]) + dot(ends[count:], w_ends_ref[width:, :])
    hidden = silu(pre).astype(BF16)
    centred, scale = norm_parts(dot(hidden, w_out_ref[...]))
    new = (edges_ref[...].astype(F32) + centred * scale).astype(BF16)
    new_ref[...] = new
    sums = dot(picks_ref[...], new).astype(BF16)
    for at in range(sums_ref.shape[0]):
        sums_ref[at] = sums[at * CO_DEV : (at + 1) * CO_DEV, :]


def fine_kernel(
    even_ref, nodes_ref, odd_ref, w_ends_ref, w_out_ref,
    edges_hbm, w_in_hbm, send_hbm, recv_hbm, wn_in_hbm, wn_out_hbm, after,
    new_hbm, out_ref, agg_ref, npart_ref, wn_agg_ref, wn_out_ref,
    edges_ref, w_self_ref, send_ref, recv_ref, wn_self_ref, new_ref, sems, out_sems,
):
    nodes = nodes_ref[...]
    count, width = nodes.shape
    copies = start_copies(
        [
            send_hbm, recv_hbm, edges_hbm, w_in_hbm.at[pl.ds(0, width)],
            wn_in_hbm.at[pl.ds(0, width)], wn_in_hbm.at[pl.ds(width, width)], wn_out_hbm,
        ],
        [send_ref, recv_ref, edges_ref, w_self_ref, wn_self_ref, wn_agg_ref, wn_out_ref],
        sems,
    )
    odd = (lax.axis_index(GROUP_AXES) % 2).astype(F32)
    met, other = even_ref[...].astype(F32), odd_ref[...].astype(F32)
    prev = (met * odd + other * (1.0 - odd)).astype(BF16)
    following = (other * odd + met * (1.0 - odd)).astype(BF16)
    extended = jnp.concatenate([prev, nodes, following], axis=0)
    ones = jnp.ones((count, 128), BF16)
    total = jnp.zeros((count, width), F32)
    for copy in copies[:4]:
        copy.wait()
    outs = []
    for at in range(0, edges_ref.shape[0], STEP):
        rows = pl.ds(at, STEP)
        picks = onehot_t(count, recv_ref[:, rows])
        senders = dot_t(onehot_t(extended.shape[0], send_ref[:, rows]), extended).astype(BF16)
        receivers = dot_t(picks, nodes).astype(BF16)
        valid = dot_t(picks, ones)[:, 0:1]
        edges = edges_ref[rows, :]
        pre = dot(edges, w_self_ref[...]) + dot(senders, w_ends_ref[0:width, :]) + dot(receivers, w_ends_ref[width:, :])
        hidden = silu(pre).astype(BF16)
        centred, scale = norm_parts(dot(hidden, w_out_ref[...]))
        new = (edges.astype(F32) + centred * (scale * valid)).astype(BF16)
        new_ref[rows, :] = new
        copy = pltpu.make_async_copy(new_ref.at[rows], new_hbm.at[rows], out_sems.at[at // STEP])
        copy.start()
        outs.append(copy)
        total = total + dot(picks, new)
    agg_ref[...] = total[0:TOP]
    for copy in copies[4:]:
        copy.wait()
    pre = dot(nodes, wn_self_ref[...])
    npart_ref[...] = pre[0:TOP]
    pre = pre + dot(total.astype(BF16), wn_agg_ref[...])
    hidden = silu(pre).astype(BF16)
    centred, scale = norm_parts(dot(hidden, wn_out_ref[...]))
    out_ref[...] = (nodes.astype(F32) + centred * scale).astype(BF16)
    for copy in outs:
        copy.wait()


def top_kernel(got_ref, agg_ref, part_ref, nodes_ref, wn_agg_ref, wn_out_ref, rest_ref, out_ref):
    width = agg_ref.shape[1]
    sums = got_ref[0].astype(F32)
    for at in range(1, got_ref.shape[0]):
        sums = sums + got_ref[at].astype(F32)
    sums = jnp.concatenate([sums, jnp.zeros((TOP - CO_DEV, width), F32)], axis=0)
    agg = (agg_ref[...] + sums).astype(BF16)
    hidden = silu(part_ref[...] + dot(agg, wn_agg_ref[...])).astype(BF16)
    centred, scale = norm_parts(dot(hidden, wn_out_ref[...]))
    out_ref[...] = (nodes_ref[0:TOP, :].astype(F32) + centred * scale).astype(BF16)


def in_hbm(*arrays):
    return [pltpu.with_memory_space_constraint(a, pltpu.HBM) for a in arrays]


def cost(flops, moved=0):
    return pl.CostEstimate(flops=flops, bytes_accessed=moved, transcendentals=0)


def call(kernel, name, outs, ins, out_specs=None, scratch=(), hbm=(), flops=0, **more):
    return pl.pallas_call(
        kernel,
        out_shape=outs,
        in_specs=[ANY if i in hbm else VMEM for i in range(len(ins))],
        out_specs=[VMEM] * len(outs) if out_specs is None else out_specs,
        scratch_shapes=scratch,
        compiler_params=pltpu.CompilerParams(vmem_limit_bytes=16 * MIB),
        cost_estimate=cost(flops),
        name=name,
        **more,
    )(*ins)


def body(
    node_latents,
    edge_latents,
    coarse_edges,
    w_edge_in,
    w_edge_out,
    w_node_in,
    w_node_out,
    fine_senders,
    fine_receivers,
    halo_lists,
    coarse_senders,
    coarse_receivers,
):
    count, width = node_latents.shape
    edge_count = edge_latents.shape[0]
    cedge_count = coarse_edges.shape[0]
    halo = halo_lists.shape[2]
    group = lax.axis_size(GROUP_AXES)
    coarse_count = group * CO_DEV
    shape = jax.ShapeDtypeStruct
    like = lambda a: shape(a.shape, a.dtype)
    vmem = pltpu.VMEM
    dma = pltpu.SemaphoreType.DMA
    square = 2 * width * width
    blocks = shape((group, CO_DEV, width), BF16)
    ids = lambda a: a[None, :]

    (head,) = call(
        head_kernel, "head", (shape((CO_DEV, width), BF16),), in_hbm(node_latents), hbm=(0,),
        scratch=[vmem((TOP, width), BF16), dma(())],
    )
    sub, patch = lax.axis_size("sub"), lax.axis_size("patch")
    assert sub & (sub - 1) == 0 and patch % 2 == 0
    masks = list(reversed(range(1, sub)))
    turns = sorted(range(1, patch), key=lambda by: (min(by, patch - by), by))
    near = [swap(head, mask, "sub") for mask in masks]
    nodes, cedges, w_ends, w_out, to_even, to_odd, gather, picks, coarse_part = call(
        load_kernel,
        "load",
        (
            like(node_latents),
            like(coarse_edges),
            shape((2 * width, width), BF16),
            like(w_edge_out),
            shape((halo, width), BF16),
            shape((halo, width), BF16),
            shape((2 * cedge_count, coarse_count), BF16),
            shape((coarse_count, cedge_count), BF16),
            shape((cedge_count, width), F32),
        ),
        in_hbm(node_latents, halo_lists, coarse_edges, w_edge_in, ids(coarse_senders), ids(coarse_receivers), w_edge_out)
        + [head],
        hbm=range(8),
        scratch=[
            vmem(halo_lists.shape, jnp.int32), vmem((width, width), BF16),
            vmem((1, cedge_count), jnp.int32), vmem((1, cedge_count), jnp.int32), dma((8,)),
        ],
        flops=edge_count * square,
    )
    (lat,) = call(
        functools.partial(join_kernel, masks), "join", (shape((sub * CO_DEV, width), BF16),), [head] + near + [nodes], hbm=(sub,),
    )
    far = [turn(lat, by) for by in turns]
    to_even, to_odd = call(
        pass_kernel, "pass", (like(to_even), like(to_odd)), [to_even, to_odd, lat], hbm=range(3), out_specs=[ANY, ANY],
        input_output_aliases={0: 0, 1: 1},
    )
    from_even, from_odd = pair(to_even, 0), pair(to_odd, 1)
    new_coarse, sums = call(
        functools.partial(coarse_kernel, turns), "coarse", (like(coarse_edges), blocks),
        [lat] + far + [cedges, coarse_part, gather, picks, w_ends, w_out], flops=0,
    )
    got = lax.all_to_all(sums, GROUP_AXES, 0, 0)
    new_edges, rest, agg, node_part, wn_agg, wn_out = call(
        fine_kernel,
        "fine",
        (
            like(edge_latents),
            like(node_latents),
            shape((TOP, width), F32),
            shape((TOP, width), F32),
            shape((width, width), BF16),
            like(w_node_out),
        ),
        [from_even, nodes, from_odd, w_ends, w_out]
        + in_hbm(edge_latents, w_edge_in, ids(fine_senders), ids(fine_receivers), w_node_in, w_node_out)
        + [sums],
        hbm=range(5, 12),
        out_specs=[ANY] + [VMEM] * 5,
        scratch=[
            vmem(edge_latents.shape, BF16), vmem((width, width), BF16), vmem((1, edge_count), jnp.int32),
            vmem((1, edge_count), jnp.int32), vmem((width, width), BF16), vmem(edge_latents.shape, BF16), dma((7,)),
            dma((edge_count // STEP,)),
        ],
        flops=64 * edge_count * square,
    )
    new_nodes = pl.pallas_call(
        top_kernel,
        grid=(1,),
        out_shape=like(node_latents),
        in_specs=[VMEM] * 6 + [ANY],
        out_specs=pl.BlockSpec((TOP, width), lambda i: (0, 0)),
        input_output_aliases={6: 0},
        compiler_params=pltpu.CompilerParams(vmem_limit_bytes=16 * MIB),
        name="top",
    )(got, agg, node_part, nodes, wn_agg, wn_out, rest)
    return (new_nodes, new_edges, new_coarse)


def solution(mesh):
    rows = P(("parts", "patch", "sub"), None)
    ids = P(("parts", "patch", "sub"))
    in_specs = (
        rows, rows, rows, P(), P(), P(), P(), ids, ids, P(("parts", "patch", "sub"), None, None), ids, ids,
    )
    return jax.shard_map(body, mesh=mesh, in_specs=in_specs, out_specs=(rows, rows, rows), check_vma=False)
```

```python
import functools

import jax
import jax.numpy as jnp
from jax import lax
from jax.experimental import pallas as pl
from jax.experimental.pallas import tpu as pltpu
from jax.sharding import PartitionSpec as P

CO_DEV = 4
GROUP_AXES = ("patch", "sub")
TOP = 16
STEP = 128
MIB = 1 << 20
ANY = pl.BlockSpec(memory_space=pl.ANY)
VMEM = pl.BlockSpec(memory_space=pltpu.VMEM)
BF16, F32 = jnp.bfloat16, jnp.float32


def plan(devices):
    sends = []
    top = devices // 2
    while top > 1:
        sends += [(top, 1)] + [(top + low, 2) for low in range(1, top)] + [(top, 0)]
        top //= 2
    return sends + [(1, 2)] * (devices > 1)


def spread(value, axis):
    devices = lax.axis_size(axis)
    got = []
    for mask, who in plan(devices):
        senders = [i for i in range(devices) if who == 2 or int(i & mask != 0) == who]
        got.append(lax.ppermute(value, axis, [(i, i ^ mask) for i in senders]))
    return got


def pair(value, first):
    devices = lax.axis_size(GROUP_AXES)
    pairs = [(i, (i + 1) % devices) for i in range(first, devices, 2)]
    return lax.ppermute(value, GROUP_AXES, pairs + [(b, a) for a, b in pairs])


def dot(a, b):
    return jnp.dot(a, b, preferred_element_type=F32)


def dot_t(a, b):
    return lax.dot_general(a, b, (((0,), (0,)), ((), ())), preferred_element_type=F32)


def onehot_t(rows, ids):
    at = lax.broadcasted_iota(jnp.int32, (rows, ids.shape[1]), 0)
    return jnp.where(at == ids, 1.0, 0.0).astype(BF16)


def silu(v):
    half = 0.5 * v
    return half + half * jnp.tanh(half)


def norm_parts(values):
    mean = jnp.mean(values, axis=-1, keepdims=True)
    centred = values - mean
    return centred, lax.rsqrt(jnp.mean(centred * centred, axis=-1, keepdims=True) + 1e-05)


def head_kernel(nodes_hbm, head_ref, rows_ref, sem):
    copy = pltpu.make_async_copy(nodes_hbm.at[pl.ds(0, TOP)], rows_ref, sem)
    copy.start()
    copy.wait()
    head_ref[...] = rows_ref[0:CO_DEV, :]


def join_rows(refs, axis):
    devices, me = lax.axis_size(axis), lax.axis_index(axis)
    rows = [refs[0][...].astype(F32)] + [None] * (devices - 1)
    for (mask, who), ref in zip(plan(devices), refs[1:]):
        value = ref[...].astype(F32)
        if who == 0:
            value = jnp.where((me & mask) != 0, value, rows[mask])
        rows[mask] = value
    return jnp.concatenate(rows, axis=0).astype(BF16)


def join_kernel(*refs):
    refs, (after, out_ref) = refs[:-2], refs[-2:]
    out_ref[...] = join_rows(refs, "sub")


def pass_kernel(even_ref, odd_ref, after, even_out, odd_out):
    pass


def start_copies(sources, targets, sems):
    copies = [pltpu.make_async_copy(a, b, sems.at[i]) for i, (a, b) in enumerate(zip(sources, targets))]
    for copy in copies:
        copy.start()
    return copies


def load_kernel(
    nodes_hbm, lists_hbm, cedges_hbm, w_in_hbm, csend_hbm, crecv_hbm, w_out_hbm, after,
    nodes_ref, cedges_ref, w_ends_ref, w_out_ref, even_ref, odd_ref, gather_ref, picks_ref, part_ref,
    lists_ref, w_self_ref, csend_ref, crecv_ref, sems,
):
    width = nodes_ref.shape[1]
    copies = start_copies(
        [
            nodes_hbm, lists_hbm, cedges_hbm, w_in_hbm.at[pl.ds(0, width)], csend_hbm, crecv_hbm,
            w_in_hbm.at[pl.ds(width, 2 * width)], w_out_hbm,
        ],
        [nodes_ref, lists_ref, cedges_ref, w_self_ref, csend_ref, crecv_ref, w_ends_ref, w_out_ref],
        sems,
    )
    for copy in copies[:2]:
        copy.wait()
    nodes = nodes_ref[...]
    count = nodes.shape[0]
    lists = lists_ref[0]
    me = lax.axis_index(GROUP_AXES)
    odd = me % 2
    first = lists[0:1, :] * (1 - odd) + lists[1:2, :] * odd
    second = lists[1:2, :] * (1 - odd) + lists[0:1, :] * odd
    even_ref[...] = dot_t(onehot_t(count, first), nodes).astype(BF16)
    odd_ref[...] = dot_t(onehot_t(count, second), nodes).astype(BF16)
    for copy in copies[2:6]:
        copy.wait()
    part_ref[...] = dot(cedges_ref[...], w_self_ref[...])
    rows, ids = picks_ref.shape
    send = onehot_t(rows, csend_ref[...] ^ (me * CO_DEV))
    recv = onehot_t(rows, crecv_ref[...] ^ (me * CO_DEV))
    picks_ref[...] = onehot_t(rows, crecv_ref[...])
    across = lax.broadcasted_iota(jnp.int32, (rows, rows), 0) == lax.broadcasted_iota(jnp.int32, (rows, rows), 1)
    eye = jnp.where(across, 1.0, 0.0).astype(BF16)
    gather_ref[0:ids, :] = dot_t(send, eye).astype(BF16)
    gather_ref[ids:, :] = dot_t(recv, eye).astype(BF16)
    for copy in copies[6:]:
        copy.wait()


def coarse_kernel(parts, *refs):
    lats, refs = refs[:parts], refs[parts:]
    edges_ref, part_ref, gather_ref, picks_ref, w_ends_ref, w_out_ref, new_ref, sums_ref = refs
    count, width = edges_ref.shape
    lat = join_rows(lats, "patch")
    ends = dot(gather_ref[...], lat).astype(BF16)
    pre = part_ref[...] + dot(ends[0:count], w_ends_ref[0:width, :]) + dot(ends[count:], w_ends_ref[width:, :])
    hidden = silu(pre).astype(BF16)
    centred, scale = norm_parts(dot(hidden, w_out_ref[...]))
    new = (edges_ref[...].astype(F32) + centred * scale).astype(BF16)
    new_ref[...] = new
    sums = dot(picks_ref[...], new).astype(BF16)
    for at in range(sums_ref.shape[0]):
        sums_ref[at] = sums[at * CO_DEV : (at + 1) * CO_DEV, :]


def fine_kernel(
    even_ref, nodes_ref, odd_ref, w_ends_ref, w_out_ref,
    edges_hbm, w_in_hbm, send_hbm, recv_hbm, wn_in_hbm, wn_out_hbm, after,
    new_hbm, out_ref, agg_ref, npart_ref, wn_agg_ref, wn_out_ref,
    edges_ref, w_self_ref, send_ref, recv_ref, wn_self_ref, new_ref, sems, out_sems,
):
    nodes = nodes_ref[...]
    count, width = nodes.shape
    copies = start_copies(
        [
            send_hbm, recv_hbm, edges_hbm, w_in_hbm.at[pl.ds(0, width)],
            wn_in_hbm.at[pl.ds(0, width)], wn_in_hbm.at[pl.ds(width, width)], wn_out_hbm,
        ],
        [send_ref, recv_ref, edges_ref, w_self_ref, wn_self_ref, wn_agg_ref, wn_out_ref],
        sems,
    )
    odd = (lax.axis_index(GROUP_AXES) % 2).astype(F32)
    met, other = even_ref[...].astype(F32), odd_ref[...].astype(F32)
    prev = (met * odd + other * (1.0 - odd)).astype(BF16)
    following = (other * odd + met * (1.0 - odd)).astype(BF16)
    extended = jnp.concatenate([prev, nodes, following], axis=0)
    ones = jnp.ones((count, 128), BF16)
    total = jnp.zeros((count, width), F32)
    for copy in copies[:4]:
        copy.wait()
    outs = []
    for at in range(0, edges_ref.shape[0], STEP):
        rows = pl.ds(at, STEP)
        picks = onehot_t(count, recv_ref[:, rows])
        senders = dot_t(onehot_t(extended.shape[0], send_ref[:, rows]), extended).astype(BF16)
        receivers = dot_t(picks, nodes).astype(BF16)
        valid = dot_t(picks, ones)[:, 0:1]
        edges = edges_ref[rows, :]
        pre = dot(edges, w_self_ref[...]) + dot(senders, w_ends_ref[0:width, :]) + dot(receivers, w_ends_ref[width:, :])
        hidden = silu(pre).astype(BF16)
        centred, scale = norm_parts(dot(hidden, w_out_ref[...]))
        new = (edges.astype(F32) + centred * (scale * valid)).astype(BF16)
        new_ref[rows, :] = new
        copy = pltpu.make_async_copy(new_ref.at[rows], new_hbm.at[rows], out_sems.at[at // STEP])
        copy.start()
        outs.append(copy)
        total = total + dot(picks, new)
    agg_ref[...] = total[0:TOP]
    for copy in copies[4:]:
        copy.wait()
    pre = dot(nodes, wn_self_ref[...])
    npart_ref[...] = pre[0:TOP]
    pre = pre + dot(total.astype(BF16), wn_agg_ref[...])
    hidden = silu(pre).astype(BF16)
    centred, scale = norm_parts(dot(hidden, wn_out_ref[...]))
    out_ref[...] = (nodes.astype(F32) + centred * scale).astype(BF16)
    for copy in outs:
        copy.wait()


def top_kernel(got_ref, agg_ref, part_ref, nodes_ref, wn_agg_ref, wn_out_ref, rest_ref, out_ref):
    width = agg_ref.shape[1]
    sums = got_ref[0].astype(F32)
    for at in range(1, got_ref.shape[0]):
        sums = sums + got_ref[at].astype(F32)
    sums = jnp.concatenate([sums, jnp.zeros((TOP - CO_DEV, width), F32)], axis=0)
    agg = (agg_ref[...] + sums).astype(BF16)
    hidden = silu(part_ref[...] + dot(agg, wn_agg_ref[...])).astype(BF16)
    centred, scale = norm_parts(dot(hidden, wn_out_ref[...]))
    out_ref[...] = (nodes_ref[0:TOP, :].astype(F32) + centred * scale).astype(BF16)


def in_hbm(*arrays):
    return [pltpu.with_memory_space_constraint(a, pltpu.HBM) for a in arrays]


def cost(flops, moved=0):
    return pl.CostEstimate(flops=flops, bytes_accessed=moved, transcendentals=0)


def call(kernel, name, outs, ins, out_specs=None, scratch=(), hbm=(), flops=0, **more):
    return pl.pallas_call(
        kernel,
        out_shape=outs,
        in_specs=[ANY if i in hbm else VMEM for i in range(len(ins))],
        out_specs=[VMEM] * len(outs) if out_specs is None else out_specs,
        scratch_shapes=scratch,
        compiler_params=pltpu.CompilerParams(vmem_limit_bytes=16 * MIB),
        cost_estimate=cost(flops),
        name=name,
        **more,
    )(*ins)


def body(
    node_latents,
    edge_latents,
    coarse_edges,
    w_edge_in,
    w_edge_out,
    w_node_in,
    w_node_out,
    fine_senders,
    fine_receivers,
    halo_lists,
    coarse_senders,
    coarse_receivers,
):
    count, width = node_latents.shape
    edge_count = edge_latents.shape[0]
    cedge_count = coarse_edges.shape[0]
    halo = halo_lists.shape[2]
    group = lax.axis_size(GROUP_AXES)
    coarse_count = group * CO_DEV
    shape = jax.ShapeDtypeStruct
    like = lambda a: shape(a.shape, a.dtype)
    vmem = pltpu.VMEM
    dma = pltpu.SemaphoreType.DMA
    square = 2 * width * width
    blocks = shape((group, CO_DEV, width), BF16)
    ids = lambda a: a[None, :]

    (head,) = call(
        head_kernel, "head", (shape((CO_DEV, width), BF16),), in_hbm(node_latents), hbm=(0,),
        scratch=[vmem((TOP, width), BF16), dma(())],
    )
    sub, patch = lax.axis_size("sub"), lax.axis_size("patch")
    assert sub & (sub - 1) == 0 and patch & (patch - 1) == 0
    near = spread(head, "sub")
    nodes, cedges, w_ends, w_out, to_even, to_odd, gather, picks, coarse_part = call(
        load_kernel,
        "load",
        (
            like(node_latents),
            like(coarse_edges),
            shape((2 * width, width), BF16),
            like(w_edge_out),
            shape((halo, width), BF16),
            shape((halo, width), BF16),
            shape((2 * cedge_count, coarse_count), BF16),
            shape((coarse_count, cedge_count), BF16),
            shape((cedge_count, width), F32),
        ),
        in_hbm(node_latents, halo_lists, coarse_edges, w_edge_in, ids(coarse_senders), ids(coarse_receivers), w_edge_out)
        + [head],
        hbm=range(8),
        scratch=[
            vmem(halo_lists.shape, jnp.int32), vmem((width, width), BF16),
            vmem((1, cedge_count), jnp.int32), vmem((1, cedge_count), jnp.int32), dma((8,)),
        ],
        flops=edge_count * square,
    )
    (lat,) = call(
        join_kernel, "join", (shape((sub * CO_DEV, width), BF16),), [head] + near + [nodes], hbm=(len(near) + 1,),
    )
    far = spread(lat, "patch")
    to_even, to_odd = call(
        pass_kernel, "pass", (like(to_even), like(to_odd)), [to_even, to_odd, lat], hbm=range(3), out_specs=[ANY, ANY],
        input_output_aliases={0: 0, 1: 1},
    )
    from_even, from_odd = pair(to_even, 0), pair(to_odd, 1)
    new_coarse, sums = call(
        functools.partial(coarse_kernel, len(far) + 1), "coarse", (like(coarse_edges), blocks),
        [lat] + far + [cedges, coarse_part, gather, picks, w_ends, w_out], flops=0,
    )
    got = lax.all_to_all(sums, GROUP_AXES, 0, 0)
    new_edges, rest, agg, node_part, wn_agg, wn_out = call(
        fine_kernel,
        "fine",
        (
            like(edge_latents),
            like(node_latents),
            shape((TOP, width), F32),
            shape((TOP, width), F32),
            shape((width, width), BF16),
            like(w_node_out),
        ),
        [from_even, nodes, from_odd, w_ends, w_out]
        + in_hbm(edge_latents, w_edge_in, ids(fine_senders), ids(fine_receivers), w_node_in, w_node_out)
        + [sums],
        hbm=range(5, 12),
        out_specs=[ANY] + [VMEM] * 5,
        scratch=[
            vmem(edge_latents.shape, BF16), vmem((width, width), BF16), vmem((1, edge_count), jnp.int32),
            vmem((1, edge_count), jnp.int32), vmem((width, width), BF16), vmem(edge_latents.shape, BF16), dma((7,)),
            dma((edge_count // STEP,)),
        ],
        flops=64 * edge_count * square,
    )
    new_nodes = pl.pallas_call(
        top_kernel,
        grid=(1,),
        out_shape=like(node_latents),
        in_specs=[VMEM] * 6 + [ANY],
        out_specs=pl.BlockSpec((TOP, width), lambda i: (0, 0)),
        input_output_aliases={6: 0},
        compiler_params=pltpu.CompilerParams(vmem_limit_bytes=16 * MIB),
        name="top",
    )(got, agg, node_part, nodes, wn_agg, wn_out, rest)
    return (new_nodes, new_edges, new_coarse)


def solution(mesh):
    rows = P(("parts", "patch", "sub"), None)
    ids = P(("parts", "patch", "sub"))
    in_specs = (
        rows, rows, rows, P(), P(), P(), P(), ids, ids, P(("parts", "patch", "sub"), None, None), ids, ids,
    )
    return jax.shard_map(body, mesh=mesh, in_specs=in_specs, out_specs=(rows, rows, rows), check_vma=False)
```

```python
import functools

import jax
import jax.numpy as jnp
from jax import lax
from jax.experimental import pallas as pl
from jax.experimental.pallas import tpu as pltpu
from jax.sharding import PartitionSpec as P

CO_DEV = 4
GROUP_AXES = ("patch", "sub")
TOP = 16
STEP = 128
MIB = 1 << 20
ANY = pl.BlockSpec(memory_space=pl.ANY)
VMEM = pl.BlockSpec(memory_space=pltpu.VMEM)
BF16, F32 = jnp.bfloat16, jnp.float32


def swap(value, mask, axis):
    return lax.ppermute(value, axis, [(i, i ^ mask) for i in range(lax.axis_size(axis))])


def ring_place(index, devices):
    half = devices // 2
    return 2 * (index % half) + index // half


def ring_device(place, devices):
    return (place % 2) * (devices // 2) + place // 2


def turn(value, by):
    devices = lax.axis_size("patch")
    ring = [ring_device(place, devices) for place in range(devices)]
    return lax.ppermute(value, "patch", [(ring[i], ring[(i + by) % devices]) for i in range(devices)])


def pair(value, first):
    devices = lax.axis_size(GROUP_AXES)
    pairs = [(i, (i + 1) % devices) for i in range(first, devices, 2)]
    return lax.ppermute(value, GROUP_AXES, pairs + [(b, a) for a, b in pairs])


def dot(a, b):
    return jnp.dot(a, b, preferred_element_type=F32)


def dot_t(a, b):
    return lax.dot_general(a, b, (((0,), (0,)), ((), ())), preferred_element_type=F32)


def onehot_t(rows, ids):
    at = lax.broadcasted_iota(jnp.int32, (rows, ids.shape[1]), 0)
    return jnp.where(at == ids, 1.0, 0.0).astype(BF16)


def silu(v):
    half = 0.5 * v
    return half + half * jnp.tanh(half)


def norm_parts(values):
    mean = jnp.mean(values, axis=-1, keepdims=True)
    centred = values - mean
    return centred, lax.rsqrt(jnp.mean(centred * centred, axis=-1, keepdims=True) + 1e-05)


def head_kernel(nodes_hbm, head_ref, rows_ref, sem):
    copy = pltpu.make_async_copy(nodes_hbm.at[pl.ds(0, TOP)], rows_ref, sem)
    copy.start()
    copy.wait()
    head_ref[...] = rows_ref[0:CO_DEV, :]


def join_rows(refs, order):
    refs = [refs[0]] + [ref for _, ref in sorted(zip(order, refs[1:]), key=lambda item: item[0])]
    if refs[0].shape[0] % TOP == 0:
        return jnp.concatenate([ref[...] for ref in refs], axis=0)
    return jnp.concatenate([ref[...].astype(F32) for ref in refs], axis=0).astype(BF16)


def join_kernel(masks, *refs):
    refs, (after, out_ref) = refs[:-2], refs[-2:]
    out_ref[...] = join_rows(refs, masks)


def pass_kernel(even_ref, odd_ref, after, even_out, odd_out):
    pass


def start_copies(sources, targets, sems):
    copies = [pltpu.make_async_copy(a, b, sems.at[i]) for i, (a, b) in enumerate(zip(sources, targets))]
    for copy in copies:
        copy.start()
    return copies


def load_kernel(
    nodes_hbm, lists_hbm, cedges_hbm, w_in_hbm, csend_hbm, crecv_hbm, w_out_hbm, after,
    nodes_ref, cedges_ref, w_ends_ref, w_out_ref, even_ref, odd_ref, gather_ref, picks_ref, part_ref,
    lists_ref, w_self_ref, csend_ref, crecv_ref, sems,
):
    width = nodes_ref.shape[1]
    copies = start_copies(
        [
            nodes_hbm, lists_hbm, cedges_hbm, w_in_hbm.at[pl.ds(0, width)], csend_hbm, crecv_hbm,
            w_in_hbm.at[pl.ds(width, 2 * width)], w_out_hbm,
        ],
        [nodes_ref, lists_ref, cedges_ref, w_self_ref, csend_ref, crecv_ref, w_ends_ref, w_out_ref],
        sems,
    )
    for copy in copies[:2]:
        copy.wait()
    nodes = nodes_ref[...]
    count = nodes.shape[0]
    lists = lists_ref[0]
    me = lax.axis_index(GROUP_AXES)
    odd = me % 2
    first = lists[0:1, :] * (1 - odd) + lists[1:2, :] * odd
    second = lists[1:2, :] * (1 - odd) + lists[0:1, :] * odd
    even_ref[...] = dot_t(onehot_t(count, first), nodes).astype(BF16)
    odd_ref[...] = dot_t(onehot_t(count, second), nodes).astype(BF16)
    for copy in copies[2:6]:
        copy.wait()
    part_ref[...] = dot(cedges_ref[...], w_self_ref[...])
    rows, ids = picks_ref.shape
    sub, patch = lax.axis_size("sub"), lax.axis_size("patch")
    at = lax.broadcasted_iota(jnp.int32, (rows, ids), 0)
    block = at // CO_DEV
    place = ring_place(lax.axis_index("patch"), patch) + patch - block // sub
    device = ring_device(place % patch, patch) * sub + (lax.axis_index("sub") ^ (block % sub))
    node = device * CO_DEV + at % CO_DEV
    send = jnp.where(node == csend_ref[...], 1.0, 0.0).astype(BF16)
    recv = jnp.where(node == crecv_ref[...], 1.0, 0.0).astype(BF16)
    picks_ref[...] = onehot_t(rows, crecv_ref[...])
    across = lax.broadcasted_iota(jnp.int32, (rows, rows), 0) == lax.broadcasted_iota(jnp.int32, (rows, rows), 1)
    eye = jnp.where(across, 1.0, 0.0).astype(BF16)
    gather_ref[0:ids, :] = dot_t(send, eye).astype(BF16)
    gather_ref[ids:, :] = dot_t(recv, eye).astype(BF16)
    for copy in copies[6:]:
        copy.wait()


def coarse_kernel(turns, *refs):
    parts = len(turns) + 1
    lats, refs = refs[:parts], refs[parts:]
    edges_ref, part_ref, gather_ref, picks_ref, w_ends_ref, w_out_ref, new_ref, sums_ref = refs
    count, width = edges_ref.shape
    lat = join_rows(lats, turns)
    ends = dot(gather_ref[...], lat).astype(BF16)
    ends = jnp.concatenate([ends[0:count], ends[count:]], axis=1)
    hidden = silu(part_ref[...] + dot(ends, w_ends_ref[...])).astype(BF16)
    centred, scale = norm_parts(dot(hidden, w_out_ref[...]))
    new = (edges_ref[...].astype(F32) + centred * scale).astype(BF16)
    new_ref[...] = new
    sums = dot(picks_ref[...], new).astype(BF16)
    for at in range(sums_ref.shape[0]):
        sums_ref[at] = sums[at * CO_DEV : (at + 1) * CO_DEV, :]


def fine_kernel(
    even_ref, nodes_ref, odd_ref, w_ends_ref, w_out_ref,
    edges_hbm, w_in_hbm, send_hbm, recv_hbm, wn_in_hbm, wn_out_hbm, after,
    new_hbm, out_ref, agg_ref, npart_ref, wn_agg_ref, wn_out_ref,
    edges_ref, w_self_ref, send_ref, recv_ref, wn_self_ref, new_ref, sems, out_sems,
):
    nodes = nodes_ref[...]
    count, width = nodes.shape
    copies = start_copies(
        [
            send_hbm, recv_hbm, edges_hbm, w_in_hbm.at[pl.ds(0, width)],
            wn_in_hbm.at[pl.ds(0, width)], wn_in_hbm.at[pl.ds(width, width)], wn_out_hbm,
        ],
        [send_ref, recv_ref, edges_ref, w_self_ref, wn_self_ref, wn_agg_ref, wn_out_ref],
        sems,
    )
    odd = (lax.axis_index(GROUP_AXES) % 2).astype(F32)
    met, other = even_ref[...].astype(F32), odd_ref[...].astype(F32)
    prev = (met * odd + other * (1.0 - odd)).astype(BF16)
    following = (other * odd + met * (1.0 - odd)).astype(BF16)
    extended = jnp.concatenate([prev, nodes, following], axis=0)
    ones = jnp.ones((count, 128), BF16)
    total = jnp.zeros((count, width), F32)
    for copy in copies[:4]:
        copy.wait()
    outs = []
    for at in range(0, edges_ref.shape[0], STEP):
        rows = pl.ds(at, STEP)
        picks = onehot_t(count, recv_ref[:, rows])
        senders = dot_t(onehot_t(extended.shape[0], send_ref[:, rows]), extended).astype(BF16)
        receivers = dot_t(picks, nodes).astype(BF16)
        valid = dot_t(picks, ones)[:, 0:1]
        edges = edges_ref[rows, :]
        pre = dot(edges, w_self_ref[...]) + dot(senders, w_ends_ref[0:width, :]) + dot(receivers, w_ends_ref[width:, :])
        hidden = silu(pre).astype(BF16)
        centred, scale = norm_parts(dot(hidden, w_out_ref[...]))
        new = (edges.astype(F32) + centred * (scale * valid)).astype(BF16)
        new_ref[rows, :] = new
        copy = pltpu.make_async_copy(new_ref.at[rows], new_hbm.at[rows], out_sems.at[at // STEP])
        copy.start()
        outs.append(copy)
        total = total + dot(picks, new)
    agg_ref[...] = total[0:TOP]
    for copy in copies[4:]:
        copy.wait()
    pre = dot(nodes, wn_self_ref[...])
    npart_ref[...] = pre[0:TOP]
    pre = pre + dot(total.astype(BF16), wn_agg_ref[...])
    hidden = silu(pre).astype(BF16)
    centred, scale = norm_parts(dot(hidden, wn_out_ref[...]))
    out_ref[...] = (nodes.astype(F32) + centred * scale).astype(BF16)
    for copy in outs:
        copy.wait()


def top_kernel(got_ref, agg_ref, part_ref, nodes_ref, wn_agg_ref, wn_out_ref, rest_ref, out_ref):
    width = agg_ref.shape[1]
    terms = [got_ref[at].astype(F32) for at in range(got_ref.shape[0])]
    while len(terms) > 1:
        half = len(terms) // 2
        terms = [a + b for a, b in zip(terms[:half], terms[half:])] + terms[2 * half :]
    sums = jnp.concatenate([terms[0], jnp.zeros((TOP - CO_DEV, width), F32)], axis=0)
    agg = (agg_ref[...] + sums).astype(BF16)
    hidden = silu(part_ref[...] + dot(agg, wn_agg_ref[...])).astype(BF16)
    centred, scale = norm_parts(dot(hidden, wn_out_ref[...]))
    out_ref[...] = (nodes_ref[0:TOP, :].astype(F32) + centred * scale).astype(BF16)


def in_hbm(*arrays):
    return [pltpu.with_memory_space_constraint(a, pltpu.HBM) for a in arrays]


def cost(flops, moved=0):
    return pl.CostEstimate(flops=flops, bytes_accessed=moved, transcendentals=0)


def call(kernel, name, outs, ins, out_specs=None, scratch=(), hbm=(), flops=0, **more):
    return pl.pallas_call(
        kernel,
        out_shape=outs,
        in_specs=[ANY if i in hbm else VMEM for i in range(len(ins))],
        out_specs=[VMEM] * len(outs) if out_specs is None else out_specs,
        scratch_shapes=scratch,
        compiler_params=pltpu.CompilerParams(vmem_limit_bytes=16 * MIB),
        cost_estimate=cost(flops),
        name=name,
        **more,
    )(*ins)


def body(
    node_latents,
    edge_latents,
    coarse_edges,
    w_edge_in,
    w_edge_out,
    w_node_in,
    w_node_out,
    fine_senders,
    fine_receivers,
    halo_lists,
    coarse_senders,
    coarse_receivers,
):
    count, width = node_latents.shape
    edge_count = edge_latents.shape[0]
    cedge_count = coarse_edges.shape[0]
    halo = halo_lists.shape[2]
    group = lax.axis_size(GROUP_AXES)
    coarse_count = group * CO_DEV
    shape = jax.ShapeDtypeStruct
    like = lambda a: shape(a.shape, a.dtype)
    vmem = pltpu.VMEM
    dma = pltpu.SemaphoreType.DMA
    square = 2 * width * width
    blocks = shape((group, CO_DEV, width), BF16)
    ids = lambda a: a[None, :]

    (head,) = call(
        head_kernel, "head", (shape((CO_DEV, width), BF16),), in_hbm(node_latents), hbm=(0,),
        scratch=[vmem((TOP, width), BF16), dma(())],
    )
    sub, patch = lax.axis_size("sub"), lax.axis_size("patch")
    assert sub & (sub - 1) == 0 and patch % 2 == 0
    masks = list(reversed(range(1, sub)))
    turns = sorted(range(1, patch), key=lambda by: (min(by, patch - by), by))
    near = [swap(head, mask, "sub") for mask in masks]
    nodes, cedges, w_ends, w_out, to_even, to_odd, gather, picks, coarse_part = call(
        load_kernel,
        "load",
        (
            like(node_latents),
            like(coarse_edges),
            shape((2 * width, width), BF16),
            like(w_edge_out),
            shape((halo, width), BF16),
            shape((halo, width), BF16),
            shape((2 * cedge_count, coarse_count), BF16),
            shape((coarse_count, cedge_count), BF16),
            shape((cedge_count, width), F32),
        ),
        in_hbm(node_latents, halo_lists, coarse_edges, w_edge_in, ids(coarse_senders), ids(coarse_receivers), w_edge_out)
        + [head],
        hbm=range(8),
        scratch=[
            vmem(halo_lists.shape, jnp.int32), vmem((width, width), BF16),
            vmem((1, cedge_count), jnp.int32), vmem((1, cedge_count), jnp.int32), dma((8,)),
        ],
        flops=edge_count * square,
    )
    (lat,) = call(
        functools.partial(join_kernel, masks), "join", (shape((sub * CO_DEV, width), BF16),), [head] + near + [nodes], hbm=(sub,),
    )
    far = [turn(lat, by) for by in turns]
    to_even, to_odd = call(
        pass_kernel, "pass", (like(to_even), like(to_odd)), [to_even, to_odd, lat], hbm=range(3), out_specs=[ANY, ANY],
        input_output_aliases={0: 0, 1: 1},
    )
    from_even, from_odd = pair(to_even, 0), pair(to_odd, 1)
    new_coarse, sums = call(
        functools.partial(coarse_kernel, turns), "coarse", (like(coarse_edges), blocks),
        [lat] + far + [cedges, coarse_part, gather, picks, w_ends, w_out], flops=0,
    )
    got = lax.all_to_all(sums, GROUP_AXES, 0, 0)
    new_edges, rest, agg, node_part, wn_agg, wn_out = call(
        fine_kernel,
        "fine",
        (
            like(edge_latents),
            like(node_latents),
            shape((TOP, width), F32),
            shape((TOP, width), F32),
            shape((width, width), BF16),
            like(w_node_out),
        ),
        [from_even, nodes, from_odd, w_ends, w_out]
        + in_hbm(edge_latents, w_edge_in, ids(fine_senders), ids(fine_receivers), w_node_in, w_node_out)
        + [sums],
        hbm=range(5, 12),
        out_specs=[ANY] + [VMEM] * 5,
        scratch=[
            vmem(edge_latents.shape, BF16), vmem((width, width), BF16), vmem((1, edge_count), jnp.int32),
            vmem((1, edge_count), jnp.int32), vmem((width, width), BF16), vmem(edge_latents.shape, BF16), dma((7,)),
            dma((edge_count // STEP,)),
        ],
        flops=64 * edge_count * square,
    )
    new_nodes = pl.pallas_call(
        top_kernel,
        grid=(1,),
        out_shape=like(node_latents),
        in_specs=[VMEM] * 6 + [ANY],
        out_specs=pl.BlockSpec((TOP, width), lambda i: (0, 0)),
        input_output_aliases={6: 0},
        compiler_params=pltpu.CompilerParams(vmem_limit_bytes=16 * MIB),
        name="top",
    )(got, agg, node_part, nodes, wn_agg, wn_out, rest)
    return (new_nodes, new_edges, new_coarse)


def solution(mesh):
    rows = P(("parts", "patch", "sub"), None)
    ids = P(("parts", "patch", "sub"))
    in_specs = (
        rows, rows, rows, P(), P(), P(), P(), ids, ids, P(("parts", "patch", "sub"), None, None), ids, ids,
    )
    return jax.shard_map(body, mesh=mesh, in_specs=in_specs, out_specs=(rows, rows, rows), check_vma=False)
```

```python
import functools

import jax
import jax.numpy as jnp
from jax import lax
from jax.experimental import pallas as pl
from jax.experimental.pallas import tpu as pltpu
from jax.sharding import PartitionSpec as P

CO_DEV = 4
GROUP_AXES = ("patch", "sub")
TOP = 16
STEP = 256
MIB = 1 << 20
ANY = pl.BlockSpec(memory_space=pl.ANY)
VMEM = pl.BlockSpec(memory_space=pltpu.VMEM)
BF16, F32 = jnp.bfloat16, jnp.float32


def swap(value, mask, axis):
    return lax.ppermute(value, axis, [(i, i ^ mask) for i in range(lax.axis_size(axis))])


def ring_place(index, devices):
    half = devices // 2
    return 2 * (index % half) + index // half


def ring_device(place, devices):
    return (place % 2) * (devices // 2) + place // 2


def turn(value, by):
    devices = lax.axis_size("patch")
    ring = [ring_device(place, devices) for place in range(devices)]
    return lax.ppermute(value, "patch", [(ring[i], ring[(i + by) % devices]) for i in range(devices)])


def pair(value, first):
    devices = lax.axis_size(GROUP_AXES)
    pairs = [(i, (i + 1) % devices) for i in range(first, devices, 2)]
    return lax.ppermute(value, GROUP_AXES, pairs + [(b, a) for a, b in pairs])


def dot(a, b):
    return jnp.dot(a, b, preferred_element_type=F32)


def dot_t(a, b):
    return lax.dot_general(a, b, (((0,), (0,)), ((), ())), preferred_element_type=F32)


def onehot_t(rows, ids):
    at = lax.broadcasted_iota(jnp.int32, (rows, ids.shape[1]), 0)
    return jnp.where(at == ids, 1.0, 0.0).astype(BF16)


def silu(v):
    half = 0.5 * v
    return half + half * jnp.tanh(half)


def norm_parts(values):
    mean = jnp.mean(values, axis=-1, keepdims=True)
    centred = values - mean
    return centred, lax.rsqrt(jnp.mean(centred * centred, axis=-1, keepdims=True) + 1e-05)


def head_kernel(nodes_hbm, head_ref, rows_ref, sem):
    copy = pltpu.make_async_copy(nodes_hbm.at[pl.ds(0, TOP)], rows_ref, sem)
    copy.start()
    copy.wait()
    head_ref[...] = rows_ref[0:CO_DEV, :]


def join_rows(refs, order):
    refs = [refs[0]] + [ref for _, ref in sorted(zip(order, refs[1:]), key=lambda item: item[0])]
    if refs[0].shape[0] % TOP == 0:
        return jnp.concatenate([ref[...] for ref in refs], axis=0)
    return jnp.concatenate([ref[...].astype(F32) for ref in refs], axis=0).astype(BF16)


def join_kernel(masks, *refs):
    refs, (after, out_ref) = refs[:-2], refs[-2:]
    out_ref[...] = join_rows(refs, masks)


def pass_kernel(even_ref, odd_ref, after, even_out, odd_out):
    pass


def start_copies(sources, targets, sems):
    copies = [pltpu.make_async_copy(a, b, sems.at[i]) for i, (a, b) in enumerate(zip(sources, targets))]
    for copy in copies:
        copy.start()
    return copies


def load_kernel(
    nodes_hbm, lists_hbm, cedges_hbm, w_in_hbm, csend_hbm, crecv_hbm, w_out_hbm, after,
    nodes_ref, cedges_ref, w_ends_ref, w_out_ref, even_ref, odd_ref, gather_ref, picks_ref, part_ref,
    lists_ref, w_self_ref, csend_ref, crecv_ref, sems,
):
    width = nodes_ref.shape[1]
    copies = start_copies(
        [
            nodes_hbm, lists_hbm, cedges_hbm, w_in_hbm.at[pl.ds(0, width)], csend_hbm, crecv_hbm,
            w_in_hbm.at[pl.ds(width, 2 * width)], w_out_hbm,
        ],
        [nodes_ref, lists_ref, cedges_ref, w_self_ref, csend_ref, crecv_ref, w_ends_ref, w_out_ref],
        sems,
    )
    for copy in copies[:2]:
        copy.wait()
    nodes = nodes_ref[...]
    count = nodes.shape[0]
    lists = lists_ref[0]
    me = lax.axis_index(GROUP_AXES)
    odd = me % 2
    first = lists[0:1, :] * (1 - odd) + lists[1:2, :] * odd
    second = lists[1:2, :] * (1 - odd) + lists[0:1, :] * odd
    even_ref[...] = dot_t(onehot_t(count, first), nodes).astype(BF16)
    odd_ref[...] = dot_t(onehot_t(count, second), nodes).astype(BF16)
    for copy in copies[2:6]:
        copy.wait()
    part_ref[...] = dot(cedges_ref[...], w_self_ref[...])
    rows, ids = picks_ref.shape
    sub, patch = lax.axis_size("sub"), lax.axis_size("patch")
    at = lax.broadcasted_iota(jnp.int32, (rows, ids), 0)
    block = at // CO_DEV
    place = ring_place(lax.axis_index("patch"), patch) + patch - block // sub
    device = ring_device(place % patch, patch) * sub + (lax.axis_index("sub") ^ (block % sub))
    node = device * CO_DEV + at % CO_DEV
    send = jnp.where(node == csend_ref[...], 1.0, 0.0).astype(BF16)
    recv = jnp.where(node == crecv_ref[...], 1.0, 0.0).astype(BF16)
    picks_ref[...] = onehot_t(rows, crecv_ref[...])
    across = lax.broadcasted_iota(jnp.int32, (rows, rows), 0) == lax.broadcasted_iota(jnp.int32, (rows, rows), 1)
    eye = jnp.where(across, 1.0, 0.0).astype(BF16)
    gather_ref[0:ids, :] = dot_t(send, eye).astype(BF16)
    gather_ref[ids:, :] = dot_t(recv, eye).astype(BF16)
    for copy in copies[6:]:
        copy.wait()


def coarse_kernel(turns, *refs):
    parts = len(turns) + 1
    lats, refs = refs[:parts], refs[parts:]
    edges_ref, part_ref, gather_ref, picks_ref, w_ends_ref, w_out_ref, new_ref, sums_ref = refs
    count, width = edges_ref.shape
    lat = join_rows(lats, turns)
    ends = dot(gather_ref[...], lat).astype(BF16)
    ends = jnp.concatenate([ends[0:count], ends[count:]], axis=1)
    hidden = silu(part_ref[...] + dot(ends, w_ends_ref[...])).astype(BF16)
    centred, scale = norm_parts(dot(hidden, w_out_ref[...]))
    new = (edges_ref[...].astype(F32) + centred * scale).astype(BF16)
    new_ref[...] = new
    sums = dot(picks_ref[...], new).astype(BF16)
    for at in range(sums_ref.shape[0]):
        sums_ref[at] = sums[at * CO_DEV : (at + 1) * CO_DEV, :]


def fine_kernel(
    even_ref, nodes_ref, odd_ref, w_ends_ref, w_out_ref,
    edges_hbm, w_in_hbm, send_hbm, recv_hbm, wn_in_hbm, wn_out_hbm, after,
    new_hbm, out_ref, agg_ref, npart_ref, wn_agg_ref, wn_out_ref,
    edges_ref, w_self_ref, send_ref, recv_ref, wn_self_ref, new_ref, sems, out_sems,
):
    nodes = nodes_ref[...]
    count, width = nodes.shape
    copies = start_copies(
        [
            send_hbm, recv_hbm, edges_hbm, w_in_hbm.at[pl.ds(0, width)],
            wn_in_hbm.at[pl.ds(0, width)], wn_in_hbm.at[pl.ds(width, width)], wn_out_hbm,
        ],
        [send_ref, recv_ref, edges_ref, w_self_ref, wn_self_ref, wn_agg_ref, wn_out_ref],
        sems,
    )
    odd = (lax.axis_index(GROUP_AXES) % 2).astype(F32)
    met, other = even_ref[...].astype(F32), odd_ref[...].astype(F32)
    prev = (met * odd + other * (1.0 - odd)).astype(BF16)
    following = (other * odd + met * (1.0 - odd)).astype(BF16)
    extended = jnp.concatenate([prev, nodes, following], axis=0)
    ones = jnp.ones((count, 128), BF16)
    total = jnp.zeros((count, width), F32)
    for copy in copies[:2]:
        copy.wait()
    outs = []
    for at in range(0, edges_ref.shape[0], STEP):
        rows = pl.ds(at, STEP)
        picks = onehot_t(count, recv_ref[:, rows])
        senders = dot_t(onehot_t(extended.shape[0], send_ref[:, rows]), extended).astype(BF16)
        receivers = dot_t(picks, nodes).astype(BF16)
        valid = dot_t(picks, ones)[:, 0:1]
        pre = dot(jnp.concatenate([senders, receivers], axis=1), w_ends_ref[...])
        if at == 0:
            for copy in copies[2:4]:
                copy.wait()
        edges = edges_ref[rows, :]
        pre = pre + dot(edges, w_self_ref[...])
        hidden = silu(pre).astype(BF16)
        centred, scale = norm_parts(dot(hidden, w_out_ref[...]))
        new = (edges.astype(F32) + centred * (scale * valid)).astype(BF16)
        new_ref[rows, :] = new
        copy = pltpu.make_async_copy(new_ref.at[rows], new_hbm.at[rows], out_sems.at[at // STEP])
        copy.start()
        outs.append(copy)
        total = total + dot(picks, new)
    agg_ref[...] = total[0:TOP]
    for copy in copies[4:]:
        copy.wait()
    pre = dot(nodes, wn_self_ref[...])
    npart_ref[...] = pre[0:TOP]
    pre = pre + dot(total.astype(BF16), wn_agg_ref[...])
    hidden = silu(pre).astype(BF16)
    centred, scale = norm_parts(dot(hidden, wn_out_ref[...]))
    out_ref[...] = (nodes.astype(F32) + centred * scale).astype(BF16)
    for copy in outs:
        copy.wait()


def top_kernel(got_ref, agg_ref, part_ref, nodes_ref, wn_agg_ref, wn_out_ref, rest_ref, out_ref):
    width = agg_ref.shape[1]
    terms = [got_ref[at].astype(F32) for at in range(got_ref.shape[0])]
    while len(terms) > 1:
        half = len(terms) // 2
        terms = [a + b for a, b in zip(terms[:half], terms[half:])] + terms[2 * half :]
    sums = jnp.concatenate([terms[0], jnp.zeros((TOP - CO_DEV, width), F32)], axis=0)
    agg = (agg_ref[...] + sums).astype(BF16)
    hidden = silu(part_ref[...] + dot(agg, wn_agg_ref[...])).astype(BF16)
    centred, scale = norm_parts(dot(hidden, wn_out_ref[...]))
    out_ref[...] = (nodes_ref[0:TOP, :].astype(F32) + centred * scale).astype(BF16)


def in_hbm(*arrays):
    return [pltpu.with_memory_space_constraint(a, pltpu.HBM) for a in arrays]


def cost(flops, moved=0):
    return pl.CostEstimate(flops=flops, bytes_accessed=moved, transcendentals=0)


def call(kernel, name, outs, ins, out_specs=None, scratch=(), hbm=(), flops=0, **more):
    return pl.pallas_call(
        kernel,
        out_shape=outs,
        in_specs=[ANY if i in hbm else VMEM for i in range(len(ins))],
        out_specs=[VMEM] * len(outs) if out_specs is None else out_specs,
        scratch_shapes=scratch,
        compiler_params=pltpu.CompilerParams(vmem_limit_bytes=16 * MIB),
        cost_estimate=cost(flops),
        name=name,
        **more,
    )(*ins)


def body(
    node_latents,
    edge_latents,
    coarse_edges,
    w_edge_in,
    w_edge_out,
    w_node_in,
    w_node_out,
    fine_senders,
    fine_receivers,
    halo_lists,
    coarse_senders,
    coarse_receivers,
):
    count, width = node_latents.shape
    edge_count = edge_latents.shape[0]
    cedge_count = coarse_edges.shape[0]
    halo = halo_lists.shape[2]
    group = lax.axis_size(GROUP_AXES)
    coarse_count = group * CO_DEV
    shape = jax.ShapeDtypeStruct
    like = lambda a: shape(a.shape, a.dtype)
    vmem = pltpu.VMEM
    dma = pltpu.SemaphoreType.DMA
    square = 2 * width * width
    blocks = shape((group, CO_DEV, width), BF16)
    ids = lambda a: a[None, :]

    (head,) = call(
        head_kernel, "head", (shape((CO_DEV, width), BF16),), in_hbm(node_latents), hbm=(0,),
        scratch=[vmem((TOP, width), BF16), dma(())],
    )
    sub, patch = lax.axis_size("sub"), lax.axis_size("patch")
    assert sub & (sub - 1) == 0 and patch % 2 == 0
    masks = list(reversed(range(1, sub)))
    turns = sorted(range(1, patch), key=lambda by: (min(by, patch - by), by))
    near = [swap(head, mask, "sub") for mask in masks]
    nodes, cedges, w_ends, w_out, to_even, to_odd, gather, picks, coarse_part = call(
        load_kernel,
        "load",
        (
            like(node_latents),
            like(coarse_edges),
            shape((2 * width, width), BF16),
            like(w_edge_out),
            shape((halo, width), BF16),
            shape((halo, width), BF16),
            shape((2 * cedge_count, coarse_count), BF16),
            shape((coarse_count, cedge_count), BF16),
            shape((cedge_count, width), F32),
        ),
        in_hbm(node_latents, halo_lists, coarse_edges, w_edge_in, ids(coarse_senders), ids(coarse_receivers), w_edge_out)
        + [head],
        hbm=range(8),
        scratch=[
            vmem(halo_lists.shape, jnp.int32), vmem((width, width), BF16),
            vmem((1, cedge_count), jnp.int32), vmem((1, cedge_count), jnp.int32), dma((8,)),
        ],
        flops=edge_count * square,
    )
    (lat,) = call(
        functools.partial(join_kernel, masks), "join", (shape((sub * CO_DEV, width), BF16),), [head] + near + [nodes], hbm=(sub,),
    )
    far = [turn(lat, by) for by in turns]
    to_even, to_odd = call(
        pass_kernel, "pass", (like(to_even), like(to_odd)), [to_even, to_odd, lat], hbm=range(3), out_specs=[ANY, ANY],
        input_output_aliases={0: 0, 1: 1},
    )
    from_even, from_odd = pair(to_even, 0), pair(to_odd, 1)
    new_coarse, sums = call(
        functools.partial(coarse_kernel, turns), "coarse", (like(coarse_edges), blocks),
        [lat] + far + [cedges, coarse_part, gather, picks, w_ends, w_out], flops=0,
    )
    got = lax.all_to_all(sums, GROUP_AXES, 0, 0)
    new_edges, rest, agg, node_part, wn_agg, wn_out = call(
        fine_kernel,
        "fine",
        (
            like(edge_latents),
            like(node_latents),
            shape((TOP, width), F32),
            shape((TOP, width), F32),
            shape((width, width), BF16),
            like(w_node_out),
        ),
        [from_even, nodes, from_odd, w_ends, w_out]
        + in_hbm(edge_latents, w_edge_in, ids(fine_senders), ids(fine_receivers), w_node_in, w_node_out)
        + [sums],
        hbm=range(5, 12),
        out_specs=[ANY] + [VMEM] * 5,
        scratch=[
            vmem(edge_latents.shape, BF16), vmem((width, width), BF16), vmem((1, edge_count), jnp.int32),
            vmem((1, edge_count), jnp.int32), vmem((width, width), BF16), vmem(edge_latents.shape, BF16), dma((7,)),
            dma((edge_count // STEP,)),
        ],
        flops=64 * edge_count * square,
    )
    new_nodes = pl.pallas_call(
        top_kernel,
        grid=(1,),
        out_shape=like(node_latents),
        in_specs=[VMEM] * 6 + [ANY],
        out_specs=pl.BlockSpec((TOP, width), lambda i: (0, 0)),
        input_output_aliases={6: 0},
        compiler_params=pltpu.CompilerParams(vmem_limit_bytes=16 * MIB),
        name="top",
    )(got, agg, node_part, nodes, wn_agg, wn_out, rest)
    return (new_nodes, new_edges, new_coarse)


def solution(mesh):
    rows = P(("parts", "patch", "sub"), None)
    ids = P(("parts", "patch", "sub"))
    in_specs = (
        rows, rows, rows, P(), P(), P(), P(), ids, ids, P(("parts", "patch", "sub"), None, None), ids, ids,
    )
    return jax.shard_map(body, mesh=mesh, in_specs=in_specs, out_specs=(rows, rows, rows), check_vma=False)
```

```python
import functools

import jax
import jax.numpy as jnp
from jax import lax
from jax.experimental import pallas as pl
from jax.experimental.pallas import tpu as pltpu
from jax.sharding import PartitionSpec as P

CO_DEV = 4
GROUP_AXES = ("patch", "sub")
TOP = 16
STEP = 256
MIB = 1 << 20
ANY = pl.BlockSpec(memory_space=pl.ANY)
VMEM = pl.BlockSpec(memory_space=pltpu.VMEM)
BF16, F32 = jnp.bfloat16, jnp.float32


def swap(value, mask, axis):
    return lax.ppermute(value, axis, [(i, i ^ mask) for i in range(lax.axis_size(axis))])


def ring_place(index, devices):
    half = devices // 2
    return 2 * (index % half) + index // half


def ring_device(place, devices):
    return (place % 2) * (devices // 2) + place // 2


def turn(value, by):
    devices = lax.axis_size("patch")
    ring = [ring_device(place, devices) for place in range(devices)]
    return lax.ppermute(value, "patch", [(ring[i], ring[(i + by) % devices]) for i in range(devices)])


def pair(value, first):
    devices = lax.axis_size(GROUP_AXES)
    pairs = [(i, (i + 1) % devices) for i in range(first, devices, 2)]
    return lax.ppermute(value, GROUP_AXES, pairs + [(b, a) for a, b in pairs])


def dot(a, b):
    return jnp.dot(a, b, preferred_element_type=F32)


def dot_t(a, b):
    return lax.dot_general(a, b, (((0,), (0,)), ((), ())), preferred_element_type=F32)


def onehot_t(rows, ids):
    at = lax.broadcasted_iota(jnp.int32, (rows, ids.shape[1]), 0)
    return jnp.where(at == ids, 1.0, 0.0).astype(BF16)


def silu(v):
    half = 0.5 * v
    return half + half * jnp.tanh(half)


def norm_parts(values):
    mean = jnp.mean(values, axis=-1, keepdims=True)
    centred = values - mean
    return centred, lax.rsqrt(jnp.mean(centred * centred, axis=-1, keepdims=True) + 1e-05)


def head_kernel(nodes_hbm, head_ref, rows_ref, sem):
    copy = pltpu.make_async_copy(nodes_hbm.at[pl.ds(0, TOP)], rows_ref, sem)
    copy.start()
    copy.wait()
    head_ref[...] = rows_ref[0:CO_DEV, :]


def join_rows(refs, order):
    refs = [refs[0]] + [ref for _, ref in sorted(zip(order, refs[1:]), key=lambda item: item[0])]
    if refs[0].shape[0] % TOP == 0:
        return jnp.concatenate([ref[...] for ref in refs], axis=0)
    return jnp.concatenate([ref[...].astype(F32) for ref in refs], axis=0).astype(BF16)


def join_kernel(masks, *refs):
    refs, (after, out_ref) = refs[:-2], refs[-2:]
    out_ref[...] = join_rows(refs, masks)


def pass_kernel(even_ref, odd_ref, after, even_out, odd_out):
    pass


def start_copies(sources, targets, sems):
    copies = [pltpu.make_async_copy(a, b, sems.at[i]) for i, (a, b) in enumerate(zip(sources, targets))]
    for copy in copies:
        copy.start()
    return copies


def load_kernel(
    nodes_hbm, lists_hbm, cedges_hbm, w_in_hbm, csend_hbm, crecv_hbm, w_out_hbm, after,
    nodes_ref, cedges_ref, w_ends_ref, w_out_ref, even_ref, odd_ref, gather_ref, picks_ref, part_ref,
    lists_ref, w_self_ref, csend_ref, crecv_ref, sems,
):
    width = nodes_ref.shape[1]
    copies = start_copies(
        [
            nodes_hbm, lists_hbm, cedges_hbm, w_in_hbm.at[pl.ds(0, width)], csend_hbm, crecv_hbm,
            w_in_hbm.at[pl.ds(width, 2 * width)], w_out_hbm,
        ],
        [nodes_ref, lists_ref, cedges_ref, w_self_ref, csend_ref, crecv_ref, w_ends_ref, w_out_ref],
        sems,
    )
    for copy in copies[:2]:
        copy.wait()
    nodes = nodes_ref[...]
    count = nodes.shape[0]
    lists = lists_ref[0]
    me = lax.axis_index(GROUP_AXES)
    odd = me % 2
    first = lists[0:1, :] * (1 - odd) + lists[1:2, :] * odd
    second = lists[1:2, :] * (1 - odd) + lists[0:1, :] * odd
    even_ref[...] = dot_t(onehot_t(count, first), nodes).astype(BF16)
    odd_ref[...] = dot_t(onehot_t(count, second), nodes).astype(BF16)
    for copy in copies[2:6]:
        copy.wait()
    part_ref[...] = dot(cedges_ref[...], w_self_ref[...])
    rows, ids = picks_ref.shape
    sub, patch = lax.axis_size("sub"), lax.axis_size("patch")
    at = lax.broadcasted_iota(jnp.int32, (rows, ids), 0)
    block = at // CO_DEV
    place = ring_place(lax.axis_index("patch"), patch) + patch - block // sub
    device = ring_device(place % patch, patch) * sub + (lax.axis_index("sub") ^ (block % sub))
    node = device * CO_DEV + at % CO_DEV
    send = jnp.where(node == csend_ref[...], 1.0, 0.0).astype(BF16)
    recv = jnp.where(node == crecv_ref[...], 1.0, 0.0).astype(BF16)
    picks_ref[...] = onehot_t(rows, crecv_ref[...])
    across = lax.broadcasted_iota(jnp.int32, (rows, rows), 0) == lax.broadcasted_iota(jnp.int32, (rows, rows), 1)
    eye = jnp.where(across, 1.0, 0.0).astype(BF16)
    gather_ref[0:ids, :] = dot_t(send, eye).astype(BF16)
    gather_ref[ids:, :] = dot_t(recv, eye).astype(BF16)
    for copy in copies[6:]:
        copy.wait()


def coarse_kernel(turns, *refs):
    parts = len(turns) + 1
    lats, refs = refs[:parts], refs[parts:]
    edges_ref, part_ref, gather_ref, picks_ref, w_ends_ref, w_out_ref, new_ref, sums_hbm, sums_ref, sem = refs
    count, width = edges_ref.shape
    lat = join_rows(lats, turns)
    ends = dot(gather_ref[...], lat).astype(BF16)
    ends = jnp.concatenate([ends[0:count], ends[count:]], axis=1)
    hidden = silu(part_ref[...] + dot(ends, w_ends_ref[...])).astype(BF16)
    centred, scale = norm_parts(dot(hidden, w_out_ref[...]))
    new = (edges_ref[...].astype(F32) + centred * scale).astype(BF16)
    new_ref[...] = new
    sums = dot(picks_ref[...], new).astype(BF16)
    for at in range(sums_ref.shape[0]):
        sums_ref[at] = sums[at * CO_DEV : (at + 1) * CO_DEV, :]
    copy = pltpu.make_async_copy(sums_ref, sums_hbm, sem)
    copy.start()
    copy.wait()


def fine_kernel(
    even_ref, nodes_ref, odd_ref, w_ends_ref, w_out_ref, coarse_ref,
    edges_hbm, w_in_hbm, send_hbm, recv_hbm, wn_in_hbm, wn_out_hbm, after,
    new_hbm, coarse_hbm, out_ref, agg_ref, npart_ref, wn_agg_ref, wn_out_ref,
    edges_ref, w_self_ref, send_ref, recv_ref, wn_self_ref, new_ref, sems, out_sems,
):
    nodes = nodes_ref[...]
    count, width = nodes.shape
    copies = start_copies(
        [
            send_hbm, recv_hbm, edges_hbm, w_in_hbm.at[pl.ds(0, width)],
            wn_in_hbm.at[pl.ds(0, width)], wn_in_hbm.at[pl.ds(width, width)], wn_out_hbm,
        ],
        [send_ref, recv_ref, edges_ref, w_self_ref, wn_self_ref, wn_agg_ref, wn_out_ref],
        sems,
    )
    odd = (lax.axis_index(GROUP_AXES) % 2).astype(F32)
    met, other = even_ref[...].astype(F32), odd_ref[...].astype(F32)
    prev = (met * odd + other * (1.0 - odd)).astype(BF16)
    following = (other * odd + met * (1.0 - odd)).astype(BF16)
    extended = jnp.concatenate([prev, nodes, following], axis=0)
    ones = jnp.ones((count, 128), BF16)
    total = jnp.zeros((count, width), F32)
    for copy in copies[:2]:
        copy.wait()
    outs = [pltpu.make_async_copy(coarse_ref, coarse_hbm, out_sems.at[0])]
    outs[0].start()
    for at in range(0, edges_ref.shape[0], STEP):
        rows = pl.ds(at, STEP)
        picks = onehot_t(count, recv_ref[:, rows])
        senders = dot_t(onehot_t(extended.shape[0], send_ref[:, rows]), extended).astype(BF16)
        receivers = dot_t(picks, nodes).astype(BF16)
        valid = dot_t(picks, ones)[:, 0:1]
        pre = dot(jnp.concatenate([senders, receivers], axis=1), w_ends_ref[...])
        if at == 0:
            for copy in copies[2:4]:
                copy.wait()
        edges = edges_ref[rows, :]
        pre = pre + dot(edges, w_self_ref[...])
        hidden = silu(pre).astype(BF16)
        centred, scale = norm_parts(dot(hidden, w_out_ref[...]))
        new = (edges.astype(F32) + centred * (scale * valid)).astype(BF16)
        new_ref[rows, :] = new
        copy = pltpu.make_async_copy(new_ref.at[rows], new_hbm.at[rows], out_sems.at[at // STEP + 1])
        copy.start()
        outs.append(copy)
        total = total + dot(picks, new)
    agg_ref[...] = total[0:TOP]
    for copy in copies[4:]:
        copy.wait()
    pre = dot(nodes, wn_self_ref[...])
    npart_ref[...] = pre[0:TOP]
    pre = pre + dot(total.astype(BF16), wn_agg_ref[...])
    hidden = silu(pre).astype(BF16)
    centred, scale = norm_parts(dot(hidden, wn_out_ref[...]))
    out_ref[...] = (nodes.astype(F32) + centred * scale).astype(BF16)
    for copy in outs:
        copy.wait()


def top_kernel(got_ref, agg_ref, part_ref, nodes_ref, wn_agg_ref, wn_out_ref, rest_ref, out_ref):
    width = agg_ref.shape[1]
    terms = [got_ref[at].astype(F32) for at in range(got_ref.shape[0])]
    while len(terms) > 1:
        half = len(terms) // 2
        terms = [a + b for a, b in zip(terms[:half], terms[half:])] + terms[2 * half :]
    sums = jnp.concatenate([terms[0], jnp.zeros((TOP - CO_DEV, width), F32)], axis=0)
    agg = (agg_ref[...] + sums).astype(BF16)
    hidden = silu(part_ref[...] + dot(agg, wn_agg_ref[...])).astype(BF16)
    centred, scale = norm_parts(dot(hidden, wn_out_ref[...]))
    out_ref[...] = (nodes_ref[0:TOP, :].astype(F32) + centred * scale).astype(BF16)


def in_hbm(*arrays):
    return [pltpu.with_memory_space_constraint(a, pltpu.HBM) for a in arrays]


def cost(flops, moved=0):
    return pl.CostEstimate(flops=flops, bytes_accessed=moved, transcendentals=0)


def call(kernel, name, outs, ins, out_specs=None, scratch=(), hbm=(), flops=0, **more):
    return pl.pallas_call(
        kernel,
        out_shape=outs,
        in_specs=[ANY if i in hbm else VMEM for i in range(len(ins))],
        out_specs=[VMEM] * len(outs) if out_specs is None else out_specs,
        scratch_shapes=scratch,
        compiler_params=pltpu.CompilerParams(vmem_limit_bytes=16 * MIB),
        cost_estimate=cost(flops),
        name=name,
        **more,
    )(*ins)


def body(
    node_latents,
    edge_latents,
    coarse_edges,
    w_edge_in,
    w_edge_out,
    w_node_in,
    w_node_out,
    fine_senders,
    fine_receivers,
    halo_lists,
    coarse_senders,
    coarse_receivers,
):
    count, width = node_latents.shape
    edge_count = edge_latents.shape[0]
    cedge_count = coarse_edges.shape[0]
    halo = halo_lists.shape[2]
    group = lax.axis_size(GROUP_AXES)
    coarse_count = group * CO_DEV
    shape = jax.ShapeDtypeStruct
    like = lambda a: shape(a.shape, a.dtype)
    vmem = pltpu.VMEM
    dma = pltpu.SemaphoreType.DMA
    square = 2 * width * width
    blocks = shape((group, CO_DEV, width), BF16)
    ids = lambda a: a[None, :]

    (head,) = call(
        head_kernel, "head", (shape((CO_DEV, width), BF16),), in_hbm(node_latents), hbm=(0,),
        scratch=[vmem((TOP, width), BF16), dma(())],
    )
    sub, patch = lax.axis_size("sub"), lax.axis_size("patch")
    assert sub & (sub - 1) == 0 and patch % 2 == 0
    masks = list(reversed(range(1, sub)))
    turns = sorted(range(1, patch), key=lambda by: (min(by, patch - by), by))
    near = [swap(head, mask, "sub") for mask in masks]
    nodes, cedges, w_ends, w_out, to_even, to_odd, gather, picks, coarse_part = call(
        load_kernel,
        "load",
        (
            like(node_latents),
            like(coarse_edges),
            shape((2 * width, width), BF16),
            like(w_edge_out),
            shape((halo, width), BF16),
            shape((halo, width), BF16),
            shape((2 * cedge_count, coarse_count), BF16),
            shape((coarse_count, cedge_count), BF16),
            shape((cedge_count, width), F32),
        ),
        in_hbm(node_latents, halo_lists, coarse_edges, w_edge_in, ids(coarse_senders), ids(coarse_receivers), w_edge_out)
        + [head],
        hbm=range(8),
        scratch=[
            vmem(halo_lists.shape, jnp.int32), vmem((width, width), BF16),
            vmem((1, cedge_count), jnp.int32), vmem((1, cedge_count), jnp.int32), dma((8,)),
        ],
        flops=edge_count * square,
    )
    (lat,) = call(
        functools.partial(join_kernel, masks), "join", (shape((sub * CO_DEV, width), BF16),), [head] + near + [nodes], hbm=(sub,),
    )
    far = [turn(lat, by) for by in turns]
    to_even, to_odd = call(
        pass_kernel, "pass", (like(to_even), like(to_odd)), [to_even, to_odd, lat], hbm=range(3), out_specs=[ANY, ANY],
        input_output_aliases={0: 0, 1: 1},
    )
    from_even, from_odd = pair(to_even, 0), pair(to_odd, 1)
    new_coarse, sums = call(
        functools.partial(coarse_kernel, turns), "coarse", (like(coarse_edges), blocks),
        [lat] + far + [cedges, coarse_part, gather, picks, w_ends, w_out], out_specs=[VMEM, ANY],
        scratch=[vmem(blocks.shape, BF16), dma(())],
    )
    got = lax.all_to_all(sums, GROUP_AXES, 0, 0)
    new_edges, new_coarse, rest, agg, node_part, wn_agg, wn_out = call(
        fine_kernel,
        "fine",
        (
            like(edge_latents),
            like(coarse_edges),
            like(node_latents),
            shape((TOP, width), F32),
            shape((TOP, width), F32),
            shape((width, width), BF16),
            like(w_node_out),
        ),
        [from_even, nodes, from_odd, w_ends, w_out, new_coarse]
        + in_hbm(edge_latents, w_edge_in, ids(fine_senders), ids(fine_receivers), w_node_in, w_node_out)
        + [sums],
        hbm=range(6, 13),
        out_specs=[ANY] * 2 + [VMEM] * 5,
        scratch=[
            vmem(edge_latents.shape, BF16), vmem((width, width), BF16), vmem((1, edge_count), jnp.int32),
            vmem((1, edge_count), jnp.int32), vmem((width, width), BF16), vmem(edge_latents.shape, BF16), dma((7,)),
            dma((edge_count // STEP + 1,)),
        ],
        flops=64 * edge_count * square,
    )
    new_nodes = pl.pallas_call(
        top_kernel,
        grid=(1,),
        out_shape=like(node_latents),
        in_specs=[VMEM] * 6 + [ANY],
        out_specs=pl.BlockSpec((TOP, width), lambda i: (0, 0)),
        input_output_aliases={6: 0},
        compiler_params=pltpu.CompilerParams(vmem_limit_bytes=16 * MIB),
        name="top",
    )(got, agg, node_part, nodes, wn_agg, wn_out, rest)
    return (new_nodes, new_edges, new_coarse)


def solution(mesh):
    rows = P(("parts", "patch", "sub"), None)
    ids = P(("parts", "patch", "sub"))
    in_specs = (
        rows, rows, rows, P(), P(), P(), P(), ids, ids, P(("parts", "patch", "sub"), None, None), ids, ids,
    )
    return jax.shard_map(body, mesh=mesh, in_specs=in_specs, out_specs=(rows, rows, rows), check_vma=False)
```

```python
import functools

import jax
import jax.numpy as jnp
from jax import lax
from jax.experimental import pallas as pl
from jax.experimental.pallas import tpu as pltpu
from jax.sharding import PartitionSpec as P

CO_DEV = 4
GROUP_AXES = ("patch", "sub")
TOP = 16
STEP = 256
MIB = 1 << 20
ANY = pl.BlockSpec(memory_space=pl.ANY)
VMEM = pl.BlockSpec(memory_space=pltpu.VMEM)
BF16, F32 = jnp.bfloat16, jnp.float32


def swap(value, mask, axis):
    return lax.ppermute(value, axis, [(i, i ^ mask) for i in range(lax.axis_size(axis))])


def ring_place(index, devices):
    half = devices // 2
    return 2 * (index % half) + index // half


def ring_device(place, devices):
    return (place % 2) * (devices // 2) + place // 2


def turn(value, by):
    devices = lax.axis_size("patch")
    ring = [ring_device(place, devices) for place in range(devices)]
    return lax.ppermute(value, "patch", [(ring[i], ring[(i + by) % devices]) for i in range(devices)])


def pair(value, first):
    devices = lax.axis_size(GROUP_AXES)
    pairs = [(i, (i + 1) % devices) for i in range(first, devices, 2)]
    return lax.ppermute(value, GROUP_AXES, pairs + [(b, a) for a, b in pairs])


def dot(a, b):
    return jnp.dot(a, b, preferred_element_type=F32)


def dot_t(a, b):
    return lax.dot_general(a, b, (((0,), (0,)), ((), ())), preferred_element_type=F32)


def onehot_t(rows, ids):
    at = lax.broadcasted_iota(jnp.int32, (rows, ids.shape[1]), 0)
    return jnp.where(at == ids, 1.0, 0.0).astype(BF16)


def silu(v):
    half = 0.5 * v
    return half + half * jnp.tanh(half)


def norm_parts(values):
    mean = jnp.mean(values, axis=-1, keepdims=True)
    centred = values - mean
    return centred, lax.rsqrt(jnp.mean(centred * centred, axis=-1, keepdims=True) + 1e-05)


def head_kernel(nodes_hbm, head_ref, rows_ref, sem):
    copy = pltpu.make_async_copy(nodes_hbm.at[pl.ds(0, TOP)], rows_ref, sem)
    copy.start()
    copy.wait()
    head_ref[...] = rows_ref[0:CO_DEV, :]


def join_rows(refs, order):
    refs = [refs[0]] + [ref for _, ref in sorted(zip(order, refs[1:]), key=lambda item: item[0])]
    if refs[0].shape[0] % TOP == 0:
        return jnp.concatenate([ref[...] for ref in refs], axis=0)
    return jnp.concatenate([ref[...].astype(F32) for ref in refs], axis=0).astype(BF16)


def join_kernel(masks, *refs):
    refs, (after, out_ref) = refs[:-2], refs[-2:]
    out_ref[...] = join_rows(refs, masks)


def pass_kernel(even_ref, odd_ref, after, even_out, odd_out):
    pass


def start_copies(sources, targets, sems):
    copies = [pltpu.make_async_copy(a, b, sems.at[i]) for i, (a, b) in enumerate(zip(sources, targets))]
    for copy in copies:
        copy.start()
    return copies


def load_kernel(
    nodes_hbm, lists_hbm, cedges_hbm, w_in_hbm, csend_hbm, crecv_hbm, w_out_hbm, after,
    nodes_ref, cedges_ref, w_ends_ref, w_out_ref, even_ref, odd_ref, gather_ref, picks_ref, part_ref,
    lists_ref, w_self_ref, csend_ref, crecv_ref, sems,
):
    width = nodes_ref.shape[1]
    copies = start_copies(
        [
            nodes_hbm, lists_hbm, cedges_hbm, w_in_hbm.at[pl.ds(0, width)], csend_hbm, crecv_hbm,
            w_in_hbm.at[pl.ds(width, 2 * width)], w_out_hbm,
        ],
        [nodes_ref, lists_ref, cedges_ref, w_self_ref, csend_ref, crecv_ref, w_ends_ref, w_out_ref],
        sems,
    )
    for copy in copies[:2]:
        copy.wait()
    nodes = nodes_ref[...]
    count = nodes.shape[0]
    lists = lists_ref[0]
    me = lax.axis_index(GROUP_AXES)
    odd = me % 2
    first = lists[0:1, :] * (1 - odd) + lists[1:2, :] * odd
    second = lists[1:2, :] * (1 - odd) + lists[0:1, :] * odd
    even_ref[...] = dot_t(onehot_t(count, first), nodes).astype(BF16)
    odd_ref[...] = dot_t(onehot_t(count, second), nodes).astype(BF16)
    for copy in copies[2:6]:
        copy.wait()
    part_ref[...] = dot(cedges_ref[...], w_self_ref[...])
    rows, ids = picks_ref.shape
    sub, patch = lax.axis_size("sub"), lax.axis_size("patch")
    at = lax.broadcasted_iota(jnp.int32, (rows, ids), 0)
    block = at // CO_DEV
    place = ring_place(lax.axis_index("patch"), patch) + patch - block // sub
    device = ring_device(place % patch, patch) * sub + (lax.axis_index("sub") ^ (block % sub))
    node = device * CO_DEV + at % CO_DEV
    send = jnp.where(node == csend_ref[...], 1.0, 0.0).astype(BF16)
    recv = jnp.where(node == crecv_ref[...], 1.0, 0.0).astype(BF16)
    picks_ref[...] = onehot_t(rows, crecv_ref[...])
    across = lax.broadcasted_iota(jnp.int32, (rows, rows), 0) == lax.broadcasted_iota(jnp.int32, (rows, rows), 1)
    eye = jnp.where(across, 1.0, 0.0).astype(BF16)
    gather_ref[0:ids, :] = dot_t(send, eye).astype(BF16)
    gather_ref[ids:, :] = dot_t(recv, eye).astype(BF16)
    for copy in copies[6:]:
        copy.wait()


def coarse_kernel(turns, *refs):
    parts = len(turns) + 1
    lats, refs = refs[:parts], refs[parts:]
    edges_ref, part_ref, gather_ref, picks_ref, w_ends_ref, w_out_ref, new_ref, sums_hbm, sums_ref, sem = refs
    count, width = edges_ref.shape
    lat = join_rows(lats, turns)
    ends = dot(gather_ref[...], lat).astype(BF16)
    ends = jnp.concatenate([ends[0:count], ends[count:]], axis=1)
    hidden = silu(part_ref[...] + dot(ends, w_ends_ref[...])).astype(BF16)
    centred, scale = norm_parts(dot(hidden, w_out_ref[...]))
    new = (edges_ref[...].astype(F32) + centred * scale).astype(BF16)
    new_ref[...] = new
    sums = dot(picks_ref[...], new).astype(BF16)
    last = sums_ref.shape[0] - 1
    for at in range(last + 1):
        sums_ref[last - at] = sums[at * CO_DEV : (at + 1) * CO_DEV, :]
    copy = pltpu.make_async_copy(sums_ref, sums_hbm, sem)
    copy.start()
    copy.wait()


def fine_kernel(
    even_ref, nodes_ref, odd_ref, w_ends_ref, w_out_ref, coarse_ref,
    edges_hbm, w_in_hbm, send_hbm, recv_hbm, wn_in_hbm, wn_out_hbm, after,
    new_hbm, coarse_hbm, out_ref, agg_ref, npart_ref, wn_agg_ref, wn_out_ref,
    edges_ref, w_self_ref, send_ref, recv_ref, wn_self_ref, new_ref, sems, out_sems,
):
    nodes = nodes_ref[...]
    count, width = nodes.shape
    copies = start_copies(
        [
            send_hbm, recv_hbm, edges_hbm, w_in_hbm.at[pl.ds(0, width)],
            wn_in_hbm.at[pl.ds(0, width)], wn_in_hbm.at[pl.ds(width, width)], wn_out_hbm,
        ],
        [send_ref, recv_ref, edges_ref, w_self_ref, wn_self_ref, wn_agg_ref, wn_out_ref],
        sems,
    )
    odd = (lax.axis_index(GROUP_AXES) % 2).astype(F32)
    met, other = even_ref[...].astype(F32), odd_ref[...].astype(F32)
    prev = (met * odd + other * (1.0 - odd)).astype(BF16)
    following = (other * odd + met * (1.0 - odd)).astype(BF16)
    extended = jnp.concatenate([prev, nodes, following], axis=0)
    ones = jnp.ones((count, 128), BF16)
    total = jnp.zeros((count, width), F32)
    for copy in copies[:2]:
        copy.wait()
    outs = [pltpu.make_async_copy(coarse_ref, coarse_hbm, out_sems.at[0])]
    outs[0].start()
    for at in range(0, edges_ref.shape[0], STEP):
        rows = pl.ds(at, STEP)
        picks = onehot_t(count, recv_ref[:, rows])
        senders = dot_t(onehot_t(extended.shape[0], send_ref[:, rows]), extended).astype(BF16)
        receivers = dot_t(picks, nodes).astype(BF16)
        valid = dot_t(picks, ones)[:, 0:1]
        pre = dot(jnp.concatenate([senders, receivers], axis=1), w_ends_ref[...])
        if at == 0:
            for copy in copies[2:4]:
                copy.wait()
        edges = edges_ref[rows, :]
        pre = pre + dot(edges, w_self_ref[...])
        hidden = silu(pre).astype(BF16)
        centred, scale = norm_parts(dot(hidden, w_out_ref[...]))
        new = (edges.astype(F32) + centred * (scale * valid)).astype(BF16)
        new_ref[rows, :] = new
        copy = pltpu.make_async_copy(new_ref.at[rows], new_hbm.at[rows], out_sems.at[at // STEP + 1])
        copy.start()
        outs.append(copy)
        total = total + dot(picks, new)
    agg_ref[...] = total[0:TOP]
    for copy in copies[4:]:
        copy.wait()
    pre = dot(nodes, wn_self_ref[...])
    npart_ref[...] = pre[0:TOP]
    pre = pre + dot(total.astype(BF16), wn_agg_ref[...])
    hidden = silu(pre).astype(BF16)
    centred, scale = norm_parts(dot(hidden, wn_out_ref[...]))
    out_ref[...] = (nodes.astype(F32) + centred * scale).astype(BF16)
    for copy in outs:
        copy.wait()


def top_kernel(got_ref, agg_ref, part_ref, nodes_ref, wn_agg_ref, wn_out_ref, rest_ref, out_ref):
    width = agg_ref.shape[1]
    terms = [got_ref[at].astype(F32) for at in range(got_ref.shape[0])]
    while len(terms) > 1:
        half = len(terms) // 2
        terms = [a + b for a, b in zip(terms[:half], terms[half:])] + terms[2 * half :]
    sums = jnp.concatenate([terms[0], jnp.zeros((TOP - CO_DEV, width), F32)], axis=0)
    agg = (agg_ref[...] + sums).astype(BF16)
    hidden = silu(part_ref[...] + dot(agg, wn_agg_ref[...])).astype(BF16)
    centred, scale = norm_parts(dot(hidden, wn_out_ref[...]))
    out_ref[...] = (nodes_ref[0:TOP, :].astype(F32) + centred * scale).astype(BF16)


def in_hbm(*arrays):
    return [pltpu.with_memory_space_constraint(a, pltpu.HBM) for a in arrays]


def cost(flops, moved=0):
    return pl.CostEstimate(flops=flops, bytes_accessed=moved, transcendentals=0)


def call(kernel, name, outs, ins, out_specs=None, scratch=(), hbm=(), flops=0, **more):
    return pl.pallas_call(
        kernel,
        out_shape=outs,
        in_specs=[ANY if i in hbm else VMEM for i in range(len(ins))],
        out_specs=[VMEM] * len(outs) if out_specs is None else out_specs,
        scratch_shapes=scratch,
        compiler_params=pltpu.CompilerParams(vmem_limit_bytes=16 * MIB),
        cost_estimate=cost(flops),
        name=name,
        **more,
    )(*ins)


def body(
    node_latents,
    edge_latents,
    coarse_edges,
    w_edge_in,
    w_edge_out,
    w_node_in,
    w_node_out,
    fine_senders,
    fine_receivers,
    halo_lists,
    coarse_senders,
    coarse_receivers,
):
    count, width = node_latents.shape
    edge_count = edge_latents.shape[0]
    cedge_count = coarse_edges.shape[0]
    halo = halo_lists.shape[2]
    group = lax.axis_size(GROUP_AXES)
    coarse_count = group * CO_DEV
    shape = jax.ShapeDtypeStruct
    like = lambda a: shape(a.shape, a.dtype)
    vmem = pltpu.VMEM
    dma = pltpu.SemaphoreType.DMA
    square = 2 * width * width
    blocks = shape((group, CO_DEV, width), BF16)
    ids = lambda a: a[None, :]

    (head,) = call(
        head_kernel, "head", (shape((CO_DEV, width), BF16),), in_hbm(node_latents), hbm=(0,),
        scratch=[vmem((TOP, width), BF16), dma(())],
    )
    sub, patch = lax.axis_size("sub"), lax.axis_size("patch")
    assert sub & (sub - 1) == 0 and patch % 2 == 0
    masks = list(reversed(range(1, sub)))
    turns = sorted(range(1, patch), key=lambda by: (min(by, patch - by), by))
    near = [swap(head, mask, "sub") for mask in masks]
    nodes, cedges, w_ends, w_out, to_even, to_odd, gather, picks, coarse_part = call(
        load_kernel,
        "load",
        (
            like(node_latents),
            like(coarse_edges),
            shape((2 * width, width), BF16),
            like(w_edge_out),
            shape((halo, width), BF16),
            shape((halo, width), BF16),
            shape((2 * cedge_count, coarse_count), BF16),
            shape((coarse_count, cedge_count), BF16),
            shape((cedge_count, width), F32),
        ),
        in_hbm(node_latents, halo_lists, coarse_edges, w_edge_in, ids(coarse_senders), ids(coarse_receivers), w_edge_out)
        + [head],
        hbm=range(8),
        scratch=[
            vmem(halo_lists.shape, jnp.int32), vmem((width, width), BF16),
            vmem((1, cedge_count), jnp.int32), vmem((1, cedge_count), jnp.int32), dma((8,)),
        ],
        flops=edge_count * square,
    )
    (lat,) = call(
        functools.partial(join_kernel, masks), "join", (shape((sub * CO_DEV, width), BF16),), [head] + near + [nodes], hbm=(sub,),
    )
    far = [turn(lat, by) for by in turns]
    to_even, to_odd = call(
        pass_kernel, "pass", (like(to_even), like(to_odd)), [to_even, to_odd, lat], hbm=range(3), out_specs=[ANY, ANY],
        input_output_aliases={0: 0, 1: 1},
    )
    from_even, from_odd = pair(to_even, 0), pair(to_odd, 1)
    new_coarse, sums = call(
        functools.partial(coarse_kernel, turns), "coarse", (like(coarse_edges), blocks),
        [lat] + far + [cedges, coarse_part, gather, picks, w_ends, w_out], out_specs=[VMEM, ANY],
        scratch=[vmem(blocks.shape, BF16), dma(())],
    )
    got = lax.all_to_all(sums, GROUP_AXES, 0, 0, axis_index_groups=[list(reversed(range(group)))])
    new_edges, new_coarse, rest, agg, node_part, wn_agg, wn_out = call(
        fine_kernel,
        "fine",
        (
            like(edge_latents),
            like(coarse_edges),
            like(node_latents),
            shape((TOP, width), F32),
            shape((TOP, width), F32),
            shape((width, width), BF16),
            like(w_node_out),
        ),
        [from_even, nodes, from_odd, w_ends, w_out, new_coarse]
        + in_hbm(edge_latents, w_edge_in, ids(fine_senders), ids(fine_receivers), w_node_in, w_node_out)
        + [sums],
        hbm=range(6, 13),
        out_specs=[ANY] * 2 + [VMEM] * 5,
        scratch=[
            vmem(edge_latents.shape, BF16), vmem((width, width), BF16), vmem((1, edge_count), jnp.int32),
            vmem((1, edge_count), jnp.int32), vmem((width, width), BF16), vmem(edge_latents.shape, BF16), dma((7,)),
            dma((edge_count // STEP + 1,)),
        ],
        flops=64 * edge_count * square,
    )
    new_nodes = pl.pallas_call(
        top_kernel,
        grid=(1,),
        out_shape=like(node_latents),
        in_specs=[VMEM] * 6 + [ANY],
        out_specs=pl.BlockSpec((TOP, width), lambda i: (0, 0)),
        input_output_aliases={6: 0},
        compiler_params=pltpu.CompilerParams(vmem_limit_bytes=16 * MIB),
        name="top",
    )(got, agg, node_part, nodes, wn_agg, wn_out, rest)
    return (new_nodes, new_edges, new_coarse)


def solution(mesh):
    rows = P(("parts", "patch", "sub"), None)
    ids = P(("parts", "patch", "sub"))
    in_specs = (
        rows, rows, rows, P(), P(), P(), P(), ids, ids, P(("parts", "patch", "sub"), None, None), ids, ids,
    )
    return jax.shard_map(body, mesh=mesh, in_specs=in_specs, out_specs=(rows, rows, rows), check_vma=False)
```

```python
import jax
import jax.numpy as jnp
from jax import lax
from jax.experimental import pallas as pl
from jax.experimental.pallas import tpu as pltpu
from jax.sharding import PartitionSpec as P

CO_DEV = 4
GROUP_AXES = ("patch", "sub")
TOP = 16
STEP = 256
MIB = 1 << 20
ANY = pl.BlockSpec(memory_space=pl.ANY)
VMEM = pl.BlockSpec(memory_space=pltpu.VMEM)
BF16, F32 = jnp.bfloat16, jnp.float32


def first_order(group):
    return list(reversed(range(group)))


def second_order(group):
    return [(i + group // 2) % group for i in range(group)]


def pair(value, first):
    devices = lax.axis_size(GROUP_AXES)
    pairs = [(i, (i + 1) % devices) for i in range(first, devices, 2)]
    return lax.ppermute(value, GROUP_AXES, pairs + [(b, a) for a, b in pairs])


def dot(a, b):
    return jnp.dot(a, b, preferred_element_type=F32)


def dot_t(a, b):
    return lax.dot_general(a, b, (((0,), (0,)), ((), ())), preferred_element_type=F32)


def onehot_t(rows, ids):
    at = lax.broadcasted_iota(jnp.int32, (rows, ids.shape[1]), 0)
    return jnp.where(at == ids, 1.0, 0.0).astype(BF16)


def silu(v):
    half = 0.5 * v
    return half + half * jnp.tanh(half)


def norm_parts(values):
    mean = jnp.mean(values, axis=-1, keepdims=True)
    centred = values - mean
    return centred, lax.rsqrt(jnp.mean(centred * centred, axis=-1, keepdims=True) + 1e-05)


def head_kernel(nodes_hbm, heads_ref, rows_ref, sem):
    copy = pltpu.make_async_copy(nodes_hbm.at[pl.ds(0, TOP)], rows_ref, sem)
    copy.start()
    copy.wait()
    head = rows_ref[0:CO_DEV, :]
    for at in range(heads_ref.shape[0]):
        heads_ref[at] = head


def start_copies(sources, targets, sems):
    copies = [pltpu.make_async_copy(a, b, sems.at[i]) for i, (a, b) in enumerate(zip(sources, targets))]
    for copy in copies:
        copy.start()
    return copies


def load_kernel(
    nodes_hbm, lists_hbm, cedges_hbm, w_in_hbm, csend_hbm, crecv_hbm, w_out_hbm, after,
    nodes_ref, cedges_ref, w_ends_ref, w_out_ref, even_ref, odd_ref, gather_ref, picks_ref, part_ref,
    lists_ref, w_self_ref, csend_ref, crecv_ref, sems,
):
    width = nodes_ref.shape[1]
    copies = start_copies(
        [
            nodes_hbm, lists_hbm, cedges_hbm, w_in_hbm.at[pl.ds(0, width)], csend_hbm, crecv_hbm,
            w_in_hbm.at[pl.ds(width, 2 * width)], w_out_hbm,
        ],
        [nodes_ref, lists_ref, cedges_ref, w_self_ref, csend_ref, crecv_ref, w_ends_ref, w_out_ref],
        sems,
    )
    for copy in copies[:2]:
        copy.wait()
    nodes = nodes_ref[...]
    count = nodes.shape[0]
    lists = lists_ref[0]
    me = lax.axis_index(GROUP_AXES)
    odd = me % 2
    first = lists[0:1, :] * (1 - odd) + lists[1:2, :] * odd
    second = lists[1:2, :] * (1 - odd) + lists[0:1, :] * odd
    even_ref[...] = dot_t(onehot_t(count, first), nodes).astype(BF16)
    odd_ref[...] = dot_t(onehot_t(count, second), nodes).astype(BF16)
    for copy in copies[2:6]:
        copy.wait()
    part_ref[...] = dot(cedges_ref[...], w_self_ref[...])
    rows, ids = picks_ref.shape
    at = lax.broadcasted_iota(jnp.int32, (rows, ids), 0)
    node = (rows // CO_DEV - 1 - at // CO_DEV) * CO_DEV + at % CO_DEV
    send = jnp.where(node == csend_ref[...], 1.0, 0.0).astype(BF16)
    recv = jnp.where(node == crecv_ref[...], 1.0, 0.0).astype(BF16)
    picks_ref[...] = onehot_t(rows, crecv_ref[...])
    across = lax.broadcasted_iota(jnp.int32, (rows, rows), 0) == lax.broadcasted_iota(jnp.int32, (rows, rows), 1)
    eye = jnp.where(across, 1.0, 0.0).astype(BF16)
    gather_ref[0:ids, :] = dot_t(send, eye).astype(BF16)
    gather_ref[ids:, :] = dot_t(recv, eye).astype(BF16)
    for copy in copies[6:]:
        copy.wait()


def coarse_kernel(
    lat_ref, edges_ref, part_ref, gather_ref, picks_ref, w_ends_ref, w_out_ref, new_ref, sums_hbm, sums_ref, sem
):
    count, width = edges_ref.shape
    blocks = lat_ref.shape[0]
    lat = jnp.concatenate([lat_ref[at].astype(F32) for at in range(blocks)], axis=0).astype(BF16)
    ends = dot(gather_ref[...], lat).astype(BF16)
    ends = jnp.concatenate([ends[0:count], ends[count:]], axis=1)
    hidden = silu(part_ref[...] + dot(ends, w_ends_ref[...])).astype(BF16)
    centred, scale = norm_parts(dot(hidden, w_out_ref[...]))
    new = (edges_ref[...].astype(F32) + centred * scale).astype(BF16)
    new_ref[...] = new
    sums = dot(picks_ref[...], new).astype(BF16)
    for at, owner in enumerate(second_order(blocks)):
        sums_ref[at] = sums[owner * CO_DEV : (owner + 1) * CO_DEV, :]
    copy = pltpu.make_async_copy(sums_ref, sums_hbm, sem)
    copy.start()
    copy.wait()


def fine_kernel(
    even_ref, nodes_ref, odd_ref, w_ends_ref, w_out_ref, coarse_ref,
    edges_hbm, w_in_hbm, send_hbm, recv_hbm, wn_in_hbm, wn_out_hbm, after,
    new_hbm, coarse_hbm, out_ref, agg_ref, npart_ref, wn_agg_ref, wn_out_ref,
    edges_ref, w_self_ref, send_ref, recv_ref, wn_self_ref, new_ref, sems, out_sems,
):
    nodes = nodes_ref[...]
    count, width = nodes.shape
    copies = start_copies(
        [
            send_hbm, recv_hbm, edges_hbm, w_in_hbm.at[pl.ds(0, width)],
            wn_in_hbm.at[pl.ds(0, width)], wn_in_hbm.at[pl.ds(width, width)], wn_out_hbm,
        ],
        [send_ref, recv_ref, edges_ref, w_self_ref, wn_self_ref, wn_agg_ref, wn_out_ref],
        sems,
    )
    odd = (lax.axis_index(GROUP_AXES) % 2).astype(F32)
    met, other = even_ref[...].astype(F32), odd_ref[...].astype(F32)
    prev = (met * odd + other * (1.0 - odd)).astype(BF16)
    following = (other * odd + met * (1.0 - odd)).astype(BF16)
    extended = jnp.concatenate([prev, nodes, following], axis=0)
    ones = jnp.ones((count, 128), BF16)
    total = jnp.zeros((count, width), F32)
    for copy in copies[:2]:
        copy.wait()
    outs = [pltpu.make_async_copy(coarse_ref, coarse_hbm, out_sems.at[0])]
    outs[0].start()
    for at in range(0, edges_ref.shape[0], STEP):
        rows = pl.ds(at, STEP)
        picks = onehot_t(count, recv_ref[:, rows])
        senders = dot_t(onehot_t(extended.shape[0], send_ref[:, rows]), extended).astype(BF16)
        receivers = dot_t(picks, nodes).astype(BF16)
        valid = dot_t(picks, ones)[:, 0:1]
        pre = dot(jnp.concatenate([senders, receivers], axis=1), w_ends_ref[...])
        if at == 0:
            for copy in copies[2:4]:
                copy.wait()
        edges = edges_ref[rows, :]
        pre = pre + dot(edges, w_self_ref[...])
        hidden = silu(pre).astype(BF16)
        centred, scale = norm_parts(dot(hidden, w_out_ref[...]))
        new = (edges.astype(F32) + centred * (scale * valid)).astype(BF16)
        new_ref[rows, :] = new
        copy = pltpu.make_async_copy(new_ref.at[rows], new_hbm.at[rows], out_sems.at[at // STEP + 1])
        copy.start()
        outs.append(copy)
        total = total + dot(picks, new)
    agg_ref[...] = total[0:TOP]
    for copy in copies[4:]:
        copy.wait()
    pre = dot(nodes, wn_self_ref[...])
    npart_ref[...] = pre[0:TOP]
    pre = pre + dot(total.astype(BF16), wn_agg_ref[...])
    hidden = silu(pre).astype(BF16)
    centred, scale = norm_parts(dot(hidden, wn_out_ref[...]))
    out_ref[...] = (nodes.astype(F32) + centred * scale).astype(BF16)
    for copy in outs:
        copy.wait()


def top_kernel(got_ref, agg_ref, part_ref, nodes_ref, wn_agg_ref, wn_out_ref, rest_ref, out_ref):
    width = agg_ref.shape[1]
    terms = [got_ref[at].astype(F32) for at in range(got_ref.shape[0])]
    while len(terms) > 1:
        half = len(terms) // 2
        terms = [a + b for a, b in zip(terms[:half], terms[half:])] + terms[2 * half :]
    sums = jnp.concatenate([terms[0], jnp.zeros((TOP - CO_DEV, width), F32)], axis=0)
    agg = (agg_ref[...] + sums).astype(BF16)
    hidden = silu(part_ref[...] + dot(agg, wn_agg_ref[...])).astype(BF16)
    centred, scale = norm_parts(dot(hidden, wn_out_ref[...]))
    out_ref[...] = (nodes_ref[0:TOP, :].astype(F32) + centred * scale).astype(BF16)


def in_hbm(*arrays):
    return [pltpu.with_memory_space_constraint(a, pltpu.HBM) for a in arrays]


def cost(flops, moved=0):
    return pl.CostEstimate(flops=flops, bytes_accessed=moved, transcendentals=0)


def call(kernel, name, outs, ins, out_specs=None, scratch=(), hbm=(), flops=0, **more):
    return pl.pallas_call(
        kernel,
        out_shape=outs,
        in_specs=[ANY if i in hbm else VMEM for i in range(len(ins))],
        out_specs=[VMEM] * len(outs) if out_specs is None else out_specs,
        scratch_shapes=scratch,
        compiler_params=pltpu.CompilerParams(vmem_limit_bytes=16 * MIB),
        cost_estimate=cost(flops),
        name=name,
        **more,
    )(*ins)


def body(
    node_latents,
    edge_latents,
    coarse_edges,
    w_edge_in,
    w_edge_out,
    w_node_in,
    w_node_out,
    fine_senders,
    fine_receivers,
    halo_lists,
    coarse_senders,
    coarse_receivers,
):
    count, width = node_latents.shape
    edge_count = edge_latents.shape[0]
    cedge_count = coarse_edges.shape[0]
    halo = halo_lists.shape[2]
    group = lax.axis_size(GROUP_AXES)
    coarse_count = group * CO_DEV
    shape = jax.ShapeDtypeStruct
    like = lambda a: shape(a.shape, a.dtype)
    vmem = pltpu.VMEM
    dma = pltpu.SemaphoreType.DMA
    square = 2 * width * width
    blocks = shape((group, CO_DEV, width), BF16)
    ids = lambda a: a[None, :]

    (heads,) = call(
        head_kernel, "head", (blocks,), in_hbm(node_latents), hbm=(0,), scratch=[vmem((TOP, width), BF16), dma(())],
    )
    lat = lax.all_to_all(heads, GROUP_AXES, 0, 0, axis_index_groups=[first_order(group)])
    nodes, cedges, w_ends, w_out, to_even, to_odd, gather, picks, coarse_part = call(
        load_kernel,
        "load",
        (
            like(node_latents),
            like(coarse_edges),
            shape((2 * width, width), BF16),
            like(w_edge_out),
            shape((halo, width), BF16),
            shape((halo, width), BF16),
            shape((2 * cedge_count, coarse_count), BF16),
            shape((coarse_count, cedge_count), BF16),
            shape((cedge_count, width), F32),
        ),
        in_hbm(node_latents, halo_lists, coarse_edges, w_edge_in, ids(coarse_senders), ids(coarse_receivers), w_edge_out)
        + [heads],
        hbm=range(8),
        scratch=[
            vmem(halo_lists.shape, jnp.int32), vmem((width, width), BF16),
            vmem((1, cedge_count), jnp.int32), vmem((1, cedge_count), jnp.int32), dma((8,)),
        ],
        flops=edge_count * square,
    )
    from_even, from_odd = pair(to_even, 0), pair(to_odd, 1)
    new_coarse, sums = call(
        coarse_kernel, "coarse", (like(coarse_edges), blocks),
        [lat, cedges, coarse_part, gather, picks, w_ends, w_out], out_specs=[VMEM, ANY],
        scratch=[vmem(blocks.shape, BF16), dma(())],
    )
    got = lax.all_to_all(sums, GROUP_AXES, 0, 0, axis_index_groups=[second_order(group)])
    new_edges, new_coarse, rest, agg, node_part, wn_agg, wn_out = call(
        fine_kernel,
        "fine",
        (
            like(edge_latents),
            like(coarse_edges),
            like(node_latents),
            shape((TOP, width), F32),
            shape((TOP, width), F32),
            shape((width, width), BF16),
            like(w_node_out),
        ),
        [from_even, nodes, from_odd, w_ends, w_out, new_coarse]
        + in_hbm(edge_latents, w_edge_in, ids(fine_senders), ids(fine_receivers), w_node_in, w_node_out)
        + [sums],
        hbm=range(6, 13),
        out_specs=[ANY] * 2 + [VMEM] * 5,
        scratch=[
            vmem(edge_latents.shape, BF16), vmem((width, width), BF16), vmem((1, edge_count), jnp.int32),
            vmem((1, edge_count), jnp.int32), vmem((width, width), BF16), vmem(edge_latents.shape, BF16), dma((7,)),
            dma((edge_count // STEP + 1,)),
        ],
        flops=64 * edge_count * square,
    )
    new_nodes = pl.pallas_call(
        top_kernel,
        grid=(1,),
        out_shape=like(node_latents),
        in_specs=[VMEM] * 6 + [ANY],
        out_specs=pl.BlockSpec((TOP, width), lambda i: (0, 0)),
        input_output_aliases={6: 0},
        compiler_params=pltpu.CompilerParams(vmem_limit_bytes=16 * MIB),
        name="top",
    )(got, agg, node_part, nodes, wn_agg, wn_out, rest)
    return (new_nodes, new_edges, new_coarse)


def solution(mesh):
    rows = P(("parts", "patch", "sub"), None)
    ids = P(("parts", "patch", "sub"))
    in_specs = (
        rows, rows, rows, P(), P(), P(), P(), ids, ids, P(("parts", "patch", "sub"), None, None), ids, ids,
    )
    return jax.shard_map(body, mesh=mesh, in_specs=in_specs, out_specs=(rows, rows, rows), check_vma=False)
```

```python
import jax
import jax.numpy as jnp
from jax import lax
from jax.experimental import pallas as pl
from jax.experimental.pallas import tpu as pltpu
from jax.sharding import PartitionSpec as P

CO_DEV = 4
GROUP_AXES = ("patch", "sub")
TOP = 16
STEP = 256
MIB = 1 << 20
ANY = pl.BlockSpec(memory_space=pl.ANY)
VMEM = pl.BlockSpec(memory_space=pltpu.VMEM)
BF16, F32 = jnp.bfloat16, jnp.float32


def order(group):
    return list(reversed(range(group)))


def pair(value, first):
    devices = lax.axis_size(GROUP_AXES)
    pairs = [(i, (i + 1) % devices) for i in range(first, devices, 2)]
    return lax.ppermute(value, GROUP_AXES, pairs + [(b, a) for a, b in pairs])


def dot(a, b):
    return jnp.dot(a, b, preferred_element_type=F32)


def dot_t(a, b):
    return lax.dot_general(a, b, (((0,), (0,)), ((), ())), preferred_element_type=F32)


def onehot_t(rows, ids):
    at = lax.broadcasted_iota(jnp.int32, (rows, ids.shape[1]), 0)
    return jnp.where(at == ids, 1.0, 0.0).astype(BF16)


def silu(v):
    half = 0.5 * v
    return half + half * jnp.tanh(half)


def norm_parts(values):
    mean = jnp.mean(values, axis=-1, keepdims=True)
    centred = values - mean
    return centred, lax.rsqrt(jnp.mean(centred * centred, axis=-1, keepdims=True) + 1e-05)


def head_kernel(nodes_hbm, heads_ref, rows_ref, sem):
    copy = pltpu.make_async_copy(nodes_hbm.at[pl.ds(0, TOP)], rows_ref, sem)
    copy.start()
    copy.wait()
    head = rows_ref[0:CO_DEV, :]
    for at in range(heads_ref.shape[0]):
        heads_ref[at] = head


def start_copies(sources, targets, sems):
    copies = [pltpu.make_async_copy(a, b, sems.at[i]) for i, (a, b) in enumerate(zip(sources, targets))]
    for copy in copies:
        copy.start()
    return copies


def load_kernel(
    nodes_hbm, lists_hbm, cedges_hbm, w_in_hbm, csend_hbm, crecv_hbm, w_out_hbm, edges_hbm, send_hbm, recv_hbm, after,
    nodes_ref, cedges_ref, w_self_ref, w_ends_ref, w_out_ref, edges_ref, send_ref, recv_ref,
    even_ref, odd_ref, gather_ref, picks_ref, part_ref,
    lists_ref, csend_ref, crecv_ref, sems,
):
    width = nodes_ref.shape[1]
    copies = start_copies(
        [
            nodes_hbm, lists_hbm, cedges_hbm, w_in_hbm.at[pl.ds(0, width)], csend_hbm, crecv_hbm,
            w_in_hbm.at[pl.ds(width, 2 * width)], w_out_hbm, edges_hbm, send_hbm, recv_hbm,
        ],
        [
            nodes_ref, lists_ref, cedges_ref, w_self_ref, csend_ref, crecv_ref, w_ends_ref, w_out_ref, edges_ref,
            send_ref, recv_ref,
        ],
        sems,
    )
    for copy in copies[:2]:
        copy.wait()
    nodes = nodes_ref[...]
    count = nodes.shape[0]
    lists = lists_ref[0]
    me = lax.axis_index(GROUP_AXES)
    odd = me % 2
    first = lists[0:1, :] * (1 - odd) + lists[1:2, :] * odd
    second = lists[1:2, :] * (1 - odd) + lists[0:1, :] * odd
    even_ref[...] = dot_t(onehot_t(count, first), nodes).astype(BF16)
    odd_ref[...] = dot_t(onehot_t(count, second), nodes).astype(BF16)
    for copy in copies[2:6]:
        copy.wait()
    part_ref[...] = dot(cedges_ref[...], w_self_ref[...])
    rows, ids = picks_ref.shape
    at = lax.broadcasted_iota(jnp.int32, (rows, ids), 0)
    node = (rows // CO_DEV - 1 - at // CO_DEV) * CO_DEV + at % CO_DEV
    send = jnp.where(node == csend_ref[...], 1.0, 0.0).astype(BF16)
    recv = jnp.where(node == crecv_ref[...], 1.0, 0.0).astype(BF16)
    picks_ref[...] = onehot_t(rows, crecv_ref[...])
    across = lax.broadcasted_iota(jnp.int32, (rows, rows), 0) == lax.broadcasted_iota(jnp.int32, (rows, rows), 1)
    eye = jnp.where(across, 1.0, 0.0).astype(BF16)
    gather_ref[0:ids, :] = dot_t(send, eye).astype(BF16)
    gather_ref[ids:, :] = dot_t(recv, eye).astype(BF16)
    for copy in copies[6:]:
        copy.wait()


def coarse_kernel(
    lat_ref, edges_ref, part_ref, gather_ref, picks_ref, w_ends_ref, w_out_ref, new_ref, sums_hbm, sums_ref, sem
):
    count, width = edges_ref.shape
    blocks = lat_ref.shape[0]
    lat = jnp.concatenate([lat_ref[at].astype(F32) for at in range(blocks)], axis=0).astype(BF16)
    ends = dot(gather_ref[...], lat).astype(BF16)
    ends = jnp.concatenate([ends[0:count], ends[count:]], axis=1)
    hidden = silu(part_ref[...] + dot(ends, w_ends_ref[...])).astype(BF16)
    centred, scale = norm_parts(dot(hidden, w_out_ref[...]))
    new = (edges_ref[...].astype(F32) + centred * scale).astype(BF16)
    new_ref[...] = new
    sums = dot(picks_ref[...], new).astype(BF16)
    for at, owner in enumerate(order(blocks)):
        sums_ref[at] = sums[owner * CO_DEV : (owner + 1) * CO_DEV, :]
    copy = pltpu.make_async_copy(sums_ref, sums_hbm, sem)
    copy.start()
    copy.wait()


def fine_kernel(
    even_ref, nodes_ref, odd_ref, w_self_ref, w_ends_ref, w_out_ref, edges_ref, send_ref, recv_ref, coarse_ref,
    wn_in_hbm, wn_out_hbm, after,
    new_hbm, coarse_hbm, out_ref, agg_ref, npart_ref, wn_agg_ref, wn_out_ref,
    wn_self_ref, new_ref, sems, out_sems,
):
    nodes = nodes_ref[...]
    count, width = nodes.shape
    copies = start_copies(
        [wn_in_hbm.at[pl.ds(0, width)], wn_in_hbm.at[pl.ds(width, width)], wn_out_hbm],
        [wn_self_ref, wn_agg_ref, wn_out_ref],
        sems,
    )
    outs = [pltpu.make_async_copy(coarse_ref, coarse_hbm, out_sems.at[0])]
    outs[0].start()
    odd = (lax.axis_index(GROUP_AXES) % 2).astype(F32)
    met, other = even_ref[...].astype(F32), odd_ref[...].astype(F32)
    prev = (met * odd + other * (1.0 - odd)).astype(BF16)
    following = (other * odd + met * (1.0 - odd)).astype(BF16)
    extended = jnp.concatenate([prev, nodes, following], axis=0)
    ones = jnp.ones((count, 128), BF16)
    total = jnp.zeros((count, width), F32)
    for at in range(0, edges_ref.shape[0], STEP):
        rows = pl.ds(at, STEP)
        picks = onehot_t(count, recv_ref[:, rows])
        senders = dot_t(onehot_t(extended.shape[0], send_ref[:, rows]), extended).astype(BF16)
        receivers = dot_t(picks, nodes).astype(BF16)
        valid = dot_t(picks, ones)[:, 0:1]
        edges = edges_ref[rows, :]
        pre = dot(edges, w_self_ref[...]) + dot(jnp.concatenate([senders, receivers], axis=1), w_ends_ref[...])
        hidden = silu(pre).astype(BF16)
        centred, scale = norm_parts(dot(hidden, w_out_ref[...]))
        new = (edges.astype(F32) + centred * (scale * valid)).astype(BF16)
        new_ref[rows, :] = new
        copy = pltpu.make_async_copy(new_ref.at[rows], new_hbm.at[rows], out_sems.at[at // STEP + 1])
        copy.start()
        outs.append(copy)
        total = total + dot(picks, new)
    agg_ref[...] = total[0:TOP]
    for copy in copies:
        copy.wait()
    pre = dot(nodes, wn_self_ref[...])
    npart_ref[...] = pre[0:TOP]
    pre = pre + dot(total.astype(BF16), wn_agg_ref[...])
    hidden = silu(pre).astype(BF16)
    centred, scale = norm_parts(dot(hidden, wn_out_ref[...]))
    out_ref[...] = (nodes.astype(F32) + centred * scale).astype(BF16)
    for copy in outs:
        copy.wait()


def top_kernel(got_ref, agg_ref, part_ref, nodes_ref, wn_agg_ref, wn_out_ref, rest_ref, out_hbm, top_ref, sems):
    count, width = rest_ref.shape
    below = pl.ds(TOP, count - TOP)
    rest = pltpu.make_async_copy(rest_ref.at[below], out_hbm.at[below], sems.at[0])
    rest.start()
    terms = [got_ref[at].astype(F32) for at in range(got_ref.shape[0])]
    while len(terms) > 1:
        half = len(terms) // 2
        terms = [a + b for a, b in zip(terms[:half], terms[half:])] + terms[2 * half :]
    sums = jnp.concatenate([terms[0], jnp.zeros((TOP - CO_DEV, width), F32)], axis=0)
    agg = (agg_ref[...] + sums).astype(BF16)
    hidden = silu(part_ref[...] + dot(agg, wn_agg_ref[...])).astype(BF16)
    centred, scale = norm_parts(dot(hidden, wn_out_ref[...]))
    top_ref[...] = (nodes_ref[0:TOP, :].astype(F32) + centred * scale).astype(BF16)
    top = pltpu.make_async_copy(top_ref, out_hbm.at[pl.ds(0, TOP)], sems.at[1])
    top.start()
    rest.wait()
    top.wait()


def in_hbm(*arrays):
    return [pltpu.with_memory_space_constraint(a, pltpu.HBM) for a in arrays]


def cost(flops, moved=0):
    return pl.CostEstimate(flops=flops, bytes_accessed=moved, transcendentals=0)


def call(kernel, name, outs, ins, out_specs=None, scratch=(), hbm=(), flops=0, **more):
    return pl.pallas_call(
        kernel,
        out_shape=outs,
        in_specs=[ANY if i in hbm else VMEM for i in range(len(ins))],
        out_specs=[VMEM] * len(outs) if out_specs is None else out_specs,
        scratch_shapes=scratch,
        compiler_params=pltpu.CompilerParams(vmem_limit_bytes=16 * MIB),
        cost_estimate=cost(flops),
        name=name,
        **more,
    )(*ins)


def body(
    node_latents,
    edge_latents,
    coarse_edges,
    w_edge_in,
    w_edge_out,
    w_node_in,
    w_node_out,
    fine_senders,
    fine_receivers,
    halo_lists,
    coarse_senders,
    coarse_receivers,
):
    count, width = node_latents.shape
    edge_count = edge_latents.shape[0]
    cedge_count = coarse_edges.shape[0]
    halo = halo_lists.shape[2]
    group = lax.axis_size(GROUP_AXES)
    coarse_count = group * CO_DEV
    shape = jax.ShapeDtypeStruct
    like = lambda a: shape(a.shape, a.dtype)
    vmem = pltpu.VMEM
    dma = pltpu.SemaphoreType.DMA
    square = 2 * width * width
    blocks = shape((group, CO_DEV, width), BF16)
    ids = lambda a: a[None, :]

    (heads,) = call(
        head_kernel, "head", (blocks,), in_hbm(node_latents), hbm=(0,), scratch=[vmem((TOP, width), BF16), dma(())],
    )
    lat = lax.all_to_all(heads, GROUP_AXES, 0, 0, axis_index_groups=[order(group)])
    send, recv = ids(fine_senders), ids(fine_receivers)
    nodes, cedges, w_self, w_ends, w_out, edges, send, recv, to_even, to_odd, gather, picks, coarse_part = call(
        load_kernel,
        "load",
        (
            like(node_latents),
            like(coarse_edges),
            shape((width, width), BF16),
            shape((2 * width, width), BF16),
            like(w_edge_out),
            like(edge_latents),
            like(send),
            like(recv),
            shape((halo, width), BF16),
            shape((halo, width), BF16),
            shape((2 * cedge_count, coarse_count), BF16),
            shape((coarse_count, cedge_count), BF16),
            shape((cedge_count, width), F32),
        ),
        in_hbm(
            node_latents, halo_lists, coarse_edges, w_edge_in, ids(coarse_senders), ids(coarse_receivers), w_edge_out,
            edge_latents, send, recv,
        )
        + [heads],
        hbm=range(11),
        scratch=[
            vmem(halo_lists.shape, jnp.int32), vmem((1, cedge_count), jnp.int32), vmem((1, cedge_count), jnp.int32),
            dma((11,)),
        ],
        flops=edge_count * square,
    )
    from_even, from_odd = pair(to_even, 0), pair(to_odd, 1)
    new_coarse, sums = call(
        coarse_kernel, "coarse", (like(coarse_edges), blocks),
        [lat, cedges, coarse_part, gather, picks, w_ends, w_out], out_specs=[VMEM, ANY],
        scratch=[vmem(blocks.shape, BF16), dma(())],
    )
    got = lax.all_to_all(sums, GROUP_AXES, 0, 0, axis_index_groups=[order(group)])
    new_edges, new_coarse, rest, agg, node_part, wn_agg, wn_out = call(
        fine_kernel,
        "fine",
        (
            like(edge_latents),
            like(coarse_edges),
            like(node_latents),
            shape((TOP, width), F32),
            shape((TOP, width), F32),
            shape((width, width), BF16),
            like(w_node_out),
        ),
        [from_even, nodes, from_odd, w_self, w_ends, w_out, edges, send, recv, new_coarse]
        + in_hbm(w_node_in, w_node_out)
        + [sums],
        hbm=range(10, 13),
        out_specs=[ANY] * 2 + [VMEM] * 5,
        scratch=[
            vmem((width, width), BF16), vmem(edge_latents.shape, BF16), dma((3,)), dma((edge_count // STEP + 1,)),
        ],
        flops=64 * edge_count * square,
    )
    (new_nodes,) = call(
        top_kernel, "top", (like(node_latents),), [got, agg, node_part, nodes, wn_agg, wn_out, rest], out_specs=[ANY],
        scratch=[vmem((TOP, width), BF16), dma((2,))],
    )
    return (new_nodes, new_edges, new_coarse)


def solution(mesh):
    rows = P(("parts", "patch", "sub"), None)
    ids = P(("parts", "patch", "sub"))
    in_specs = (
        rows, rows, rows, P(), P(), P(), P(), ids, ids, P(("parts", "patch", "sub"), None, None), ids, ids,
    )
    return jax.shard_map(body, mesh=mesh, in_specs=in_specs, out_specs=(rows, rows, rows), check_vma=False)
```

```python
import jax
import jax.numpy as jnp
from jax import lax
from jax.experimental import pallas as pl
from jax.experimental.pallas import tpu as pltpu
from jax.sharding import PartitionSpec as P

CO_DEV = 4
GROUP_AXES = ("patch", "sub")
TOP = 16
STEP = 512
MIB = 1 << 20
FIRST, SECOND = 2, 3
ANY = pl.BlockSpec(memory_space=pl.ANY)
VMEM = pl.BlockSpec(memory_space=pltpu.VMEM)
BF16, F32 = jnp.bfloat16, jnp.float32


def order(group, quarter):
    return [(i + group * quarter // 4) % group for i in range(group)]


def pair(value, first):
    devices = lax.axis_size(GROUP_AXES)
    pairs = [(i, (i + 1) % devices) for i in range(first, devices, 2)]
    return lax.ppermute(value, GROUP_AXES, pairs + [(b, a) for a, b in pairs])


def dot(a, b):
    return jnp.dot(a, b, preferred_element_type=F32)


def dot_t(a, b):
    return lax.dot_general(a, b, (((0,), (0,)), ((), ())), preferred_element_type=F32)


def onehot_t(rows, ids):
    at = lax.broadcasted_iota(jnp.int32, (rows, ids.shape[1]), 0)
    return jnp.where(at == ids, 1.0, 0.0).astype(BF16)


def silu(v):
    half = 0.5 * v
    return half + half * jnp.tanh(half)


def norm_parts(values):
    mean = jnp.mean(values, axis=-1, keepdims=True)
    centred = values - mean
    return centred, lax.rsqrt(jnp.mean(centred * centred, axis=-1, keepdims=True) + 1e-05)


def head_kernel(nodes_hbm, heads_ref, rows_ref, sem):
    copy = pltpu.make_async_copy(nodes_hbm.at[pl.ds(0, TOP)], rows_ref, sem)
    copy.start()
    copy.wait()
    head = rows_ref[0:CO_DEV, :]
    for at in range(heads_ref.shape[0]):
        heads_ref[at] = head


def start_copies(sources, targets, sems):
    copies = [pltpu.make_async_copy(a, b, sems.at[i]) for i, (a, b) in enumerate(zip(sources, targets))]
    for copy in copies:
        copy.start()
    return copies


def load_kernel(
    nodes_hbm, lists_hbm, cedges_hbm, w_in_hbm, csend_hbm, crecv_hbm, w_out_hbm, send_hbm, recv_hbm, after,
    nodes_ref, cedges_ref, w_ends_ref, w_out_ref, send_ref, recv_ref,
    even_ref, odd_ref, gather_ref, picks_ref, part_ref,
    lists_ref, w_self_ref, csend_ref, crecv_ref, sems,
):
    width = nodes_ref.shape[1]
    copies = start_copies(
        [
            nodes_hbm, lists_hbm, cedges_hbm, w_in_hbm.at[pl.ds(0, width)], csend_hbm, crecv_hbm,
            w_in_hbm.at[pl.ds(width, 2 * width)], w_out_hbm, send_hbm, recv_hbm,
        ],
        [
            nodes_ref, lists_ref, cedges_ref, w_self_ref, csend_ref, crecv_ref, w_ends_ref, w_out_ref, send_ref, recv_ref,
        ],
        sems,
    )
    for copy in copies[:2]:
        copy.wait()
    nodes = nodes_ref[...]
    count = nodes.shape[0]
    lists = lists_ref[0]
    me = lax.axis_index(GROUP_AXES)
    odd = me % 2
    first = lists[0:1, :] * (1 - odd) + lists[1:2, :] * odd
    second = lists[1:2, :] * (1 - odd) + lists[0:1, :] * odd
    even_ref[...] = dot_t(onehot_t(count, first), nodes).astype(BF16)
    odd_ref[...] = dot_t(onehot_t(count, second), nodes).astype(BF16)
    for copy in copies[2:6]:
        copy.wait()
    part_ref[...] = dot(cedges_ref[...], w_self_ref[...])
    rows, ids = picks_ref.shape
    at = lax.broadcasted_iota(jnp.int32, (rows, ids), 0)
    node = (at + CO_DEV * order(rows // CO_DEV, FIRST)[0]) % rows
    send = jnp.where(node == csend_ref[...], 1.0, 0.0).astype(BF16)
    recv = jnp.where(node == crecv_ref[...], 1.0, 0.0).astype(BF16)
    picks_ref[...] = onehot_t(rows, crecv_ref[...])
    across = lax.broadcasted_iota(jnp.int32, (rows, rows), 0) == lax.broadcasted_iota(jnp.int32, (rows, rows), 1)
    eye = jnp.where(across, 1.0, 0.0).astype(BF16)
    gather_ref[0:ids, :] = dot_t(send, eye).astype(BF16)
    gather_ref[ids:, :] = dot_t(recv, eye).astype(BF16)
    for copy in copies[6:]:
        copy.wait()


def coarse_kernel(
    lat_ref, edges_ref, part_ref, gather_ref, picks_ref, w_ends_ref, w_out_ref, new_ref, sums_hbm, sums_ref, sem
):
    count, width = edges_ref.shape
    blocks = lat_ref.shape[0]
    lat = jnp.concatenate([lat_ref[at].astype(F32) for at in range(blocks)], axis=0).astype(BF16)
    ends = dot(gather_ref[...], lat).astype(BF16)
    ends = jnp.concatenate([ends[0:count], ends[count:]], axis=1)
    hidden = silu(part_ref[...] + dot(ends, w_ends_ref[...])).astype(BF16)
    centred, scale = norm_parts(dot(hidden, w_out_ref[...]))
    new = (edges_ref[...].astype(F32) + centred * scale).astype(BF16)
    new_ref[...] = new
    sums = dot(picks_ref[...], new).astype(BF16)
    for at, owner in enumerate(order(blocks, SECOND)):
        sums_ref[at] = sums[owner * CO_DEV : (owner + 1) * CO_DEV, :]
    copy = pltpu.make_async_copy(sums_ref, sums_hbm, sem)
    copy.start()
    copy.wait()


def fine_kernel(
    even_ref, nodes_ref, odd_ref, w_ends_ref, w_out_ref, send_ref, recv_ref, coarse_ref,
    edges_hbm, w_in_hbm, wn_in_hbm, wn_out_hbm, after,
    new_hbm, coarse_hbm, out_ref, agg_ref, npart_ref, wn_agg_ref, wn_out_ref,
    edges_ref, w_self_ref, wn_self_ref, new_ref, sems, out_sems,
):
    nodes = nodes_ref[...]
    count, width = nodes.shape
    copies = start_copies(
        [
            edges_hbm, w_in_hbm.at[pl.ds(0, width)],
            wn_in_hbm.at[pl.ds(0, width)], wn_in_hbm.at[pl.ds(width, width)], wn_out_hbm,
        ],
        [edges_ref, w_self_ref, wn_self_ref, wn_agg_ref, wn_out_ref],
        sems,
    )
    outs = [pltpu.make_async_copy(coarse_ref, coarse_hbm, out_sems.at[0])]
    outs[0].start()
    odd = (lax.axis_index(GROUP_AXES) % 2).astype(F32)
    met, other = even_ref[...].astype(F32), odd_ref[...].astype(F32)
    prev = (met * odd + other * (1.0 - odd)).astype(BF16)
    following = (other * odd + met * (1.0 - odd)).astype(BF16)
    extended = jnp.concatenate([prev, nodes, following], axis=0)
    ones = jnp.ones((count, 128), BF16)
    total = jnp.zeros((count, width), F32)
    for at in range(0, edges_ref.shape[0], STEP):
        rows = pl.ds(at, STEP)
        picks = onehot_t(count, recv_ref[:, rows])
        senders = dot_t(onehot_t(extended.shape[0], send_ref[:, rows]), extended).astype(BF16)
        receivers = dot_t(picks, nodes).astype(BF16)
        valid = dot_t(picks, ones)[:, 0:1]
        pre = dot(jnp.concatenate([senders, receivers], axis=1), w_ends_ref[...])
        if at == 0:
            for copy in copies[:2]:
                copy.wait()
        edges = edges_ref[rows, :]
        pre = pre + dot(edges, w_self_ref[...])
        hidden = silu(pre).astype(BF16)
        centred, scale = norm_parts(dot(hidden, w_out_ref[...]))
        new = (edges.astype(F32) + centred * (scale * valid)).astype(BF16)
        new_ref[rows, :] = new
        copy = pltpu.make_async_copy(new_ref.at[rows], new_hbm.at[rows], out_sems.at[at // STEP + 1])
        copy.start()
        outs.append(copy)
        total = total + dot(picks, new)
    agg_ref[...] = total[0:TOP]
    for copy in copies[2:]:
        copy.wait()
    pre = dot(nodes, wn_self_ref[...])
    npart_ref[...] = pre[0:TOP]
    pre = pre + dot(total.astype(BF16), wn_agg_ref[...])
    hidden = silu(pre).astype(BF16)
    centred, scale = norm_parts(dot(hidden, wn_out_ref[...]))
    out_ref[...] = (nodes.astype(F32) + centred * scale).astype(BF16)
    for copy in outs:
        copy.wait()


def top_kernel(got_ref, agg_ref, part_ref, nodes_ref, wn_agg_ref, wn_out_ref, rest_ref, out_hbm, top_ref, sems):
    count, width = rest_ref.shape
    below = pl.ds(TOP, count - TOP)
    rest = pltpu.make_async_copy(rest_ref.at[below], out_hbm.at[below], sems.at[0])
    rest.start()
    terms = [got_ref[at].astype(F32) for at in range(got_ref.shape[0])]
    while len(terms) > 1:
        half = len(terms) // 2
        terms = [a + b for a, b in zip(terms[:half], terms[half:])] + terms[2 * half :]
    sums = jnp.concatenate([terms[0], jnp.zeros((TOP - CO_DEV, width), F32)], axis=0)
    agg = (agg_ref[...] + sums).astype(BF16)
    hidden = silu(part_ref[...] + dot(agg, wn_agg_ref[...])).astype(BF16)
    centred, scale = norm_parts(dot(hidden, wn_out_ref[...]))
    top_ref[...] = (nodes_ref[0:TOP, :].astype(F32) + centred * scale).astype(BF16)
    top = pltpu.make_async_copy(top_ref, out_hbm.at[pl.ds(0, TOP)], sems.at[1])
    top.start()
    rest.wait()
    top.wait()


def in_hbm(*arrays):
    return [pltpu.with_memory_space_constraint(a, pltpu.HBM) for a in arrays]


def cost(flops, moved=0):
    return pl.CostEstimate(flops=flops, bytes_accessed=moved, transcendentals=0)


def call(kernel, name, outs, ins, out_specs=None, scratch=(), hbm=(), flops=0, **more):
    return pl.pallas_call(
        kernel,
        out_shape=outs,
        in_specs=[ANY if i in hbm else VMEM for i in range(len(ins))],
        out_specs=[VMEM] * len(outs) if out_specs is None else out_specs,
        scratch_shapes=scratch,
        compiler_params=pltpu.CompilerParams(vmem_limit_bytes=16 * MIB),
        cost_estimate=cost(flops),
        name=name,
        **more,
    )(*ins)


def body(
    node_latents,
    edge_latents,
    coarse_edges,
    w_edge_in,
    w_edge_out,
    w_node_in,
    w_node_out,
    fine_senders,
    fine_receivers,
    halo_lists,
    coarse_senders,
    coarse_receivers,
):
    count, width = node_latents.shape
    edge_count = edge_latents.shape[0]
    cedge_count = coarse_edges.shape[0]
    halo = halo_lists.shape[2]
    group = lax.axis_size(GROUP_AXES)
    coarse_count = group * CO_DEV
    shape = jax.ShapeDtypeStruct
    like = lambda a: shape(a.shape, a.dtype)
    vmem = pltpu.VMEM
    dma = pltpu.SemaphoreType.DMA
    square = 2 * width * width
    blocks = shape((group, CO_DEV, width), BF16)
    ids = lambda a: a[None, :]

    (heads,) = call(
        head_kernel, "head", (blocks,), in_hbm(node_latents), hbm=(0,), scratch=[vmem((TOP, width), BF16), dma(())],
    )
    lat = lax.all_to_all(heads, GROUP_AXES, 0, 0, axis_index_groups=[order(group, FIRST)])
    send, recv = ids(fine_senders), ids(fine_receivers)
    nodes, cedges, w_ends, w_out, send, recv, to_even, to_odd, gather, picks, coarse_part = call(
        load_kernel,
        "load",
        (
            like(node_latents),
            like(coarse_edges),
            shape((2 * width, width), BF16),
            like(w_edge_out),
            like(send),
            like(recv),
            shape((halo, width), BF16),
            shape((halo, width), BF16),
            shape((2 * cedge_count, coarse_count), BF16),
            shape((coarse_count, cedge_count), BF16),
            shape((cedge_count, width), F32),
        ),
        in_hbm(
            node_latents, halo_lists, coarse_edges, w_edge_in, ids(coarse_senders), ids(coarse_receivers), w_edge_out,
            send, recv,
        )
        + [heads],
        hbm=range(10),
        scratch=[
            vmem(halo_lists.shape, jnp.int32), vmem((width, width), BF16),
            vmem((1, cedge_count), jnp.int32), vmem((1, cedge_count), jnp.int32), dma((10,)),
        ],
        flops=edge_count * square,
    )
    from_even, from_odd = pair(to_even, 0), pair(to_odd, 1)
    new_coarse, sums = call(
        coarse_kernel, "coarse", (like(coarse_edges), blocks),
        [lat, cedges, coarse_part, gather, picks, w_ends, w_out], out_specs=[VMEM, ANY],
        scratch=[vmem(blocks.shape, BF16), dma(())],
    )
    got = lax.all_to_all(sums, GROUP_AXES, 0, 0, axis_index_groups=[order(group, SECOND)])
    new_edges, new_coarse, rest, agg, node_part, wn_agg, wn_out = call(
        fine_kernel,
        "fine",
        (
            like(edge_latents),
            like(coarse_edges),
            like(node_latents),
            shape((TOP, width), F32),
            shape((TOP, width), F32),
            shape((width, width), BF16),
            like(w_node_out),
        ),
        [from_even, nodes, from_odd, w_ends, w_out, send, recv, new_coarse]
        + in_hbm(edge_latents, w_edge_in, w_node_in, w_node_out)
        + [sums],
        hbm=range(8, 13),
        out_specs=[ANY] * 2 + [VMEM] * 5,
        scratch=[
            vmem(edge_latents.shape, BF16), vmem((width, width), BF16), vmem((width, width), BF16),
            vmem(edge_latents.shape, BF16), dma((5,)), dma((edge_count // STEP + 1,)),
        ],
        flops=64 * edge_count * square,
    )
    (new_nodes,) = call(
        top_kernel, "top", (like(node_latents),), [got, agg, node_part, nodes, wn_agg, wn_out, rest], out_specs=[ANY],
        scratch=[vmem((TOP, width), BF16), dma((2,))],
    )
    return (new_nodes, new_edges, new_coarse)


def solution(mesh):
    rows = P(("parts", "patch", "sub"), None)
    ids = P(("parts", "patch", "sub"))
    in_specs = (
        rows, rows, rows, P(), P(), P(), P(), ids, ids, P(("parts", "patch", "sub"), None, None), ids, ids,
    )
    return jax.shard_map(body, mesh=mesh, in_specs=in_specs, out_specs=(rows, rows, rows), check_vma=False)
```

```python
import jax
import jax.numpy as jnp
from jax import lax
from jax.experimental import pallas as pl
from jax.experimental.pallas import tpu as pltpu
from jax.sharding import PartitionSpec as P

CO_DEV = 4
GROUP_AXES = ("patch", "sub")
TOP = 16
STEP = 512
MIB = 1 << 20
FIRST, SECOND = 2, 3
ANY = pl.BlockSpec(memory_space=pl.ANY)
VMEM = pl.BlockSpec(memory_space=pltpu.VMEM)
BF16, F32 = jnp.bfloat16, jnp.float32


def order(group, quarter):
    return [(group * quarter // 4 - i) % group for i in range(group)]


def pair(value, first):
    devices = lax.axis_size(GROUP_AXES)
    pairs = [(i, (i + 1) % devices) for i in range(first, devices, 2)]
    return lax.ppermute(value, GROUP_AXES, pairs + [(b, a) for a, b in pairs])


def dot(a, b):
    return jnp.dot(a, b, preferred_element_type=F32)


def dot_t(a, b):
    return lax.dot_general(a, b, (((0,), (0,)), ((), ())), preferred_element_type=F32)


def onehot_t(rows, ids):
    at = lax.broadcasted_iota(jnp.int32, (rows, ids.shape[1]), 0)
    return jnp.where(at == ids, 1.0, 0.0).astype(BF16)


def silu(v):
    half = 0.5 * v
    return half + half * jnp.tanh(half)


def norm_parts(values):
    mean = jnp.mean(values, axis=-1, keepdims=True)
    centred = values - mean
    return centred, lax.rsqrt(jnp.mean(centred * centred, axis=-1, keepdims=True) + 1e-05)


def head_kernel(nodes_hbm, heads_ref, rows_ref, sem):
    copy = pltpu.make_async_copy(nodes_hbm.at[pl.ds(0, TOP)], rows_ref, sem)
    copy.start()
    copy.wait()
    head = rows_ref[0:CO_DEV, :]
    for at in range(heads_ref.shape[0]):
        heads_ref[at] = head


def start_copies(sources, targets, sems):
    copies = [pltpu.make_async_copy(a, b, sems.at[i]) for i, (a, b) in enumerate(zip(sources, targets))]
    for copy in copies:
        copy.start()
    return copies


def load_kernel(
    nodes_hbm, lists_hbm, cedges_hbm, w_in_hbm, csend_hbm, crecv_hbm, w_out_hbm, send_hbm, recv_hbm, after,
    nodes_ref, cedges_ref, w_ends_ref, w_out_ref, send_ref, recv_ref,
    even_ref, odd_ref, gather_ref, picks_ref, part_ref,
    lists_ref, w_self_ref, csend_ref, crecv_ref, sems,
):
    width = nodes_ref.shape[1]
    copies = start_copies(
        [
            nodes_hbm, lists_hbm, cedges_hbm, w_in_hbm.at[pl.ds(0, width)], csend_hbm, crecv_hbm,
            w_in_hbm.at[pl.ds(width, 2 * width)], w_out_hbm, send_hbm, recv_hbm,
        ],
        [
            nodes_ref, lists_ref, cedges_ref, w_self_ref, csend_ref, crecv_ref, w_ends_ref, w_out_ref, send_ref, recv_ref,
        ],
        sems,
    )
    for copy in copies[:2]:
        copy.wait()
    nodes = nodes_ref[...]
    count = nodes.shape[0]
    lists = lists_ref[0]
    me = lax.axis_index(GROUP_AXES)
    odd = me % 2
    first = lists[0:1, :] * (1 - odd) + lists[1:2, :] * odd
    second = lists[1:2, :] * (1 - odd) + lists[0:1, :] * odd
    even_ref[...] = dot_t(onehot_t(count, first), nodes).astype(BF16)
    odd_ref[...] = dot_t(onehot_t(count, second), nodes).astype(BF16)
    for copy in copies[2:6]:
        copy.wait()
    part_ref[...] = dot(cedges_ref[...], w_self_ref[...])
    rows, ids = picks_ref.shape
    at = lax.broadcasted_iota(jnp.int32, (rows, ids), 0)
    count = rows // CO_DEV
    node = (order(count, FIRST)[0] + count - at // CO_DEV) % count * CO_DEV + at % CO_DEV
    send = jnp.where(node == csend_ref[...], 1.0, 0.0).astype(BF16)
    recv = jnp.where(node == crecv_ref[...], 1.0, 0.0).astype(BF16)
    picks_ref[...] = onehot_t(rows, crecv_ref[...])
    across = lax.broadcasted_iota(jnp.int32, (rows, rows), 0) == lax.broadcasted_iota(jnp.int32, (rows, rows), 1)
    eye = jnp.where(across, 1.0, 0.0).astype(BF16)
    gather_ref[0:ids, :] = dot_t(send, eye).astype(BF16)
    gather_ref[ids:, :] = dot_t(recv, eye).astype(BF16)
    for copy in copies[6:]:
        copy.wait()


def coarse_kernel(
    lat_ref, edges_ref, part_ref, gather_ref, picks_ref, w_ends_ref, w_out_ref, new_ref, sums_hbm, sums_ref, sem
):
    count, width = edges_ref.shape
    blocks = lat_ref.shape[0]
    lat = jnp.concatenate([lat_ref[at].astype(F32) for at in range(blocks)], axis=0).astype(BF16)
    ends = dot(gather_ref[...], lat).astype(BF16)
    ends = jnp.concatenate([ends[0:count], ends[count:]], axis=1)
    hidden = silu(part_ref[...] + dot(ends, w_ends_ref[...])).astype(BF16)
    centred, scale = norm_parts(dot(hidden, w_out_ref[...]))
    new = (edges_ref[...].astype(F32) + centred * scale).astype(BF16)
    new_ref[...] = new
    sums = dot(picks_ref[...], new).astype(BF16)
    for at, owner in enumerate(order(blocks, SECOND)):
        sums_ref[at] = sums[owner * CO_DEV : (owner + 1) * CO_DEV, :]
    copy = pltpu.make_async_copy(sums_ref, sums_hbm, sem)
    copy.start()
    copy.wait()


def fine_kernel(
    even_ref, nodes_ref, odd_ref, w_ends_ref, w_out_ref, send_ref, recv_ref, coarse_ref,
    edges_hbm, w_in_hbm, wn_in_hbm, wn_out_hbm, after,
    new_hbm, coarse_hbm, out_ref, agg_ref, npart_ref, wn_agg_ref, wn_out_ref,
    edges_ref, w_self_ref, wn_self_ref, new_ref, sems, out_sems,
):
    nodes = nodes_ref[...]
    count, width = nodes.shape
    copies = start_copies(
        [
            edges_hbm, w_in_hbm.at[pl.ds(0, width)],
            wn_in_hbm.at[pl.ds(0, width)], wn_in_hbm.at[pl.ds(width, width)], wn_out_hbm,
        ],
        [edges_ref, w_self_ref, wn_self_ref, wn_agg_ref, wn_out_ref],
        sems,
    )
    outs = [pltpu.make_async_copy(coarse_ref, coarse_hbm, out_sems.at[0])]
    outs[0].start()
    odd = (lax.axis_index(GROUP_AXES) % 2).astype(F32)
    met, other = even_ref[...].astype(F32), odd_ref[...].astype(F32)
    prev = (met * odd + other * (1.0 - odd)).astype(BF16)
    following = (other * odd + met * (1.0 - odd)).astype(BF16)
    extended = jnp.concatenate([prev, nodes, following], axis=0)
    ones = jnp.ones((count, 128), BF16)
    total = jnp.zeros((count, width), F32)
    for at in range(0, edges_ref.shape[0], STEP):
        rows = pl.ds(at, STEP)
        picks = onehot_t(count, recv_ref[:, rows])
        senders = dot_t(onehot_t(extended.shape[0], send_ref[:, rows]), extended).astype(BF16)
        receivers = dot_t(picks, nodes).astype(BF16)
        valid = dot_t(picks, ones)[:, 0:1]
        pre = dot(jnp.concatenate([senders, receivers], axis=1), w_ends_ref[...])
        if at == 0:
            for copy in copies[:2]:
                copy.wait()
        edges = edges_ref[rows, :]
        pre = pre + dot(edges, w_self_ref[...])
        hidden = silu(pre).astype(BF16)
        centred, scale = norm_parts(dot(hidden, w_out_ref[...]))
        new = (edges.astype(F32) + centred * (scale * valid)).astype(BF16)
        new_ref[rows, :] = new
        copy = pltpu.make_async_copy(new_ref.at[rows], new_hbm.at[rows], out_sems.at[at // STEP + 1])
        copy.start()
        outs.append(copy)
        total = total + dot(picks, new)
    agg_ref[...] = total[0:TOP]
    for copy in copies[2:]:
        copy.wait()
    pre = dot(nodes, wn_self_ref[...])
    npart_ref[...] = pre[0:TOP]
    pre = pre + dot(total.astype(BF16), wn_agg_ref[...])
    hidden = silu(pre).astype(BF16)
    centred, scale = norm_parts(dot(hidden, wn_out_ref[...]))
    out_ref[...] = (nodes.astype(F32) + centred * scale).astype(BF16)
    for copy in outs:
        copy.wait()


def top_kernel(got_ref, agg_ref, part_ref, nodes_ref, wn_agg_ref, wn_out_ref, rest_ref, out_hbm, top_ref, sems):
    count, width = rest_ref.shape
    below = pl.ds(TOP, count - TOP)
    rest = pltpu.make_async_copy(rest_ref.at[below], out_hbm.at[below], sems.at[0])
    rest.start()
    terms = [got_ref[at].astype(F32) for at in range(got_ref.shape[0])]
    while len(terms) > 1:
        half = len(terms) // 2
        terms = [a + b for a, b in zip(terms[:half], terms[half:])] + terms[2 * half :]
    sums = jnp.concatenate([terms[0], jnp.zeros((TOP - CO_DEV, width), F32)], axis=0)
    agg = (agg_ref[...] + sums).astype(BF16)
    hidden = silu(part_ref[...] + dot(agg, wn_agg_ref[...])).astype(BF16)
    centred, scale = norm_parts(dot(hidden, wn_out_ref[...]))
    top_ref[...] = (nodes_ref[0:TOP, :].astype(F32) + centred * scale).astype(BF16)
    top = pltpu.make_async_copy(top_ref, out_hbm.at[pl.ds(0, TOP)], sems.at[1])
    top.start()
    rest.wait()
    top.wait()


def in_hbm(*arrays):
    return [pltpu.with_memory_space_constraint(a, pltpu.HBM) for a in arrays]


def cost(flops, moved=0):
    return pl.CostEstimate(flops=flops, bytes_accessed=moved, transcendentals=0)


def call(kernel, name, outs, ins, out_specs=None, scratch=(), hbm=(), flops=0, **more):
    return pl.pallas_call(
        kernel,
        out_shape=outs,
        in_specs=[ANY if i in hbm else VMEM for i in range(len(ins))],
        out_specs=[VMEM] * len(outs) if out_specs is None else out_specs,
        scratch_shapes=scratch,
        compiler_params=pltpu.CompilerParams(vmem_limit_bytes=16 * MIB),
        cost_estimate=cost(flops),
        name=name,
        **more,
    )(*ins)


def body(
    node_latents,
    edge_latents,
    coarse_edges,
    w_edge_in,
    w_edge_out,
    w_node_in,
    w_node_out,
    fine_senders,
    fine_receivers,
    halo_lists,
    coarse_senders,
    coarse_receivers,
):
    count, width = node_latents.shape
    edge_count = edge_latents.shape[0]
    cedge_count = coarse_edges.shape[0]
    halo = halo_lists.shape[2]
    group = lax.axis_size(GROUP_AXES)
    coarse_count = group * CO_DEV
    shape = jax.ShapeDtypeStruct
    like = lambda a: shape(a.shape, a.dtype)
    vmem = pltpu.VMEM
    dma = pltpu.SemaphoreType.DMA
    square = 2 * width * width
    blocks = shape((group, CO_DEV, width), BF16)
    ids = lambda a: a[None, :]

    (heads,) = call(
        head_kernel, "head", (blocks,), in_hbm(node_latents), hbm=(0,), scratch=[vmem((TOP, width), BF16), dma(())],
    )
    lat = lax.all_to_all(heads, GROUP_AXES, 0, 0, axis_index_groups=[order(group, FIRST)])
    send, recv = ids(fine_senders), ids(fine_receivers)
    nodes, cedges, w_ends, w_out, send, recv, to_even, to_odd, gather, picks, coarse_part = call(
        load_kernel,
        "load",
        (
            like(node_latents),
            like(coarse_edges),
            shape((2 * width, width), BF16),
            like(w_edge_out),
            like(send),
            like(recv),
            shape((halo, width), BF16),
            shape((halo, width), BF16),
            shape((2 * cedge_count, coarse_count), BF16),
            shape((coarse_count, cedge_count), BF16),
            shape((cedge_count, width), F32),
        ),
        in_hbm(
            node_latents, halo_lists, coarse_edges, w_edge_in, ids(coarse_senders), ids(coarse_receivers), w_edge_out,
            send, recv,
        )
        + [heads],
        hbm=range(10),
        scratch=[
            vmem(halo_lists.shape, jnp.int32), vmem((width, width), BF16),
            vmem((1, cedge_count), jnp.int32), vmem((1, cedge_count), jnp.int32), dma((10,)),
        ],
        flops=edge_count * square,
    )
    from_even, from_odd = pair(to_even, 0), pair(to_odd, 1)
    new_coarse, sums = call(
        coarse_kernel, "coarse", (like(coarse_edges), blocks),
        [lat, cedges, coarse_part, gather, picks, w_ends, w_out], out_specs=[VMEM, ANY],
        scratch=[vmem(blocks.shape, BF16), dma(())],
    )
    got = lax.all_to_all(sums, GROUP_AXES, 0, 0, axis_index_groups=[order(group, SECOND)])
    new_edges, new_coarse, rest, agg, node_part, wn_agg, wn_out = call(
        fine_kernel,
        "fine",
        (
            like(edge_latents),
            like(coarse_edges),
            like(node_latents),
            shape((TOP, width), F32),
            shape((TOP, width), F32),
            shape((width, width), BF16),
            like(w_node_out),
        ),
        [from_even, nodes, from_odd, w_ends, w_out, send, recv, new_coarse]
        + in_hbm(edge_latents, w_edge_in, w_node_in, w_node_out)
        + [sums],
        hbm=range(8, 13),
        out_specs=[ANY] * 2 + [VMEM] * 5,
        scratch=[
            vmem(edge_latents.shape, BF16), vmem((width, width), BF16), vmem((width, width), BF16),
            vmem(edge_latents.shape, BF16), dma((5,)), dma((edge_count // STEP + 1,)),
        ],
        flops=64 * edge_count * square,
    )
    (new_nodes,) = call(
        top_kernel, "top", (like(node_latents),), [got, agg, node_part, nodes, wn_agg, wn_out, rest], out_specs=[ANY],
        scratch=[vmem((TOP, width), BF16), dma((2,))],
    )
    return (new_nodes, new_edges, new_coarse)


def solution(mesh):
    rows = P(("parts", "patch", "sub"), None)
    ids = P(("parts", "patch", "sub"))
    in_specs = (
        rows, rows, rows, P(), P(), P(), P(), ids, ids, P(("parts", "patch", "sub"), None, None), ids, ids,
    )
    return jax.shard_map(body, mesh=mesh, in_specs=in_specs, out_specs=(rows, rows, rows), check_vma=False)
```

```python
import jax
import jax.numpy as jnp
from jax import lax
from jax.experimental import pallas as pl
from jax.experimental.pallas import tpu as pltpu
from jax.sharding import PartitionSpec as P

CO_DEV = 4
GROUP_AXES = ("patch", "sub")
TOP = 16
STEP = 512
MIB = 1 << 20
FIRST, SECOND = 2, 2
ANY = pl.BlockSpec(memory_space=pl.ANY)
VMEM = pl.BlockSpec(memory_space=pltpu.VMEM)
BF16, F32 = jnp.bfloat16, jnp.float32


def order(group, quarter):
    return [(i + group * quarter // 4) % group for i in range(group)]


def pair(value, first):
    devices = lax.axis_size(GROUP_AXES)
    pairs = [(i, (i + 1) % devices) for i in range(first, devices, 2)]
    return lax.ppermute(value, GROUP_AXES, pairs + [(b, a) for a, b in pairs])


def dot(a, b):
    return jnp.dot(a, b, preferred_element_type=F32)


def dot_t(a, b):
    return lax.dot_general(a, b, (((0,), (0,)), ((), ())), preferred_element_type=F32)


def onehot_t(rows, ids):
    at = lax.broadcasted_iota(jnp.int32, (rows, ids.shape[1]), 0)
    return jnp.where(at == ids, 1.0, 0.0).astype(BF16)


def silu(v):
    half = 0.5 * v
    return half + half * jnp.tanh(half)


def norm_parts(values):
    mean = jnp.mean(values, axis=-1, keepdims=True)
    centred = values - mean
    return centred, lax.rsqrt(jnp.mean(centred * centred, axis=-1, keepdims=True) + 1e-05)


def head_kernel(nodes_hbm, heads_ref, rows_ref, sem):
    copy = pltpu.make_async_copy(nodes_hbm.at[pl.ds(0, TOP)], rows_ref, sem)
    copy.start()
    copy.wait()
    head = rows_ref[0:CO_DEV, :]
    for at in range(heads_ref.shape[0]):
        heads_ref[at] = head


def start_copies(sources, targets, sems):
    copies = [pltpu.make_async_copy(a, b, sems.at[i]) for i, (a, b) in enumerate(zip(sources, targets))]
    for copy in copies:
        copy.start()
    return copies


def load_kernel(
    nodes_hbm, lists_hbm, cedges_hbm, w_in_hbm, csend_hbm, crecv_hbm, w_out_hbm, send_hbm, recv_hbm, after,
    nodes_ref, cedges_ref, w_ends_ref, w_out_ref, send_ref, recv_ref,
    even_ref, odd_ref, gather_ref, picks_ref, part_ref,
    lists_ref, w_self_ref, csend_ref, crecv_ref, sems,
):
    width = nodes_ref.shape[1]
    copies = start_copies(
        [
            nodes_hbm, lists_hbm, cedges_hbm, w_in_hbm.at[pl.ds(0, width)], csend_hbm, crecv_hbm,
            w_in_hbm.at[pl.ds(width, 2 * width)], w_out_hbm, send_hbm, recv_hbm,
        ],
        [
            nodes_ref, lists_ref, cedges_ref, w_self_ref, csend_ref, crecv_ref, w_ends_ref, w_out_ref, send_ref, recv_ref,
        ],
        sems,
    )
    for copy in copies[:2]:
        copy.wait()
    nodes = nodes_ref[...]
    count = nodes.shape[0]
    lists = lists_ref[0]
    me = lax.axis_index(GROUP_AXES)
    odd = me % 2
    first = lists[0:1, :] * (1 - odd) + lists[1:2, :] * odd
    second = lists[1:2, :] * (1 - odd) + lists[0:1, :] * odd
    even_ref[...] = dot_t(onehot_t(count, first), nodes).astype(BF16)
    odd_ref[...] = dot_t(onehot_t(count, second), nodes).astype(BF16)
    for copy in copies[2:6]:
        copy.wait()
    part_ref[...] = dot(cedges_ref[...], w_self_ref[...])
    rows, ids = picks_ref.shape
    at = lax.broadcasted_iota(jnp.int32, (rows, ids), 0)
    node = (at + CO_DEV * order(rows // CO_DEV, FIRST)[0]) % rows
    send = jnp.where(node == csend_ref[...], 1.0, 0.0).astype(BF16)
    recv = jnp.where(node == crecv_ref[...], 1.0, 0.0).astype(BF16)
    picks_ref[...] = onehot_t(rows, crecv_ref[...])
    across = lax.broadcasted_iota(jnp.int32, (rows, rows), 0) == lax.broadcasted_iota(jnp.int32, (rows, rows), 1)
    eye = jnp.where(across, 1.0, 0.0).astype(BF16)
    gather_ref[0:ids, :] = dot_t(send, eye).astype(BF16)
    gather_ref[ids:, :] = dot_t(recv, eye).astype(BF16)
    for copy in copies[6:]:
        copy.wait()


def coarse_kernel(
    lat_ref, edges_ref, part_ref, gather_ref, picks_ref, w_ends_ref, w_out_ref, new_ref, sums_hbm, sums_ref, sem
):
    count, width = edges_ref.shape
    blocks = lat_ref.shape[0]
    lat = jnp.concatenate([lat_ref[at].astype(F32) for at in range(blocks)], axis=0).astype(BF16)
    ends = dot(gather_ref[...], lat).astype(BF16)
    ends = jnp.concatenate([ends[0:count], ends[count:]], axis=1)
    hidden = silu(part_ref[...] + dot(ends, w_ends_ref[...])).astype(BF16)
    centred, scale = norm_parts(dot(hidden, w_out_ref[...]))
    new = (edges_ref[...].astype(F32) + centred * scale).astype(BF16)
    new_ref[...] = new
    sums = dot(picks_ref[...], new).astype(BF16)
    for at, owner in enumerate(order(blocks, SECOND)):
        sums_ref[at] = sums[owner * CO_DEV : (owner + 1) * CO_DEV, :]
    copy = pltpu.make_async_copy(sums_ref, sums_hbm, sem)
    copy.start()
    copy.wait()


def fine_kernel(
    even_ref, nodes_ref, odd_ref, w_ends_ref, w_out_ref, send_ref, recv_ref, coarse_ref,
    edges_hbm, w_in_hbm, wn_in_hbm, wn_out_hbm, after,
    new_hbm, coarse_hbm, out_ref, agg_ref, npart_ref, wn_agg_ref, wn_out_ref,
    edges_ref, w_self_ref, wn_self_ref, new_ref, sems, out_sems,
):
    nodes = nodes_ref[...]
    count, width = nodes.shape
    copies = start_copies(
        [
            edges_hbm, w_in_hbm.at[pl.ds(0, width)],
            wn_in_hbm.at[pl.ds(0, width)], wn_in_hbm.at[pl.ds(width, width)], wn_out_hbm,
        ],
        [edges_ref, w_self_ref, wn_self_ref, wn_agg_ref, wn_out_ref],
        sems,
    )
    outs = [pltpu.make_async_copy(coarse_ref, coarse_hbm, out_sems.at[0])]
    outs[0].start()
    odd = (lax.axis_index(GROUP_AXES) % 2).astype(F32)
    met, other = even_ref[...].astype(F32), odd_ref[...].astype(F32)
    prev = (met * odd + other * (1.0 - odd)).astype(BF16)
    following = (other * odd + met * (1.0 - odd)).astype(BF16)
    extended = jnp.concatenate([prev, nodes, following], axis=0)
    ones = jnp.ones((count, 128), BF16)
    total = jnp.zeros((count, width), F32)
    for at in range(0, edges_ref.shape[0], STEP):
        rows = pl.ds(at, STEP)
        picks = onehot_t(count, recv_ref[:, rows])
        senders = dot_t(onehot_t(extended.shape[0], send_ref[:, rows]), extended).astype(BF16)
        receivers = dot_t(picks, nodes).astype(BF16)
        valid = dot_t(picks, ones)[:, 0:1]
        pre = dot(jnp.concatenate([senders, receivers], axis=1), w_ends_ref[...])
        if at == 0:
            for copy in copies[:2]:
                copy.wait()
        edges = edges_ref[rows, :]
        pre = pre + dot(edges, w_self_ref[...])
        hidden = silu(pre).astype(BF16)
        centred, scale = norm_parts(dot(hidden, w_out_ref[...]))
        new = (edges.astype(F32) + centred * (scale * valid)).astype(BF16)
        new_ref[rows, :] = new
        copy = pltpu.make_async_copy(new_ref.at[rows], new_hbm.at[rows], out_sems.at[at // STEP + 1])
        copy.start()
        outs.append(copy)
        total = total + dot(picks, new)
    agg_ref[...] = total[0:TOP]
    for copy in copies[2:]:
        copy.wait()
    pre = dot(nodes, wn_self_ref[...])
    npart_ref[...] = pre[0:TOP]
    pre = pre + dot(total.astype(BF16), wn_agg_ref[...])
    hidden = silu(pre).astype(BF16)
    centred, scale = norm_parts(dot(hidden, wn_out_ref[...]))
    out_ref[...] = (nodes.astype(F32) + centred * scale).astype(BF16)
    for copy in outs:
        copy.wait()


def top_kernel(got_ref, agg_ref, part_ref, nodes_ref, wn_agg_ref, wn_out_ref, rest_ref, out_hbm, top_ref, sems):
    count, width = rest_ref.shape
    below = pl.ds(TOP, count - TOP)
    rest = pltpu.make_async_copy(rest_ref.at[below], out_hbm.at[below], sems.at[0])
    rest.start()
    terms = [got_ref[at].astype(F32) for at in range(got_ref.shape[0])]
    while len(terms) > 1:
        half = len(terms) // 2
        terms = [a + b for a, b in zip(terms[:half], terms[half:])] + terms[2 * half :]
    sums = jnp.concatenate([terms[0], jnp.zeros((TOP - CO_DEV, width), F32)], axis=0)
    agg = (agg_ref[...] + sums).astype(BF16)
    hidden = silu(part_ref[...] + dot(agg, wn_agg_ref[...])).astype(BF16)
    centred, scale = norm_parts(dot(hidden, wn_out_ref[...]))
    top_ref[...] = (nodes_ref[0:TOP, :].astype(F32) + centred * scale).astype(BF16)
    top = pltpu.make_async_copy(top_ref, out_hbm.at[pl.ds(0, TOP)], sems.at[1])
    top.start()
    rest.wait()
    top.wait()


def in_hbm(*arrays):
    return [pltpu.with_memory_space_constraint(a, pltpu.HBM) for a in arrays]


def cost(flops, moved=0):
    return pl.CostEstimate(flops=flops, bytes_accessed=moved, transcendentals=0)


def call(kernel, name, outs, ins, out_specs=None, scratch=(), hbm=(), flops=0, **more):
    return pl.pallas_call(
        kernel,
        out_shape=outs,
        in_specs=[ANY if i in hbm else VMEM for i in range(len(ins))],
        out_specs=[VMEM] * len(outs) if out_specs is None else out_specs,
        scratch_shapes=scratch,
        compiler_params=pltpu.CompilerParams(vmem_limit_bytes=16 * MIB),
        cost_estimate=cost(flops),
        name=name,
        **more,
    )(*ins)


def body(
    node_latents,
    edge_latents,
    coarse_edges,
    w_edge_in,
    w_edge_out,
    w_node_in,
    w_node_out,
    fine_senders,
    fine_receivers,
    halo_lists,
    coarse_senders,
    coarse_receivers,
):
    count, width = node_latents.shape
    edge_count = edge_latents.shape[0]
    cedge_count = coarse_edges.shape[0]
    halo = halo_lists.shape[2]
    group = lax.axis_size(GROUP_AXES)
    coarse_count = group * CO_DEV
    shape = jax.ShapeDtypeStruct
    like = lambda a: shape(a.shape, a.dtype)
    vmem = pltpu.VMEM
    dma = pltpu.SemaphoreType.DMA
    square = 2 * width * width
    blocks = shape((group, CO_DEV, width), BF16)
    ids = lambda a: a[None, :]

    (heads,) = call(
        head_kernel, "head", (blocks,), in_hbm(node_latents), hbm=(0,), scratch=[vmem((TOP, width), BF16), dma(())],
    )
    lat = lax.all_to_all(heads, GROUP_AXES, 0, 0, axis_index_groups=[order(group, FIRST)])
    send, recv = ids(fine_senders), ids(fine_receivers)
    nodes, cedges, w_ends, w_out, send, recv, to_even, to_odd, gather, picks, coarse_part = call(
        load_kernel,
        "load",
        (
            like(node_latents),
            like(coarse_edges),
            shape((2 * width, width), BF16),
            like(w_edge_out),
            like(send),
            like(recv),
            shape((halo, width), BF16),
            shape((halo, width), BF16),
            shape((2 * cedge_count, coarse_count), BF16),
            shape((coarse_count, cedge_count), BF16),
            shape((cedge_count, width), F32),
        ),
        in_hbm(
            node_latents, halo_lists, coarse_edges, w_edge_in, ids(coarse_senders), ids(coarse_receivers), w_edge_out,
            send, recv,
        )
        + [heads],
        hbm=range(10),
        scratch=[
            vmem(halo_lists.shape, jnp.int32), vmem((width, width), BF16),
            vmem((1, cedge_count), jnp.int32), vmem((1, cedge_count), jnp.int32), dma((10,)),
        ],
        flops=edge_count * square,
    )
    from_even, from_odd = pair(to_even, 0), pair(to_odd, 1)
    new_coarse, sums = call(
        coarse_kernel, "coarse", (like(coarse_edges), blocks),
        [lat, cedges, coarse_part, gather, picks, w_ends, w_out], out_specs=[VMEM, ANY],
        scratch=[vmem(blocks.shape, BF16), dma(())],
    )
    got = lax.all_to_all(sums, GROUP_AXES, 0, 0, axis_index_groups=[order(group, SECOND)])
    new_edges, new_coarse, rest, agg, node_part, wn_agg, wn_out = call(
        fine_kernel,
        "fine",
        (
            like(edge_latents),
            like(coarse_edges),
            like(node_latents),
            shape((TOP, width), F32),
            shape((TOP, width), F32),
            shape((width, width), BF16),
            like(w_node_out),
        ),
        [from_even, nodes, from_odd, w_ends, w_out, send, recv, new_coarse]
        + in_hbm(edge_latents, w_edge_in, w_node_in, w_node_out)
        + [sums],
        hbm=range(8, 13),
        out_specs=[ANY] * 2 + [VMEM] * 5,
        scratch=[
            vmem(edge_latents.shape, BF16), vmem((width, width), BF16), vmem((width, width), BF16),
            vmem(edge_latents.shape, BF16), dma((5,)), dma((edge_count // STEP + 1,)),
        ],
        flops=64 * edge_count * square,
    )
    (new_nodes,) = call(
        top_kernel, "top", (like(node_latents),), [got, agg, node_part, nodes, wn_agg, wn_out, rest], out_specs=[ANY],
        scratch=[vmem((TOP, width), BF16), dma((2,))],
    )
    return (new_nodes, new_edges, new_coarse)


def solution(mesh):
    rows = P(("parts", "patch", "sub"), None)
    ids = P(("parts", "patch", "sub"))
    in_specs = (
        rows, rows, rows, P(), P(), P(), P(), ids, ids, P(("parts", "patch", "sub"), None, None), ids, ids,
    )
    return jax.shard_map(body, mesh=mesh, in_specs=in_specs, out_specs=(rows, rows, rows), check_vma=False)
```

```python
import jax
import jax.numpy as jnp
from jax import lax
from jax.experimental import pallas as pl
from jax.experimental.pallas import tpu as pltpu
from jax.sharding import PartitionSpec as P

CO_DEV = 4
GROUP_AXES = ("patch", "sub")
TOP = 16
STEP = 512
MIB = 1 << 20
FIRST, SECOND = 2, 2
ANY = pl.BlockSpec(memory_space=pl.ANY)
VMEM = pl.BlockSpec(memory_space=pltpu.VMEM)
BF16, F32 = jnp.bfloat16, jnp.float32


def order(group, quarter):
    return [(i + group * quarter // 4) % group for i in range(group)]


def pair(value, first):
    devices = lax.axis_size(GROUP_AXES)
    pairs = [(i, (i + 1) % devices) for i in range(first, devices, 2)]
    return lax.ppermute(value, GROUP_AXES, pairs + [(b, a) for a, b in pairs])


def dot(a, b):
    return jnp.dot(a, b, preferred_element_type=F32)


def dot_t(a, b):
    return lax.dot_general(a, b, (((0,), (0,)), ((), ())), preferred_element_type=F32)


def onehot_t(rows, ids):
    at = lax.broadcasted_iota(jnp.int32, (rows, ids.shape[1]), 0)
    return jnp.where(at == ids, 1.0, 0.0).astype(BF16)


def silu(v):
    half = 0.5 * v
    return half + half * jnp.tanh(half)


def norm_parts(values):
    mean = jnp.mean(values, axis=-1, keepdims=True)
    centred = values - mean
    return centred, lax.rsqrt(jnp.mean(centred * centred, axis=-1, keepdims=True) + 1e-05)


def head_kernel(nodes_hbm, heads_ref, rows_ref, sem):
    copy = pltpu.make_async_copy(nodes_hbm.at[pl.ds(0, TOP)], rows_ref, sem)
    copy.start()
    copy.wait()
    head = rows_ref[0:CO_DEV, :]
    for at in range(heads_ref.shape[0]):
        heads_ref[at] = head


def start_copies(sources, targets, sems):
    copies = [pltpu.make_async_copy(a, b, sems.at[i]) for i, (a, b) in enumerate(zip(sources, targets))]
    for copy in copies:
        copy.start()
    return copies


def load_kernel(
    nodes_hbm, lists_hbm, cedges_hbm, w_in_hbm, csend_hbm, crecv_hbm, w_out_hbm, send_hbm, recv_hbm, after,
    nodes_ref, cedges_ref, w_ends_ref, w_out_ref, send_ref, recv_ref,
    even_ref, odd_ref, gather_ref, picks_ref, part_ref,
    lists_ref, w_self_ref, csend_ref, crecv_ref, sems,
):
    width = nodes_ref.shape[1]
    copies = start_copies(
        [
            nodes_hbm, lists_hbm, cedges_hbm, w_in_hbm.at[pl.ds(0, width)], csend_hbm, crecv_hbm,
            w_in_hbm.at[pl.ds(width, 2 * width)], w_out_hbm, send_hbm, recv_hbm,
        ],
        [
            nodes_ref, lists_ref, cedges_ref, w_self_ref, csend_ref, crecv_ref, w_ends_ref, w_out_ref, send_ref, recv_ref,
        ],
        sems,
    )
    for copy in copies[:2]:
        copy.wait()
    nodes = nodes_ref[...]
    count = nodes.shape[0]
    lists = lists_ref[0]
    me = lax.axis_index(GROUP_AXES)
    odd = me % 2
    first = lists[0:1, :] * (1 - odd) + lists[1:2, :] * odd
    second = lists[1:2, :] * (1 - odd) + lists[0:1, :] * odd
    even_ref[...] = dot_t(onehot_t(count, first), nodes).astype(BF16)
    odd_ref[...] = dot_t(onehot_t(count, second), nodes).astype(BF16)
    for copy in copies[2:6]:
        copy.wait()
    part_ref[...] = dot(cedges_ref[...], w_self_ref[...])
    rows, ids = picks_ref.shape
    at = lax.broadcasted_iota(jnp.int32, (rows, ids), 0)
    node = (at + CO_DEV * order(rows // CO_DEV, FIRST)[0]) % rows
    send = jnp.where(node == csend_ref[...], 1.0, 0.0).astype(BF16)
    recv = jnp.where(node == crecv_ref[...], 1.0, 0.0).astype(BF16)
    picks_ref[...] = onehot_t(rows, crecv_ref[...])
    across = lax.broadcasted_iota(jnp.int32, (rows, rows), 0) == lax.broadcasted_iota(jnp.int32, (rows, rows), 1)
    eye = jnp.where(across, 1.0, 0.0).astype(BF16)
    gather_ref[0:ids, :] = dot_t(send, eye).astype(BF16)
    gather_ref[ids:, :] = dot_t(recv, eye).astype(BF16)
    for copy in copies[6:]:
        copy.wait()


def coarse_kernel(
    lat_ref, edges_ref, part_ref, gather_ref, picks_ref, w_ends_ref, w_out_ref, new_ref, sums_ref
):
    count, width = edges_ref.shape
    blocks = lat_ref.shape[0]
    lat = jnp.concatenate([lat_ref[at].astype(F32) for at in range(blocks)], axis=0).astype(BF16)
    ends = dot(gather_ref[...], lat).astype(BF16)
    ends = jnp.concatenate([ends[0:count], ends[count:]], axis=1)
    hidden = silu(part_ref[...] + dot(ends, w_ends_ref[...])).astype(BF16)
    centred, scale = norm_parts(dot(hidden, w_out_ref[...]))
    new = (edges_ref[...].astype(F32) + centred * scale).astype(BF16)
    new_ref[...] = new
    sums = dot(picks_ref[...], new).astype(BF16)
    for at, owner in enumerate(order(blocks, SECOND)):
        sums_ref[at] = sums[owner * CO_DEV : (owner + 1) * CO_DEV, :]


def fine_kernel(
    even_ref, nodes_ref, odd_ref, w_ends_ref, w_out_ref, send_ref, recv_ref, coarse_ref,
    edges_hbm, w_in_hbm, wn_in_hbm, wn_out_hbm, after,
    new_hbm, coarse_hbm, out_ref, agg_ref, npart_ref, wn_agg_ref, wn_out_ref,
    edges_ref, w_self_ref, wn_self_ref, new_ref, sems, out_sems,
):
    nodes = nodes_ref[...]
    count, width = nodes.shape
    copies = start_copies(
        [
            edges_hbm, w_in_hbm.at[pl.ds(0, width)],
            wn_in_hbm.at[pl.ds(0, width)], wn_in_hbm.at[pl.ds(width, width)], wn_out_hbm,
        ],
        [edges_ref, w_self_ref, wn_self_ref, wn_agg_ref, wn_out_ref],
        sems,
    )
    outs = [pltpu.make_async_copy(coarse_ref, coarse_hbm, out_sems.at[0])]
    outs[0].start()
    odd = (lax.axis_index(GROUP_AXES) % 2).astype(F32)
    met, other = even_ref[...].astype(F32), odd_ref[...].astype(F32)
    prev = (met * odd + other * (1.0 - odd)).astype(BF16)
    following = (other * odd + met * (1.0 - odd)).astype(BF16)
    extended = jnp.concatenate([prev, nodes, following], axis=0)
    ones = jnp.ones((count, 128), BF16)
    total = jnp.zeros((count, width), F32)
    for at in range(0, edges_ref.shape[0], STEP):
        rows = pl.ds(at, STEP)
        picks = onehot_t(count, recv_ref[:, rows])
        senders = dot_t(onehot_t(extended.shape[0], send_ref[:, rows]), extended).astype(BF16)
        receivers = dot_t(picks, nodes).astype(BF16)
        valid = dot_t(picks, ones)[:, 0:1]
        pre = dot(jnp.concatenate([senders, receivers], axis=1), w_ends_ref[...])
        if at == 0:
            for copy in copies[:2]:
                copy.wait()
        edges = edges_ref[rows, :]
        pre = pre + dot(edges, w_self_ref[...])
        hidden = silu(pre).astype(BF16)
        centred, scale = norm_parts(dot(hidden, w_out_ref[...]))
        new = (edges.astype(F32) + centred * (scale * valid)).astype(BF16)
        new_ref[rows, :] = new
        copy = pltpu.make_async_copy(new_ref.at[rows], new_hbm.at[rows], out_sems.at[at // STEP + 1])
        copy.start()
        outs.append(copy)
        total = total + dot(picks, new)
    agg_ref[...] = total[0:TOP]
    for copy in copies[2:]:
        copy.wait()
    pre = dot(nodes, wn_self_ref[...])
    npart_ref[...] = pre[0:TOP]
    pre = pre + dot(total.astype(BF16), wn_agg_ref[...])
    hidden = silu(pre).astype(BF16)
    centred, scale = norm_parts(dot(hidden, wn_out_ref[...]))
    out_ref[...] = (nodes.astype(F32) + centred * scale).astype(BF16)
    for copy in outs:
        copy.wait()


def top_kernel(got_ref, agg_ref, part_ref, nodes_ref, wn_agg_ref, wn_out_ref, rest_ref, out_hbm, top_ref, sems):
    count, width = rest_ref.shape
    below = pl.ds(TOP, count - TOP)
    rest = pltpu.make_async_copy(rest_ref.at[below], out_hbm.at[below], sems.at[0])
    rest.start()
    terms = [got_ref[at].astype(F32) for at in range(got_ref.shape[0])]
    while len(terms) > 1:
        half = len(terms) // 2
        terms = [a + b for a, b in zip(terms[:half], terms[half:])] + terms[2 * half :]
    sums = jnp.concatenate([terms[0], jnp.zeros((TOP - CO_DEV, width), F32)], axis=0)
    agg = (agg_ref[...] + sums).astype(BF16)
    hidden = silu(part_ref[...] + dot(agg, wn_agg_ref[...])).astype(BF16)
    centred, scale = norm_parts(dot(hidden, wn_out_ref[...]))
    top_ref[...] = (nodes_ref[0:TOP, :].astype(F32) + centred * scale).astype(BF16)
    top = pltpu.make_async_copy(top_ref, out_hbm.at[pl.ds(0, TOP)], sems.at[1])
    top.start()
    rest.wait()
    top.wait()


def in_hbm(*arrays):
    return [pltpu.with_memory_space_constraint(a, pltpu.HBM) for a in arrays]


def cost(flops, moved=0):
    return pl.CostEstimate(flops=flops, bytes_accessed=moved, transcendentals=0)


def call(kernel, name, outs, ins, out_specs=None, scratch=(), hbm=(), flops=0, **more):
    return pl.pallas_call(
        kernel,
        out_shape=outs,
        in_specs=[ANY if i in hbm else VMEM for i in range(len(ins))],
        out_specs=[VMEM] * len(outs) if out_specs is None else out_specs,
        scratch_shapes=scratch,
        compiler_params=pltpu.CompilerParams(vmem_limit_bytes=16 * MIB),
        cost_estimate=cost(flops),
        name=name,
        **more,
    )(*ins)


def body(
    node_latents,
    edge_latents,
    coarse_edges,
    w_edge_in,
    w_edge_out,
    w_node_in,
    w_node_out,
    fine_senders,
    fine_receivers,
    halo_lists,
    coarse_senders,
    coarse_receivers,
):
    count, width = node_latents.shape
    edge_count = edge_latents.shape[0]
    cedge_count = coarse_edges.shape[0]
    halo = halo_lists.shape[2]
    group = lax.axis_size(GROUP_AXES)
    coarse_count = group * CO_DEV
    shape = jax.ShapeDtypeStruct
    like = lambda a: shape(a.shape, a.dtype)
    vmem = pltpu.VMEM
    dma = pltpu.SemaphoreType.DMA
    square = 2 * width * width
    blocks = pltpu.VMEM((group, CO_DEV, width), BF16)
    ids = lambda a: a[None, :]

    (heads,) = call(
        head_kernel, "head", (blocks,), in_hbm(node_latents), hbm=(0,), scratch=[vmem((TOP, width), BF16), dma(())],
    )
    lat = lax.all_to_all(heads, GROUP_AXES, 0, 0, axis_index_groups=[order(group, FIRST)])
    send, recv = ids(fine_senders), ids(fine_receivers)
    nodes, cedges, w_ends, w_out, send, recv, to_even, to_odd, gather, picks, coarse_part = call(
        load_kernel,
        "load",
        (
            like(node_latents),
            like(coarse_edges),
            shape((2 * width, width), BF16),
            like(w_edge_out),
            like(send),
            like(recv),
            shape((halo, width), BF16),
            shape((halo, width), BF16),
            shape((2 * cedge_count, coarse_count), BF16),
            shape((coarse_count, cedge_count), BF16),
            shape((cedge_count, width), F32),
        ),
        in_hbm(
            node_latents, halo_lists, coarse_edges, w_edge_in, ids(coarse_senders), ids(coarse_receivers), w_edge_out,
            send, recv,
        )
        + [heads],
        hbm=range(10),
        scratch=[
            vmem(halo_lists.shape, jnp.int32), vmem((width, width), BF16),
            vmem((1, cedge_count), jnp.int32), vmem((1, cedge_count), jnp.int32), dma((10,)),
        ],
        flops=edge_count * square,
    )
    from_even, from_odd = pair(to_even, 0), pair(to_odd, 1)
    new_coarse, sums = call(
        coarse_kernel, "coarse", (like(coarse_edges), blocks),
        [lat, cedges, coarse_part, gather, picks, w_ends, w_out],
    )
    got = lax.all_to_all(sums, GROUP_AXES, 0, 0, axis_index_groups=[order(group, SECOND)])
    new_edges, new_coarse, rest, agg, node_part, wn_agg, wn_out = call(
        fine_kernel,
        "fine",
        (
            like(edge_latents),
            like(coarse_edges),
            like(node_latents),
            shape((TOP, width), F32),
            shape((TOP, width), F32),
            shape((width, width), BF16),
            like(w_node_out),
        ),
        [from_even, nodes, from_odd, w_ends, w_out, send, recv, new_coarse]
        + in_hbm(edge_latents, w_edge_in, w_node_in, w_node_out)
        + [sums],
        hbm=range(8, 13),
        out_specs=[ANY] * 2 + [VMEM] * 5,
        scratch=[
            vmem(edge_latents.shape, BF16), vmem((width, width), BF16), vmem((width, width), BF16),
            vmem(edge_latents.shape, BF16), dma((5,)), dma((edge_count // STEP + 1,)),
        ],
        flops=64 * edge_count * square,
    )
    (new_nodes,) = call(
        top_kernel, "top", (like(node_latents),), [got, agg, node_part, nodes, wn_agg, wn_out, rest], out_specs=[ANY],
        scratch=[vmem((TOP, width), BF16), dma((2,))],
    )
    return (new_nodes, new_edges, new_coarse)


def solution(mesh):
    rows = P(("parts", "patch", "sub"), None)
    ids = P(("parts", "patch", "sub"))
    in_specs = (
        rows, rows, rows, P(), P(), P(), P(), ids, ids, P(("parts", "patch", "sub"), None, None), ids, ids,
    )
    return jax.shard_map(body, mesh=mesh, in_specs=in_specs, out_specs=(rows, rows, rows), check_vma=False)
```

```python
import jax
import jax.numpy as jnp
from jax import lax
from jax.experimental import pallas as pl
from jax.experimental.pallas import tpu as pltpu
from jax.sharding import PartitionSpec as P

CO_DEV = 4
GROUP_AXES = ("patch", "sub")
TOP = 16
STEP = 512
MIB = 1 << 20
FIRST, SECOND = 4, 5
ANY = pl.BlockSpec(memory_space=pl.ANY)
VMEM = pl.BlockSpec(memory_space=pltpu.VMEM)
BF16, F32 = jnp.bfloat16, jnp.float32


def order(group, eighth):
    return [(i + group * eighth // 8) % group for i in range(group)]


def pair(value, first):
    devices = lax.axis_size(GROUP_AXES)
    pairs = [(i, (i + 1) % devices) for i in range(first, devices, 2)]
    return lax.ppermute(value, GROUP_AXES, pairs + [(b, a) for a, b in pairs])


def dot(a, b):
    return jnp.dot(a, b, preferred_element_type=F32)


def dot_t(a, b):
    return lax.dot_general(a, b, (((0,), (0,)), ((), ())), preferred_element_type=F32)


def onehot_t(rows, ids):
    at = lax.broadcasted_iota(jnp.int32, (rows, ids.shape[1]), 0)
    return jnp.where(at == ids, 1.0, 0.0).astype(BF16)


def silu(v):
    half = 0.5 * v
    return half + half * jnp.tanh(half)


def centre(weights):
    values = weights.astype(F32)
    return (values - jnp.mean(values, axis=-1, keepdims=True)).astype(BF16)


def spread(centred):
    return lax.rsqrt(jnp.mean(centred * centred, axis=-1, keepdims=True) + 1e-05)


def head_kernel(nodes_hbm, heads_ref, rows_ref, sem):
    copy = pltpu.make_async_copy(nodes_hbm.at[pl.ds(0, TOP)], rows_ref, sem)
    copy.start()
    copy.wait()
    head = rows_ref[0:CO_DEV, :]
    for at in range(heads_ref.shape[0]):
        heads_ref[at] = head


def start_copies(sources, targets, sems):
    copies = [pltpu.make_async_copy(a, b, sems.at[i]) for i, (a, b) in enumerate(zip(sources, targets))]
    for copy in copies:
        copy.start()
    return copies


def load_kernel(
    nodes_hbm, lists_hbm, cedges_hbm, w_in_hbm, csend_hbm, crecv_hbm, w_out_hbm, send_hbm, recv_hbm, after,
    nodes_ref, cedges_ref, w_ends_ref, w_out_ref, send_ref, recv_ref,
    even_ref, odd_ref, gather_ref, picks_ref, part_ref,
    lists_ref, w_self_ref, w_raw_ref, csend_ref, crecv_ref, sems,
):
    width = nodes_ref.shape[1]
    copies = start_copies(
        [
            nodes_hbm, lists_hbm, w_out_hbm, cedges_hbm, w_in_hbm.at[pl.ds(0, width)], csend_hbm, crecv_hbm,
            w_in_hbm.at[pl.ds(width, 2 * width)], send_hbm, recv_hbm,
        ],
        [
            nodes_ref, lists_ref, w_raw_ref, cedges_ref, w_self_ref, csend_ref, crecv_ref, w_ends_ref, send_ref, recv_ref,
        ],
        sems,
    )
    for copy in copies[:2]:
        copy.wait()
    nodes = nodes_ref[...]
    count = nodes.shape[0]
    lists = lists_ref[0]
    me = lax.axis_index(GROUP_AXES)
    odd = me % 2
    first = lists[0:1, :] * (1 - odd) + lists[1:2, :] * odd
    second = lists[1:2, :] * (1 - odd) + lists[0:1, :] * odd
    even_ref[...] = dot_t(onehot_t(count, first), nodes).astype(BF16)
    odd_ref[...] = dot_t(onehot_t(count, second), nodes).astype(BF16)
    copies[2].wait()
    w_out_ref[...] = centre(w_raw_ref[...])
    for copy in copies[3:7]:
        copy.wait()
    part_ref[...] = dot(cedges_ref[...], w_self_ref[...])
    rows, ids = picks_ref.shape
    at = lax.broadcasted_iota(jnp.int32, (rows, ids), 0)
    node = (at + CO_DEV * order(rows // CO_DEV, FIRST)[0]) % rows
    send = jnp.where(node == csend_ref[...], 1.0, 0.0).astype(BF16)
    recv = jnp.where(node == crecv_ref[...], 1.0, 0.0).astype(BF16)
    picks_ref[...] = onehot_t(rows, crecv_ref[...])
    across = lax.broadcasted_iota(jnp.int32, (rows, rows), 0) == lax.broadcasted_iota(jnp.int32, (rows, rows), 1)
    eye = jnp.where(across, 1.0, 0.0).astype(BF16)
    gather_ref[0:ids, :] = dot_t(send, eye).astype(BF16)
    gather_ref[ids:, :] = dot_t(recv, eye).astype(BF16)
    for copy in copies[7:]:
        copy.wait()


def coarse_kernel(
    lat_ref, edges_ref, part_ref, gather_ref, picks_ref, w_ends_ref, w_out_ref, new_ref, sums_ref
):
    count, width = edges_ref.shape
    blocks = lat_ref.shape[0]
    lat = jnp.concatenate([lat_ref[at].astype(F32) for at in range(blocks)], axis=0).astype(BF16)
    ends = dot(gather_ref[...], lat).astype(BF16)
    ends = jnp.concatenate([ends[0:count], ends[count:]], axis=1)
    hidden = silu(part_ref[...] + dot(ends, w_ends_ref[...])).astype(BF16)
    centred = dot(hidden, w_out_ref[...])
    new = (edges_ref[...].astype(F32) + centred * spread(centred)).astype(BF16)
    new_ref[...] = new
    sums = dot(picks_ref[...], new).astype(BF16)
    for at, owner in enumerate(order(blocks, SECOND)):
        sums_ref[at] = sums[owner * CO_DEV : (owner + 1) * CO_DEV, :]


def fine_kernel(
    even_ref, nodes_ref, odd_ref, w_ends_ref, w_out_ref, send_ref, recv_ref, coarse_ref,
    edges_hbm, w_in_hbm, wn_in_hbm, wn_out_hbm, after,
    new_hbm, coarse_hbm, out_ref, agg_ref, npart_ref, wn_agg_ref, wn_out_ref,
    edges_ref, w_self_ref, wn_self_ref, wn_raw_ref, new_ref, sems, out_sems,
):
    nodes = nodes_ref[...]
    count, width = nodes.shape
    copies = start_copies(
        [
            edges_hbm, w_in_hbm.at[pl.ds(0, width)],
            wn_in_hbm.at[pl.ds(0, width)], wn_in_hbm.at[pl.ds(width, width)], wn_out_hbm,
        ],
        [edges_ref, w_self_ref, wn_self_ref, wn_agg_ref, wn_raw_ref],
        sems,
    )
    outs = [pltpu.make_async_copy(coarse_ref, coarse_hbm, out_sems.at[0])]
    outs[0].start()
    odd = (lax.axis_index(GROUP_AXES) % 2).astype(F32)
    met, other = even_ref[...].astype(F32), odd_ref[...].astype(F32)
    prev = (met * odd + other * (1.0 - odd)).astype(BF16)
    following = (other * odd + met * (1.0 - odd)).astype(BF16)
    extended = jnp.concatenate([prev, nodes, following], axis=0)
    ones = jnp.ones((count, 128), BF16)
    total = jnp.zeros((count, width), F32)
    for at in range(0, edges_ref.shape[0], STEP):
        rows = pl.ds(at, STEP)
        picks = onehot_t(count, recv_ref[:, rows])
        senders = dot_t(onehot_t(extended.shape[0], send_ref[:, rows]), extended).astype(BF16)
        receivers = dot_t(picks, nodes).astype(BF16)
        valid = dot_t(picks, ones)[:, 0:1]
        pre = dot(jnp.concatenate([senders, receivers], axis=1), w_ends_ref[...])
        if at == 0:
            for copy in copies[:2]:
                copy.wait()
        edges = edges_ref[rows, :]
        pre = pre + dot(edges, w_self_ref[...])
        hidden = silu(pre).astype(BF16)
        centred = dot(hidden, w_out_ref[...])
        new = (edges.astype(F32) + centred * (spread(centred) * valid)).astype(BF16)
        new_ref[rows, :] = new
        copy = pltpu.make_async_copy(new_ref.at[rows], new_hbm.at[rows], out_sems.at[at // STEP + 1])
        copy.start()
        outs.append(copy)
        total = total + dot(picks, new)
    agg_ref[...] = total[0:TOP]
    for copy in copies[2:]:
        copy.wait()
    wn_out_ref[...] = centre(wn_raw_ref[...])
    pre = dot(nodes, wn_self_ref[...])
    npart_ref[...] = pre[0:TOP]
    pre = pre + dot(total.astype(BF16), wn_agg_ref[...])
    hidden = silu(pre).astype(BF16)
    centred = dot(hidden, wn_out_ref[...])
    out_ref[...] = (nodes.astype(F32) + centred * spread(centred)).astype(BF16)
    for copy in outs:
        copy.wait()


def top_kernel(got_ref, agg_ref, part_ref, nodes_ref, wn_agg_ref, wn_out_ref, rest_ref, out_hbm, top_ref, sems):
    count, width = rest_ref.shape
    below = pl.ds(TOP, count - TOP)
    rest = pltpu.make_async_copy(rest_ref.at[below], out_hbm.at[below], sems.at[0])
    rest.start()
    terms = [got_ref[at].astype(F32) for at in range(got_ref.shape[0])]
    while len(terms) > 1:
        half = len(terms) // 2
        terms = [a + b for a, b in zip(terms[:half], terms[half:])] + terms[2 * half :]
    sums = jnp.concatenate([terms[0], jnp.zeros((TOP - CO_DEV, width), F32)], axis=0)
    agg = (agg_ref[...] + sums).astype(BF16)
    hidden = silu(part_ref[...] + dot(agg, wn_agg_ref[...])).astype(BF16)
    centred = dot(hidden, wn_out_ref[...])
    top_ref[...] = (nodes_ref[0:TOP, :].astype(F32) + centred * spread(centred)).astype(BF16)
    top = pltpu.make_async_copy(top_ref, out_hbm.at[pl.ds(0, TOP)], sems.at[1])
    top.start()
    rest.wait()
    top.wait()


def in_hbm(*arrays):
    return [pltpu.with_memory_space_constraint(a, pltpu.HBM) for a in arrays]


def cost(flops, moved=0):
    return pl.CostEstimate(flops=flops, bytes_accessed=moved, transcendentals=0)


def call(kernel, name, outs, ins, out_specs=None, scratch=(), hbm=(), flops=0, **more):
    return pl.pallas_call(
        kernel,
        out_shape=outs,
        in_specs=[ANY if i in hbm else VMEM for i in range(len(ins))],
        out_specs=[VMEM] * len(outs) if out_specs is None else out_specs,
        scratch_shapes=scratch,
        compiler_params=pltpu.CompilerParams(vmem_limit_bytes=16 * MIB),
        cost_estimate=cost(flops),
        name=name,
        **more,
    )(*ins)


def body(
    node_latents,
    edge_latents,
    coarse_edges,
    w_edge_in,
    w_edge_out,
    w_node_in,
    w_node_out,
    fine_senders,
    fine_receivers,
    halo_lists,
    coarse_senders,
    coarse_receivers,
):
    count, width = node_latents.shape
    edge_count = edge_latents.shape[0]
    cedge_count = coarse_edges.shape[0]
    halo = halo_lists.shape[2]
    group = lax.axis_size(GROUP_AXES)
    coarse_count = group * CO_DEV
    shape = jax.ShapeDtypeStruct
    like = lambda a: shape(a.shape, a.dtype)
    vmem = pltpu.VMEM
    dma = pltpu.SemaphoreType.DMA
    square = 2 * width * width
    blocks = pltpu.VMEM((group, CO_DEV, width), BF16)
    ids = lambda a: a[None, :]

    (heads,) = call(
        head_kernel, "head", (blocks,), in_hbm(node_latents), hbm=(0,), scratch=[vmem((TOP, width), BF16), dma(())],
    )
    lat = lax.all_to_all(heads, GROUP_AXES, 0, 0, axis_index_groups=[order(group, FIRST)])
    send, recv = ids(fine_senders), ids(fine_receivers)
    nodes, cedges, w_ends, w_out, send, recv, to_even, to_odd, gather, picks, coarse_part = call(
        load_kernel,
        "load",
        (
            like(node_latents),
            like(coarse_edges),
            shape((2 * width, width), BF16),
            like(w_edge_out),
            like(send),
            like(recv),
            shape((halo, width), BF16),
            shape((halo, width), BF16),
            shape((2 * cedge_count, coarse_count), BF16),
            shape((coarse_count, cedge_count), BF16),
            shape((cedge_count, width), F32),
        ),
        in_hbm(
            node_latents, halo_lists, coarse_edges, w_edge_in, ids(coarse_senders), ids(coarse_receivers), w_edge_out,
            send, recv,
        )
        + [heads],
        hbm=range(10),
        scratch=[
            vmem(halo_lists.shape, jnp.int32), vmem((width, width), BF16), vmem((width, width), BF16),
            vmem((1, cedge_count), jnp.int32), vmem((1, cedge_count), jnp.int32), dma((10,)),
        ],
        flops=edge_count * square,
    )
    from_even, from_odd = pair(to_even, 0), pair(to_odd, 1)
    new_coarse, sums = call(
        coarse_kernel, "coarse", (like(coarse_edges), blocks),
        [lat, cedges, coarse_part, gather, picks, w_ends, w_out],
    )
    got = lax.all_to_all(sums, GROUP_AXES, 0, 0, axis_index_groups=[order(group, SECOND)])
    new_edges, new_coarse, rest, agg, node_part, wn_agg, wn_out = call(
        fine_kernel,
        "fine",
        (
            like(edge_latents),
            like(coarse_edges),
            like(node_latents),
            shape((TOP, width), F32),
            shape((TOP, width), F32),
            shape((width, width), BF16),
            like(w_node_out),
        ),
        [from_even, nodes, from_odd, w_ends, w_out, send, recv, new_coarse]
        + in_hbm(edge_latents, w_edge_in, w_node_in, w_node_out)
        + [sums],
        hbm=range(8, 13),
        out_specs=[ANY] * 2 + [VMEM] * 5,
        scratch=[
            vmem(edge_latents.shape, BF16), vmem((width, width), BF16), vmem((width, width), BF16),
            vmem((width, width), BF16), vmem(edge_latents.shape, BF16), dma((5,)), dma((edge_count // STEP + 1,)),
        ],
        flops=64 * edge_count * square,
    )
    (new_nodes,) = call(
        top_kernel, "top", (like(node_latents),), [got, agg, node_part, nodes, wn_agg, wn_out, rest], out_specs=[ANY],
        scratch=[vmem((TOP, width), BF16), dma((2,))],
    )
    return (new_nodes, new_edges, new_coarse)


def solution(mesh):
    rows = P(("parts", "patch", "sub"), None)
    ids = P(("parts", "patch", "sub"))
    in_specs = (
        rows, rows, rows, P(), P(), P(), P(), ids, ids, P(("parts", "patch", "sub"), None, None), ids, ids,
    )
    return jax.shard_map(body, mesh=mesh, in_specs=in_specs, out_specs=(rows, rows, rows), check_vma=False)
```

```python
import jax
import jax.numpy as jnp
from jax import lax
from jax.experimental import pallas as pl
from jax.experimental.pallas import tpu as pltpu
from jax.sharding import PartitionSpec as P

CO_DEV = 4
GROUP_AXES = ("patch", "sub")
TOP = 16
STEP = 512
MIB = 1 << 20
FIRST, SECOND = 2, 2
ANY = pl.BlockSpec(memory_space=pl.ANY)
VMEM = pl.BlockSpec(memory_space=pltpu.VMEM)
BF16, F32 = jnp.bfloat16, jnp.float32


def order(group, quarter):
    return [(i + group * quarter // 4) % group for i in range(group)]


def pair(value, first):
    devices = lax.axis_size(GROUP_AXES)
    pairs = [(i, (i + 1) % devices) for i in range(first, devices, 2)]
    return lax.ppermute(value, GROUP_AXES, pairs + [(b, a) for a, b in pairs])


def dot(a, b):
    return jnp.dot(a, b, preferred_element_type=F32)


def dot_t(a, b):
    return lax.dot_general(a, b, (((0,), (0,)), ((), ())), preferred_element_type=F32)


def onehot_t(rows, ids):
    at = lax.broadcasted_iota(jnp.int32, (rows, ids.shape[1]), 0)
    return jnp.where(at == ids, 1.0, 0.0).astype(BF16)


def silu(v):
    half = 0.5 * v
    return half + half * jnp.tanh(half)


def norm_parts(values):
    mean = jnp.mean(values, axis=-1, keepdims=True)
    centred = values - mean
    return centred, lax.rsqrt(jnp.mean(centred * centred, axis=-1, keepdims=True) + 1e-05)


def head_kernel(nodes_hbm, heads_ref, rows_ref, sem):
    copy = pltpu.make_async_copy(nodes_hbm.at[pl.ds(0, TOP)], rows_ref, sem)
    copy.start()
    copy.wait()
    head = rows_ref[0:CO_DEV, :]
    for at in range(heads_ref.shape[0]):
        heads_ref[at] = head


def start_copies(sources, targets, sems):
    copies = [pltpu.make_async_copy(a, b, sems.at[i]) for i, (a, b) in enumerate(zip(sources, targets))]
    for copy in copies:
        copy.start()
    return copies


def load_kernel(
    nodes_hbm, lists_hbm, cedges_hbm, w_in_hbm, csend_hbm, crecv_hbm, w_out_hbm, send_hbm, recv_hbm, after,
    nodes_ref, cedges_ref, w_ends_ref, w_out_ref, send_ref, recv_ref,
    even_ref, odd_ref, gather_ref, picks_ref, part_ref,
    lists_ref, w_self_ref, csend_ref, crecv_ref, sems,
):
    width = nodes_ref.shape[1]
    copies = start_copies(
        [
            nodes_hbm, lists_hbm, cedges_hbm, w_in_hbm.at[pl.ds(0, width)], csend_hbm, crecv_hbm,
            w_in_hbm.at[pl.ds(width, 2 * width)], w_out_hbm, send_hbm, recv_hbm,
        ],
        [
            nodes_ref, lists_ref, cedges_ref, w_self_ref, csend_ref, crecv_ref, w_ends_ref, w_out_ref, send_ref, recv_ref,
        ],
        sems,
    )
    for copy in copies[:2]:
        copy.wait()
    nodes = nodes_ref[...]
    count = nodes.shape[0]
    lists = lists_ref[0]
    me = lax.axis_index(GROUP_AXES)
    odd = me % 2
    first = lists[0:1, :] * (1 - odd) + lists[1:2, :] * odd
    second = lists[1:2, :] * (1 - odd) + lists[0:1, :] * odd
    even_ref[...] = dot_t(onehot_t(count, first), nodes).astype(BF16)
    odd_ref[...] = dot_t(onehot_t(count, second), nodes).astype(BF16)
    for copy in copies[2:6]:
        copy.wait()
    part_ref[...] = dot(cedges_ref[...], w_self_ref[...])
    rows, ids = picks_ref.shape
    at = lax.broadcasted_iota(jnp.int32, (rows, ids), 0)
    node = (at + CO_DEV * order(rows // CO_DEV, FIRST)[0]) % rows
    send = jnp.where(node == csend_ref[...], 1.0, 0.0).astype(BF16)
    recv = jnp.where(node == crecv_ref[...], 1.0, 0.0).astype(BF16)
    picks_ref[...] = onehot_t(rows, crecv_ref[...])
    across = lax.broadcasted_iota(jnp.int32, (rows, rows), 0) == lax.broadcasted_iota(jnp.int32, (rows, rows), 1)
    eye = jnp.where(across, 1.0, 0.0).astype(BF16)
    gather_ref[0:ids, :] = dot_t(send, eye).astype(BF16)
    gather_ref[ids:, :] = dot_t(recv, eye).astype(BF16)
    for copy in copies[6:]:
        copy.wait()


def coarse_kernel(
    lat_ref, edges_ref, part_ref, gather_ref, picks_ref, w_ends_ref, w_out_ref, new_ref, sums_ref
):
    count, width = edges_ref.shape
    blocks = lat_ref.shape[0]
    lat = jnp.concatenate([lat_ref[at].astype(F32) for at in range(blocks)], axis=0).astype(BF16)
    ends = dot(gather_ref[...], lat).astype(BF16)
    ends = jnp.concatenate([ends[0:count], ends[count:]], axis=1)
    hidden = silu(part_ref[...] + dot(ends, w_ends_ref[...])).astype(BF16)
    centred, scale = norm_parts(dot(hidden, w_out_ref[...]))
    new = (edges_ref[...].astype(F32) + centred * scale).astype(BF16)
    new_ref[...] = new
    sums = dot(picks_ref[...], new).astype(BF16)
    for at, owner in enumerate(order(blocks, SECOND)):
        sums_ref[at] = sums[owner * CO_DEV : (owner + 1) * CO_DEV, :]


def fine_kernel(
    even_ref, nodes_ref, odd_ref, w_ends_ref, w_out_ref, send_ref, recv_ref, coarse_ref,
    edges_hbm, w_in_hbm, wn_in_hbm, wn_out_hbm, after,
    new_hbm, coarse_hbm, out_ref, agg_ref, npart_ref, wn_agg_ref, wn_out_ref,
    edges_ref, w_self_ref, wn_self_ref, new_ref, sems, out_sems,
):
    nodes = nodes_ref[...]
    count, width = nodes.shape
    copies = start_copies([edges_hbm, w_in_hbm.at[pl.ds(0, width)]], [edges_ref, w_self_ref], sems.at[0])
    outs = [pltpu.make_async_copy(coarse_ref, coarse_hbm, out_sems.at[0])]
    outs[0].start()
    odd = (lax.axis_index(GROUP_AXES) % 2).astype(F32)
    met, other = even_ref[...].astype(F32), odd_ref[...].astype(F32)
    prev = (met * odd + other * (1.0 - odd)).astype(BF16)
    following = (other * odd + met * (1.0 - odd)).astype(BF16)
    extended = jnp.concatenate([prev, nodes, following], axis=0)
    ones = jnp.ones((count, 128), BF16)
    total = jnp.zeros((count, width), F32)
    for at in range(0, edges_ref.shape[0], STEP):
        rows = pl.ds(at, STEP)
        picks = onehot_t(count, recv_ref[:, rows])
        senders = dot_t(onehot_t(extended.shape[0], send_ref[:, rows]), extended).astype(BF16)
        receivers = dot_t(picks, nodes).astype(BF16)
        valid = dot_t(picks, ones)[:, 0:1]
        pre = dot(jnp.concatenate([senders, receivers], axis=1), w_ends_ref[...])
        if at == 0:
            for copy in copies:
                copy.wait()
            copies = start_copies(
                [wn_in_hbm.at[pl.ds(0, width)], wn_in_hbm.at[pl.ds(width, width)], wn_out_hbm],
                [wn_self_ref, wn_agg_ref, wn_out_ref],
                sems.at[1],
            )
        edges = edges_ref[rows, :]
        pre = pre + dot(edges, w_self_ref[...])
        hidden = silu(pre).astype(BF16)
        centred, scale = norm_parts(dot(hidden, w_out_ref[...]))
        new = (edges.astype(F32) + centred * (scale * valid)).astype(BF16)
        new_ref[rows, :] = new
        copy = pltpu.make_async_copy(new_ref.at[rows], new_hbm.at[rows], out_sems.at[at // STEP + 1])
        copy.start()
        outs.append(copy)
        total = total + dot(picks, new)
    agg_ref[...] = total[0:TOP]
    for copy in copies:
        copy.wait()
    pre = dot(nodes, wn_self_ref[...])
    npart_ref[...] = pre[0:TOP]
    pre = pre + dot(total.astype(BF16), wn_agg_ref[...])
    hidden = silu(pre).astype(BF16)
    centred, scale = norm_parts(dot(hidden, wn_out_ref[...]))
    out_ref[...] = (nodes.astype(F32) + centred * scale).astype(BF16)
    for copy in outs:
        copy.wait()


def top_kernel(got_ref, agg_ref, part_ref, nodes_ref, wn_agg_ref, wn_out_ref, rest_ref, out_hbm, top_ref, sems):
    count, width = rest_ref.shape
    below = pl.ds(TOP, count - TOP)
    rest = pltpu.make_async_copy(rest_ref.at[below], out_hbm.at[below], sems.at[0])
    rest.start()
    terms = [got_ref[at].astype(F32) for at in range(got_ref.shape[0])]
    while len(terms) > 1:
        half = len(terms) // 2
        terms = [a + b for a, b in zip(terms[:half], terms[half:])] + terms[2 * half :]
    sums = jnp.concatenate([terms[0], jnp.zeros((TOP - CO_DEV, width), F32)], axis=0)
    agg = (agg_ref[...] + sums).astype(BF16)
    hidden = silu(part_ref[...] + dot(agg, wn_agg_ref[...])).astype(BF16)
    centred, scale = norm_parts(dot(hidden, wn_out_ref[...]))
    top_ref[...] = (nodes_ref[0:TOP, :].astype(F32) + centred * scale).astype(BF16)
    top = pltpu.make_async_copy(top_ref, out_hbm.at[pl.ds(0, TOP)], sems.at[1])
    top.start()
    rest.wait()
    top.wait()


def in_hbm(*arrays):
    return [pltpu.with_memory_space_constraint(a, pltpu.HBM) for a in arrays]


def cost(flops, moved=0):
    return pl.CostEstimate(flops=flops, bytes_accessed=moved, transcendentals=0)


def call(kernel, name, outs, ins, out_specs=None, scratch=(), hbm=(), flops=0, **more):
    return pl.pallas_call(
        kernel,
        out_shape=outs,
        in_specs=[ANY if i in hbm else VMEM for i in range(len(ins))],
        out_specs=[VMEM] * len(outs) if out_specs is None else out_specs,
        scratch_shapes=scratch,
        compiler_params=pltpu.CompilerParams(vmem_limit_bytes=16 * MIB),
        cost_estimate=cost(flops),
        name=name,
        **more,
    )(*ins)


def body(
    node_latents,
    edge_latents,
    coarse_edges,
    w_edge_in,
    w_edge_out,
    w_node_in,
    w_node_out,
    fine_senders,
    fine_receivers,
    halo_lists,
    coarse_senders,
    coarse_receivers,
):
    count, width = node_latents.shape
    edge_count = edge_latents.shape[0]
    cedge_count = coarse_edges.shape[0]
    halo = halo_lists.shape[2]
    group = lax.axis_size(GROUP_AXES)
    coarse_count = group * CO_DEV
    shape = jax.ShapeDtypeStruct
    like = lambda a: shape(a.shape, a.dtype)
    vmem = pltpu.VMEM
    dma = pltpu.SemaphoreType.DMA
    square = 2 * width * width
    blocks = pltpu.VMEM((group, CO_DEV, width), BF16)
    ids = lambda a: a[None, :]

    (heads,) = call(
        head_kernel, "head", (blocks,), in_hbm(node_latents), hbm=(0,), scratch=[vmem((TOP, width), BF16), dma(())],
    )
    lat = lax.all_to_all(heads, GROUP_AXES, 0, 0, axis_index_groups=[order(group, FIRST)])
    send, recv = ids(fine_senders), ids(fine_receivers)
    nodes, cedges, w_ends, w_out, send, recv, to_even, to_odd, gather, picks, coarse_part = call(
        load_kernel,
        "load",
        (
            like(node_latents),
            like(coarse_edges),
            shape((2 * width, width), BF16),
            like(w_edge_out),
            like(send),
            like(recv),
            shape((halo, width), BF16),
            shape((halo, width), BF16),
            shape((2 * cedge_count, coarse_count), BF16),
            shape((coarse_count, cedge_count), BF16),
            shape((cedge_count, width), F32),
        ),
        in_hbm(
            node_latents, halo_lists, coarse_edges, w_edge_in, ids(coarse_senders), ids(coarse_receivers), w_edge_out,
            send, recv,
        )
        + [heads],
        hbm=range(10),
        scratch=[
            vmem(halo_lists.shape, jnp.int32), vmem((width, width), BF16),
            vmem((1, cedge_count), jnp.int32), vmem((1, cedge_count), jnp.int32), dma((10,)),
        ],
        flops=edge_count * square,
    )
    from_even, from_odd = pair(to_even, 0), pair(to_odd, 1)
    new_coarse, sums = call(
        coarse_kernel, "coarse", (like(coarse_edges), blocks),
        [lat, cedges, coarse_part, gather, picks, w_ends, w_out],
    )
    got = lax.all_to_all(sums, GROUP_AXES, 0, 0, axis_index_groups=[order(group, SECOND)])
    new_edges, new_coarse, rest, agg, node_part, wn_agg, wn_out = call(
        fine_kernel,
        "fine",
        (
            like(edge_latents),
            like(coarse_edges),
            like(node_latents),
            shape((TOP, width), F32),
            shape((TOP, width), F32),
            shape((width, width), BF16),
            like(w_node_out),
        ),
        [from_even, nodes, from_odd, w_ends, w_out, send, recv, new_coarse]
        + in_hbm(edge_latents, w_edge_in, w_node_in, w_node_out)
        + [sums],
        hbm=range(8, 13),
        out_specs=[ANY] * 2 + [VMEM] * 5,
        scratch=[
            vmem(edge_latents.shape, BF16), vmem((width, width), BF16), vmem((width, width), BF16),
            vmem(edge_latents.shape, BF16), dma((2, 3)), dma((edge_count // STEP + 1,)),
        ],
        flops=64 * edge_count * square,
    )
    (new_nodes,) = call(
        top_kernel, "top", (like(node_latents),), [got, agg, node_part, nodes, wn_agg, wn_out, rest], out_specs=[ANY],
        scratch=[vmem((TOP, width), BF16), dma((2,))],
    )
    return (new_nodes, new_edges, new_coarse)


def solution(mesh):
    rows = P(("parts", "patch", "sub"), None)
    ids = P(("parts", "patch", "sub"))
    in_specs = (
        rows, rows, rows, P(), P(), P(), P(), ids, ids, P(("parts", "patch", "sub"), None, None), ids, ids,
    )
    return jax.shard_map(body, mesh=mesh, in_specs=in_specs, out_specs=(rows, rows, rows), check_vma=False)
```

```python
import jax
import jax.numpy as jnp
from jax import lax
from jax.experimental import pallas as pl
from jax.experimental.pallas import tpu as pltpu
from jax.sharding import PartitionSpec as P

CO_DEV = 4
GROUP_AXES = ("patch", "sub")
TOP = 16
STEP = 512
MIB = 1 << 20
ANY = pl.BlockSpec(memory_space=pl.ANY)
VMEM = pl.BlockSpec(memory_space=pltpu.VMEM)
BF16, F32 = jnp.bfloat16, jnp.float32


def order(group, sub):
    patch = group // sub
    return [(i + patch // 2) % patch * sub + j for j in range(sub) for i in range(patch)]


def pair(value, first):
    devices = lax.axis_size(GROUP_AXES)
    pairs = [(i, (i + 1) % devices) for i in range(first, devices, 2)]
    return lax.ppermute(value, GROUP_AXES, pairs + [(b, a) for a, b in pairs])


def dot(a, b):
    return jnp.dot(a, b, preferred_element_type=F32)


def dot_t(a, b):
    return lax.dot_general(a, b, (((0,), (0,)), ((), ())), preferred_element_type=F32)


def onehot_t(rows, ids):
    at = lax.broadcasted_iota(jnp.int32, (rows, ids.shape[1]), 0)
    return jnp.where(at == ids, 1.0, 0.0).astype(BF16)


def silu(v):
    half = 0.5 * v
    return half + half * jnp.tanh(half)


def norm_parts(values):
    mean = jnp.mean(values, axis=-1, keepdims=True)
    centred = values - mean
    return centred, lax.rsqrt(jnp.mean(centred * centred, axis=-1, keepdims=True) + 1e-05)


def head_kernel(nodes_hbm, heads_ref, rows_ref, sem):
    copy = pltpu.make_async_copy(nodes_hbm.at[pl.ds(0, TOP)], rows_ref, sem)
    copy.start()
    copy.wait()
    head = rows_ref[0:CO_DEV, :]
    for at in range(heads_ref.shape[0]):
        heads_ref[at] = head


def start_copies(sources, targets, sems):
    copies = [pltpu.make_async_copy(a, b, sems.at[i]) for i, (a, b) in enumerate(zip(sources, targets))]
    for copy in copies:
        copy.start()
    return copies


def load_kernel(
    nodes_hbm, lists_hbm, cedges_hbm, w_in_hbm, csend_hbm, crecv_hbm, w_out_hbm, send_hbm, recv_hbm, after,
    nodes_ref, cedges_ref, w_ends_ref, w_out_ref, send_ref, recv_ref,
    even_ref, odd_ref, gather_ref, picks_ref, part_ref,
    lists_ref, w_self_ref, csend_ref, crecv_ref, sems,
):
    width = nodes_ref.shape[1]
    copies = start_copies(
        [
            nodes_hbm, lists_hbm, cedges_hbm, w_in_hbm.at[pl.ds(0, width)], csend_hbm, crecv_hbm,
            w_in_hbm.at[pl.ds(width, 2 * width)], w_out_hbm, send_hbm, recv_hbm,
        ],
        [
            nodes_ref, lists_ref, cedges_ref, w_self_ref, csend_ref, crecv_ref, w_ends_ref, w_out_ref, send_ref, recv_ref,
        ],
        sems,
    )
    for copy in copies[:2]:
        copy.wait()
    nodes = nodes_ref[...]
    count = nodes.shape[0]
    lists = lists_ref[0]
    me = lax.axis_index(GROUP_AXES)
    odd = me % 2
    first = lists[0:1, :] * (1 - odd) + lists[1:2, :] * odd
    second = lists[1:2, :] * (1 - odd) + lists[0:1, :] * odd
    even_ref[...] = dot_t(onehot_t(count, first), nodes).astype(BF16)
    odd_ref[...] = dot_t(onehot_t(count, second), nodes).astype(BF16)
    for copy in copies[2:6]:
        copy.wait()
    part_ref[...] = dot(cedges_ref[...], w_self_ref[...])
    rows, ids = picks_ref.shape
    at = lax.broadcasted_iota(jnp.int32, (rows, ids), 0)
    sub, patch = lax.axis_size("sub"), lax.axis_size("patch")
    block = at // CO_DEV
    device = (block % patch + patch // 2) % patch * sub + block // patch
    node = device * CO_DEV + at % CO_DEV
    send = jnp.where(node == csend_ref[...], 1.0, 0.0).astype(BF16)
    recv = jnp.where(node == crecv_ref[...], 1.0, 0.0).astype(BF16)
    picks_ref[...] = onehot_t(rows, crecv_ref[...])
    across = lax.broadcasted_iota(jnp.int32, (rows, rows), 0) == lax.broadcasted_iota(jnp.int32, (rows, rows), 1)
    eye = jnp.where(across, 1.0, 0.0).astype(BF16)
    gather_ref[0:ids, :] = dot_t(send, eye).astype(BF16)
    gather_ref[ids:, :] = dot_t(recv, eye).astype(BF16)
    for copy in copies[6:]:
        copy.wait()


def coarse_kernel(
    lat_ref, edges_ref, part_ref, gather_ref, picks_ref, w_ends_ref, w_out_ref, new_ref, sums_ref
):
    count, width = edges_ref.shape
    blocks = lat_ref.shape[0]
    lat = jnp.concatenate([lat_ref[at].astype(F32) for at in range(blocks)], axis=0).astype(BF16)
    ends = dot(gather_ref[...], lat).astype(BF16)
    ends = jnp.concatenate([ends[0:count], ends[count:]], axis=1)
    hidden = silu(part_ref[...] + dot(ends, w_ends_ref[...])).astype(BF16)
    centred, scale = norm_parts(dot(hidden, w_out_ref[...]))
    new = (edges_ref[...].astype(F32) + centred * scale).astype(BF16)
    new_ref[...] = new
    sums = dot(picks_ref[...], new).astype(BF16)
    for at, owner in enumerate(order(blocks, lax.axis_size("sub"))):
        sums_ref[at] = sums[owner * CO_DEV : (owner + 1) * CO_DEV, :]


def fine_kernel(
    even_ref, nodes_ref, odd_ref, w_ends_ref, w_out_ref, send_ref, recv_ref, coarse_ref,
    edges_hbm, w_in_hbm, wn_in_hbm, wn_out_hbm, after,
    new_hbm, coarse_hbm, out_ref, agg_ref, npart_ref, wn_agg_ref, wn_out_ref,
    edges_ref, w_self_ref, wn_self_ref, new_ref, sems, out_sems,
):
    nodes = nodes_ref[...]
    count, width = nodes.shape
    copies = start_copies(
        [
            edges_hbm, w_in_hbm.at[pl.ds(0, width)],
            wn_in_hbm.at[pl.ds(0, width)], wn_in_hbm.at[pl.ds(width, width)], wn_out_hbm,
        ],
        [edges_ref, w_self_ref, wn_self_ref, wn_agg_ref, wn_out_ref],
        sems,
    )
    outs = [pltpu.make_async_copy(coarse_ref, coarse_hbm, out_sems.at[0])]
    outs[0].start()
    odd = (lax.axis_index(GROUP_AXES) % 2).astype(F32)
    met, other = even_ref[...].astype(F32), odd_ref[...].astype(F32)
    prev = (met * odd + other * (1.0 - odd)).astype(BF16)
    following = (other * odd + met * (1.0 - odd)).astype(BF16)
    extended = jnp.concatenate([prev, nodes, following], axis=0)
    ones = jnp.ones((count, 128), BF16)
    total = jnp.zeros((count, width), F32)
    for at in range(0, edges_ref.shape[0], STEP):
        rows = pl.ds(at, STEP)
        picks = onehot_t(count, recv_ref[:, rows])
        senders = dot_t(onehot_t(extended.shape[0], send_ref[:, rows]), extended).astype(BF16)
        receivers = dot_t(picks, nodes).astype(BF16)
        valid = dot_t(picks, ones)[:, 0:1]
        pre = dot(jnp.concatenate([senders, receivers], axis=1), w_ends_ref[...])
        if at == 0:
            for copy in copies[:2]:
                copy.wait()
        edges = edges_ref[rows, :]
        pre = pre + dot(edges, w_self_ref[...])
        hidden = silu(pre).astype(BF16)
        centred, scale = norm_parts(dot(hidden, w_out_ref[...]))
        new = (edges.astype(F32) + centred * (scale * valid)).astype(BF16)
        new_ref[rows, :] = new
        copy = pltpu.make_async_copy(new_ref.at[rows], new_hbm.at[rows], out_sems.at[at // STEP + 1])
        copy.start()
        outs.append(copy)
        total = total + dot(picks, new)
    agg_ref[...] = total[0:TOP]
    for copy in copies[2:]:
        copy.wait()
    pre = dot(nodes, wn_self_ref[...])
    npart_ref[...] = pre[0:TOP]
    pre = pre + dot(total.astype(BF16), wn_agg_ref[...])
    hidden = silu(pre).astype(BF16)
    centred, scale = norm_parts(dot(hidden, wn_out_ref[...]))
    out_ref[...] = (nodes.astype(F32) + centred * scale).astype(BF16)
    for copy in outs:
        copy.wait()


def top_kernel(got_ref, agg_ref, part_ref, nodes_ref, wn_agg_ref, wn_out_ref, rest_ref, out_hbm, top_ref, sems):
    count, width = rest_ref.shape
    below = pl.ds(TOP, count - TOP)
    rest = pltpu.make_async_copy(rest_ref.at[below], out_hbm.at[below], sems.at[0])
    rest.start()
    terms = [got_ref[at].astype(F32) for at in range(got_ref.shape[0])]
    while len(terms) > 1:
        half = len(terms) // 2
        terms = [a + b for a, b in zip(terms[:half], terms[half:])] + terms[2 * half :]
    sums = jnp.concatenate([terms[0], jnp.zeros((TOP - CO_DEV, width), F32)], axis=0)
    agg = (agg_ref[...] + sums).astype(BF16)
    hidden = silu(part_ref[...] + dot(agg, wn_agg_ref[...])).astype(BF16)
    centred, scale = norm_parts(dot(hidden, wn_out_ref[...]))
    top_ref[...] = (nodes_ref[0:TOP, :].astype(F32) + centred * scale).astype(BF16)
    top = pltpu.make_async_copy(top_ref, out_hbm.at[pl.ds(0, TOP)], sems.at[1])
    top.start()
    rest.wait()
    top.wait()


def in_hbm(*arrays):
    return [pltpu.with_memory_space_constraint(a, pltpu.HBM) for a in arrays]


def cost(flops, moved=0):
    return pl.CostEstimate(flops=flops, bytes_accessed=moved, transcendentals=0)


def call(kernel, name, outs, ins, out_specs=None, scratch=(), hbm=(), flops=0, **more):
    return pl.pallas_call(
        kernel,
        out_shape=outs,
        in_specs=[ANY if i in hbm else VMEM for i in range(len(ins))],
        out_specs=[VMEM] * len(outs) if out_specs is None else out_specs,
        scratch_shapes=scratch,
        compiler_params=pltpu.CompilerParams(vmem_limit_bytes=16 * MIB),
        cost_estimate=cost(flops),
        name=name,
        **more,
    )(*ins)


def body(
    node_latents,
    edge_latents,
    coarse_edges,
    w_edge_in,
    w_edge_out,
    w_node_in,
    w_node_out,
    fine_senders,
    fine_receivers,
    halo_lists,
    coarse_senders,
    coarse_receivers,
):
    count, width = node_latents.shape
    edge_count = edge_latents.shape[0]
    cedge_count = coarse_edges.shape[0]
    halo = halo_lists.shape[2]
    group = lax.axis_size(GROUP_AXES)
    coarse_count = group * CO_DEV
    sub = lax.axis_size("sub")
    shape = jax.ShapeDtypeStruct
    like = lambda a: shape(a.shape, a.dtype)
    vmem = pltpu.VMEM
    dma = pltpu.SemaphoreType.DMA
    square = 2 * width * width
    blocks = pltpu.VMEM((group, CO_DEV, width), BF16)
    ids = lambda a: a[None, :]

    (heads,) = call(
        head_kernel, "head", (blocks,), in_hbm(node_latents), hbm=(0,), scratch=[vmem((TOP, width), BF16), dma(())],
    )
    lat = lax.all_to_all(heads, GROUP_AXES, 0, 0, axis_index_groups=[order(group, sub)])
    send, recv = ids(fine_senders), ids(fine_receivers)
    nodes, cedges, w_ends, w_out, send, recv, to_even, to_odd, gather, picks, coarse_part = call(
        load_kernel,
        "load",
        (
            like(node_latents),
            like(coarse_edges),
            shape((2 * width, width), BF16),
            like(w_edge_out),
            like(send),
            like(recv),
            shape((halo, width), BF16),
            shape((halo, width), BF16),
            shape((2 * cedge_count, coarse_count), BF16),
            shape((coarse_count, cedge_count), BF16),
            shape((cedge_count, width), F32),
        ),
        in_hbm(
            node_latents, halo_lists, coarse_edges, w_edge_in, ids(coarse_senders), ids(coarse_receivers), w_edge_out,
            send, recv,
        )
        + [heads],
        hbm=range(10),
        scratch=[
            vmem(halo_lists.shape, jnp.int32), vmem((width, width), BF16),
            vmem((1, cedge_count), jnp.int32), vmem((1, cedge_count), jnp.int32), dma((10,)),
        ],
        flops=edge_count * square,
    )
    from_even, from_odd = pair(to_even, 0), pair(to_odd, 1)
    new_coarse, sums = call(
        coarse_kernel, "coarse", (like(coarse_edges), blocks),
        [lat, cedges, coarse_part, gather, picks, w_ends, w_out],
    )
    got = lax.all_to_all(sums, GROUP_AXES, 0, 0, axis_index_groups=[order(group, sub)])
    new_edges, new_coarse, rest, agg, node_part, wn_agg, wn_out = call(
        fine_kernel,
        "fine",
        (
            like(edge_latents),
            like(coarse_edges),
            like(node_latents),
            shape((TOP, width), F32),
            shape((TOP, width), F32),
            shape((width, width), BF16),
            like(w_node_out),
        ),
        [from_even, nodes, from_odd, w_ends, w_out, send, recv, new_coarse]
        + in_hbm(edge_latents, w_edge_in, w_node_in, w_node_out)
        + [sums],
        hbm=range(8, 13),
        out_specs=[ANY] * 2 + [VMEM] * 5,
        scratch=[
            vmem(edge_latents.shape, BF16), vmem((width, width), BF16), vmem((width, width), BF16),
            vmem(edge_latents.shape, BF16), dma((5,)), dma((edge_count // STEP + 1,)),
        ],
        flops=64 * edge_count * square,
    )
    (new_nodes,) = call(
        top_kernel, "top", (like(node_latents),), [got, agg, node_part, nodes, wn_agg, wn_out, rest], out_specs=[ANY],
        scratch=[vmem((TOP, width), BF16), dma((2,))],
    )
    return (new_nodes, new_edges, new_coarse)


def solution(mesh):
    rows = P(("parts", "patch", "sub"), None)
    ids = P(("parts", "patch", "sub"))
    in_specs = (
        rows, rows, rows, P(), P(), P(), P(), ids, ids, P(("parts", "patch", "sub"), None, None), ids, ids,
    )
    return jax.shard_map(body, mesh=mesh, in_specs=in_specs, out_specs=(rows, rows, rows), check_vma=False)
```

```python
import jax
import jax.numpy as jnp
from jax import lax
from jax.experimental import pallas as pl
from jax.experimental.pallas import tpu as pltpu
from jax.sharding import PartitionSpec as P

CO_DEV = 4
GROUP_AXES = ("patch", "sub")
TOP = 16
MIB = 1 << 20
ANY = pl.BlockSpec(memory_space=pl.ANY)
VMEM = pl.BlockSpec(memory_space=pltpu.VMEM)
BF16, F32 = jnp.bfloat16, jnp.float32


def order(group, sub):
    patch = group // sub
    return [(i + patch // 2) % patch * sub + j for j in range(sub) for i in range(patch)]


def pair(value, first):
    devices = lax.axis_size(GROUP_AXES)
    pairs = [(i, (i + 1) % devices) for i in range(first, devices, 2)]
    return lax.ppermute(value, GROUP_AXES, pairs + [(b, a) for a, b in pairs])


def dot(a, b):
    return jnp.dot(a, b, preferred_element_type=F32)


def dot_t(a, b):
    return lax.dot_general(a, b, (((0,), (0,)), ((), ())), preferred_element_type=F32)


def onehot_t(rows, ids):
    at = lax.broadcasted_iota(jnp.int32, (rows, ids.shape[1]), 0)
    return jnp.where(at == ids, 1.0, 0.0).astype(BF16)


def silu(v):
    half = 0.5 * v
    return half + half * jnp.tanh(half)


def norm_parts(values):
    mean = jnp.mean(values, axis=-1, keepdims=True)
    centred = values - mean
    return centred, lax.rsqrt(jnp.mean(centred * centred, axis=-1, keepdims=True) + 1e-05)


def head_kernel(nodes_hbm, heads_ref, rows_ref, sem):
    copy = pltpu.make_async_copy(nodes_hbm.at[pl.ds(0, TOP)], rows_ref, sem)
    copy.start()
    copy.wait()
    head = rows_ref[0:CO_DEV, :]
    for at in range(heads_ref.shape[0]):
        heads_ref[at] = head


def start_copies(sources, targets, sems):
    copies = [pltpu.make_async_copy(a, b, sems.at[i]) for i, (a, b) in enumerate(zip(sources, targets))]
    for copy in copies:
        copy.start()
    return copies


def load_kernel(
    nodes_hbm, lists_hbm, cedges_hbm, w_in_hbm, csend_hbm, crecv_hbm, w_out_hbm, send_hbm, recv_hbm, after,
    nodes_ref, cedges_ref, w_ends_ref, w_out_ref, send_ref, recv_ref,
    even_ref, odd_ref, gather_ref, picks_ref, part_ref,
    lists_ref, w_self_ref, csend_ref, crecv_ref, sems,
):
    width = nodes_ref.shape[1]
    copies = start_copies(
        [
            nodes_hbm, lists_hbm, cedges_hbm, w_in_hbm.at[pl.ds(0, width)], csend_hbm, crecv_hbm,
            w_in_hbm.at[pl.ds(width, 2 * width)], w_out_hbm, send_hbm, recv_hbm,
        ],
        [
            nodes_ref, lists_ref, cedges_ref, w_self_ref, csend_ref, crecv_ref, w_ends_ref, w_out_ref, send_ref, recv_ref,
        ],
        sems,
    )
    for copy in copies[:2]:
        copy.wait()
    nodes = nodes_ref[...]
    count = nodes.shape[0]
    lists = lists_ref[0]
    me = lax.axis_index(GROUP_AXES)
    odd = me % 2
    first = lists[0:1, :] * (1 - odd) + lists[1:2, :] * odd
    second = lists[1:2, :] * (1 - odd) + lists[0:1, :] * odd
    even_ref[...] = dot_t(onehot_t(count, first), nodes).astype(BF16)
    odd_ref[...] = dot_t(onehot_t(count, second), nodes).astype(BF16)
    for copy in copies[2:6]:
        copy.wait()
    part_ref[...] = dot(cedges_ref[...], w_self_ref[...])
    rows, ids = picks_ref.shape
    at = lax.broadcasted_iota(jnp.int32, (rows, ids), 0)
    sub, patch = lax.axis_size("sub"), lax.axis_size("patch")
    block = at // CO_DEV
    device = (block % patch + patch // 2) % patch * sub + block // patch
    node = device * CO_DEV + at % CO_DEV
    send = jnp.where(node == csend_ref[...], 1.0, 0.0).astype(BF16)
    recv = jnp.where(node == crecv_ref[...], 1.0, 0.0).astype(BF16)
    picks_ref[...] = onehot_t(rows, crecv_ref[...])
    across = lax.broadcasted_iota(jnp.int32, (rows, rows), 0) == lax.broadcasted_iota(jnp.int32, (rows, rows), 1)
    eye = jnp.where(across, 1.0, 0.0).astype(BF16)
    gather_ref[0:ids, :] = dot_t(send, eye).astype(BF16)
    gather_ref[ids:, :] = dot_t(recv, eye).astype(BF16)
    for copy in copies[6:]:
        copy.wait()


def coarse_kernel(
    lat_ref, edges_ref, part_ref, gather_ref, picks_ref, w_ends_ref, w_out_ref, new_ref, sums_ref
):
    count, width = edges_ref.shape
    blocks = lat_ref.shape[0]
    lat = jnp.concatenate([lat_ref[at].astype(F32) for at in range(blocks)], axis=0).astype(BF16)
    ends = dot(gather_ref[...], lat).astype(BF16)
    ends = jnp.concatenate([ends[0:count], ends[count:]], axis=1)
    hidden = silu(part_ref[...] + dot(ends, w_ends_ref[...])).astype(BF16)
    centred, scale = norm_parts(dot(hidden, w_out_ref[...]))
    new = (edges_ref[...].astype(F32) + centred * scale).astype(BF16)
    new_ref[...] = new
    sums = dot(picks_ref[...], new).astype(BF16)
    for at, owner in enumerate(order(blocks, lax.axis_size("sub"))):
        sums_ref[at] = sums[owner * CO_DEV : (owner + 1) * CO_DEV, :]


def fine_kernel(
    even_ref, nodes_ref, odd_ref, w_ends_ref, w_out_ref, send_ref, recv_ref, coarse_ref,
    edges_hbm, w_in_hbm, wn_in_hbm, wn_out_hbm, after,
    new_hbm, coarse_hbm, out_ref, agg_ref, npart_ref, wn_agg_ref, wn_out_ref,
    edges_ref, w_self_ref, wn_self_ref, new_ref, sems, out_sems,
):
    nodes = nodes_ref[...]
    count, width = nodes.shape
    copies = start_copies(
        [
            edges_hbm, w_in_hbm.at[pl.ds(0, width)],
            wn_in_hbm.at[pl.ds(0, width)], wn_in_hbm.at[pl.ds(width, width)], wn_out_hbm,
        ],
        [edges_ref, w_self_ref, wn_self_ref, wn_agg_ref, wn_out_ref],
        sems,
    )
    outs = [pltpu.make_async_copy(coarse_ref, coarse_hbm, out_sems.at[0])]
    outs[0].start()
    odd = (lax.axis_index(GROUP_AXES) % 2).astype(F32)
    met, other = even_ref[...].astype(F32), odd_ref[...].astype(F32)
    prev = (met * odd + other * (1.0 - odd)).astype(BF16)
    following = (other * odd + met * (1.0 - odd)).astype(BF16)
    extended = jnp.concatenate([prev, nodes, following], axis=0)
    picks = onehot_t(count, recv_ref[...])
    senders = dot_t(onehot_t(extended.shape[0], send_ref[...]), extended).astype(BF16)
    receivers = dot_t(picks, nodes).astype(BF16)
    valid = dot_t(picks, jnp.ones((count, 128), BF16))[:, 0:1]
    pre = dot(jnp.concatenate([senders, receivers], axis=1), w_ends_ref[...])
    for copy in copies[:2]:
        copy.wait()
    edges = edges_ref[...]
    pre = pre + dot(edges, w_self_ref[...])
    hidden = silu(pre).astype(BF16)
    centred, scale = norm_parts(dot(hidden, w_out_ref[...]))
    new = (edges.astype(F32) + centred * (scale * valid)).astype(BF16)
    new_ref[...] = new
    outs.append(pltpu.make_async_copy(new_ref, new_hbm, out_sems.at[1]))
    outs[1].start()
    total = dot(picks, new)
    agg_ref[...] = total[0:TOP]
    for copy in copies[2:]:
        copy.wait()
    pre = dot(nodes, wn_self_ref[...])
    npart_ref[...] = pre[0:TOP]
    pre = pre + dot(total.astype(BF16), wn_agg_ref[...])
    hidden = silu(pre).astype(BF16)
    centred, scale = norm_parts(dot(hidden, wn_out_ref[...]))
    out_ref[...] = (nodes.astype(F32) + centred * scale).astype(BF16)
    for copy in outs:
        copy.wait()


def top_kernel(got_ref, agg_ref, part_ref, nodes_ref, wn_agg_ref, wn_out_ref, rest_ref, out_hbm, top_ref, sems):
    count, width = rest_ref.shape
    below = pl.ds(TOP, count - TOP)
    rest = pltpu.make_async_copy(rest_ref.at[below], out_hbm.at[below], sems.at[0])
    rest.start()
    terms = [got_ref[at].astype(F32) for at in range(got_ref.shape[0])]
    while len(terms) > 1:
        half = len(terms) // 2
        terms = [a + b for a, b in zip(terms[:half], terms[half:])] + terms[2 * half :]
    sums = jnp.concatenate([terms[0], jnp.zeros((TOP - CO_DEV, width), F32)], axis=0)
    agg = (agg_ref[...] + sums).astype(BF16)
    hidden = silu(part_ref[...] + dot(agg, wn_agg_ref[...])).astype(BF16)
    centred, scale = norm_parts(dot(hidden, wn_out_ref[...]))
    top_ref[...] = (nodes_ref[0:TOP, :].astype(F32) + centred * scale).astype(BF16)
    top = pltpu.make_async_copy(top_ref, out_hbm.at[pl.ds(0, TOP)], sems.at[1])
    top.start()
    rest.wait()
    top.wait()


def in_hbm(*arrays):
    return [pltpu.with_memory_space_constraint(a, pltpu.HBM) for a in arrays]


def cost(flops, moved=0):
    return pl.CostEstimate(flops=flops, bytes_accessed=moved, transcendentals=0)


def call(kernel, name, outs, ins, out_specs=None, scratch=(), hbm=(), flops=0, **more):
    return pl.pallas_call(
        kernel,
        out_shape=outs,
        in_specs=[ANY if i in hbm else VMEM for i in range(len(ins))],
        out_specs=[VMEM] * len(outs) if out_specs is None else out_specs,
        scratch_shapes=scratch,
        compiler_params=pltpu.CompilerParams(vmem_limit_bytes=16 * MIB),
        cost_estimate=cost(flops),
        name=name,
        **more,
    )(*ins)


def body(
    node_latents,
    edge_latents,
    coarse_edges,
    w_edge_in,
    w_edge_out,
    w_node_in,
    w_node_out,
    fine_senders,
    fine_receivers,
    halo_lists,
    coarse_senders,
    coarse_receivers,
):
    count, width = node_latents.shape
    edge_count = edge_latents.shape[0]
    cedge_count = coarse_edges.shape[0]
    halo = halo_lists.shape[2]
    group = lax.axis_size(GROUP_AXES)
    coarse_count = group * CO_DEV
    sub = lax.axis_size("sub")
    shape = jax.ShapeDtypeStruct
    like = lambda a: shape(a.shape, a.dtype)
    vmem = pltpu.VMEM
    dma = pltpu.SemaphoreType.DMA
    square = 2 * width * width
    blocks = pltpu.VMEM((group, CO_DEV, width), BF16)
    ids = lambda a: a[None, :]

    (heads,) = call(
        head_kernel, "head", (blocks,), in_hbm(node_latents), hbm=(0,), scratch=[vmem((TOP, width), BF16), dma(())],
    )
    lat = lax.all_to_all(heads, GROUP_AXES, 0, 0, axis_index_groups=[order(group, sub)])
    send, recv = ids(fine_senders), ids(fine_receivers)
    nodes, cedges, w_ends, w_out, send, recv, to_even, to_odd, gather, picks, coarse_part = call(
        load_kernel,
        "load",
        (
            like(node_latents),
            like(coarse_edges),
            shape((2 * width, width), BF16),
            like(w_edge_out),
            like(send),
            like(recv),
            shape((halo, width), BF16),
            shape((halo, width), BF16),
            shape((2 * cedge_count, coarse_count), BF16),
            shape((coarse_count, cedge_count), BF16),
            shape((cedge_count, width), F32),
        ),
        in_hbm(
            node_latents, halo_lists, coarse_edges, w_edge_in, ids(coarse_senders), ids(coarse_receivers), w_edge_out,
            send, recv,
        )
        + [heads],
        hbm=range(10),
        scratch=[
            vmem(halo_lists.shape, jnp.int32), vmem((width, width), BF16),
            vmem((1, cedge_count), jnp.int32), vmem((1, cedge_count), jnp.int32), dma((10,)),
        ],
        flops=edge_count * square,
    )
    from_even, from_odd = pair(to_even, 0), pair(to_odd, 1)
    new_coarse, sums = call(
        coarse_kernel, "coarse", (like(coarse_edges), blocks),
        [lat, cedges, coarse_part, gather, picks, w_ends, w_out],
    )
    got = lax.all_to_all(sums, GROUP_AXES, 0, 0, axis_index_groups=[order(group, sub)])
    new_edges, new_coarse, rest, agg, node_part, wn_agg, wn_out = call(
        fine_kernel,
        "fine",
        (
            like(edge_latents),
            like(coarse_edges),
            like(node_latents),
            shape((TOP, width), F32),
            shape((TOP, width), F32),
            shape((width, width), BF16),
            like(w_node_out),
        ),
        [from_even, nodes, from_odd, w_ends, w_out, send, recv, new_coarse]
        + in_hbm(edge_latents, w_edge_in, w_node_in, w_node_out)
        + [sums],
        hbm=range(8, 13),
        out_specs=[ANY] * 2 + [VMEM] * 5,
        scratch=[
            vmem(edge_latents.shape, BF16), vmem((width, width), BF16), vmem((width, width), BF16),
            vmem(edge_latents.shape, BF16), dma((5,)), dma((2,)),
        ],
        flops=64 * edge_count * square,
    )
    (new_nodes,) = call(
        top_kernel, "top", (like(node_latents),), [got, agg, node_part, nodes, wn_agg, wn_out, rest], out_specs=[ANY],
        scratch=[vmem((TOP, width), BF16), dma((2,))],
    )
    return (new_nodes, new_edges, new_coarse)


def solution(mesh):
    rows = P(("parts", "patch", "sub"), None)
    ids = P(("parts", "patch", "sub"))
    in_specs = (
        rows, rows, rows, P(), P(), P(), P(), ids, ids, P(("parts", "patch", "sub"), None, None), ids, ids,
    )
    return jax.shard_map(body, mesh=mesh, in_specs=in_specs, out_specs=(rows, rows, rows), check_vma=False)
```

```python
import jax
import jax.numpy as jnp
from jax import lax
from jax.experimental import pallas as pl
from jax.experimental.pallas import tpu as pltpu
from jax.sharding import PartitionSpec as P

CO_DEV = 4
GROUP_AXES = ("patch", "sub")
TOP = 16
MIB = 1 << 20
ANY = pl.BlockSpec(memory_space=pl.ANY)
VMEM = pl.BlockSpec(memory_space=pltpu.VMEM)
BF16, F32 = jnp.bfloat16, jnp.float32


def first_order(group, sub):
    return [(i + group // sub // 2 * sub) % group for i in range(group)]


def second_order(group, sub):
    patch = group // sub
    return [(i + patch // 2) % patch * sub + j for j in range(sub) for i in range(patch)]


def pair(value, first):
    devices = lax.axis_size(GROUP_AXES)
    pairs = [(i, (i + 1) % devices) for i in range(first, devices, 2)]
    return lax.ppermute(value, GROUP_AXES, pairs + [(b, a) for a, b in pairs])


def dot(a, b):
    return jnp.dot(a, b, preferred_element_type=F32)


def dot_t(a, b):
    return lax.dot_general(a, b, (((0,), (0,)), ((), ())), preferred_element_type=F32)


def onehot_t(rows, ids):
    at = lax.broadcasted_iota(jnp.int32, (rows, ids.shape[1]), 0)
    return jnp.where(at == ids, 1.0, 0.0).astype(BF16)


def silu(v):
    half = 0.5 * v
    return half + half * jnp.tanh(half)


def norm_parts(values):
    mean = jnp.mean(values, axis=-1, keepdims=True)
    centred = values - mean
    return centred, lax.rsqrt(jnp.mean(centred * centred, axis=-1, keepdims=True) + 1e-05)


def head_kernel(nodes_hbm, heads_ref, rows_ref, sem):
    copy = pltpu.make_async_copy(nodes_hbm.at[pl.ds(0, TOP)], rows_ref, sem)
    copy.start()
    copy.wait()
    head = rows_ref[0:CO_DEV, :]
    for at in range(heads_ref.shape[0]):
        heads_ref[at] = head


def start_copies(sources, targets, sems):
    copies = [pltpu.make_async_copy(a, b, sems.at[i]) for i, (a, b) in enumerate(zip(sources, targets))]
    for copy in copies:
        copy.start()
    return copies


def load_kernel(
    nodes_hbm, lists_hbm, cedges_hbm, w_in_hbm, csend_hbm, crecv_hbm, w_out_hbm, send_hbm, recv_hbm, after,
    nodes_ref, cedges_ref, w_ends_ref, w_out_ref, send_ref, recv_ref,
    even_ref, odd_ref, gather_ref, picks_ref, part_ref,
    lists_ref, w_self_ref, csend_ref, crecv_ref, sems,
):
    width = nodes_ref.shape[1]
    copies = start_copies(
        [
            nodes_hbm, lists_hbm, cedges_hbm, w_in_hbm.at[pl.ds(0, width)], csend_hbm, crecv_hbm,
            w_in_hbm.at[pl.ds(width, 2 * width)], w_out_hbm, send_hbm, recv_hbm,
        ],
        [
            nodes_ref, lists_ref, cedges_ref, w_self_ref, csend_ref, crecv_ref, w_ends_ref, w_out_ref, send_ref, recv_ref,
        ],
        sems,
    )
    for copy in copies[:2]:
        copy.wait()
    nodes = nodes_ref[...]
    count = nodes.shape[0]
    lists = lists_ref[0]
    me = lax.axis_index(GROUP_AXES)
    odd = me % 2
    first = lists[0:1, :] * (1 - odd) + lists[1:2, :] * odd
    second = lists[1:2, :] * (1 - odd) + lists[0:1, :] * odd
    even_ref[...] = dot_t(onehot_t(count, first), nodes).astype(BF16)
    odd_ref[...] = dot_t(onehot_t(count, second), nodes).astype(BF16)
    for copy in copies[2:6]:
        copy.wait()
    part_ref[...] = dot(cedges_ref[...], w_self_ref[...])
    rows, ids = picks_ref.shape
    at = lax.broadcasted_iota(jnp.int32, (rows, ids), 0)
    node = (at + CO_DEV * first_order(rows // CO_DEV, lax.axis_size("sub"))[0]) % rows
    send = jnp.where(node == csend_ref[...], 1.0, 0.0).astype(BF16)
    recv = jnp.where(node == crecv_ref[...], 1.0, 0.0).astype(BF16)
    picks_ref[...] = onehot_t(rows, crecv_ref[...])
    across = lax.broadcasted_iota(jnp.int32, (rows, rows), 0) == lax.broadcasted_iota(jnp.int32, (rows, rows), 1)
    eye = jnp.where(across, 1.0, 0.0).astype(BF16)
    gather_ref[0:ids, :] = dot_t(send, eye).astype(BF16)
    gather_ref[ids:, :] = dot_t(recv, eye).astype(BF16)
    for copy in copies[6:]:
        copy.wait()


def coarse_kernel(
    lat_ref, edges_ref, part_ref, gather_ref, picks_ref, w_ends_ref, w_out_ref, new_ref, sums_ref
):
    count, width = edges_ref.shape
    blocks = lat_ref.shape[0]
    lat = jnp.concatenate([lat_ref[at].astype(F32) for at in range(blocks)], axis=0).astype(BF16)
    ends = dot(gather_ref[...], lat).astype(BF16)
    ends = jnp.concatenate([ends[0:count], ends[count:]], axis=1)
    hidden = silu(part_ref[...] + dot(ends, w_ends_ref[...])).astype(BF16)
    centred, scale = norm_parts(dot(hidden, w_out_ref[...]))
    new = (edges_ref[...].astype(F32) + centred * scale).astype(BF16)
    new_ref[...] = new
    sums = dot(picks_ref[...], new).astype(BF16)
    for at, owner in enumerate(second_order(blocks, lax.axis_size("sub"))):
        sums_ref[at] = sums[owner * CO_DEV : (owner + 1) * CO_DEV, :]


def fine_kernel(
    even_ref, nodes_ref, odd_ref, w_ends_ref, w_out_ref, send_ref, recv_ref, coarse_ref,
    edges_hbm, w_in_hbm, wn_in_hbm, wn_out_hbm, after,
    new_hbm, coarse_hbm, out_ref, agg_ref, npart_ref, wn_agg_ref, wn_out_ref,
    edges_ref, w_self_ref, wn_self_ref, new_ref, sems, out_sems,
):
    nodes = nodes_ref[...]
    count, width = nodes.shape
    copies = start_copies(
        [
            edges_hbm, w_in_hbm.at[pl.ds(0, width)],
            wn_in_hbm.at[pl.ds(0, width)], wn_in_hbm.at[pl.ds(width, width)], wn_out_hbm,
        ],
        [edges_ref, w_self_ref, wn_self_ref, wn_agg_ref, wn_out_ref],
        sems,
    )
    outs = [pltpu.make_async_copy(coarse_ref, coarse_hbm, out_sems.at[0])]
    outs[0].start()
    odd = (lax.axis_index(GROUP_AXES) % 2).astype(F32)
    met, other = even_ref[...].astype(F32), odd_ref[...].astype(F32)
    prev = (met * odd + other * (1.0 - odd)).astype(BF16)
    following = (other * odd + met * (1.0 - odd)).astype(BF16)
    extended = jnp.concatenate([prev, nodes, following], axis=0)
    picks = onehot_t(count, recv_ref[...])
    senders = dot_t(onehot_t(extended.shape[0], send_ref[...]), extended).astype(BF16)
    receivers = dot_t(picks, nodes).astype(BF16)
    valid = dot_t(picks, jnp.ones((count, 128), BF16))[:, 0:1]
    pre = dot(jnp.concatenate([senders, receivers], axis=1), w_ends_ref[...])
    for copy in copies[:2]:
        copy.wait()
    edges = edges_ref[...]
    pre = pre + dot(edges, w_self_ref[...])
    hidden = silu(pre).astype(BF16)
    centred, scale = norm_parts(dot(hidden, w_out_ref[...]))
    new = (edges.astype(F32) + centred * (scale * valid)).astype(BF16)
    new_ref[...] = new
    outs.append(pltpu.make_async_copy(new_ref, new_hbm, out_sems.at[1]))
    outs[1].start()
    total = dot(picks, new)
    agg_ref[...] = total[0:TOP]
    for copy in copies[2:]:
        copy.wait()
    pre = dot(nodes, wn_self_ref[...])
    npart_ref[...] = pre[0:TOP]
    pre = pre + dot(total.astype(BF16), wn_agg_ref[...])
    hidden = silu(pre).astype(BF16)
    centred, scale = norm_parts(dot(hidden, wn_out_ref[...]))
    out_ref[...] = (nodes.astype(F32) + centred * scale).astype(BF16)
    for copy in outs:
        copy.wait()


def top_kernel(got_ref, agg_ref, part_ref, nodes_ref, wn_agg_ref, wn_out_ref, rest_ref, out_hbm, top_ref, sems):
    count, width = rest_ref.shape
    below = pl.ds(TOP, count - TOP)
    rest = pltpu.make_async_copy(rest_ref.at[below], out_hbm.at[below], sems.at[0])
    rest.start()
    terms = [got_ref[at].astype(F32) for at in range(got_ref.shape[0])]
    while len(terms) > 1:
        half = len(terms) // 2
        terms = [a + b for a, b in zip(terms[:half], terms[half:])] + terms[2 * half :]
    sums = jnp.concatenate([terms[0], jnp.zeros((TOP - CO_DEV, width), F32)], axis=0)
    agg = (agg_ref[...] + sums).astype(BF16)
    hidden = silu(part_ref[...] + dot(agg, wn_agg_ref[...])).astype(BF16)
    centred, scale = norm_parts(dot(hidden, wn_out_ref[...]))
    top_ref[...] = (nodes_ref[0:TOP, :].astype(F32) + centred * scale).astype(BF16)
    top = pltpu.make_async_copy(top_ref, out_hbm.at[pl.ds(0, TOP)], sems.at[1])
    top.start()
    rest.wait()
    top.wait()


def in_hbm(*arrays):
    return [pltpu.with_memory_space_constraint(a, pltpu.HBM) for a in arrays]


def cost(flops, moved=0):
    return pl.CostEstimate(flops=flops, bytes_accessed=moved, transcendentals=0)


def call(kernel, name, outs, ins, out_specs=None, scratch=(), hbm=(), flops=0, **more):
    return pl.pallas_call(
        kernel,
        out_shape=outs,
        in_specs=[ANY if i in hbm else VMEM for i in range(len(ins))],
        out_specs=[VMEM] * len(outs) if out_specs is None else out_specs,
        scratch_shapes=scratch,
        compiler_params=pltpu.CompilerParams(vmem_limit_bytes=16 * MIB),
        cost_estimate=cost(flops),
        name=name,
        **more,
    )(*ins)


def body(
    node_latents,
    edge_latents,
    coarse_edges,
    w_edge_in,
    w_edge_out,
    w_node_in,
    w_node_out,
    fine_senders,
    fine_receivers,
    halo_lists,
    coarse_senders,
    coarse_receivers,
):
    count, width = node_latents.shape
    edge_count = edge_latents.shape[0]
    cedge_count = coarse_edges.shape[0]
    halo = halo_lists.shape[2]
    group = lax.axis_size(GROUP_AXES)
    coarse_count = group * CO_DEV
    sub = lax.axis_size("sub")
    shape = jax.ShapeDtypeStruct
    like = lambda a: shape(a.shape, a.dtype)
    vmem = pltpu.VMEM
    dma = pltpu.SemaphoreType.DMA
    square = 2 * width * width
    blocks = pltpu.VMEM((group, CO_DEV, width), BF16)
    ids = lambda a: a[None, :]

    (heads,) = call(
        head_kernel, "head", (blocks,), in_hbm(node_latents), hbm=(0,), scratch=[vmem((TOP, width), BF16), dma(())],
    )
    lat = lax.all_to_all(heads, GROUP_AXES, 0, 0, axis_index_groups=[first_order(group, sub)])
    send, recv = ids(fine_senders), ids(fine_receivers)
    nodes, cedges, w_ends, w_out, send, recv, to_even, to_odd, gather, picks, coarse_part = call(
        load_kernel,
        "load",
        (
            like(node_latents),
            like(coarse_edges),
            shape((2 * width, width), BF16),
            like(w_edge_out),
            like(send),
            like(recv),
            shape((halo, width), BF16),
            shape((halo, width), BF16),
            shape((2 * cedge_count, coarse_count), BF16),
            shape((coarse_count, cedge_count), BF16),
            shape((cedge_count, width), F32),
        ),
        in_hbm(
            node_latents, halo_lists, coarse_edges, w_edge_in, ids(coarse_senders), ids(coarse_receivers), w_edge_out,
            send, recv,
        )
        + [heads],
        hbm=range(10),
        scratch=[
            vmem(halo_lists.shape, jnp.int32), vmem((width, width), BF16),
            vmem((1, cedge_count), jnp.int32), vmem((1, cedge_count), jnp.int32), dma((10,)),
        ],
        flops=edge_count * square,
    )
    from_even, from_odd = pair(to_even, 0), pair(to_odd, 1)
    new_coarse, sums = call(
        coarse_kernel, "coarse", (like(coarse_edges), blocks),
        [lat, cedges, coarse_part, gather, picks, w_ends, w_out],
    )
    got = lax.all_to_all(sums, GROUP_AXES, 0, 0, axis_index_groups=[second_order(group, sub)])
    new_edges, new_coarse, rest, agg, node_part, wn_agg, wn_out = call(
        fine_kernel,
        "fine",
        (
            like(edge_latents),
            like(coarse_edges),
            like(node_latents),
            shape((TOP, width), F32),
            shape((TOP, width), F32),
            shape((width, width), BF16),
            like(w_node_out),
        ),
        [from_even, nodes, from_odd, w_ends, w_out, send, recv, new_coarse]
        + in_hbm(edge_latents, w_edge_in, w_node_in, w_node_out)
        + [sums],
        hbm=range(8, 13),
        out_specs=[ANY] * 2 + [VMEM] * 5,
        scratch=[
            vmem(edge_latents.shape, BF16), vmem((width, width), BF16), vmem((width, width), BF16),
            vmem(edge_latents.shape, BF16), dma((5,)), dma((2,)),
        ],
        flops=64 * edge_count * square,
    )
    (new_nodes,) = call(
        top_kernel, "top", (like(node_latents),), [got, agg, node_part, nodes, wn_agg, wn_out, rest], out_specs=[ANY],
        scratch=[vmem((TOP, width), BF16), dma((2,))],
    )
    return (new_nodes, new_edges, new_coarse)


def solution(mesh):
    rows = P(("parts", "patch", "sub"), None)
    ids = P(("parts", "patch", "sub"))
    in_specs = (
        rows, rows, rows, P(), P(), P(), P(), ids, ids, P(("parts", "patch", "sub"), None, None), ids, ids,
    )
    return jax.shard_map(body, mesh=mesh, in_specs=in_specs, out_specs=(rows, rows, rows), check_vma=False)
```

```python
import jax
import jax.numpy as jnp
from jax import lax
from jax.experimental import pallas as pl
from jax.experimental.pallas import tpu as pltpu
from jax.sharding import PartitionSpec as P

CO_DEV = 4
GROUP_AXES = ("patch", "sub")
TOP = 16
MIB = 1 << 20
ANY = pl.BlockSpec(memory_space=pl.ANY)
VMEM = pl.BlockSpec(memory_space=pltpu.VMEM)
BF16, F32 = jnp.bfloat16, jnp.float32


def order(group, sub):
    patch = group // sub
    return [(i + patch // 2) % patch * sub + j for j in range(sub) for i in range(patch)]


def pair(value, first):
    devices = lax.axis_size(GROUP_AXES)
    pairs = [(i, (i + 1) % devices) for i in range(first, devices, 2)]
    return lax.ppermute(value, GROUP_AXES, pairs + [(b, a) for a, b in pairs])


def dot(a, b):
    return jnp.dot(a, b, preferred_element_type=F32)


def dot_t(a, b):
    return lax.dot_general(a, b, (((0,), (0,)), ((), ())), preferred_element_type=F32)


def onehot_t(rows, ids):
    at = lax.broadcasted_iota(jnp.int32, (rows, ids.shape[1]), 0)
    return jnp.where(at == ids, 1.0, 0.0).astype(BF16)


def silu(v):
    half = 0.5 * v
    return half + half * jnp.tanh(half)


def norm_parts(values):
    mean = jnp.mean(values, axis=-1, keepdims=True)
    centred = values - mean
    return centred, lax.rsqrt(jnp.mean(centred * centred, axis=-1, keepdims=True) + 1e-05)


def head_kernel(nodes_hbm, heads_ref, rows_ref, sem):
    copy = pltpu.make_async_copy(nodes_hbm.at[pl.ds(0, TOP)], rows_ref, sem)
    copy.start()
    copy.wait()
    head = rows_ref[0:CO_DEV, :]
    for at in range(heads_ref.shape[0]):
        heads_ref[at] = head


def start_copies(sources, targets, sems):
    copies = [pltpu.make_async_copy(a, b, sems.at[i]) for i, (a, b) in enumerate(zip(sources, targets))]
    for copy in copies:
        copy.start()
    return copies


def load_kernel(
    nodes_hbm, lists_hbm, cedges_hbm, w_in_hbm, csend_hbm, crecv_hbm, w_out_hbm, send_hbm, recv_hbm, after,
    nodes_ref, cedges_ref, w_ends_ref, w_out_ref, send_ref, recv_ref,
    even_ref, odd_ref, gather_ref, picks_ref, part_ref,
    lists_ref, w_self_ref, csend_ref, crecv_ref, sems,
):
    width = nodes_ref.shape[1]
    copies = start_copies(
        [
            nodes_hbm, lists_hbm, cedges_hbm, w_in_hbm.at[pl.ds(0, width)], csend_hbm, crecv_hbm,
            w_in_hbm.at[pl.ds(width, 2 * width)], w_out_hbm, send_hbm, recv_hbm,
        ],
        [
            nodes_ref, lists_ref, cedges_ref, w_self_ref, csend_ref, crecv_ref, w_ends_ref, w_out_ref, send_ref, recv_ref,
        ],
        sems,
    )
    for copy in copies[:2]:
        copy.wait()
    nodes = nodes_ref[...]
    count = nodes.shape[0]
    lists = lists_ref[0]
    me = lax.axis_index(GROUP_AXES)
    odd = me % 2
    first = lists[0:1, :] * (1 - odd) + lists[1:2, :] * odd
    second = lists[1:2, :] * (1 - odd) + lists[0:1, :] * odd
    even_ref[...] = dot_t(onehot_t(count, first), nodes).astype(BF16)
    odd_ref[...] = dot_t(onehot_t(count, second), nodes).astype(BF16)
    for copy in copies[2:6]:
        copy.wait()
    part_ref[...] = dot(cedges_ref[...], w_self_ref[...])
    rows, ids = picks_ref.shape
    at = lax.broadcasted_iota(jnp.int32, (rows, ids), 0)
    sub, patch = lax.axis_size("sub"), lax.axis_size("patch")
    block = at // CO_DEV
    device = (block % patch + patch // 2) % patch * sub + block // patch
    node = device * CO_DEV + at % CO_DEV
    send = jnp.where(node == csend_ref[...], 1.0, 0.0).astype(BF16)
    recv = jnp.where(node == crecv_ref[...], 1.0, 0.0).astype(BF16)
    picks_ref[...] = onehot_t(rows, crecv_ref[...])
    across = lax.broadcasted_iota(jnp.int32, (rows, rows), 0) == lax.broadcasted_iota(jnp.int32, (rows, rows), 1)
    eye = jnp.where(across, 1.0, 0.0).astype(BF16)
    gather_ref[0:ids, :] = dot_t(send, eye).astype(BF16)
    gather_ref[ids:, :] = dot_t(recv, eye).astype(BF16)
    for copy in copies[6:]:
        copy.wait()


def coarse_kernel(
    lat_ref, edges_ref, part_ref, gather_ref, picks_ref, w_ends_ref, w_out_ref, new_ref, sums_ref
):
    count, width = edges_ref.shape
    blocks = lat_ref.shape[0]
    lat = jnp.concatenate([lat_ref[at].astype(F32) for at in range(blocks)], axis=0).astype(BF16)
    ends = dot(gather_ref[...], lat).astype(BF16)
    ends = jnp.concatenate([ends[0:count], ends[count:]], axis=1)
    hidden = silu(part_ref[...] + dot(ends, w_ends_ref[...])).astype(BF16)
    centred, scale = norm_parts(dot(hidden, w_out_ref[...]))
    new = (edges_ref[...].astype(F32) + centred * scale).astype(BF16)
    new_ref[...] = new
    sums = dot(picks_ref[...], new).astype(BF16)
    for at, owner in enumerate(order(blocks, lax.axis_size("sub"))):
        sums_ref[at] = sums[owner * CO_DEV : (owner + 1) * CO_DEV, :]


def fine_kernel(
    odd_ref, nodes_ref, even_ref, w_ends_ref, w_out_ref, send_ref, recv_ref, coarse_ref,
    edges_hbm, w_in_hbm, wn_in_hbm, wn_out_hbm, after,
    new_hbm, coarse_hbm, out_ref, agg_ref, npart_ref, wn_agg_ref, wn_out_ref,
    edges_ref, w_self_ref, wn_self_ref, new_ref, sems, out_sems,
):
    nodes = nodes_ref[...]
    count, width = nodes.shape
    copies = start_copies(
        [
            edges_hbm, w_in_hbm.at[pl.ds(0, width)],
            wn_in_hbm.at[pl.ds(0, width)], wn_in_hbm.at[pl.ds(width, width)], wn_out_hbm,
        ],
        [edges_ref, w_self_ref, wn_self_ref, wn_agg_ref, wn_out_ref],
        sems,
    )
    outs = [pltpu.make_async_copy(coarse_ref, coarse_hbm, out_sems.at[0])]
    outs[0].start()
    odd = (lax.axis_index(GROUP_AXES) % 2).astype(F32)
    met, other = even_ref[...].astype(F32), odd_ref[...].astype(F32)
    prev = (met * odd + other * (1.0 - odd)).astype(BF16)
    following = (other * odd + met * (1.0 - odd)).astype(BF16)
    extended = jnp.concatenate([prev, nodes, following], axis=0)
    picks = onehot_t(count, recv_ref[...])
    senders = dot_t(onehot_t(extended.shape[0], send_ref[...]), extended).astype(BF16)
    receivers = dot_t(picks, nodes).astype(BF16)
    valid = dot_t(picks, jnp.ones((count, 128), BF16))[:, 0:1]
    pre = dot(jnp.concatenate([senders, receivers], axis=1), w_ends_ref[...])
    for copy in copies[:2]:
        copy.wait()
    edges = edges_ref[...]
    pre = pre + dot(edges, w_self_ref[...])
    hidden = silu(pre).astype(BF16)
    centred, scale = norm_parts(dot(hidden, w_out_ref[...]))
    new = (edges.astype(F32) + centred * (scale * valid)).astype(BF16)
    new_ref[...] = new
    outs.append(pltpu.make_async_copy(new_ref, new_hbm, out_sems.at[1]))
    outs[1].start()
    total = dot(picks, new)
    agg_ref[...] = total[0:TOP]
    for copy in copies[2:]:
        copy.wait()
    pre = dot(nodes, wn_self_ref[...])
    npart_ref[...] = pre[0:TOP]
    pre = pre + dot(total.astype(BF16), wn_agg_ref[...])
    hidden = silu(pre).astype(BF16)
    centred, scale = norm_parts(dot(hidden, wn_out_ref[...]))
    out_ref[...] = (nodes.astype(F32) + centred * scale).astype(BF16)
    for copy in outs:
        copy.wait()


def top_kernel(got_ref, agg_ref, part_ref, nodes_ref, wn_agg_ref, wn_out_ref, rest_ref, out_hbm, top_ref, sems):
    count, width = rest_ref.shape
    below = pl.ds(TOP, count - TOP)
    rest = pltpu.make_async_copy(rest_ref.at[below], out_hbm.at[below], sems.at[0])
    rest.start()
    terms = [got_ref[at].astype(F32) for at in range(got_ref.shape[0])]
    while len(terms) > 1:
        half = len(terms) // 2
        terms = [a + b for a, b in zip(terms[:half], terms[half:])] + terms[2 * half :]
    sums = jnp.concatenate([terms[0], jnp.zeros((TOP - CO_DEV, width), F32)], axis=0)
    agg = (agg_ref[...] + sums).astype(BF16)
    hidden = silu(part_ref[...] + dot(agg, wn_agg_ref[...])).astype(BF16)
    centred, scale = norm_parts(dot(hidden, wn_out_ref[...]))
    top_ref[...] = (nodes_ref[0:TOP, :].astype(F32) + centred * scale).astype(BF16)
    top = pltpu.make_async_copy(top_ref, out_hbm.at[pl.ds(0, TOP)], sems.at[1])
    top.start()
    rest.wait()
    top.wait()


def in_hbm(*arrays):
    return [pltpu.with_memory_space_constraint(a, pltpu.HBM) for a in arrays]


def cost(flops, moved=0):
    return pl.CostEstimate(flops=flops, bytes_accessed=moved, transcendentals=0)


def call(kernel, name, outs, ins, out_specs=None, scratch=(), hbm=(), flops=0, **more):
    return pl.pallas_call(
        kernel,
        out_shape=outs,
        in_specs=[ANY if i in hbm else VMEM for i in range(len(ins))],
        out_specs=[VMEM] * len(outs) if out_specs is None else out_specs,
        scratch_shapes=scratch,
        compiler_params=pltpu.CompilerParams(vmem_limit_bytes=16 * MIB),
        cost_estimate=cost(flops),
        name=name,
        **more,
    )(*ins)


def body(
    node_latents,
    edge_latents,
    coarse_edges,
    w_edge_in,
    w_edge_out,
    w_node_in,
    w_node_out,
    fine_senders,
    fine_receivers,
    halo_lists,
    coarse_senders,
    coarse_receivers,
):
    count, width = node_latents.shape
    edge_count = edge_latents.shape[0]
    cedge_count = coarse_edges.shape[0]
    halo = halo_lists.shape[2]
    group = lax.axis_size(GROUP_AXES)
    coarse_count = group * CO_DEV
    sub = lax.axis_size("sub")
    shape = jax.ShapeDtypeStruct
    like = lambda a: shape(a.shape, a.dtype)
    vmem = pltpu.VMEM
    dma = pltpu.SemaphoreType.DMA
    square = 2 * width * width
    blocks = pltpu.VMEM((group, CO_DEV, width), BF16)
    ids = lambda a: a[None, :]

    (heads,) = call(
        head_kernel, "head", (blocks,), in_hbm(node_latents), hbm=(0,), scratch=[vmem((TOP, width), BF16), dma(())],
    )
    lat = lax.all_to_all(heads, GROUP_AXES, 0, 0, axis_index_groups=[order(group, sub)])
    send, recv = ids(fine_senders), ids(fine_receivers)
    nodes, cedges, w_ends, w_out, send, recv, to_even, to_odd, gather, picks, coarse_part = call(
        load_kernel,
        "load",
        (
            like(node_latents),
            like(coarse_edges),
            shape((2 * width, width), BF16),
            like(w_edge_out),
            like(send),
            like(recv),
            shape((halo, width), BF16),
            shape((halo, width), BF16),
            shape((2 * cedge_count, coarse_count), BF16),
            shape((coarse_count, cedge_count), BF16),
            shape((cedge_count, width), F32),
        ),
        in_hbm(
            node_latents, halo_lists, coarse_edges, w_edge_in, ids(coarse_senders), ids(coarse_receivers), w_edge_out,
            send, recv,
        )
        + [heads],
        hbm=range(10),
        scratch=[
            vmem(halo_lists.shape, jnp.int32), vmem((width, width), BF16),
            vmem((1, cedge_count), jnp.int32), vmem((1, cedge_count), jnp.int32), dma((10,)),
        ],
        flops=edge_count * square,
    )
    from_odd, from_even = pair(to_odd, 1), pair(to_even, 0)
    new_coarse, sums = call(
        coarse_kernel, "coarse", (like(coarse_edges), blocks),
        [lat, cedges, coarse_part, gather, picks, w_ends, w_out],
    )
    got = lax.all_to_all(sums, GROUP_AXES, 0, 0, axis_index_groups=[order(group, sub)])
    new_edges, new_coarse, rest, agg, node_part, wn_agg, wn_out = call(
        fine_kernel,
        "fine",
        (
            like(edge_latents),
            like(coarse_edges),
            like(node_latents),
            shape((TOP, width), F32),
            shape((TOP, width), F32),
            shape((width, width), BF16),
            like(w_node_out),
        ),
        [from_odd, nodes, from_even, w_ends, w_out, send, recv, new_coarse]
        + in_hbm(edge_latents, w_edge_in, w_node_in, w_node_out)
        + [sums],
        hbm=range(8, 13),
        out_specs=[ANY] * 2 + [VMEM] * 5,
        scratch=[
            vmem(edge_latents.shape, BF16), vmem((width, width), BF16), vmem((width, width), BF16),
            vmem(edge_latents.shape, BF16), dma((5,)), dma((2,)),
        ],
        flops=64 * edge_count * square,
    )
    (new_nodes,) = call(
        top_kernel, "top", (like(node_latents),), [got, agg, node_part, nodes, wn_agg, wn_out, rest], out_specs=[ANY],
        scratch=[vmem((TOP, width), BF16), dma((2,))],
    )
    return (new_nodes, new_edges, new_coarse)


def solution(mesh):
    rows = P(("parts", "patch", "sub"), None)
    ids = P(("parts", "patch", "sub"))
    in_specs = (
        rows, rows, rows, P(), P(), P(), P(), ids, ids, P(("parts", "patch", "sub"), None, None), ids, ids,
    )
    return jax.shard_map(body, mesh=mesh, in_specs=in_specs, out_specs=(rows, rows, rows), check_vma=False)
```

```python
import jax
import jax.numpy as jnp
from jax import lax
from jax.experimental import pallas as pl
from jax.experimental.pallas import tpu as pltpu
from jax.sharding import PartitionSpec as P

CO_DEV = 4
GROUP_AXES = ("patch", "sub")
TOP = 16
MIB = 1 << 20
ANY = pl.BlockSpec(memory_space=pl.ANY)
VMEM = pl.BlockSpec(memory_space=pltpu.VMEM)
BF16, F32 = jnp.bfloat16, jnp.float32


def order(group, sub, first=0):
    patch = group // sub
    return [(i + patch // 2) % patch * sub + (j + first) % sub for j in range(sub) for i in range(patch)]


def pair(value, first):
    devices = lax.axis_size(GROUP_AXES)
    pairs = [(i, (i + 1) % devices) for i in range(first, devices, 2)]
    return lax.ppermute(value, GROUP_AXES, pairs + [(b, a) for a, b in pairs])


def dot(a, b):
    return jnp.dot(a, b, preferred_element_type=F32)


def dot_t(a, b):
    return lax.dot_general(a, b, (((0,), (0,)), ((), ())), preferred_element_type=F32)


def onehot_t(rows, ids):
    at = lax.broadcasted_iota(jnp.int32, (rows, ids.shape[1]), 0)
    return jnp.where(at == ids, 1.0, 0.0).astype(BF16)


def silu(v):
    half = 0.5 * v
    return half + half * jnp.tanh(half)


def norm_parts(values):
    mean = jnp.mean(values, axis=-1, keepdims=True)
    centred = values - mean
    return centred, lax.rsqrt(jnp.mean(centred * centred, axis=-1, keepdims=True) + 1e-05)


def head_kernel(nodes_hbm, heads_ref, rows_ref, sem):
    copy = pltpu.make_async_copy(nodes_hbm.at[pl.ds(0, TOP)], rows_ref, sem)
    copy.start()
    copy.wait()
    head = rows_ref[0:CO_DEV, :]
    for at in range(heads_ref.shape[0]):
        heads_ref[at] = head


def start_copies(sources, targets, sems):
    copies = [pltpu.make_async_copy(a, b, sems.at[i]) for i, (a, b) in enumerate(zip(sources, targets))]
    for copy in copies:
        copy.start()
    return copies


def load_kernel(
    nodes_hbm, lists_hbm, cedges_hbm, w_in_hbm, csend_hbm, crecv_hbm, w_out_hbm, send_hbm, recv_hbm, after,
    nodes_ref, cedges_ref, w_ends_ref, w_out_ref, send_ref, recv_ref,
    even_ref, odd_ref, gather_ref, picks_ref, part_ref,
    lists_ref, w_self_ref, csend_ref, crecv_ref, sems,
):
    width = nodes_ref.shape[1]
    copies = start_copies(
        [
            nodes_hbm, lists_hbm, cedges_hbm, w_in_hbm.at[pl.ds(0, width)], csend_hbm, crecv_hbm,
            w_in_hbm.at[pl.ds(width, 2 * width)], w_out_hbm, send_hbm, recv_hbm,
        ],
        [
            nodes_ref, lists_ref, cedges_ref, w_self_ref, csend_ref, crecv_ref, w_ends_ref, w_out_ref, send_ref, recv_ref,
        ],
        sems,
    )
    for copy in copies[:2]:
        copy.wait()
    nodes = nodes_ref[...]
    count = nodes.shape[0]
    lists = lists_ref[0]
    me = lax.axis_index(GROUP_AXES)
    odd = me % 2
    first = lists[0:1, :] * (1 - odd) + lists[1:2, :] * odd
    second = lists[1:2, :] * (1 - odd) + lists[0:1, :] * odd
    even_ref[...] = dot_t(onehot_t(count, first), nodes).astype(BF16)
    odd_ref[...] = dot_t(onehot_t(count, second), nodes).astype(BF16)
    for copy in copies[2:6]:
        copy.wait()
    part_ref[...] = dot(cedges_ref[...], w_self_ref[...])
    rows, ids = picks_ref.shape
    at = lax.broadcasted_iota(jnp.int32, (rows, ids), 0)
    sub, patch = lax.axis_size("sub"), lax.axis_size("patch")
    block = at // CO_DEV
    device = (block % patch + patch // 2) % patch * sub + (block // patch + sub // 2) % sub
    node = device * CO_DEV + at % CO_DEV
    send = jnp.where(node == csend_ref[...], 1.0, 0.0).astype(BF16)
    recv = jnp.where(node == crecv_ref[...], 1.0, 0.0).astype(BF16)
    picks_ref[...] = onehot_t(rows, crecv_ref[...])
    across = lax.broadcasted_iota(jnp.int32, (rows, rows), 0) == lax.broadcasted_iota(jnp.int32, (rows, rows), 1)
    eye = jnp.where(across, 1.0, 0.0).astype(BF16)
    gather_ref[0:ids, :] = dot_t(send, eye).astype(BF16)
    gather_ref[ids:, :] = dot_t(recv, eye).astype(BF16)
    for copy in copies[6:]:
        copy.wait()


def coarse_kernel(
    lat_ref, edges_ref, part_ref, gather_ref, picks_ref, w_ends_ref, w_out_ref, new_ref, sums_ref
):
    count, width = edges_ref.shape
    blocks = lat_ref.shape[0]
    lat = jnp.concatenate([lat_ref[at].astype(F32) for at in range(blocks)], axis=0).astype(BF16)
    ends = dot(gather_ref[...], lat).astype(BF16)
    ends = jnp.concatenate([ends[0:count], ends[count:]], axis=1)
    hidden = silu(part_ref[...] + dot(ends, w_ends_ref[...])).astype(BF16)
    centred, scale = norm_parts(dot(hidden, w_out_ref[...]))
    new = (edges_ref[...].astype(F32) + centred * scale).astype(BF16)
    new_ref[...] = new
    sums = dot(picks_ref[...], new).astype(BF16)
    for at, owner in enumerate(order(blocks, lax.axis_size("sub"))):
        sums_ref[at] = sums[owner * CO_DEV : (owner + 1) * CO_DEV, :]


def fine_kernel(
    even_ref, nodes_ref, odd_ref, w_ends_ref, w_out_ref, send_ref, recv_ref, coarse_ref,
    edges_hbm, w_in_hbm, wn_in_hbm, wn_out_hbm, after,
    new_hbm, coarse_hbm, out_ref, agg_ref, npart_ref, wn_agg_ref, wn_out_ref,
    edges_ref, w_self_ref, wn_self_ref, new_ref, sems, out_sems,
):
    nodes = nodes_ref[...]
    count, width = nodes.shape
    copies = start_copies(
        [
            edges_hbm, w_in_hbm.at[pl.ds(0, width)],
            wn_in_hbm.at[pl.ds(0, width)], wn_in_hbm.at[pl.ds(width, width)], wn_out_hbm,
        ],
        [edges_ref, w_self_ref, wn_self_ref, wn_agg_ref, wn_out_ref],
        sems,
    )
    outs = [pltpu.make_async_copy(coarse_ref, coarse_hbm, out_sems.at[0])]
    outs[0].start()
    odd = (lax.axis_index(GROUP_AXES) % 2).astype(F32)
    met, other = even_ref[...].astype(F32), odd_ref[...].astype(F32)
    prev = (met * odd + other * (1.0 - odd)).astype(BF16)
    following = (other * odd + met * (1.0 - odd)).astype(BF16)
    extended = jnp.concatenate([prev, nodes, following], axis=0)
    picks = onehot_t(count, recv_ref[...])
    senders = dot_t(onehot_t(extended.shape[0], send_ref[...]), extended).astype(BF16)
    receivers = dot_t(picks, nodes).astype(BF16)
    valid = dot_t(picks, jnp.ones((count, 128), BF16))[:, 0:1]
    pre = dot(jnp.concatenate([senders, receivers], axis=1), w_ends_ref[...])
    for copy in copies[:2]:
        copy.wait()
    edges = edges_ref[...]
    pre = pre + dot(edges, w_self_ref[...])
    hidden = silu(pre).astype(BF16)
    centred, scale = norm_parts(dot(hidden, w_out_ref[...]))
    new = (edges.astype(F32) + centred * (scale * valid)).astype(BF16)
    new_ref[...] = new
    outs.append(pltpu.make_async_copy(new_ref, new_hbm, out_sems.at[1]))
    outs[1].start()
    total = dot(picks, new)
    agg_ref[...] = total[0:TOP]
    for copy in copies[2:]:
        copy.wait()
    pre = dot(nodes, wn_self_ref[...])
    npart_ref[...] = pre[0:TOP]
    pre = pre + dot(total.astype(BF16), wn_agg_ref[...])
    hidden = silu(pre).astype(BF16)
    centred, scale = norm_parts(dot(hidden, wn_out_ref[...]))
    out_ref[...] = (nodes.astype(F32) + centred * scale).astype(BF16)
    for copy in outs:
        copy.wait()


def top_kernel(got_ref, agg_ref, part_ref, nodes_ref, wn_agg_ref, wn_out_ref, rest_ref, out_hbm, top_ref, sems):
    count, width = rest_ref.shape
    below = pl.ds(TOP, count - TOP)
    rest = pltpu.make_async_copy(rest_ref.at[below], out_hbm.at[below], sems.at[0])
    rest.start()
    terms = [got_ref[at].astype(F32) for at in range(got_ref.shape[0])]
    while len(terms) > 1:
        half = len(terms) // 2
        terms = [a + b for a, b in zip(terms[:half], terms[half:])] + terms[2 * half :]
    sums = jnp.concatenate([terms[0], jnp.zeros((TOP - CO_DEV, width), F32)], axis=0)
    agg = (agg_ref[...] + sums).astype(BF16)
    hidden = silu(part_ref[...] + dot(agg, wn_agg_ref[...])).astype(BF16)
    centred, scale = norm_parts(dot(hidden, wn_out_ref[...]))
    top_ref[...] = (nodes_ref[0:TOP, :].astype(F32) + centred * scale).astype(BF16)
    top = pltpu.make_async_copy(top_ref, out_hbm.at[pl.ds(0, TOP)], sems.at[1])
    top.start()
    rest.wait()
    top.wait()


def in_hbm(*arrays):
    return [pltpu.with_memory_space_constraint(a, pltpu.HBM) for a in arrays]


def cost(flops, moved=0):
    return pl.CostEstimate(flops=flops, bytes_accessed=moved, transcendentals=0)


def call(kernel, name, outs, ins, out_specs=None, scratch=(), hbm=(), flops=0, **more):
    return pl.pallas_call(
        kernel,
        out_shape=outs,
        in_specs=[ANY if i in hbm else VMEM for i in range(len(ins))],
        out_specs=[VMEM] * len(outs) if out_specs is None else out_specs,
        scratch_shapes=scratch,
        compiler_params=pltpu.CompilerParams(vmem_limit_bytes=16 * MIB),
        cost_estimate=cost(flops),
        name=name,
        **more,
    )(*ins)


def body(
    node_latents,
    edge_latents,
    coarse_edges,
    w_edge_in,
    w_edge_out,
    w_node_in,
    w_node_out,
    fine_senders,
    fine_receivers,
    halo_lists,
    coarse_senders,
    coarse_receivers,
):
    count, width = node_latents.shape
    edge_count = edge_latents.shape[0]
    cedge_count = coarse_edges.shape[0]
    halo = halo_lists.shape[2]
    group = lax.axis_size(GROUP_AXES)
    coarse_count = group * CO_DEV
    sub = lax.axis_size("sub")
    shape = jax.ShapeDtypeStruct
    like = lambda a: shape(a.shape, a.dtype)
    vmem = pltpu.VMEM
    dma = pltpu.SemaphoreType.DMA
    square = 2 * width * width
    blocks = pltpu.VMEM((group, CO_DEV, width), BF16)
    ids = lambda a: a[None, :]

    (heads,) = call(
        head_kernel, "head", (blocks,), in_hbm(node_latents), hbm=(0,), scratch=[vmem((TOP, width), BF16), dma(())],
    )
    lat = lax.all_to_all(heads, GROUP_AXES, 0, 0, axis_index_groups=[order(group, sub, sub // 2)])
    send, recv = ids(fine_senders), ids(fine_receivers)
    nodes, cedges, w_ends, w_out, send, recv, to_even, to_odd, gather, picks, coarse_part = call(
        load_kernel,
        "load",
        (
            like(node_latents),
            like(coarse_edges),
            shape((2 * width, width), BF16),
            like(w_edge_out),
            like(send),
            like(recv),
            shape((halo, width), BF16),
            shape((halo, width), BF16),
            shape((2 * cedge_count, coarse_count), BF16),
            shape((coarse_count, cedge_count), BF16),
            shape((cedge_count, width), F32),
        ),
        in_hbm(
            node_latents, halo_lists, coarse_edges, w_edge_in, ids(coarse_senders), ids(coarse_receivers), w_edge_out,
            send, recv,
        )
        + [heads],
        hbm=range(10),
        scratch=[
            vmem(halo_lists.shape, jnp.int32), vmem((width, width), BF16),
            vmem((1, cedge_count), jnp.int32), vmem((1, cedge_count), jnp.int32), dma((10,)),
        ],
        flops=edge_count * square,
    )
    from_even, from_odd = pair(to_even, 0), pair(to_odd, 1)
    new_coarse, sums = call(
        coarse_kernel, "coarse", (like(coarse_edges), blocks),
        [lat, cedges, coarse_part, gather, picks, w_ends, w_out],
    )
    got = lax.all_to_all(sums, GROUP_AXES, 0, 0, axis_index_groups=[order(group, sub)])
    new_edges, new_coarse, rest, agg, node_part, wn_agg, wn_out = call(
        fine_kernel,
        "fine",
        (
            like(edge_latents),
            like(coarse_edges),
            like(node_latents),
            shape((TOP, width), F32),
            shape((TOP, width), F32),
            shape((width, width), BF16),
            like(w_node_out),
        ),
        [from_even, nodes, from_odd, w_ends, w_out, send, recv, new_coarse]
        + in_hbm(edge_latents, w_edge_in, w_node_in, w_node_out)
        + [sums],
        hbm=range(8, 13),
        out_specs=[ANY] * 2 + [VMEM] * 5,
        scratch=[
            vmem(edge_latents.shape, BF16), vmem((width, width), BF16), vmem((width, width), BF16),
            vmem(edge_latents.shape, BF16), dma((5,)), dma((2,)),
        ],
        flops=64 * edge_count * square,
    )
    (new_nodes,) = call(
        top_kernel, "top", (like(node_latents),), [got, agg, node_part, nodes, wn_agg, wn_out, rest], out_specs=[ANY],
        scratch=[vmem((TOP, width), BF16), dma((2,))],
    )
    return (new_nodes, new_edges, new_coarse)


def solution(mesh):
    rows = P(("parts", "patch", "sub"), None)
    ids = P(("parts", "patch", "sub"))
    in_specs = (
        rows, rows, rows, P(), P(), P(), P(), ids, ids, P(("parts", "patch", "sub"), None, None), ids, ids,
    )
    return jax.shard_map(body, mesh=mesh, in_specs=in_specs, out_specs=(rows, rows, rows), check_vma=False)
```
